32 devices in a mesh: island: 2 (over y), blk: 4 (over z), sub: 2 (over x), pair: 2 (over core).
Axes of the slice: x: 2, y: 2, z: 4, core: 2. Of those that a mesh axis runs over, the one named last changes fastest.
Arguments:
- embeddings: bfloat16 [6144, 768], P(('island', 'blk', 'sub', 'pair')), parts along dimension 0, may hold values from -6 to 6
- group_of: int32 [6144, 1], P(('island', 'blk', 'sub', 'pair')), parts along dimension 0, may hold values from 0 to 3; in each aligned block of 192 rows (0 to 191, 192 to 383, ...) at most 96 rows name the same one
- cluster_id: int32 [6144], P(('island', 'blk', 'sub', 'pair')), parts along dimension 0, may hold values from 0 to 47
Outputs:
- neighbour_mean: bfloat16 [6144, 768], P(('island', 'blk', 'sub', 'pair')), parts along dimension 0
The draws below stay inside these ranges and needn't reach their ends.
There are 2 independent parts, one for each index of `island`. The reference program is written for one: setup_inputs(seed, part) draws one part's arguments, and reference() takes and returns one part's arrays. A program takes and returns all parts, laid end to end along the dimension named above; each array names one. Nothing has to cross between parts.
Inputs may be any that keep to these rules, and one draw needn't show every extreme that they name: `group_of`: among the rows of one device, at most 96 name the same group; this bound is reached in every draw.
All inputs are finite; a program needn't handle non-finite values.
Results may differ from the reference program's by a relative error of at most 0.0045.
Values may be sent and summed in bfloat16 or wider, within the bound.
No kernel may reach another device: no remote copies, remote signals or barrier semaphores. Data moves between devices by JAX's collectives and lax.ppermute only.
A program may use at most 64 MiB of HBM per device.

```python
import math
import jax
import jax.numpy as jnp
import numpy as np
from jax import lax

D = 768
ROWS_DEV = 192
GROUPS = 4
CAP = 96
CLUSTERS = 48
ROWS = 3072


def with_ends(values, key, smallest, top_value):
    index_at = [jax.random.randint(jax.random.fold_in(key, axis), (), 0, length) for axis, length in enumerate(values.shape)]
    widest = values.shape.index(max(values.shape))
    beside = index_at[:widest] + [(index_at[widest] + 1) % values.shape[widest]] + index_at[widest + 1:]
    return values.at[tuple(index_at)].set(smallest).at[tuple(beside)].set(top_value)


def block_scale(stream_key, dims, pieces, low, top_value):
    def one(position, blocks):
        steps = jax.random.uniform(jax.random.fold_in(jax.random.fold_in(stream_key, 6), position), (blocks,), jnp.float32, low / len(pieces), top_value / len(pieces))
        return jnp.repeat(jnp.exp(steps), dims[position] // blocks).reshape((-1,) + (1,) * (len(dims) - position - 1))

    gain = one(*pieces[0])
    for cut in pieces[1:]:
        gain = gain * one(*cut)
    return gain


def deal_out(stream_key, own, number, rows, number_of, top, most, skew):
    sequence = jax.random.permutation(stream_key, number_of)
    packed, ordinary = load_shares(number_of, rows * top, most, skew, True), load_shares(number_of, rows * top, most, skew, False)
    places = jnp.arange(number_of)

    def named(tallies, rotation):
        used = int((tallies > 0).sum())
        fixed = max(1, used // 4)
        passed = fixed + (places - fixed + rotation * (used - fixed)) % max(1, number_of - fixed)
        return jnp.zeros((number_of,), jnp.int32).at[sequence[jnp.where(places < fixed, places, passed)]].set(jnp.asarray(tallies, jnp.int32))

    tallies = jnp.where(number % 4 == 0, named(packed, number // 4), named(ordinary, number - number // 4 - 1))
    mixed = jax.random.permutation(jax.random.fold_in(own, 3), number_of)
    donor, taker = mixed[0:number_of // 2 * 2:2], mixed[1:number_of // 2 * 2:2]
    margin = jnp.minimum(tallies[donor] - 1, most - tallies[taker]) // 2
    margin = jnp.where((donor == sequence[0]) | (taker == sequence[0]) | (tallies[taker] == 0), 0, jnp.maximum(margin, 0))
    passed = jax.random.randint(jax.random.fold_in(own, 4), (number_of // 2,), 0, 1 << 20) % (margin + 1)
    tallies = tallies.at[donor].add(-passed).at[taker].add(passed)
    items = jnp.searchsorted(jnp.cumsum(tallies), jnp.arange(rows * top), side="right").astype(jnp.int32)
    table = items.reshape(top, rows).T
    table = table[jax.random.permutation(jax.random.fold_in(own, 1), rows)]
    rotation = jax.random.randint(jax.random.fold_in(own, 2), (rows, 1), 0, top)
    return jnp.take_along_axis(table, (jnp.arange(top)[None, :] + rotation) % top, axis=1)


def load_shares(number_of, total, reach, skew, full):
    portions = [(1 << 20) // math.isqrt(grade ** skew) + 1 for grade in range(1, number_of + 1)]
    largest = reach if full else min(reach, max(-(-total // number_of), total * portions[0] // sum(portions)))
    least = 1 if total - largest >= number_of - 1 else 0
    given, surplus = [largest] + [least] * (number_of - 1), total - largest - least * (number_of - 1)
    while surplus > 0:
        free = [i for i in range(1, number_of) if given[i] < largest] or [i for i in range(1, number_of) if given[i] < reach]
        mass, remaining = sum([portions[i] for i in free]), surplus
        for i in free:
            more = min(reach - given[i], max(1, remaining * portions[i] // mass), surplus)
            given[i] = given[i] + more
            surplus = surplus - more
    return np.array(given)


def noise(rng, extent, scale, reach, shards=(), held_as=jnp.bfloat16):
    level = block_scale(rng, extent, shards, -0.22, 0.18) if shards else 1.0
    entries = jax.random.normal(rng, extent, jnp.float32) * scale * level
    return jnp.minimum(jnp.maximum(entries, -reach), reach).astype(held_as)


def setup_inputs(seed: int = 0, part: int = 0) -> dict:
    arg_keys = jax.random.split(jax.random.key(seed), 4)
    own_keys = jax.random.split(jax.random.fold_in(arg_keys[3], part), 4)
    embeddings = noise(own_keys[0], (ROWS, D), 1.0, 6.0, ((0, 16),))
    group_of_keys = jax.random.split(jax.random.fold_in(own_keys[1], 1), ROWS // ROWS_DEV)
    group_of_turns = jax.random.permutation(jax.random.fold_in(own_keys[1], 3), ROWS // ROWS_DEV)
    group_of = jax.vmap(lambda own, number: deal_out(jax.random.fold_in(own_keys[1], 2), own, number, ROWS_DEV, GROUPS, 1, CAP, 2))(group_of_keys, group_of_turns).reshape((ROWS, 1))
    cluster_id = with_ends(jax.random.randint(own_keys[2], (ROWS,), 0, CLUSTERS), jax.random.fold_in(own_keys[2], 1), 0, CLUSTERS - 1).astype(jnp.int32)
    return dict(embeddings=embeddings, group_of=group_of, cluster_id=cluster_id)


def reference(embeddings, group_of, cluster_id):
    total = embeddings.shape[0]
    blocksize = math.gcd(total, 512)
    wide = embeddings.astype(jnp.float32)
    scales = lax.rsqrt(lax.optimization_barrier(jnp.sum(wide * wide, axis=1)) + 1e-06)
    groups = group_of[:, 0]

    def one_block(start):
        rows_here = lax.dynamic_slice_in_dim(embeddings, start, blocksize, 0)
        scale_here = lax.dynamic_slice_in_dim(scales, start, blocksize, 0)
        group_here = lax.dynamic_slice_in_dim(groups, start, blocksize, 0)
        clust_here = lax.dynamic_slice_in_dim(cluster_id, start, blocksize, 0)
        grams = lax.dot_general(rows_here, embeddings, (((1,), (1,)), ((), ())), preferred_element_type=jnp.float32)
        cosine = grams * scale_here[:, None] * scales[None, :]
        same = (group_here[:, None] == groups[None, :]) & (clust_here[:, None] == cluster_id[None, :])
        weight = jax.nn.sigmoid(8.0 * cosine - 2.0) * same.astype(jnp.float32)
        numer = jnp.dot(weight.astype(jnp.bfloat16), embeddings, preferred_element_type=jnp.float32)
        denom = lax.optimization_barrier(jnp.sum(weight, axis=1))
        return (numer / denom[:, None]).astype(jnp.bfloat16)
    starts = (jnp.arange(total // blocksize) * blocksize).astype(jnp.int32)
    result = lax.map(one_block, starts)
    return result.reshape(total, embeddings.shape[1])
```

```python
import functools

import jax
import jax.numpy as jnp
from jax import lax
from jax.experimental import pallas as pl
from jax.experimental.pallas import tpu as pltpu
from jax.sharding import PartitionSpec as P

F32 = jnp.float32
BF16 = jnp.bfloat16
VMEM_BYTES = 24 * 1024 * 1024
GATHER_LIMIT = 8 * 1024 * 1024


def unit_scale(rows_in):
    wide = rows_in.astype(F32)
    return lax.rsqrt(jnp.sum(wide * wide, axis=1) + 1e-06)


def tile_weights(left_rows, left_clust, left_scale, right_rows, right_clust, right_scale):
    grams = lax.dot_general(
        left_rows, right_rows, (((1,), (1,)), ((), ())), preferred_element_type=F32
    )
    cosine = grams * left_scale[:, None] * right_scale[None, :]
    same = (left_clust[:, None] == right_clust[None, :]).astype(F32)
    return jax.nn.sigmoid(8.0 * cosine - 2.0) * same


def by_group(embeddings, group_of, cluster_id):
    rows_here, width = embeddings.shape
    groups = lax.axis_size("sub") * lax.axis_size("pair")
    capacity = 2 * rows_here // groups
    slots = groups * capacity
    target = group_of[:, 0]
    onehot = (target[:, None] == jnp.arange(groups, dtype=jnp.int32)[None, :]).astype(jnp.int32)
    position = jnp.sum((jnp.cumsum(onehot, axis=0) - onehot) * onehot, axis=1)
    send_rows = jnp.zeros((groups, capacity, width), BF16).at[target, position].set(embeddings)
    send_clust = jnp.full((groups, capacity), -1, jnp.int32).at[target, position].set(cluster_id)
    recv_rows, recv_clust = (
        lax.all_to_all(send_rows, ("sub", "pair"), split_axis=0, concat_axis=0, tiled=True),
        lax.all_to_all(send_clust, ("sub", "pair"), split_axis=0, concat_axis=0, tiled=True),
    )
    own_rows = recv_rows.reshape(slots, width)
    own_clust = recv_clust.reshape(slots)
    own_scale = unit_scale(own_rows)
    piece_rows = lax.all_gather(own_rows, "blk", axis=0, tiled=True)
    piece_clust = lax.all_gather(own_clust, "blk", axis=0, tiled=True)
    weight = tile_weights(
        own_rows, own_clust, own_scale, piece_rows, piece_clust, unit_scale(piece_rows)
    )
    numer = jnp.dot(weight.astype(BF16), piece_rows, preferred_element_type=F32)
    denom = jnp.sum(weight, axis=1)
    result = (numer / denom[:, None]).astype(BF16).reshape(groups, capacity, width)
    returned = lax.all_to_all(result, ("sub", "pair"), split_axis=0, concat_axis=0, tiled=True)
    return returned[target, position]


def diagonal(size):
    shape = (size, size)
    return lax.broadcasted_iota(jnp.int32, shape, 0) == lax.broadcasted_iota(jnp.int32, shape, 1)


def to_column(row):
    size = row.shape[1]
    return jnp.sum(jnp.where(diagonal(size), row, jnp.zeros_like(row)), axis=1, keepdims=True)


def to_row(column):
    size = column.shape[0]
    return jnp.sum(jnp.where(diagonal(size), column, jnp.zeros_like(column)), axis=0, keepdims=True)


def scale_column(rows):
    wide = rows.astype(F32)
    return lax.rsqrt(jnp.sum(wide * wide, axis=1, keepdims=True) + 1e-06)


def step_kernel(n_blocks, first, *refs):
    refs = list(refs)
    left = [refs.pop(0), refs.pop(0)]
    left_key = [refs.pop(0), refs.pop(0)]
    right = [refs.pop(0) for _ in range(n_blocks)]
    right_key = [refs.pop(0) for _ in range(n_blocks)]
    before = None if first else [refs.pop(0), refs.pop(0)]
    out = refs
    width = left[0].shape[1]
    right_rows = [ref[...] for ref in right]
    right_scale = [to_row(scale_column(rows)) for rows in right_rows]
    for side in range(2):
        rows = left[side][...]
        key = to_column(left_key[side][...])
        scale = scale_column(rows) * 4.0
        numer = None if first else before[side][:, :width]
        denom = None if first else before[side][:, width:]
        for block in range(n_blocks):
            grams = lax.dot_general(
                rows, right_rows[block], (((1,), (1,)), ((), ())), preferred_element_type=F32
            )
            half = jnp.tanh(grams * scale * right_scale[block] - 1.0)
            weight = jnp.where(key == right_key[block][...], 0.5 + 0.5 * half, 0.0)
            add = jnp.dot(weight.astype(BF16), right_rows[block], preferred_element_type=F32)
            add_denom = jnp.sum(weight, axis=1, keepdims=True)
            numer = add if numer is None else numer + add
            denom = add_denom if denom is None else denom + add_denom
        out[side][:, :width] = numer
        out[side][:, width:] = jnp.broadcast_to(denom, (rows.shape[0], 128))


def mean_kernel(own, other, out):
    width = out.shape[1]
    denom = own[:, width : width + 1] + other[:, width : width + 1]
    out[...] = ((own[:, :width] + other[:, :width]) / denom).astype(BF16)


def whole_in_vmem(count):
    return [pl.BlockSpec(memory_space=pltpu.VMEM)] * count


def step(left, left_key, right, right_key, before):
    rows_here, width = left[0].shape
    args = list(left) + list(left_key) + list(right) + list(right_key)
    aliases = {}
    if before is not None:
        aliases = {len(args): 0, len(args) + 1: 1}
        args += list(before)
    shape = jax.ShapeDtypeStruct((rows_here, width + 128), F32)
    return pl.pallas_call(
        functools.partial(step_kernel, len(right), before is None),
        out_shape=[shape, shape],
        in_specs=whole_in_vmem(len(args)),
        out_specs=whole_in_vmem(2),
        input_output_aliases=aliases,
        compiler_params=pltpu.CompilerParams(vmem_limit_bytes=VMEM_BYTES),
    )(*args)


def folded_ring(size):
    return [0] + list(range(1, size, 2)) + list(range(2, size, 2))[::-1]


def by_block(embeddings, group_of, cluster_id):
    rows_here, width = embeddings.shape
    n_blk = lax.axis_size("blk")
    order = folded_ring(n_blk)
    swap = [(0, 1), (1, 0)]

    def along(rows, steps):
        return lax.ppermute(
            rows, "blk", [(order[i], order[(i + steps) % n_blk]) for i in range(n_blk)]
        )

    def across(rows):
        return lax.ppermute(rows, "sub", swap)

    def along_across(rows, steps):
        perm = []
        for i in range(n_blk):
            for j in range(2):
                perm.append((order[i] * 2 + j, order[(i + steps) % n_blk] * 2 + 1 - j))
        return lax.ppermute(rows, ("blk", "sub"), perm)

    def other_core(rows):
        return lax.ppermute(rows, "pair", swap)

    key = group_of.reshape(1, rows_here) * 65536 + cluster_id.reshape(1, rows_here)
    left = (embeddings, other_core(embeddings))
    left_key = (key, other_core(key))
    moved = embeddings
    total = None
    for steps in range(n_blk):
        if steps:
            moved = along(moved, 1)
        right = (moved, across(moved))
        if steps:
            right_key = (along(key, steps), along_across(key, steps))
        else:
            right_key = (key, across(key))
        total = step(left, left_key, right, right_key, total)
    own, others = total
    back = other_core(others)
    return pl.pallas_call(
        mean_kernel,
        out_shape=jax.ShapeDtypeStruct((rows_here, width), BF16),
        in_specs=whole_in_vmem(2),
        out_specs=pl.BlockSpec(memory_space=pltpu.VMEM),
        compiler_params=pltpu.CompilerParams(vmem_limit_bytes=VMEM_BYTES),
    )(own, back)


def per_device(embeddings, group_of, cluster_id):
    rows_here, width = embeddings.shape
    devices = lax.axis_size("blk") * lax.axis_size("sub") * lax.axis_size("pair")
    small = devices * rows_here * width * 2 <= GATHER_LIMIT
    if small and lax.axis_size("sub") == 2 and lax.axis_size("pair") == 2:
        return by_block(embeddings, group_of, cluster_id)
    return by_group(embeddings, group_of, cluster_id)


def solution(mesh):
    return jax.shard_map(
        per_device,
        mesh=mesh,
        in_specs=(
            P(("island", "blk", "sub", "pair"), None),
            P(("island", "blk", "sub", "pair"), None),
            P(("island", "blk", "sub", "pair")),
        ),
        out_specs=P(("island", "blk", "sub", "pair"), None),
        check_vma=False,
    )
```

```python
import functools

import jax
import jax.numpy as jnp
from jax import lax
from jax.experimental import pallas as pl
from jax.experimental.pallas import tpu as pltpu
from jax.sharding import PartitionSpec as P

F32 = jnp.float32
BF16 = jnp.bfloat16
VMEM_BYTES = 24 * 1024 * 1024
GATHER_LIMIT = 8 * 1024 * 1024


def unit_scale(rows_in):
    wide = rows_in.astype(F32)
    return lax.rsqrt(jnp.sum(wide * wide, axis=1) + 1e-06)


def tile_weights(left_rows, left_clust, left_scale, right_rows, right_clust, right_scale):
    grams = lax.dot_general(
        left_rows, right_rows, (((1,), (1,)), ((), ())), preferred_element_type=F32
    )
    cosine = grams * left_scale[:, None] * right_scale[None, :]
    same = (left_clust[:, None] == right_clust[None, :]).astype(F32)
    return jax.nn.sigmoid(8.0 * cosine - 2.0) * same


def by_group(embeddings, group_of, cluster_id):
    rows_here, width = embeddings.shape
    groups = lax.axis_size("sub") * lax.axis_size("pair")
    capacity = 2 * rows_here // groups
    slots = groups * capacity
    target = group_of[:, 0]
    onehot = (target[:, None] == jnp.arange(groups, dtype=jnp.int32)[None, :]).astype(jnp.int32)
    position = jnp.sum((jnp.cumsum(onehot, axis=0) - onehot) * onehot, axis=1)
    send_rows = jnp.zeros((groups, capacity, width), BF16).at[target, position].set(embeddings)
    send_clust = jnp.full((groups, capacity), -1, jnp.int32).at[target, position].set(cluster_id)
    recv_rows, recv_clust = (
        lax.all_to_all(send_rows, ("sub", "pair"), split_axis=0, concat_axis=0, tiled=True),
        lax.all_to_all(send_clust, ("sub", "pair"), split_axis=0, concat_axis=0, tiled=True),
    )
    own_rows = recv_rows.reshape(slots, width)
    own_clust = recv_clust.reshape(slots)
    own_scale = unit_scale(own_rows)
    piece_rows = lax.all_gather(own_rows, "blk", axis=0, tiled=True)
    piece_clust = lax.all_gather(own_clust, "blk", axis=0, tiled=True)
    weight = tile_weights(
        own_rows, own_clust, own_scale, piece_rows, piece_clust, unit_scale(piece_rows)
    )
    numer = jnp.dot(weight.astype(BF16), piece_rows, preferred_element_type=F32)
    denom = jnp.sum(weight, axis=1)
    result = (numer / denom[:, None]).astype(BF16).reshape(groups, capacity, width)
    returned = lax.all_to_all(result, ("sub", "pair"), split_axis=0, concat_axis=0, tiled=True)
    return returned[target, position]


def diagonal(size):
    shape = (size, size)
    return lax.broadcasted_iota(jnp.int32, shape, 0) == lax.broadcasted_iota(jnp.int32, shape, 1)


def to_column(row):
    size = row.shape[1]
    return jnp.sum(jnp.where(diagonal(size), row, jnp.zeros_like(row)), axis=1, keepdims=True)


def to_row(column):
    size = column.shape[0]
    return jnp.sum(jnp.where(diagonal(size), column, jnp.zeros_like(column)), axis=0, keepdims=True)


def scale_column(rows):
    wide = rows.astype(F32)
    return lax.rsqrt(jnp.sum(wide * wide, axis=1, keepdims=True) + 1e-06)


def pack_kernel(rows, group, cluster, whole, first, second):
    rows_here, width = rows.shape
    half = rows_here // 2
    line = lax.broadcasted_iota(jnp.int32, (8, rows_here), 0)
    named = jnp.where(line == 0, group[...], jnp.where(line == 1, cluster[...], 0))
    named = named.astype(F32).astype(BF16)
    whole[:rows_here, :] = rows[...]
    whole[rows_here:, :] = jnp.zeros((8, width), BF16)
    whole[rows_here:, :rows_here] = named
    first[:half, :] = rows[:half, :]
    first[half:, :] = jnp.zeros((8, width), BF16)
    first[half:, :rows_here] = named
    second[...] = rows[half:, :]


def key_row(named):
    wide = named.astype(F32)
    return wide[0:1, :] * 256.0 + wide[1:2, :]


def from_whole(ref):
    rows_here = ref.shape[0] - 8
    return ref[:rows_here, :], key_row(ref[rows_here:, :rows_here])


def from_halves(first, second):
    half = second.shape[0]
    rows = jnp.concatenate([first[:half, :], second[...]], axis=0)
    return rows, key_row(first[half:, : 2 * half])


def add_blocks(left, blocks, numer, denom):
    rows, key = left
    key = to_column(key)
    scale = scale_column(rows) * 4.0
    for right_rows, right_key, right_scale in blocks:
        grams = lax.dot_general(
            rows, right_rows, (((1,), (1,)), ((), ())), preferred_element_type=F32
        )
        half = jnp.tanh(grams * scale * right_scale - 1.0)
        weight = jnp.where(key == right_key, 0.5 + 0.5 * half, 0.0)
        add = jnp.dot(weight.astype(BF16), right_rows, preferred_element_type=F32)
        add_denom = jnp.sum(weight, axis=1, keepdims=True)
        numer = add if numer is None else numer + add
        denom = add_denom if denom is None else denom + add_denom
    return numer, denom


def with_scale(block):
    rows, key = block
    return rows, key, to_row(scale_column(rows))


def step_kernel(n_blocks, first, *refs):
    refs = list(refs)
    left = [from_whole(refs.pop(0)), from_whole(refs.pop(0))]
    blocks = [with_scale(left[0])] if first else []
    for _ in range(n_blocks):
        blocks.append(with_scale(from_halves(refs.pop(0), refs.pop(0))))
    before = None if first else [refs.pop(0), refs.pop(0)]
    width = left[0][0].shape[1]
    for side in range(2):
        numer = None if first else before[side][:, :width]
        denom = None if first else before[side][:, width : width + 1]
        numer, denom = add_blocks(left[side], blocks, numer, denom)
        refs[side][:, :width] = numer
        refs[side][:, width:] = jnp.broadcast_to(denom, (numer.shape[0], 128))


def last_kernel(own, first, second, first_other, second_other, mine, theirs, out):
    width = out.shape[1]
    blocks = [
        with_scale(from_halves(first, second)),
        with_scale(from_halves(first_other, second_other)),
    ]
    numer = mine[:, :width] + theirs[:, :width]
    denom = mine[:, width : width + 1] + theirs[:, width : width + 1]
    numer, denom = add_blocks(from_whole(own), blocks, numer, denom)
    out[...] = (numer / denom).astype(BF16)


def whole_in_vmem(count):
    return [pl.BlockSpec(memory_space=pltpu.VMEM)] * count


def call(kernel, shapes, args, aliases={}):
    return pl.pallas_call(
        kernel,
        out_shape=shapes,
        in_specs=whole_in_vmem(len(args)),
        out_specs=whole_in_vmem(len(shapes)),
        input_output_aliases=aliases,
        compiler_params=pltpu.CompilerParams(vmem_limit_bytes=VMEM_BYTES),
    )(*args)


def step(left, right, before):
    rows_here, width = left[0].shape
    args = list(left) + [half for block in right for half in block]
    aliases = {}
    if before is not None:
        aliases = {len(args): 0, len(args) + 1: 1}
        args += list(before)
    shape = jax.ShapeDtypeStruct((rows_here - 8, width + 128), F32)
    return call(
        functools.partial(step_kernel, len(right), before is None), [shape, shape], args, aliases
    )


def folded_ring(size):
    return [0] + list(range(1, size, 2)) + list(range(2, size, 2))[::-1]


def together(*arrays):
    return lax.optimization_barrier(arrays)


def by_block(embeddings, group_of, cluster_id):
    rows_here, width = embeddings.shape
    half = rows_here // 2
    n_blk = lax.axis_size("blk")
    order = folded_ring(n_blk)
    swap = [(0, 1), (1, 0)]

    def along(rows):
        return lax.ppermute(rows, "blk", [(order[i - 1], order[i]) for i in range(n_blk)])

    def across(rows):
        return lax.ppermute(rows, "sub", swap)

    def other_core(rows):
        return lax.ppermute(rows, "pair", swap)

    whole, first, second = call(
        pack_kernel,
        [
            jax.ShapeDtypeStruct((rows_here + 8, width), BF16),
            jax.ShapeDtypeStruct((half + 8, width), BF16),
            jax.ShapeDtypeStruct((half, width), BF16),
        ],
        [embeddings, group_of.reshape(1, rows_here), cluster_id.reshape(1, rows_here)],
    )
    along_by = [(first, second)]
    across_by = []
    for s in range(1, n_blk):
        moved = [along(piece) for piece in along_by[-1]]
        swapped = [across(piece) for piece in along_by[-1]]
        pairs = [together(m, w) for m, w in zip(moved, swapped)]
        along_by.append(tuple(pair[0] for pair in pairs))
        across_by.append(tuple(pair[1] for pair in pairs))
    left = (whole, other_core(whole))
    early = n_blk // 2
    total = step(left, across_by[:early] + along_by[1:early], None)
    far, total = together(along_by[-1][0], total)
    last_first = across(far)
    last_second = along(across_by[-1][1])
    mine, theirs = step(left, across_by[early:] + along_by[early:], total)
    last_first, last_second, theirs = together(last_first, last_second, other_core(theirs))
    (out,) = call(
        last_kernel,
        [jax.ShapeDtypeStruct((rows_here, width), BF16)],
        [
            whole,
            last_first,
            last_second,
            other_core(last_first),
            other_core(last_second),
            mine,
            theirs,
        ],
    )
    return out


def per_device(embeddings, group_of, cluster_id):
    rows_here, width = embeddings.shape
    devices = lax.axis_size("blk") * lax.axis_size("sub") * lax.axis_size("pair")
    small = devices * rows_here * width * 2 <= GATHER_LIMIT
    if small and lax.axis_size("sub") == 2 and lax.axis_size("pair") == 2:
        return by_block(embeddings, group_of, cluster_id)
    return by_group(embeddings, group_of, cluster_id)


def solution(mesh):
    return jax.shard_map(
        per_device,
        mesh=mesh,
        in_specs=(
            P(("island", "blk", "sub", "pair"), None),
            P(("island", "blk", "sub", "pair"), None),
            P(("island", "blk", "sub", "pair")),
        ),
        out_specs=P(("island", "blk", "sub", "pair"), None),
        check_vma=False,
    )
```

```python
import functools

import jax
import jax.numpy as jnp
from jax import lax
from jax.experimental import pallas as pl
from jax.experimental.pallas import tpu as pltpu
from jax.sharding import PartitionSpec as P

F32 = jnp.float32
BF16 = jnp.bfloat16
VMEM_BYTES = 24 * 1024 * 1024
PACK_BYTES = 48 * 1024 * 1024
GATHER_LIMIT = 8 * 1024 * 1024


def unit_scale(rows_in):
    wide = rows_in.astype(F32)
    return lax.rsqrt(jnp.sum(wide * wide, axis=1) + 1e-06)


def tile_weights(left_rows, left_clust, left_scale, right_rows, right_clust, right_scale):
    grams = lax.dot_general(
        left_rows, right_rows, (((1,), (1,)), ((), ())), preferred_element_type=F32
    )
    cosine = grams * left_scale[:, None] * right_scale[None, :]
    same = (left_clust[:, None] == right_clust[None, :]).astype(F32)
    return jax.nn.sigmoid(8.0 * cosine - 2.0) * same


def by_group(embeddings, group_of, cluster_id):
    rows_here, width = embeddings.shape
    groups = lax.axis_size("sub") * lax.axis_size("pair")
    capacity = 2 * rows_here // groups
    slots = groups * capacity
    target = group_of[:, 0]
    onehot = (target[:, None] == jnp.arange(groups, dtype=jnp.int32)[None, :]).astype(jnp.int32)
    position = jnp.sum((jnp.cumsum(onehot, axis=0) - onehot) * onehot, axis=1)
    send_rows = jnp.zeros((groups, capacity, width), BF16).at[target, position].set(embeddings)
    send_clust = jnp.full((groups, capacity), -1, jnp.int32).at[target, position].set(cluster_id)
    recv_rows, recv_clust = (
        lax.all_to_all(send_rows, ("sub", "pair"), split_axis=0, concat_axis=0, tiled=True),
        lax.all_to_all(send_clust, ("sub", "pair"), split_axis=0, concat_axis=0, tiled=True),
    )
    own_rows = recv_rows.reshape(slots, width)
    own_clust = recv_clust.reshape(slots)
    own_scale = unit_scale(own_rows)
    piece_rows = lax.all_gather(own_rows, "blk", axis=0, tiled=True)
    piece_clust = lax.all_gather(own_clust, "blk", axis=0, tiled=True)
    weight = tile_weights(
        own_rows, own_clust, own_scale, piece_rows, piece_clust, unit_scale(piece_rows)
    )
    numer = jnp.dot(weight.astype(BF16), piece_rows, preferred_element_type=F32)
    denom = jnp.sum(weight, axis=1)
    result = (numer / denom[:, None]).astype(BF16).reshape(groups, capacity, width)
    returned = lax.all_to_all(result, ("sub", "pair"), split_axis=0, concat_axis=0, tiled=True)
    return returned[target, position]


def diagonal(size):
    shape = (size, size)
    return lax.broadcasted_iota(jnp.int32, shape, 0) == lax.broadcasted_iota(jnp.int32, shape, 1)


def to_column(row):
    size = row.shape[1]
    return jnp.sum(jnp.where(diagonal(size), row, jnp.zeros_like(row)), axis=1, keepdims=True)


def to_row(column):
    size = column.shape[0]
    return jnp.sum(jnp.where(diagonal(size), column, jnp.zeros_like(column)), axis=0, keepdims=True)


def scale_column(rows):
    wide = rows.astype(F32)
    return lax.rsqrt(jnp.sum(wide * wide, axis=1, keepdims=True) + 1e-06)


def pack_kernel(rows, group, cluster, whole, first, second, group_here, cluster_here, sems):
    rows_here, width = rows.shape
    half = rows_here // 2
    copies = [
        pltpu.make_async_copy(group, group_here, sems.at[0]),
        pltpu.make_async_copy(cluster, cluster_here, sems.at[1]),
        pltpu.make_async_copy(rows.at[:half, :], first.at[:half, :], sems.at[2]),
        pltpu.make_async_copy(rows.at[half:, :], second, sems.at[3]),
        pltpu.make_async_copy(rows, whole.at[:rows_here, :], sems.at[4]),
    ]
    for copy in copies:
        copy.start()
    copies[0].wait()
    copies[1].wait()
    line = lax.broadcasted_iota(jnp.int32, (8, rows_here), 0)
    named = jnp.where(line == 0, group_here[...], jnp.where(line == 1, cluster_here[...], 0))
    named = named.astype(F32).astype(BF16)
    for out, top in ((whole, rows_here), (first, half)):
        out[top:, :] = jnp.zeros((8, width), BF16)
        out[top:, :rows_here] = named
    for copy in copies[2:]:
        copy.wait()


def key_row(named):
    wide = named.astype(F32)
    return wide[0:1, :] * 256.0 + wide[1:2, :]


def from_whole(ref):
    rows_here = ref.shape[0] - 8
    return ref[:rows_here, :], key_row(ref[rows_here:, :rows_here])


def from_halves(first, second):
    half = second.shape[0]
    rows = jnp.concatenate([first[:half, :], second[...]], axis=0)
    return rows, key_row(first[half:, : 2 * half])


def add_blocks(left, blocks, numer, denom):
    rows, key = left
    key = to_column(key)
    scale = scale_column(rows) * 4.0
    for right_rows, right_key, right_scale in blocks:
        grams = lax.dot_general(
            rows, right_rows, (((1,), (1,)), ((), ())), preferred_element_type=F32
        )
        half = jnp.tanh(grams * scale * right_scale - 1.0)
        weight = jnp.where(key == right_key, 0.5 + 0.5 * half, 0.0)
        add = jnp.dot(weight.astype(BF16), right_rows, preferred_element_type=F32)
        add_denom = jnp.sum(weight, axis=1, keepdims=True)
        numer = add if numer is None else numer + add
        denom = add_denom if denom is None else denom + add_denom
    return numer, denom


def with_scale(block):
    rows, key = block
    return rows, key, to_row(scale_column(rows))


def take_blocks(refs, count):
    return [with_scale(from_halves(refs.pop(0), refs.pop(0))) for _ in range(count)]


def add_side(left, blocks, before, out):
    width = left[0].shape[1]
    numer = None if before is None else before[:, :width]
    denom = None if before is None else before[:, width : width + 1]
    numer, denom = add_blocks(left, blocks, numer, denom)
    out[:, :width] = numer
    out[:, width:] = jnp.broadcast_to(denom, (numer.shape[0], 128))


def start_kernel(n_blocks, own, other, *refs):
    refs = list(refs)
    left = [from_whole(own), from_whole(other)]
    blocks = [with_scale(left[0])] + take_blocks(refs, n_blocks)
    for side in range(2):
        add_side(left[side], blocks, None, refs[side])


def both_kernel(n_blocks, own, other, *refs):
    refs = list(refs)
    blocks = take_blocks(refs, n_blocks)
    for side, left in enumerate((own, other)):
        add_side(from_whole(left), blocks, refs[side], refs[2 + side])


def one_kernel(n_blocks, left, *refs):
    refs = list(refs)
    blocks = take_blocks(refs, n_blocks)
    add_side(from_whole(left), blocks, refs[0], refs[1])


def mean_kernel(mine, theirs, out):
    width = out.shape[1]
    denom = mine[:, width : width + 1] + theirs[:, width : width + 1]
    out[...] = ((mine[:, :width] + theirs[:, :width]) / denom).astype(BF16)


def whole_in_vmem(count):
    return [pl.BlockSpec(memory_space=pltpu.VMEM)] * count


def call(kernel, shapes, args, aliases={}):
    return pl.pallas_call(
        kernel,
        out_shape=shapes,
        in_specs=whole_in_vmem(len(args)),
        out_specs=whole_in_vmem(len(shapes)),
        input_output_aliases=aliases,
        compiler_params=pltpu.CompilerParams(vmem_limit_bytes=VMEM_BYTES),
    )(*args)


def pack(embeddings, group_of, cluster_id):
    rows_here, width = embeddings.shape
    half = rows_here // 2
    line = (1, rows_here)
    return pl.pallas_call(
        pack_kernel,
        out_shape=[
            jax.ShapeDtypeStruct((rows_here + 8, width), BF16),
            jax.ShapeDtypeStruct((half + 8, width), BF16),
            jax.ShapeDtypeStruct((half, width), BF16),
        ],
        in_specs=[pl.BlockSpec(memory_space=pltpu.HBM)] * 3,
        out_specs=whole_in_vmem(3),
        scratch_shapes=[
            pltpu.VMEM(line, jnp.int32),
            pltpu.VMEM(line, jnp.int32),
            pltpu.SemaphoreType.DMA((5,)),
        ],
        compiler_params=pltpu.CompilerParams(vmem_limit_bytes=PACK_BYTES),
    )(embeddings, group_of.reshape(line), cluster_id.reshape(line))


def start_both(left, right):
    rows_here, width = left[0].shape
    shape = jax.ShapeDtypeStruct((rows_here - 8, width + 128), F32)
    args = list(left) + [half for block in right for half in block]
    return call(functools.partial(start_kernel, len(right)), [shape, shape], args)


def add_both(left, right, before):
    args = list(left) + [half for block in right for half in block] + list(before)
    at = len(args) - 2
    shapes = [jax.ShapeDtypeStruct(total.shape, F32) for total in before]
    return call(
        functools.partial(both_kernel, len(right)), shapes, args, {at: 0, at + 1: 1}
    )


def add_one(left, right, before):
    args = [left] + [half for block in right for half in block] + [before]
    shapes = [jax.ShapeDtypeStruct(before.shape, F32)]
    return call(functools.partial(one_kernel, len(right)), shapes, args, {len(args) - 1: 0})[0]


def folded_ring(size):
    return [0] + list(range(1, size, 2)) + list(range(2, size, 2))[::-1]


def together(*arrays):
    return lax.optimization_barrier(arrays)


def by_block(embeddings, group_of, cluster_id):
    rows_here, width = embeddings.shape
    n_blk = lax.axis_size("blk")
    order = folded_ring(n_blk)
    swap = [(0, 1), (1, 0)]

    def along(rows):
        return lax.ppermute(rows, "blk", [(order[i - 1], order[i]) for i in range(n_blk)])

    def across(rows):
        return lax.ppermute(rows, "sub", swap)

    def other_core(rows):
        return lax.ppermute(rows, "pair", swap)

    whole, first, second = pack(embeddings, group_of, cluster_id)
    along_by = [(first, second)]
    across_by = []
    for s in range(1, n_blk):
        moved = [along(piece) for piece in along_by[-1]]
        swapped = [across(piece) for piece in along_by[-1]]
        pairs = [together(m, w) for m, w in zip(moved, swapped)]
        along_by.append(tuple(pair[0] for pair in pairs))
        across_by.append(tuple(pair[1] for pair in pairs))
    left = (whole, other_core(whole))
    total = start_both(left, across_by[:-1] + along_by[1:-1])
    far_first, mine, theirs = together(along_by[-1][0], *total)
    last = (across(far_first), along(across_by[-1][1]))
    mine, theirs = add_both(left, [across_by[-1], along_by[-1]], (mine, theirs))
    theirs = other_core(add_one(left[1], [last], theirs))
    mine = add_one(left[0], [last], mine)
    (out,) = call(
        mean_kernel, [jax.ShapeDtypeStruct((rows_here, width), BF16)], [mine, theirs]
    )
    return out


def per_device(embeddings, group_of, cluster_id):
    rows_here, width = embeddings.shape
    devices = lax.axis_size("blk") * lax.axis_size("sub") * lax.axis_size("pair")
    small = devices * rows_here * width * 2 <= GATHER_LIMIT
    if small and lax.axis_size("sub") == 2 and lax.axis_size("pair") == 2:
        return by_block(embeddings, group_of, cluster_id)
    return by_group(embeddings, group_of, cluster_id)


def solution(mesh):
    return jax.shard_map(
        per_device,
        mesh=mesh,
        in_specs=(
            P(("island", "blk", "sub", "pair"), None),
            P(("island", "blk", "sub", "pair"), None),
            P(("island", "blk", "sub", "pair")),
        ),
        out_specs=P(("island", "blk", "sub", "pair"), None),
        check_vma=False,
    )
```

```python
import functools

import jax
import jax.numpy as jnp
from jax import lax
from jax.experimental import pallas as pl
from jax.experimental.pallas import tpu as pltpu
from jax.sharding import PartitionSpec as P

F32 = jnp.float32
BF16 = jnp.bfloat16
VMEM_BYTES = 24 * 1024 * 1024
PACK_BYTES = 48 * 1024 * 1024
GATHER_LIMIT = 8 * 1024 * 1024


def unit_scale(rows_in):
    wide = rows_in.astype(F32)
    return lax.rsqrt(jnp.sum(wide * wide, axis=1) + 1e-06)


def tile_weights(left_rows, left_clust, left_scale, right_rows, right_clust, right_scale):
    grams = lax.dot_general(
        left_rows, right_rows, (((1,), (1,)), ((), ())), preferred_element_type=F32
    )
    cosine = grams * left_scale[:, None] * right_scale[None, :]
    same = (left_clust[:, None] == right_clust[None, :]).astype(F32)
    return jax.nn.sigmoid(8.0 * cosine - 2.0) * same


def by_group(embeddings, group_of, cluster_id):
    rows_here, width = embeddings.shape
    groups = lax.axis_size("sub") * lax.axis_size("pair")
    capacity = 2 * rows_here // groups
    slots = groups * capacity
    target = group_of[:, 0]
    onehot = (target[:, None] == jnp.arange(groups, dtype=jnp.int32)[None, :]).astype(jnp.int32)
    position = jnp.sum((jnp.cumsum(onehot, axis=0) - onehot) * onehot, axis=1)
    send_rows = jnp.zeros((groups, capacity, width), BF16).at[target, position].set(embeddings)
    send_clust = jnp.full((groups, capacity), -1, jnp.int32).at[target, position].set(cluster_id)
    recv_rows, recv_clust = (
        lax.all_to_all(send_rows, ("sub", "pair"), split_axis=0, concat_axis=0, tiled=True),
        lax.all_to_all(send_clust, ("sub", "pair"), split_axis=0, concat_axis=0, tiled=True),
    )
    own_rows = recv_rows.reshape(slots, width)
    own_clust = recv_clust.reshape(slots)
    own_scale = unit_scale(own_rows)
    piece_rows = lax.all_gather(own_rows, "blk", axis=0, tiled=True)
    piece_clust = lax.all_gather(own_clust, "blk", axis=0, tiled=True)
    weight = tile_weights(
        own_rows, own_clust, own_scale, piece_rows, piece_clust, unit_scale(piece_rows)
    )
    numer = jnp.dot(weight.astype(BF16), piece_rows, preferred_element_type=F32)
    denom = jnp.sum(weight, axis=1)
    result = (numer / denom[:, None]).astype(BF16).reshape(groups, capacity, width)
    returned = lax.all_to_all(result, ("sub", "pair"), split_axis=0, concat_axis=0, tiled=True)
    return returned[target, position]


def diagonal(size):
    shape = (size, size)
    return lax.broadcasted_iota(jnp.int32, shape, 0) == lax.broadcasted_iota(jnp.int32, shape, 1)


def to_column(row):
    size = row.shape[1]
    return jnp.sum(jnp.where(diagonal(size), row, jnp.zeros_like(row)), axis=1, keepdims=True)


def to_row(column):
    size = column.shape[0]
    return jnp.sum(jnp.where(diagonal(size), column, jnp.zeros_like(column)), axis=0, keepdims=True)


def scale_column(rows):
    wide = rows.astype(F32)
    return lax.rsqrt(jnp.sum(wide * wide, axis=1, keepdims=True) + 1e-06)


def pack_kernel(rows, group, cluster, whole, first, second, group_here, cluster_here, sems):
    rows_here, width = rows.shape
    half = rows_here // 2
    copies = [
        pltpu.make_async_copy(group, group_here, sems.at[0]),
        pltpu.make_async_copy(cluster, cluster_here, sems.at[1]),
        pltpu.make_async_copy(rows.at[:half, :], first.at[:half, :], sems.at[2]),
        pltpu.make_async_copy(rows.at[half:, :], second, sems.at[3]),
        pltpu.make_async_copy(rows, whole.at[:rows_here, :], sems.at[4]),
    ]
    for copy in copies:
        copy.start()
    copies[0].wait()
    copies[1].wait()
    line = lax.broadcasted_iota(jnp.int32, (8, rows_here), 0)
    named = jnp.where(line == 0, group_here[...], jnp.where(line == 1, cluster_here[...], 0))
    named = named.astype(F32).astype(BF16)
    for out, top in ((whole, rows_here), (first, half)):
        out[top:, :] = jnp.zeros((8, width), BF16)
        out[top:, :rows_here] = named
    for copy in copies[2:]:
        copy.wait()


def key_row(named):
    wide = named.astype(F32)
    return wide[0:1, :] * 256.0 + wide[1:2, :]


def from_whole(ref):
    rows_here = ref.shape[0] - 8
    return ref[:rows_here, :], key_row(ref[rows_here:, :rows_here])


def from_halves(first, second):
    half = second.shape[0]
    rows = jnp.concatenate([first[:half, :], second[...]], axis=0)
    return rows, key_row(first[half:, : 2 * half])


def add_blocks(left, blocks, numer, denom):
    rows, key = left
    key = to_column(key)
    scale = scale_column(rows) * 4.0
    for right_rows, right_key, right_scale in blocks:
        grams = lax.dot_general(
            rows, right_rows, (((1,), (1,)), ((), ())), preferred_element_type=F32
        )
        half = jnp.tanh(grams * scale * right_scale - 1.0)
        weight = jnp.where(key == right_key, 0.5 + 0.5 * half, 0.0)
        add = jnp.dot(weight.astype(BF16), right_rows, preferred_element_type=F32)
        add_denom = jnp.sum(weight, axis=1, keepdims=True)
        numer = add if numer is None else numer + add
        denom = add_denom if denom is None else denom + add_denom
    return numer, denom


def with_scale(block):
    rows, key = block
    return rows, key, to_row(scale_column(rows))


def take_blocks(refs, count):
    return [with_scale(from_halves(refs.pop(0), refs.pop(0))) for _ in range(count)]


def add_side(left, blocks, before, out):
    width = left[0].shape[1]
    numer = None if before is None else before[:, :width]
    denom = None if before is None else before[:, width : width + 1]
    numer, denom = add_blocks(left, blocks, numer, denom)
    out[:, :width] = numer
    out[:, width:] = jnp.broadcast_to(denom, (numer.shape[0], 128))


def start_kernel(n_blocks, own, other, *refs):
    refs = list(refs)
    left = [from_whole(own), from_whole(other)]
    blocks = [with_scale(left[0])] + take_blocks(refs, n_blocks)
    for side in range(2):
        add_side(left[side], blocks, None, refs[side])


def both_kernel(n_blocks, own, other, *refs):
    refs = list(refs)
    blocks = take_blocks(refs, n_blocks)
    for side, left in enumerate((own, other)):
        add_side(from_whole(left), blocks, refs[side], refs[2 + side])


def one_kernel(n_blocks, left, *refs):
    refs = list(refs)
    blocks = take_blocks(refs, n_blocks)
    add_side(from_whole(left), blocks, refs[0], refs[1])


def mean_kernel(mine, theirs, out):
    width = out.shape[1]
    denom = mine[:, width : width + 1] + theirs[:, width : width + 1]
    out[...] = ((mine[:, :width] + theirs[:, :width]) / denom).astype(BF16)


def whole_in_vmem(count):
    return [pl.BlockSpec(memory_space=pltpu.VMEM)] * count


def call(kernel, shapes, args, aliases={}):
    return pl.pallas_call(
        kernel,
        out_shape=shapes,
        in_specs=whole_in_vmem(len(args)),
        out_specs=whole_in_vmem(len(shapes)),
        input_output_aliases=aliases,
        compiler_params=pltpu.CompilerParams(vmem_limit_bytes=VMEM_BYTES),
    )(*args)


def pack(embeddings, group_of, cluster_id):
    rows_here, width = embeddings.shape
    half = rows_here // 2
    line = (1, rows_here)
    return pl.pallas_call(
        pack_kernel,
        out_shape=[
            jax.ShapeDtypeStruct((rows_here + 8, width), BF16),
            jax.ShapeDtypeStruct((half + 8, width), BF16),
            jax.ShapeDtypeStruct((half, width), BF16),
        ],
        in_specs=[pl.BlockSpec(memory_space=pltpu.HBM)] * 3,
        out_specs=whole_in_vmem(3),
        scratch_shapes=[
            pltpu.VMEM(line, jnp.int32),
            pltpu.VMEM(line, jnp.int32),
            pltpu.SemaphoreType.DMA((5,)),
        ],
        compiler_params=pltpu.CompilerParams(vmem_limit_bytes=PACK_BYTES),
    )(embeddings, group_of.reshape(line), cluster_id.reshape(line))


def start_both(left, right):
    rows_here, width = left[0].shape
    shape = jax.ShapeDtypeStruct((rows_here - 8, width + 128), F32)
    args = list(left) + [half for block in right for half in block]
    return call(functools.partial(start_kernel, len(right)), [shape, shape], args)


def add_both(left, right, before):
    args = list(left) + [half for block in right for half in block] + list(before)
    at = len(args) - 2
    shapes = [jax.ShapeDtypeStruct(total.shape, F32) for total in before]
    return call(
        functools.partial(both_kernel, len(right)), shapes, args, {at: 0, at + 1: 1}
    )


def add_one(left, right, before):
    args = [left] + [half for block in right for half in block] + [before]
    shapes = [jax.ShapeDtypeStruct(before.shape, F32)]
    return call(functools.partial(one_kernel, len(right)), shapes, args, {len(args) - 1: 0})[0]


def folded_ring(size):
    return [0] + list(range(1, size, 2)) + list(range(2, size, 2))[::-1]


def together(*arrays):
    return lax.optimization_barrier(arrays)


def by_block(embeddings, group_of, cluster_id):
    rows_here, width = embeddings.shape
    n_blk = lax.axis_size("blk")
    order = folded_ring(n_blk)
    swap = [(0, 1), (1, 0)]

    def along(rows):
        return lax.ppermute(rows, "blk", [(order[i - 1], order[i]) for i in range(n_blk)])

    def across(rows):
        return lax.ppermute(rows, "sub", swap)

    def other_core(rows):
        return lax.ppermute(rows, "pair", swap)

    whole, first, second = pack(embeddings, group_of, cluster_id)
    along_by = [(first, second)]
    across_by = []
    other = other_core(whole)
    in_flight = [other]
    for s in range(1, n_blk):
        pieces = along_by.pop()
        if s > 1:
            pieces = tuple(together(piece, in_flight.pop(0))[0] for piece in pieces)
        along_by += [pieces, tuple(along(piece) for piece in pieces)]
        across_by.append(tuple(across(piece) for piece in pieces))
        in_flight += across_by[-1]
    left = (whole, other)
    total = start_both(left, across_by[:-1] + along_by[1:-1])
    far_first, _, mine, theirs = together(along_by[-1][0], across_by[-1][0], *total)
    near_second, _ = together(across_by[-1][1], along_by[-1][1])
    last = (across(far_first), along(near_second))
    mine, theirs = add_both(left, [across_by[-1], along_by[-1]], (mine, theirs))
    theirs = other_core(add_one(left[1], [last], theirs))
    mine = add_one(left[0], [last], mine)
    (out,) = call(
        mean_kernel, [jax.ShapeDtypeStruct((rows_here, width), BF16)], [mine, theirs]
    )
    return out


def per_device(embeddings, group_of, cluster_id):
    rows_here, width = embeddings.shape
    devices = lax.axis_size("blk") * lax.axis_size("sub") * lax.axis_size("pair")
    small = devices * rows_here * width * 2 <= GATHER_LIMIT
    if small and lax.axis_size("sub") == 2 and lax.axis_size("pair") == 2:
        return by_block(embeddings, group_of, cluster_id)
    return by_group(embeddings, group_of, cluster_id)


def solution(mesh):
    return jax.shard_map(
        per_device,
        mesh=mesh,
        in_specs=(
            P(("island", "blk", "sub", "pair"), None),
            P(("island", "blk", "sub", "pair"), None),
            P(("island", "blk", "sub", "pair")),
        ),
        out_specs=P(("island", "blk", "sub", "pair"), None),
        check_vma=False,
    )
```

```python
import functools

import jax
import jax.numpy as jnp
from jax import lax
from jax.experimental import pallas as pl
from jax.experimental.pallas import tpu as pltpu
from jax.sharding import PartitionSpec as P

F32 = jnp.float32
BF16 = jnp.bfloat16
VMEM_BYTES = 24 * 1024 * 1024
PACK_BYTES = 48 * 1024 * 1024
GATHER_LIMIT = 8 * 1024 * 1024


def unit_scale(rows_in):
    wide = rows_in.astype(F32)
    return lax.rsqrt(jnp.sum(wide * wide, axis=1) + 1e-06)


def tile_weights(left_rows, left_clust, left_scale, right_rows, right_clust, right_scale):
    grams = lax.dot_general(
        left_rows, right_rows, (((1,), (1,)), ((), ())), preferred_element_type=F32
    )
    cosine = grams * left_scale[:, None] * right_scale[None, :]
    same = (left_clust[:, None] == right_clust[None, :]).astype(F32)
    return jax.nn.sigmoid(8.0 * cosine - 2.0) * same


def by_group(embeddings, group_of, cluster_id):
    rows_here, width = embeddings.shape
    groups = lax.axis_size("sub") * lax.axis_size("pair")
    capacity = 2 * rows_here // groups
    slots = groups * capacity
    target = group_of[:, 0]
    onehot = (target[:, None] == jnp.arange(groups, dtype=jnp.int32)[None, :]).astype(jnp.int32)
    position = jnp.sum((jnp.cumsum(onehot, axis=0) - onehot) * onehot, axis=1)
    send_rows = jnp.zeros((groups, capacity, width), BF16).at[target, position].set(embeddings)
    send_clust = jnp.full((groups, capacity), -1, jnp.int32).at[target, position].set(cluster_id)
    recv_rows, recv_clust = (
        lax.all_to_all(send_rows, ("sub", "pair"), split_axis=0, concat_axis=0, tiled=True),
        lax.all_to_all(send_clust, ("sub", "pair"), split_axis=0, concat_axis=0, tiled=True),
    )
    own_rows = recv_rows.reshape(slots, width)
    own_clust = recv_clust.reshape(slots)
    own_scale = unit_scale(own_rows)
    piece_rows = lax.all_gather(own_rows, "blk", axis=0, tiled=True)
    piece_clust = lax.all_gather(own_clust, "blk", axis=0, tiled=True)
    weight = tile_weights(
        own_rows, own_clust, own_scale, piece_rows, piece_clust, unit_scale(piece_rows)
    )
    numer = jnp.dot(weight.astype(BF16), piece_rows, preferred_element_type=F32)
    denom = jnp.sum(weight, axis=1)
    result = (numer / denom[:, None]).astype(BF16).reshape(groups, capacity, width)
    returned = lax.all_to_all(result, ("sub", "pair"), split_axis=0, concat_axis=0, tiled=True)
    return returned[target, position]


def diagonal(size):
    shape = (size, size)
    return lax.broadcasted_iota(jnp.int32, shape, 0) == lax.broadcasted_iota(jnp.int32, shape, 1)


def to_column(row):
    size = row.shape[1]
    return jnp.sum(jnp.where(diagonal(size), row, jnp.zeros_like(row)), axis=1, keepdims=True)


def to_row(column):
    size = column.shape[0]
    return jnp.sum(jnp.where(diagonal(size), column, jnp.zeros_like(column)), axis=0, keepdims=True)


def scale_column(rows):
    wide = rows.astype(F32)
    return lax.rsqrt(jnp.sum(wide * wide, axis=1, keepdims=True) + 1e-06)


def pack_kernel(rows, group, cluster, out, group_here, cluster_here, sems):
    rows_here, width = rows.shape
    copies = [
        pltpu.make_async_copy(group, group_here, sems.at[0]),
        pltpu.make_async_copy(cluster, cluster_here, sems.at[1]),
        pltpu.make_async_copy(rows, out.at[:rows_here, :], sems.at[2]),
    ]
    for copy in copies:
        copy.start()
    copies[0].wait()
    copies[1].wait()
    line = lax.broadcasted_iota(jnp.int32, (8, rows_here), 0)
    named = jnp.where(line == 0, group_here[...], jnp.where(line == 1, cluster_here[...], 0))
    out[rows_here:, :] = jnp.zeros((8, width), BF16)
    out[rows_here:, :rows_here] = named.astype(F32).astype(BF16)
    copies[2].wait()


def key_row(named):
    wide = named.astype(F32)
    return wide[0:1, :] * 256.0 + wide[1:2, :]


def from_whole(ref):
    rows_here = ref.shape[0] - 8
    return ref[:rows_here, :], key_row(ref[rows_here:, :rows_here])


def from_halves(first, second):
    half = first.shape[0]
    rows = jnp.concatenate([first[...], second[:half, :]], axis=0)
    return rows, key_row(second[half:, : 2 * half])


def add_blocks(left, blocks, numer, denom):
    rows, key = left
    key = to_column(key)
    scale = scale_column(rows) * 4.0
    for right_rows, right_key, right_scale in blocks:
        grams = lax.dot_general(
            rows, right_rows, (((1,), (1,)), ((), ())), preferred_element_type=F32
        )
        half = jnp.tanh(grams * scale * right_scale - 1.0)
        weight = jnp.where(key == right_key, 0.5 + 0.5 * half, 0.0)
        add = jnp.dot(weight.astype(BF16), right_rows, preferred_element_type=F32)
        add_denom = jnp.sum(weight, axis=1, keepdims=True)
        numer = add if numer is None else numer + add
        denom = add_denom if denom is None else denom + add_denom
    return numer, denom


def with_scale(block):
    rows, key = block
    return rows, key, to_row(scale_column(rows))


def add_side(left, blocks, before, out):
    width = left[0].shape[1]
    numer = None if before is None else before[:, :width]
    denom = None if before is None else before[:, width : width + 1]
    numer, denom = add_blocks(left, blocks, numer, denom)
    out[:, :width] = numer
    out[:, width:] = jnp.broadcast_to(denom, (numer.shape[0], 128))


def start_kernel(n_blocks, own, other, *refs):
    left = [from_whole(own), from_whole(other)]
    blocks = [with_scale(left[0])] + [with_scale(from_whole(ref)) for ref in refs[:n_blocks]]
    for side in range(2):
        add_side(left[side], blocks, None, refs[n_blocks + side])


def both_kernel(n_blocks, own, other, *refs):
    blocks = [with_scale(from_whole(ref)) for ref in refs[:n_blocks]]
    for side, left in enumerate((own, other)):
        add_side(from_whole(left), blocks, refs[n_blocks + side], refs[n_blocks + 2 + side])


def last_kernel(left, first, second, before, out):
    add_side(from_whole(left), [with_scale(from_halves(first, second))], before, out)


def mean_kernel(mine, theirs, out):
    width = out.shape[1]
    denom = mine[:, width : width + 1] + theirs[:, width : width + 1]
    out[...] = ((mine[:, :width] + theirs[:, :width]) / denom).astype(BF16)


def whole_in_vmem(count):
    return [pl.BlockSpec(memory_space=pltpu.VMEM)] * count


def call(kernel, shapes, args, aliases={}):
    return pl.pallas_call(
        kernel,
        out_shape=shapes,
        in_specs=whole_in_vmem(len(args)),
        out_specs=whole_in_vmem(len(shapes)),
        input_output_aliases=aliases,
        compiler_params=pltpu.CompilerParams(vmem_limit_bytes=VMEM_BYTES),
    )(*args)


def pack(embeddings, group_of, cluster_id):
    rows_here, width = embeddings.shape
    line = (1, rows_here)
    return pl.pallas_call(
        pack_kernel,
        out_shape=jax.ShapeDtypeStruct((rows_here + 8, width), BF16),
        in_specs=[pl.BlockSpec(memory_space=pl.ANY)] * 3,
        out_specs=pl.BlockSpec(memory_space=pltpu.VMEM),
        scratch_shapes=[
            pltpu.VMEM(line, jnp.int32),
            pltpu.VMEM(line, jnp.int32),
            pltpu.SemaphoreType.DMA((3,)),
        ],
        compiler_params=pltpu.CompilerParams(vmem_limit_bytes=PACK_BYTES),
    )(embeddings, group_of.reshape(line), cluster_id.reshape(line))


def start_both(left, right):
    rows_here, width = left[0].shape
    shape = jax.ShapeDtypeStruct((rows_here - 8, width + 128), F32)
    return call(
        functools.partial(start_kernel, len(right)), [shape, shape], list(left) + list(right)
    )


def add_both(left, right, before):
    args = list(left) + list(right) + list(before)
    at = len(args) - 2
    shapes = [jax.ShapeDtypeStruct(total.shape, F32) for total in before]
    return call(
        functools.partial(both_kernel, len(right)), shapes, args, {at: 0, at + 1: 1}
    )


def add_last(left, halves, before):
    shapes = [jax.ShapeDtypeStruct(before.shape, F32)]
    return call(last_kernel, shapes, [left, *halves, before], {3: 0})[0]


def folded_ring(size):
    return [0] + list(range(1, size, 2)) + list(range(2, size, 2))[::-1]


def together(*arrays):
    return lax.optimization_barrier(arrays)


def by_block(embeddings, group_of, cluster_id):
    rows_here, width = embeddings.shape
    n_blk = lax.axis_size("blk")
    order = folded_ring(n_blk)
    swap = [(0, 1), (1, 0)]

    def along(rows):
        return lax.ppermute(rows, "blk", [(order[i - 1], order[i]) for i in range(n_blk)])

    def across(rows):
        return lax.ppermute(rows, "sub", swap)

    def other_core(rows):
        return lax.ppermute(rows, "pair", swap)

    block = pack(embeddings, group_of, cluster_id)
    along_by = [block]
    across_by = []
    other = other_core(block)
    in_flight = [other]
    for s in range(1, n_blk):
        if s > 1:
            along_by[-1], _ = together(along_by[-1], in_flight.pop(0))
        across_by.append(across(along_by[-1]))
        in_flight.append(across_by[-1])
        along_by.append(along(along_by[-1]))
    left = (block, other)
    total = start_both(left, across_by[:-1] + along_by[1:-1])
    half = rows_here // 2
    far, near, mine, theirs = together(along_by[-1], across_by[-1], *total)
    halves = (along(near[:half]), across(far[half:]))
    mine, theirs = add_both(left, [near, far], (mine, theirs))
    theirs = other_core(add_last(other, halves, theirs))
    mine = add_last(block, halves, mine)
    (out,) = call(
        mean_kernel, [jax.ShapeDtypeStruct((rows_here, width), BF16)], [mine, theirs]
    )
    return out


def per_device(embeddings, group_of, cluster_id):
    rows_here, width = embeddings.shape
    devices = lax.axis_size("blk") * lax.axis_size("sub") * lax.axis_size("pair")
    small = devices * rows_here * width * 2 <= GATHER_LIMIT
    if small and lax.axis_size("sub") == 2 and lax.axis_size("pair") == 2:
        return by_block(embeddings, group_of, cluster_id)
    return by_group(embeddings, group_of, cluster_id)


def solution(mesh):
    return jax.shard_map(
        per_device,
        mesh=mesh,
        in_specs=(
            P(("island", "blk", "sub", "pair"), None),
            P(("island", "blk", "sub", "pair"), None),
            P(("island", "blk", "sub", "pair")),
        ),
        out_specs=P(("island", "blk", "sub", "pair"), None),
        check_vma=False,
    )
```

```python
import functools

import jax
import jax.numpy as jnp
from jax import lax
from jax.experimental import pallas as pl
from jax.experimental.pallas import tpu as pltpu
from jax.sharding import PartitionSpec as P

F32 = jnp.float32
BF16 = jnp.bfloat16
VMEM_BYTES = 24 * 1024 * 1024
PACK_BYTES = 56 * 1024 * 1024
GATHER_LIMIT = 8 * 1024 * 1024


def unit_scale(rows_in):
    wide = rows_in.astype(F32)
    return lax.rsqrt(jnp.sum(wide * wide, axis=1) + 1e-06)


def tile_weights(left_rows, left_clust, left_scale, right_rows, right_clust, right_scale):
    grams = lax.dot_general(
        left_rows, right_rows, (((1,), (1,)), ((), ())), preferred_element_type=F32
    )
    cosine = grams * left_scale[:, None] * right_scale[None, :]
    same = (left_clust[:, None] == right_clust[None, :]).astype(F32)
    return jax.nn.sigmoid(8.0 * cosine - 2.0) * same


def by_group(embeddings, group_of, cluster_id):
    rows_here, width = embeddings.shape
    groups = lax.axis_size("sub") * lax.axis_size("pair")
    capacity = 2 * rows_here // groups
    slots = groups * capacity
    target = group_of[:, 0]
    onehot = (target[:, None] == jnp.arange(groups, dtype=jnp.int32)[None, :]).astype(jnp.int32)
    position = jnp.sum((jnp.cumsum(onehot, axis=0) - onehot) * onehot, axis=1)
    send_rows = jnp.zeros((groups, capacity, width), BF16).at[target, position].set(embeddings)
    send_clust = jnp.full((groups, capacity), -1, jnp.int32).at[target, position].set(cluster_id)
    recv_rows, recv_clust = (
        lax.all_to_all(send_rows, ("sub", "pair"), split_axis=0, concat_axis=0, tiled=True),
        lax.all_to_all(send_clust, ("sub", "pair"), split_axis=0, concat_axis=0, tiled=True),
    )
    own_rows = recv_rows.reshape(slots, width)
    own_clust = recv_clust.reshape(slots)
    own_scale = unit_scale(own_rows)
    piece_rows = lax.all_gather(own_rows, "blk", axis=0, tiled=True)
    piece_clust = lax.all_gather(own_clust, "blk", axis=0, tiled=True)
    weight = tile_weights(
        own_rows, own_clust, own_scale, piece_rows, piece_clust, unit_scale(piece_rows)
    )
    numer = jnp.dot(weight.astype(BF16), piece_rows, preferred_element_type=F32)
    denom = jnp.sum(weight, axis=1)
    result = (numer / denom[:, None]).astype(BF16).reshape(groups, capacity, width)
    returned = lax.all_to_all(result, ("sub", "pair"), split_axis=0, concat_axis=0, tiled=True)
    return returned[target, position]


def diagonal(size):
    shape = (size, size)
    return lax.broadcasted_iota(jnp.int32, shape, 0) == lax.broadcasted_iota(jnp.int32, shape, 1)


def to_column(row):
    size = row.shape[1]
    return jnp.sum(jnp.where(diagonal(size), row, jnp.zeros_like(row)), axis=1, keepdims=True)


def to_row(column):
    size = column.shape[0]
    return jnp.sum(jnp.where(diagonal(size), column, jnp.zeros_like(column)), axis=0, keepdims=True)


def scale_column(rows):
    wide = rows.astype(F32)
    return lax.rsqrt(jnp.sum(wide * wide, axis=1, keepdims=True) + 1e-06)


def name_lines(rows_here):
    return -(-rows_here // 128)


def slab_copies(rows, top, count, out, sems, first):
    copies = []
    for slab in range(rows.shape[1] // 128):
        source = rows.at[top : top + count, slab * 128 : (slab + 1) * 128]
        target = out.at[slab * count : (slab + 1) * count, :]
        copies.append(pltpu.make_async_copy(source, target, sems.at[first + slab]))
    return copies


def pack_kernel(rows, group, cluster, whole, first, second, group_here, cluster_here, names, sems):
    rows_here, width = rows.shape
    half = rows_here // 2
    slabs = width // 128
    loads = [
        pltpu.make_async_copy(group, group_here, sems.at[0]),
        pltpu.make_async_copy(cluster, cluster_here, sems.at[1]),
    ]
    copies = slab_copies(rows, 0, half, first, sems, 4)
    copies += slab_copies(rows, half, half, second, sems, 4 + slabs)
    copies += slab_copies(rows, 0, rows_here, whole, sems, 4 + 2 * slabs)
    for copy in loads + copies:
        copy.start()
    for copy in loads:
        copy.wait()
    line_at = lax.broadcasted_iota(jnp.int32, names.shape, 0)
    lines = name_lines(rows_here)
    named = jnp.zeros(names.shape, jnp.int32)
    for kind, ref in enumerate((group_here, cluster_here)):
        for line in range(lines):
            part = ref[:, line * 128 : (line + 1) * 128]
            if part.shape[1] < 128:
                rest = jnp.zeros((1, 128 - part.shape[1]), jnp.int32)
                part = jnp.concatenate([part, rest], axis=1)
            named = jnp.where(line_at == kind * lines + line, part, named)
    names[...] = named.astype(F32).astype(BF16)
    stores = [
        pltpu.make_async_copy(names, whole.at[slabs * rows_here :, :], sems.at[2]),
        pltpu.make_async_copy(names, first.at[slabs * half :, :], sems.at[3]),
    ]
    for copy in stores:
        copy.start()
    for copy in copies + stores:
        copy.wait()


def from_slabs(ref, count):
    slabs = [ref[top : top + count, :] for top in range(0, ref.shape[0] // count * count, count)]
    return jnp.concatenate(slabs, axis=1)


def key_row(ref, rows_here):
    wide = ref[ref.shape[0] - 8 :, :].astype(F32)
    lines = name_lines(rows_here)
    kinds = []
    for kind in range(2):
        parts = [wide[kind * lines + line : kind * lines + line + 1, :] for line in range(lines)]
        kinds.append(jnp.concatenate(parts, axis=1)[:, :rows_here])
    return kinds[0] * 256.0 + kinds[1]


def from_whole(ref, rows_here):
    return from_slabs(ref, rows_here), key_row(ref, rows_here)


def from_halves(first, second, rows_here):
    half = rows_here // 2
    rows = jnp.concatenate([from_slabs(first, half), from_slabs(second, half)], axis=0)
    return rows, key_row(first, rows_here)


def add_blocks(left, blocks, numer, denom):
    rows, key = left
    key = to_column(key)
    scale = scale_column(rows) * 4.0
    for right_rows, right_key, right_scale in blocks:
        grams = lax.dot_general(
            rows, right_rows, (((1,), (1,)), ((), ())), preferred_element_type=F32
        )
        half = jnp.tanh(grams * scale * right_scale - 1.0)
        weight = jnp.where(key == right_key, 0.5 + 0.5 * half, 0.0)
        add = jnp.dot(weight.astype(BF16), right_rows, preferred_element_type=F32)
        add_denom = jnp.sum(weight, axis=1, keepdims=True)
        numer = add if numer is None else numer + add
        denom = add_denom if denom is None else denom + add_denom
    return numer, denom


def with_scale(block):
    rows, key = block
    return rows, key, to_row(scale_column(rows))


def take_blocks(refs, count, rows_here):
    return [
        with_scale(from_halves(refs.pop(0), refs.pop(0), rows_here)) for _ in range(count)
    ]


def add_side(left, blocks, before, out):
    width = left[0].shape[1]
    numer = None if before is None else before[:, :width]
    denom = None if before is None else before[:, width : width + 1]
    numer, denom = add_blocks(left, blocks, numer, denom)
    out[:, :width] = numer
    out[:, width:] = jnp.broadcast_to(denom, (numer.shape[0], 128))


def start_kernel(n_blocks, own, other, *refs):
    refs = list(refs)
    rows_here = refs[-1].shape[0]
    left = [from_whole(own, rows_here), from_whole(other, rows_here)]
    blocks = [with_scale(left[0])] + take_blocks(refs, n_blocks, rows_here)
    for side in range(2):
        add_side(left[side], blocks, None, refs[side])


def both_kernel(n_blocks, own, other, *refs):
    refs = list(refs)
    rows_here = refs[-1].shape[0]
    blocks = take_blocks(refs, n_blocks, rows_here)
    for side, left in enumerate((own, other)):
        add_side(from_whole(left, rows_here), blocks, refs[side], refs[2 + side])


def one_kernel(n_blocks, left, *refs):
    refs = list(refs)
    rows_here = refs[-1].shape[0]
    blocks = take_blocks(refs, n_blocks, rows_here)
    add_side(from_whole(left, rows_here), blocks, refs[0], refs[1])


def mean_kernel(mine, theirs, out):
    width = out.shape[1]
    denom = mine[:, width : width + 1] + theirs[:, width : width + 1]
    out[...] = ((mine[:, :width] + theirs[:, :width]) / denom).astype(BF16)


def whole_in_vmem(count):
    return [pl.BlockSpec(memory_space=pltpu.VMEM)] * count


def call(kernel, shapes, args, aliases={}):
    return pl.pallas_call(
        kernel,
        out_shape=shapes,
        in_specs=whole_in_vmem(len(args)),
        out_specs=whole_in_vmem(len(shapes)),
        input_output_aliases=aliases,
        compiler_params=pltpu.CompilerParams(vmem_limit_bytes=VMEM_BYTES),
    )(*args)


def pack(embeddings, group_of, cluster_id):
    rows_here, width = embeddings.shape
    half = rows_here // 2
    slabs = width // 128
    line = (1, rows_here)
    return pl.pallas_call(
        pack_kernel,
        out_shape=[
            jax.ShapeDtypeStruct((slabs * rows_here + 8, 128), BF16),
            jax.ShapeDtypeStruct((slabs * half + 8, 128), BF16),
            jax.ShapeDtypeStruct((slabs * half, 128), BF16),
        ],
        in_specs=[pl.BlockSpec(memory_space=pl.ANY)] * 3,
        out_specs=[pl.BlockSpec(memory_space=pl.ANY)] * 3,
        scratch_shapes=[
            pltpu.VMEM(line, jnp.int32),
            pltpu.VMEM(line, jnp.int32),
            pltpu.VMEM((8, 128), BF16),
            pltpu.SemaphoreType.DMA((4 + 3 * slabs,)),
        ],
        compiler_params=pltpu.CompilerParams(vmem_limit_bytes=PACK_BYTES),
    )(embeddings, group_of.reshape(line), cluster_id.reshape(line))


def start_both(left, right, shape):
    args = list(left) + [half for block in right for half in block]
    shape = jax.ShapeDtypeStruct(shape, F32)
    return call(functools.partial(start_kernel, len(right)), [shape, shape], args)


def add_both(left, right, before):
    args = list(left) + [half for block in right for half in block] + list(before)
    at = len(args) - 2
    shapes = [jax.ShapeDtypeStruct(total.shape, F32) for total in before]
    return call(
        functools.partial(both_kernel, len(right)), shapes, args, {at: 0, at + 1: 1}
    )


def add_one(left, right, before):
    args = [left] + [half for block in right for half in block] + [before]
    shapes = [jax.ShapeDtypeStruct(before.shape, F32)]
    return call(functools.partial(one_kernel, len(right)), shapes, args, {len(args) - 1: 0})[0]


def folded_ring(size):
    return [0] + list(range(1, size, 2)) + list(range(2, size, 2))[::-1]


def together(*arrays):
    return lax.optimization_barrier(arrays)


def by_block(embeddings, group_of, cluster_id):
    rows_here, width = embeddings.shape
    n_blk = lax.axis_size("blk")
    order = folded_ring(n_blk)
    swap = [(0, 1), (1, 0)]

    def along(rows):
        return lax.ppermute(rows, "blk", [(order[i - 1], order[i]) for i in range(n_blk)])

    def across(rows):
        return lax.ppermute(rows, "sub", swap)

    def other_core(rows):
        return lax.ppermute(rows, "pair", swap)

    whole, first, second = pack(embeddings, group_of, cluster_id)
    along_by = [(first, second)]
    across_by = []
    for s in range(1, n_blk):
        moved = [along(piece) for piece in along_by[-1]]
        swapped = [across(piece) for piece in along_by[-1]]
        pairs = [together(m, w) for m, w in zip(moved, swapped)]
        along_by.append(tuple(pair[0] for pair in pairs))
        across_by.append(tuple(pair[1] for pair in pairs))
    left = (whole, other_core(whole))
    total = start_both(left, across_by[:-1] + along_by[1:-1], (rows_here, width + 128))
    far_first, mine, theirs = together(along_by[-1][0], *total)
    last = (across(far_first), along(across_by[-1][1]))
    mine, theirs = add_both(left, [across_by[-1], along_by[-1]], (mine, theirs))
    theirs = other_core(add_one(left[1], [last], theirs))
    mine = add_one(left[0], [last], mine)
    (out,) = call(
        mean_kernel, [jax.ShapeDtypeStruct((rows_here, width), BF16)], [mine, theirs]
    )
    return out


def per_device(embeddings, group_of, cluster_id):
    rows_here, width = embeddings.shape
    devices = lax.axis_size("blk") * lax.axis_size("sub") * lax.axis_size("pair")
    small = devices * rows_here * width * 2 <= GATHER_LIMIT
    fits = width % 128 == 0 and rows_here % 32 == 0 and rows_here <= 512
    if small and fits and lax.axis_size("sub") == 2 and lax.axis_size("pair") == 2:
        return by_block(embeddings, group_of, cluster_id)
    return by_group(embeddings, group_of, cluster_id)


def solution(mesh):
    return jax.shard_map(
        per_device,
        mesh=mesh,
        in_specs=(
            P(("island", "blk", "sub", "pair"), None),
            P(("island", "blk", "sub", "pair"), None),
            P(("island", "blk", "sub", "pair")),
        ),
        out_specs=P(("island", "blk", "sub", "pair"), None),
        check_vma=False,
    )
```

```python
import functools

import jax
import jax.numpy as jnp
from jax import lax
from jax.experimental import pallas as pl
from jax.experimental.pallas import tpu as pltpu
from jax.sharding import PartitionSpec as P

F32 = jnp.float32
BF16 = jnp.bfloat16
VMEM_BYTES = 24 * 1024 * 1024
GATHER_LIMIT = 8 * 1024 * 1024


def unit_scale(rows_in):
    wide = rows_in.astype(F32)
    return lax.rsqrt(jnp.sum(wide * wide, axis=1) + 1e-06)


def tile_weights(left_rows, left_clust, left_scale, right_rows, right_clust, right_scale):
    grams = lax.dot_general(
        left_rows, right_rows, (((1,), (1,)), ((), ())), preferred_element_type=F32
    )
    cosine = grams * left_scale[:, None] * right_scale[None, :]
    same = (left_clust[:, None] == right_clust[None, :]).astype(F32)
    return jax.nn.sigmoid(8.0 * cosine - 2.0) * same


def by_group(embeddings, group_of, cluster_id):
    rows_here, width = embeddings.shape
    groups = lax.axis_size("sub") * lax.axis_size("pair")
    capacity = 2 * rows_here // groups
    slots = groups * capacity
    target = group_of[:, 0]
    onehot = (target[:, None] == jnp.arange(groups, dtype=jnp.int32)[None, :]).astype(jnp.int32)
    position = jnp.sum((jnp.cumsum(onehot, axis=0) - onehot) * onehot, axis=1)
    send_rows = jnp.zeros((groups, capacity, width), BF16).at[target, position].set(embeddings)
    send_clust = jnp.full((groups, capacity), -1, jnp.int32).at[target, position].set(cluster_id)
    recv_rows, recv_clust = (
        lax.all_to_all(send_rows, ("sub", "pair"), split_axis=0, concat_axis=0, tiled=True),
        lax.all_to_all(send_clust, ("sub", "pair"), split_axis=0, concat_axis=0, tiled=True),
    )
    own_rows = recv_rows.reshape(slots, width)
    own_clust = recv_clust.reshape(slots)
    own_scale = unit_scale(own_rows)
    piece_rows = lax.all_gather(own_rows, "blk", axis=0, tiled=True)
    piece_clust = lax.all_gather(own_clust, "blk", axis=0, tiled=True)
    weight = tile_weights(
        own_rows, own_clust, own_scale, piece_rows, piece_clust, unit_scale(piece_rows)
    )
    numer = jnp.dot(weight.astype(BF16), piece_rows, preferred_element_type=F32)
    denom = jnp.sum(weight, axis=1)
    result = (numer / denom[:, None]).astype(BF16).reshape(groups, capacity, width)
    returned = lax.all_to_all(result, ("sub", "pair"), split_axis=0, concat_axis=0, tiled=True)
    return returned[target, position]


def diagonal(size):
    shape = (size, size)
    return lax.broadcasted_iota(jnp.int32, shape, 0) == lax.broadcasted_iota(jnp.int32, shape, 1)


def to_column(row):
    size = row.shape[1]
    return jnp.sum(jnp.where(diagonal(size), row, jnp.zeros_like(row)), axis=1, keepdims=True)


def to_row(column):
    size = column.shape[0]
    return jnp.sum(jnp.where(diagonal(size), column, jnp.zeros_like(column)), axis=0, keepdims=True)


def scale_column(rows):
    wide = rows.astype(F32)
    return lax.rsqrt(jnp.sum(wide * wide, axis=1, keepdims=True) + 1e-06)


def name_lines(rows_here):
    return -(-rows_here // 128)


def pack_kernel(rows, group, cluster, out):
    rows_here, width = rows.shape
    slabs = width // 128
    for slab in range(slabs):
        out[slab * rows_here : (slab + 1) * rows_here, :] = rows[
            :, slab * 128 : (slab + 1) * 128
        ]
    line_at = lax.broadcasted_iota(jnp.int32, (8, 128), 0)
    lines = name_lines(rows_here)
    named = jnp.zeros((8, 128), jnp.int32)
    for kind, ref in enumerate((group, cluster)):
        for line in range(lines):
            part = ref[:, line * 128 : (line + 1) * 128]
            if part.shape[1] < 128:
                rest = jnp.zeros((1, 128 - part.shape[1]), jnp.int32)
                part = jnp.concatenate([part, rest], axis=1)
            named = jnp.where(line_at == kind * lines + line, part, named)
    out[slabs * rows_here :, :] = named.astype(F32).astype(BF16)


def from_slabs(ref, count):
    slabs = [ref[top : top + count, :] for top in range(0, ref.shape[0] // count * count, count)]
    return jnp.concatenate(slabs, axis=1)


def key_row(ref, rows_here):
    wide = ref[ref.shape[0] - 8 :, :].astype(F32)
    lines = name_lines(rows_here)
    kinds = []
    for kind in range(2):
        parts = [wide[kind * lines + line : kind * lines + line + 1, :] for line in range(lines)]
        kinds.append(jnp.concatenate(parts, axis=1)[:, :rows_here])
    return kinds[0] * 256.0 + kinds[1]


def computes():
    return lax.axis_index("pair") == 0


def with_scale(ref, rows_here):
    rows = from_slabs(ref, rows_here)
    return rows, key_row(ref, rows_here), to_row(scale_column(rows))


def add_blocks(left, info, blocks, numer, denom):
    key = info[:, 0:1]
    scale = info[:, 1:2]
    for right_rows, right_key, right_scale in blocks:
        grams = lax.dot_general(
            left, right_rows, (((1,), (1,)), ((), ())), preferred_element_type=F32
        )
        half = jnp.tanh(grams * scale * right_scale - 1.0)
        weight = jnp.where(key == right_key, 0.5 + 0.5 * half, 0.0)
        add = jnp.dot(weight.astype(BF16), right_rows, preferred_element_type=F32)
        add_denom = jnp.sum(weight, axis=1, keepdims=True)
        numer = add if numer is None else numer + add
        denom = add_denom if denom is None else denom + add_denom
    return numer, denom


def left_rows(own, other, rows_here):
    return jnp.concatenate([from_slabs(own, rows_here), from_slabs(other, rows_here)], axis=0)


def start_kernel(own, other, numer_out, denom_out, info_out):
    @pl.when(computes())
    def _():
        rows_here = numer_out.shape[0] // 2
        left = left_rows(own, other, rows_here)
        key = jnp.concatenate([to_column(key_row(ref, rows_here)) for ref in (own, other)], axis=0)
        scale = scale_column(left)
        lane = lax.broadcasted_iota(jnp.int32, info_out.shape, 1)
        info = jnp.where(lane == 0, key, 4.0 * scale)
        info_out[...] = info
        blocks = [
            (
                left[top : top + rows_here],
                key_row(ref, rows_here),
                to_row(scale[top : top + rows_here]),
            )
            for top, ref in ((0, own), (rows_here, other))
        ]
        numer, denom = add_blocks(left, info, blocks, None, None)
        numer_out[...] = numer
        denom_out[...] = jnp.broadcast_to(denom, denom_out.shape)


def add_kernel(n_blocks, own, other, info, *refs):
    numer_in, denom_in, numer_out, denom_out = refs[n_blocks:]

    @pl.when(computes())
    def _():
        rows_here = numer_out.shape[0] // 2
        left = left_rows(own, other, rows_here)
        blocks = [with_scale(ref, rows_here) for ref in refs[:n_blocks]]
        numer, denom = add_blocks(left, info[...], blocks, numer_in[...], denom_in[:, 0:1])
        numer_out[...] = numer
        denom_out[...] = jnp.broadcast_to(denom, denom_out.shape)


def last_kernel(own, other, info, right, numer_in, denom_in, mine, theirs):
    @pl.when(computes())
    def _():
        rows_here = mine.shape[0]
        left = left_rows(own, other, rows_here)
        blocks = [with_scale(right, rows_here)]
        numer, denom = add_blocks(left, info[...], blocks, numer_in[...], denom_in[:, 0:1])
        means = (numer / denom).astype(BF16)
        mine[...] = means[:rows_here]
        theirs[...] = means[rows_here:]


def out_kernel(mine, back, out):
    @pl.when(computes())
    def _():
        out[...] = mine[...]

    @pl.when(jnp.logical_not(computes()))
    def _():
        out[...] = back[...]


def whole_in_vmem(count):
    return [pl.BlockSpec(memory_space=pltpu.VMEM)] * count


def call(kernel, shapes, args, aliases={}):
    return pl.pallas_call(
        kernel,
        out_shape=[jax.ShapeDtypeStruct(shape, dtype) for shape, dtype in shapes],
        in_specs=whole_in_vmem(len(args)),
        out_specs=whole_in_vmem(len(shapes)),
        input_output_aliases=aliases,
        compiler_params=pltpu.CompilerParams(vmem_limit_bytes=VMEM_BYTES),
    )(*args)


def add_to(total, left, right):
    args = [*left, *right, *total]
    at = len(args) - 2
    shapes = [(array.shape, F32) for array in total]
    return call(functools.partial(add_kernel, len(right)), shapes, args, {at: 0, at + 1: 1})


def folded_ring(size):
    return [0] + list(range(1, size, 2)) + list(range(2, size, 2))[::-1]


def together(*arrays):
    return lax.optimization_barrier(arrays)


def by_block(embeddings, group_of, cluster_id):
    rows_here, width = embeddings.shape
    n_blk = lax.axis_size("blk")
    order = folded_ring(n_blk)
    line = (1, rows_here)

    def along(rows, core):
        hops = [(2 * order[i - 1] + core, 2 * order[i] + core) for i in range(n_blk)]
        return lax.ppermute(rows, ("blk", "pair"), hops)

    def across(rows):
        return lax.ppermute(rows, ("sub", "pair"), [(1, 2), (3, 0)])

    def hand(rows):
        return lax.ppermute(rows, "pair", [(1, 0)])

    (block,) = call(
        pack_kernel,
        [((width // 128 * rows_here + 8, 128), BF16)],
        [embeddings, group_of.reshape(line), cluster_id.reshape(line)],
    )
    other = lax.ppermute(block, "pair", [(0, 1), (1, 0)])
    moving = [block, other]
    crossed = [across(block), across(other)]
    handed = [None, None]
    moving += [along(block, 1), along(other, 1)]
    numer, denom, info = call(
        start_kernel,
        [((2 * rows_here, width), F32), ((2 * rows_here, 128), F32), ((2 * rows_here, 128), F32)],
        [block, other],
    )
    left = (block, other, info)
    total = (numer, denom)
    last = 2 * n_blk - 1
    for k in range(2, last + 1):
        ready = [crossed[k - 2]]
        if k > 3:
            ready.append(handed[k - 2])
        moving[k], *rest = together(moving[k], *total, *ready)
        total, ready = rest[:2], rest[2:]
        if k + 2 <= last:
            moving.append(along(moving[k], 1))
        if k < last:
            crossed.append(across(moving[k]))
        else:
            crossed.append(along(crossed[k - 2], 0))
        handed.append(hand(moving[k]))
        total = add_to(total, left, ready)
    total = add_to(total, left, [crossed[last - 1], handed[last - 1], handed[last]])
    mine, theirs = call(
        last_kernel,
        [((rows_here, width), BF16)] * 2,
        [*left, crossed[last], *total],
    )
    back = lax.ppermute(theirs, "pair", [(0, 1)])
    (out,) = call(out_kernel, [((rows_here, width), BF16)], [mine, back])
    return out


def per_device(embeddings, group_of, cluster_id):
    rows_here, width = embeddings.shape
    devices = lax.axis_size("blk") * lax.axis_size("sub") * lax.axis_size("pair")
    small = devices * rows_here * width * 2 <= GATHER_LIMIT
    fits = width % 128 == 0 and rows_here % 32 == 0 and rows_here <= 512
    if small and fits and lax.axis_size("sub") == 2 and lax.axis_size("pair") == 2:
        return by_block(embeddings, group_of, cluster_id)
    return by_group(embeddings, group_of, cluster_id)


def solution(mesh):
    return jax.shard_map(
        per_device,
        mesh=mesh,
        in_specs=(
            P(("island", "blk", "sub", "pair"), None),
            P(("island", "blk", "sub", "pair"), None),
            P(("island", "blk", "sub", "pair")),
        ),
        out_specs=P(("island", "blk", "sub", "pair"), None),
        check_vma=False,
    )
```

```python
import functools

import jax
import jax.numpy as jnp
from jax import lax
from jax.experimental import pallas as pl
from jax.experimental.pallas import tpu as pltpu
from jax.sharding import PartitionSpec as P

F32 = jnp.float32
BF16 = jnp.bfloat16
VMEM_BYTES = 24 * 1024 * 1024
GATHER_LIMIT = 8 * 1024 * 1024


def unit_scale(rows_in):
    wide = rows_in.astype(F32)
    return lax.rsqrt(jnp.sum(wide * wide, axis=1) + 1e-06)


def tile_weights(left_rows, left_clust, left_scale, right_rows, right_clust, right_scale):
    grams = lax.dot_general(
        left_rows, right_rows, (((1,), (1,)), ((), ())), preferred_element_type=F32
    )
    cosine = grams * left_scale[:, None] * right_scale[None, :]
    same = (left_clust[:, None] == right_clust[None, :]).astype(F32)
    return jax.nn.sigmoid(8.0 * cosine - 2.0) * same


def by_group(embeddings, group_of, cluster_id):
    rows_here, width = embeddings.shape
    groups = lax.axis_size("sub") * lax.axis_size("pair")
    capacity = 2 * rows_here // groups
    slots = groups * capacity
    target = group_of[:, 0]
    onehot = (target[:, None] == jnp.arange(groups, dtype=jnp.int32)[None, :]).astype(jnp.int32)
    position = jnp.sum((jnp.cumsum(onehot, axis=0) - onehot) * onehot, axis=1)
    send_rows = jnp.zeros((groups, capacity, width), BF16).at[target, position].set(embeddings)
    send_clust = jnp.full((groups, capacity), -1, jnp.int32).at[target, position].set(cluster_id)
    recv_rows, recv_clust = (
        lax.all_to_all(send_rows, ("sub", "pair"), split_axis=0, concat_axis=0, tiled=True),
        lax.all_to_all(send_clust, ("sub", "pair"), split_axis=0, concat_axis=0, tiled=True),
    )
    own_rows = recv_rows.reshape(slots, width)
    own_clust = recv_clust.reshape(slots)
    own_scale = unit_scale(own_rows)
    piece_rows = lax.all_gather(own_rows, "blk", axis=0, tiled=True)
    piece_clust = lax.all_gather(own_clust, "blk", axis=0, tiled=True)
    weight = tile_weights(
        own_rows, own_clust, own_scale, piece_rows, piece_clust, unit_scale(piece_rows)
    )
    numer = jnp.dot(weight.astype(BF16), piece_rows, preferred_element_type=F32)
    denom = jnp.sum(weight, axis=1)
    result = (numer / denom[:, None]).astype(BF16).reshape(groups, capacity, width)
    returned = lax.all_to_all(result, ("sub", "pair"), split_axis=0, concat_axis=0, tiled=True)
    return returned[target, position]


def diagonal(size):
    shape = (size, size)
    return lax.broadcasted_iota(jnp.int32, shape, 0) == lax.broadcasted_iota(jnp.int32, shape, 1)


def to_column(row):
    size = row.shape[1]
    return jnp.sum(jnp.where(diagonal(size), row, jnp.zeros_like(row)), axis=1, keepdims=True)


def to_row(column):
    size = column.shape[0]
    return jnp.sum(jnp.where(diagonal(size), column, jnp.zeros_like(column)), axis=0, keepdims=True)


def scale_column(rows):
    wide = rows.astype(F32)
    return lax.rsqrt(jnp.sum(wide * wide, axis=1, keepdims=True) + 1e-06)


def name_lines(rows_here):
    return -(-rows_here // 128)


def pack_kernel(rows, group, cluster, out):
    rows_here, width = rows.shape
    slabs = width // 128
    for slab in range(slabs):
        out[slab * rows_here : (slab + 1) * rows_here, :] = rows[
            :, slab * 128 : (slab + 1) * 128
        ]
    line_at = lax.broadcasted_iota(jnp.int32, (8, 128), 0)
    lines = name_lines(rows_here)
    named = jnp.zeros((8, 128), jnp.int32)
    for kind, ref in enumerate((group, cluster)):
        for line in range(lines):
            part = ref[:, line * 128 : (line + 1) * 128]
            if part.shape[1] < 128:
                rest = jnp.zeros((1, 128 - part.shape[1]), jnp.int32)
                part = jnp.concatenate([part, rest], axis=1)
            named = jnp.where(line_at == kind * lines + line, part, named)
    out[slabs * rows_here :, :] = named.astype(F32).astype(BF16)


def from_slabs(ref, count):
    slabs = [ref[top : top + count, :] for top in range(0, ref.shape[0] // count * count, count)]
    return jnp.concatenate(slabs, axis=1)


def key_row(ref, rows_here):
    wide = ref[ref.shape[0] - 8 :, :].astype(F32)
    lines = name_lines(rows_here)
    kinds = []
    for kind in range(2):
        parts = [wide[kind * lines + line : kind * lines + line + 1, :] for line in range(lines)]
        kinds.append(jnp.concatenate(parts, axis=1)[:, :rows_here])
    return kinds[0] * 256.0 + kinds[1]


def computes():
    return lax.axis_index("pair") == 0


def with_scale(ref, rows_here):
    rows = from_slabs(ref, rows_here)
    return rows, key_row(ref, rows_here), to_row(scale_column(rows))


def add_blocks(left, info, blocks, numer, denom):
    key = info[:, 0:1]
    scale = info[:, 1:2]
    for right_rows, right_key, right_scale in blocks:
        grams = lax.dot_general(
            left, right_rows, (((1,), (1,)), ((), ())), preferred_element_type=F32
        )
        half = jnp.tanh(grams * scale * right_scale - 1.0)
        weight = jnp.where(key == right_key, 0.5 + 0.5 * half, 0.0)
        add = jnp.dot(weight.astype(BF16), right_rows, preferred_element_type=F32)
        add_denom = jnp.sum(weight, axis=1, keepdims=True)
        numer = add if numer is None else numer + add
        denom = add_denom if denom is None else denom + add_denom
    return numer, denom


def left_rows(own, other, rows_here):
    return jnp.concatenate([from_slabs(own, rows_here), from_slabs(other, rows_here)], axis=0)


def start_kernel(own, other, numer_out, denom_out, info_out):
    @pl.when(computes())
    def _():
        rows_here = numer_out.shape[0] // 2
        left = left_rows(own, other, rows_here)
        key = jnp.concatenate([to_column(key_row(ref, rows_here)) for ref in (own, other)], axis=0)
        scale = scale_column(left)
        lane = lax.broadcasted_iota(jnp.int32, info_out.shape, 1)
        info = jnp.where(lane == 0, key, 4.0 * scale)
        info_out[...] = info
        blocks = [
            (
                left[top : top + rows_here],
                key_row(ref, rows_here),
                to_row(scale[top : top + rows_here]),
            )
            for top, ref in ((0, own), (rows_here, other))
        ]
        numer, denom = add_blocks(left, info, blocks, None, None)
        numer_out[...] = numer
        denom_out[...] = jnp.broadcast_to(denom, denom_out.shape)


def add_kernel(n_blocks, own, other, info, *refs):
    numer_in, denom_in, numer_out, denom_out = refs[n_blocks:]

    @pl.when(computes())
    def _():
        rows_here = numer_out.shape[0] // 2
        left = left_rows(own, other, rows_here)
        blocks = [with_scale(ref, rows_here) for ref in refs[:n_blocks]]
        numer, denom = add_blocks(left, info[...], blocks, numer_in[...], denom_in[:, 0:1])
        numer_out[...] = numer
        denom_out[...] = jnp.broadcast_to(denom, denom_out.shape)


def last_kernel(own, other, info, right, numer_in, denom_in, mine, theirs):
    @pl.when(computes())
    def _():
        rows_here = mine.shape[0]
        left = left_rows(own, other, rows_here)
        blocks = [with_scale(right, rows_here)]
        numer, denom = add_blocks(left, info[...], blocks, numer_in[...], denom_in[:, 0:1])
        means = (numer / denom).astype(BF16)
        mine[...] = means[:rows_here]
        theirs[...] = means[rows_here:]


def out_kernel(mine, back, out):
    @pl.when(computes())
    def _():
        out[...] = mine[...]

    @pl.when(jnp.logical_not(computes()))
    def _():
        out[...] = back[...]


def whole_in_vmem(count):
    return [pl.BlockSpec(memory_space=pltpu.VMEM)] * count


def call(kernel, shapes, args, aliases={}):
    return pl.pallas_call(
        kernel,
        out_shape=[jax.ShapeDtypeStruct(shape, dtype) for shape, dtype in shapes],
        in_specs=whole_in_vmem(len(args)),
        out_specs=whole_in_vmem(len(shapes)),
        input_output_aliases=aliases,
        compiler_params=pltpu.CompilerParams(vmem_limit_bytes=VMEM_BYTES),
    )(*args)


def add_to(total, left, right):
    args = [*left, *right, *total]
    at = len(args) - 2
    shapes = [(array.shape, F32) for array in total]
    return call(functools.partial(add_kernel, len(right)), shapes, args, {at: 0, at + 1: 1})


def folded_ring(size):
    return [0] + list(range(1, size, 2)) + list(range(2, size, 2))[::-1]


def together(*arrays):
    return lax.optimization_barrier(arrays)


def by_block(embeddings, group_of, cluster_id):
    rows_here, width = embeddings.shape
    n_blk = lax.axis_size("blk")
    order = folded_ring(n_blk)
    line = (1, rows_here)

    def along(rows, core):
        hops = [(2 * order[i - 1] + core, 2 * order[i] + core) for i in range(n_blk)]
        stay = [(2 * i + 1 - core, 2 * i + 1 - core) for i in range(n_blk)]
        return lax.ppermute(rows, ("blk", "pair"), hops + stay)

    def across(rows):
        return lax.ppermute(rows, ("sub", "pair"), [(1, 2), (3, 0), (0, 1), (2, 3)])

    def hand(rows):
        return lax.ppermute(rows, "pair", [(0, 1), (1, 0)])

    (block,) = call(
        pack_kernel,
        [((width // 128 * rows_here + 8, 128), BF16)],
        [embeddings, group_of.reshape(line), cluster_id.reshape(line)],
    )
    other = hand(block)
    moving = [block, other]
    crossed = [across(block), across(other)]
    handed = [None, None]
    moving += [along(block, 1), along(other, 1)]
    numer, denom, info = call(
        start_kernel,
        [((2 * rows_here, width), F32), ((2 * rows_here, 128), F32), ((2 * rows_here, 128), F32)],
        [block, other],
    )
    left = (block, other, info)
    total = (numer, denom)
    last = 2 * n_blk - 1
    for k in range(2, last + 1):
        ready = [crossed[k - 2]]
        if k > 3:
            ready.append(handed[k - 2])
        moving[k], *rest = together(moving[k], *total, *ready)
        total, ready = rest[:2], rest[2:]
        if k + 2 <= last:
            moving.append(along(moving[k], 1))
        if k < last:
            crossed.append(across(moving[k]))
        else:
            crossed.append(along(crossed[k - 2], 0))
        handed.append(hand(moving[k]))
        total = add_to(total, left, ready)
    total = add_to(total, left, [crossed[last - 1], handed[last - 1], handed[last]])
    mine, theirs = call(
        last_kernel,
        [((rows_here, width), BF16)] * 2,
        [*left, crossed[last], *total],
    )
    back = hand(theirs)
    (out,) = call(out_kernel, [((rows_here, width), BF16)], [mine, back])
    return out


def per_device(embeddings, group_of, cluster_id):
    rows_here, width = embeddings.shape
    devices = lax.axis_size("blk") * lax.axis_size("sub") * lax.axis_size("pair")
    small = devices * rows_here * width * 2 <= GATHER_LIMIT
    fits = width % 128 == 0 and rows_here % 32 == 0 and rows_here <= 512
    if small and fits and lax.axis_size("sub") == 2 and lax.axis_size("pair") == 2:
        return by_block(embeddings, group_of, cluster_id)
    return by_group(embeddings, group_of, cluster_id)


def solution(mesh):
    return jax.shard_map(
        per_device,
        mesh=mesh,
        in_specs=(
            P(("island", "blk", "sub", "pair"), None),
            P(("island", "blk", "sub", "pair"), None),
            P(("island", "blk", "sub", "pair")),
        ),
        out_specs=P(("island", "blk", "sub", "pair"), None),
        check_vma=False,
    )
```

```python
import functools

import jax
import jax.numpy as jnp
from jax import lax
from jax.experimental import pallas as pl
from jax.experimental.pallas import tpu as pltpu
from jax.sharding import PartitionSpec as P

F32 = jnp.float32
BF16 = jnp.bfloat16
VMEM_BYTES = 24 * 1024 * 1024
GATHER_LIMIT = 8 * 1024 * 1024


def unit_scale(rows_in):
    wide = rows_in.astype(F32)
    return lax.rsqrt(jnp.sum(wide * wide, axis=1) + 1e-06)


def tile_weights(left_rows, left_clust, left_scale, right_rows, right_clust, right_scale):
    grams = lax.dot_general(
        left_rows, right_rows, (((1,), (1,)), ((), ())), preferred_element_type=F32
    )
    cosine = grams * left_scale[:, None] * right_scale[None, :]
    same = (left_clust[:, None] == right_clust[None, :]).astype(F32)
    return jax.nn.sigmoid(8.0 * cosine - 2.0) * same


def by_group(embeddings, group_of, cluster_id):
    rows_here, width = embeddings.shape
    groups = lax.axis_size("sub") * lax.axis_size("pair")
    capacity = 2 * rows_here // groups
    slots = groups * capacity
    target = group_of[:, 0]
    onehot = (target[:, None] == jnp.arange(groups, dtype=jnp.int32)[None, :]).astype(jnp.int32)
    position = jnp.sum((jnp.cumsum(onehot, axis=0) - onehot) * onehot, axis=1)
    send_rows = jnp.zeros((groups, capacity, width), BF16).at[target, position].set(embeddings)
    send_clust = jnp.full((groups, capacity), -1, jnp.int32).at[target, position].set(cluster_id)
    recv_rows, recv_clust = (
        lax.all_to_all(send_rows, ("sub", "pair"), split_axis=0, concat_axis=0, tiled=True),
        lax.all_to_all(send_clust, ("sub", "pair"), split_axis=0, concat_axis=0, tiled=True),
    )
    own_rows = recv_rows.reshape(slots, width)
    own_clust = recv_clust.reshape(slots)
    own_scale = unit_scale(own_rows)
    piece_rows = lax.all_gather(own_rows, "blk", axis=0, tiled=True)
    piece_clust = lax.all_gather(own_clust, "blk", axis=0, tiled=True)
    weight = tile_weights(
        own_rows, own_clust, own_scale, piece_rows, piece_clust, unit_scale(piece_rows)
    )
    numer = jnp.dot(weight.astype(BF16), piece_rows, preferred_element_type=F32)
    denom = jnp.sum(weight, axis=1)
    result = (numer / denom[:, None]).astype(BF16).reshape(groups, capacity, width)
    returned = lax.all_to_all(result, ("sub", "pair"), split_axis=0, concat_axis=0, tiled=True)
    return returned[target, position]


def diagonal(size):
    shape = (size, size)
    return lax.broadcasted_iota(jnp.int32, shape, 0) == lax.broadcasted_iota(jnp.int32, shape, 1)


def to_column(row):
    size = row.shape[1]
    return jnp.sum(jnp.where(diagonal(size), row, jnp.zeros_like(row)), axis=1, keepdims=True)


def to_row(column):
    size = column.shape[0]
    return jnp.sum(jnp.where(diagonal(size), column, jnp.zeros_like(column)), axis=0, keepdims=True)


def scale_column(rows):
    wide = rows.astype(F32)
    return lax.rsqrt(jnp.sum(wide * wide, axis=1, keepdims=True) + 1e-06)


def name_lines(rows_here):
    return -(-rows_here // 128)


def pack_kernel(rows, group, cluster, whole, first, second):
    rows_here, width = rows.shape
    slabs = width // 128
    half = rows_here // 2
    for slab in range(slabs):
        columns = rows[:, slab * 128 : (slab + 1) * 128]
        whole[slab * rows_here : (slab + 1) * rows_here, :] = columns
        first[slab * half : (slab + 1) * half, :] = columns[:half]
        second[slab * half : (slab + 1) * half, :] = columns[half:]
    line_at = lax.broadcasted_iota(jnp.int32, (8, 128), 0)
    lines = name_lines(rows_here)
    named = jnp.zeros((8, 128), jnp.int32)
    for kind, ref in enumerate((group, cluster)):
        for line in range(lines):
            part = ref[:, line * 128 : (line + 1) * 128]
            if part.shape[1] < 128:
                rest = jnp.zeros((1, 128 - part.shape[1]), jnp.int32)
                part = jnp.concatenate([part, rest], axis=1)
            named = jnp.where(line_at == kind * lines + line, part, named)
    named = named.astype(F32).astype(BF16)
    whole[slabs * rows_here :, :] = named
    first[slabs * half :, :] = named


def from_slabs(ref, count):
    slabs = [ref[top : top + count, :] for top in range(0, ref.shape[0] // count * count, count)]
    return jnp.concatenate(slabs, axis=1)


def key_row(ref, rows_here):
    wide = ref[ref.shape[0] - 8 :, :].astype(F32)
    lines = name_lines(rows_here)
    kinds = []
    for kind in range(2):
        parts = [wide[kind * lines + line : kind * lines + line + 1, :] for line in range(lines)]
        kinds.append(jnp.concatenate(parts, axis=1)[:, :rows_here])
    return kinds[0] * 256.0 + kinds[1]


def from_halves(first, second, rows_here):
    half = rows_here // 2
    rows = jnp.concatenate([from_slabs(first, half), from_slabs(second, half)], axis=0)
    return rows, key_row(first, rows_here)


def add_blocks(left, key, scale, blocks, numer, denom):
    scale = 4.0 * scale
    for right_rows, right_key, right_scale in blocks:
        grams = lax.dot_general(
            left, right_rows, (((1,), (1,)), ((), ())), preferred_element_type=F32
        )
        half = jnp.tanh(grams * scale * right_scale - 1.0)
        weight = jnp.where(key == right_key, 0.5 + 0.5 * half, 0.0)
        add = jnp.dot(weight.astype(BF16), right_rows, preferred_element_type=F32)
        add_denom = jnp.sum(weight, axis=1, keepdims=True)
        numer = add if numer is None else numer + add
        denom = add_denom if denom is None else denom + add_denom
    return numer, denom


def left_of(refs, rows_here):
    rows = jnp.concatenate([from_slabs(ref, rows_here) for ref in refs], axis=0)
    key = jnp.concatenate([to_column(key_row(ref, rows_here)) for ref in refs], axis=0)
    return rows, key, scale_column(rows)


def take_blocks(refs, count, rows_here):
    blocks = []
    for _ in range(count):
        rows, key = from_halves(refs.pop(0), refs.pop(0), rows_here)
        blocks.append((rows, key, to_row(scale_column(rows))))
    return blocks


def store_sides(numer, denom, outs):
    rows_here, wide = outs[0].shape
    for side, out in enumerate(outs):
        top = side * rows_here
        out[:, : wide - 128] = numer[top : top + rows_here]
        out[:, wide - 128 :] = jnp.broadcast_to(denom[top : top + rows_here], (rows_here, 128))


def start_kernel(n_blocks, own, other, *refs):
    refs = list(refs)
    rows_here = refs[-1].shape[0]
    left, key, scale = left_of((own, other), rows_here)
    first = (left[:rows_here], key_row(own, rows_here), to_row(scale[:rows_here]))
    blocks = [first] + take_blocks(refs, n_blocks, rows_here)
    store_sides(*add_blocks(left, key, scale, blocks, None, None), refs)


def both_kernel(n_blocks, own, other, *refs):
    refs = list(refs)
    rows_here, wide = refs[-1].shape
    left, key, scale = left_of((own, other), rows_here)
    blocks = take_blocks(refs, n_blocks, rows_here)
    numer = jnp.concatenate([ref[:, : wide - 128] for ref in refs[:2]], axis=0)
    denom = jnp.concatenate([ref[:, wide - 128 : wide - 127] for ref in refs[:2]], axis=0)
    store_sides(*add_blocks(left, key, scale, blocks, numer, denom), refs[2:])


def one_kernel(n_blocks, left, *refs):
    refs = list(refs)
    rows_here, wide = refs[-1].shape
    blocks = take_blocks(refs, n_blocks, rows_here)
    numer = refs[0][:, : wide - 128]
    denom = refs[0][:, wide - 128 : wide - 127]
    store_sides(*add_blocks(*left_of((left,), rows_here), blocks, numer, denom), refs[1:])


def mean_kernel(mine, theirs, out):
    width = out.shape[1]
    denom = mine[:, width : width + 1] + theirs[:, width : width + 1]
    out[...] = ((mine[:, :width] + theirs[:, :width]) / denom).astype(BF16)


def whole_in_vmem(count):
    return [pl.BlockSpec(memory_space=pltpu.VMEM)] * count


def call(kernel, shapes, args, aliases={}):
    return pl.pallas_call(
        kernel,
        out_shape=[jax.ShapeDtypeStruct(shape, dtype) for shape, dtype in shapes],
        in_specs=whole_in_vmem(len(args)),
        out_specs=whole_in_vmem(len(shapes)),
        input_output_aliases=aliases,
        compiler_params=pltpu.CompilerParams(vmem_limit_bytes=VMEM_BYTES),
    )(*args)


def start_both(left, right, shape):
    args = list(left) + [half for block in right for half in block]
    return call(functools.partial(start_kernel, len(right)), [(shape, F32)] * 2, args)


def add_both(left, right, before):
    args = list(left) + [half for block in right for half in block] + list(before)
    at = len(args) - 2
    shapes = [(total.shape, F32) for total in before]
    return call(
        functools.partial(both_kernel, len(right)), shapes, args, {at: 0, at + 1: 1}
    )


def add_one(left, right, before):
    args = [left] + [half for block in right for half in block] + [before]
    shapes = [(before.shape, F32)]
    return call(functools.partial(one_kernel, len(right)), shapes, args, {len(args) - 1: 0})[0]


def folded_ring(size):
    return [0] + list(range(1, size, 2)) + list(range(2, size, 2))[::-1]


def together(*arrays):
    return lax.optimization_barrier(arrays)


def by_block(embeddings, group_of, cluster_id):
    rows_here, width = embeddings.shape
    half = rows_here // 2
    slabs = width // 128
    n_blk = lax.axis_size("blk")
    order = folded_ring(n_blk)
    line = (1, rows_here)

    def along(rows):
        hops = [
            (2 * order[i - 1] + core, 2 * order[i] + 1 - core)
            for i in range(n_blk)
            for core in range(2)
        ]
        return lax.ppermute(rows, ("blk", "pair"), hops)

    def across(rows):
        return lax.ppermute(rows, ("sub", "pair"), [(0, 3), (1, 2), (2, 1), (3, 0)])

    def other_core(rows):
        return lax.ppermute(rows, "pair", [(0, 1), (1, 0)])

    whole, first, second = call(
        pack_kernel,
        [
            ((slabs * rows_here + 8, 128), BF16),
            ((slabs * half + 8, 128), BF16),
            ((slabs * half, 128), BF16),
        ],
        [embeddings, group_of.reshape(line), cluster_id.reshape(line)],
    )
    along_by = [(first, second)]
    across_by = []
    for s in range(1, n_blk):
        moved = [along(piece) for piece in along_by[-1]]
        swapped = [across(piece) for piece in along_by[-1]]
        pairs = [together(m, w) for m, w in zip(moved, swapped)]
        along_by.append(tuple(pair[0] for pair in pairs))
        across_by.append(tuple(pair[1] for pair in pairs))
    left = (whole, other_core(whole))
    total = start_both(left, across_by[:-1] + along_by[1:-1], (rows_here, width + 128))
    far_first, mine, theirs = together(along_by[-1][0], *total)
    last = (across(far_first), along(across_by[-1][1]))
    mine, theirs = add_both(left, [across_by[-1], along_by[-1]], (mine, theirs))
    theirs = other_core(add_one(left[1], [last], theirs))
    mine = add_one(left[0], [last], mine)
    (out,) = call(mean_kernel, [((rows_here, width), BF16)], [mine, theirs])
    return out


def per_device(embeddings, group_of, cluster_id):
    rows_here, width = embeddings.shape
    devices = lax.axis_size("blk") * lax.axis_size("sub") * lax.axis_size("pair")
    small = devices * rows_here * width * 2 <= GATHER_LIMIT
    fits = width % 128 == 0 and rows_here % 32 == 0 and rows_here <= 512
    if small and fits and lax.axis_size("sub") == 2 and lax.axis_size("pair") == 2:
        return by_block(embeddings, group_of, cluster_id)
    return by_group(embeddings, group_of, cluster_id)


def solution(mesh):
    return jax.shard_map(
        per_device,
        mesh=mesh,
        in_specs=(
            P(("island", "blk", "sub", "pair"), None),
            P(("island", "blk", "sub", "pair"), None),
            P(("island", "blk", "sub", "pair")),
        ),
        out_specs=P(("island", "blk", "sub", "pair"), None),
        check_vma=False,
    )
```

```python
import functools

import jax
import jax.numpy as jnp
from jax import lax
from jax.experimental import pallas as pl
from jax.experimental.pallas import tpu as pltpu
from jax.sharding import PartitionSpec as P

F32 = jnp.float32
BF16 = jnp.bfloat16
VMEM_BYTES = 24 * 1024 * 1024
GATHER_LIMIT = 8 * 1024 * 1024


def unit_scale(rows_in):
    wide = rows_in.astype(F32)
    return lax.rsqrt(jnp.sum(wide * wide, axis=1) + 1e-06)


def tile_weights(left_rows, left_clust, left_scale, right_rows, right_clust, right_scale):
    grams = lax.dot_general(
        left_rows, right_rows, (((1,), (1,)), ((), ())), preferred_element_type=F32
    )
    cosine = grams * left_scale[:, None] * right_scale[None, :]
    same = (left_clust[:, None] == right_clust[None, :]).astype(F32)
    return jax.nn.sigmoid(8.0 * cosine - 2.0) * same


def by_group(embeddings, group_of, cluster_id):
    rows_here, width = embeddings.shape
    groups = lax.axis_size("sub") * lax.axis_size("pair")
    capacity = 2 * rows_here // groups
    slots = groups * capacity
    target = group_of[:, 0]
    onehot = (target[:, None] == jnp.arange(groups, dtype=jnp.int32)[None, :]).astype(jnp.int32)
    position = jnp.sum((jnp.cumsum(onehot, axis=0) - onehot) * onehot, axis=1)
    send_rows = jnp.zeros((groups, capacity, width), BF16).at[target, position].set(embeddings)
    send_clust = jnp.full((groups, capacity), -1, jnp.int32).at[target, position].set(cluster_id)
    recv_rows, recv_clust = (
        lax.all_to_all(send_rows, ("sub", "pair"), split_axis=0, concat_axis=0, tiled=True),
        lax.all_to_all(send_clust, ("sub", "pair"), split_axis=0, concat_axis=0, tiled=True),
    )
    own_rows = recv_rows.reshape(slots, width)
    own_clust = recv_clust.reshape(slots)
    own_scale = unit_scale(own_rows)
    piece_rows = lax.all_gather(own_rows, "blk", axis=0, tiled=True)
    piece_clust = lax.all_gather(own_clust, "blk", axis=0, tiled=True)
    weight = tile_weights(
        own_rows, own_clust, own_scale, piece_rows, piece_clust, unit_scale(piece_rows)
    )
    numer = jnp.dot(weight.astype(BF16), piece_rows, preferred_element_type=F32)
    denom = jnp.sum(weight, axis=1)
    result = (numer / denom[:, None]).astype(BF16).reshape(groups, capacity, width)
    returned = lax.all_to_all(result, ("sub", "pair"), split_axis=0, concat_axis=0, tiled=True)
    return returned[target, position]


def diagonal(size):
    shape = (size, size)
    return lax.broadcasted_iota(jnp.int32, shape, 0) == lax.broadcasted_iota(jnp.int32, shape, 1)


def to_column(row):
    size = row.shape[1]
    return jnp.sum(jnp.where(diagonal(size), row, jnp.zeros_like(row)), axis=1, keepdims=True)


def to_row(column):
    size = column.shape[0]
    return jnp.sum(jnp.where(diagonal(size), column, jnp.zeros_like(column)), axis=0, keepdims=True)


def scale_column(rows):
    wide = rows.astype(F32)
    return lax.rsqrt(jnp.sum(wide * wide, axis=1, keepdims=True) + 1e-06)


def name_lines(rows_here):
    return -(-rows_here // 128)


def pack_kernel(rows, group, cluster, whole, first, second):
    rows_here, width = rows.shape
    slabs = width // 128
    half = rows_here // 2
    for slab in range(slabs):
        columns = rows[:, slab * 128 : (slab + 1) * 128]
        whole[slab * rows_here : (slab + 1) * rows_here, :] = columns
        first[slab * half : (slab + 1) * half, :] = columns[:half]
        second[slab * half : (slab + 1) * half, :] = columns[half:]
    line_at = lax.broadcasted_iota(jnp.int32, (8, 128), 0)
    lines = name_lines(rows_here)
    named = jnp.zeros((8, 128), jnp.int32)
    for kind, ref in enumerate((group, cluster)):
        for line in range(lines):
            part = ref[:, line * 128 : (line + 1) * 128]
            if part.shape[1] < 128:
                rest = jnp.zeros((1, 128 - part.shape[1]), jnp.int32)
                part = jnp.concatenate([part, rest], axis=1)
            named = jnp.where(line_at == kind * lines + line, part, named)
    named = named.astype(F32).astype(BF16)
    whole[slabs * rows_here :, :] = named
    first[slabs * half :, :] = named


def from_slabs(ref, count):
    slabs = [ref[top : top + count, :] for top in range(0, ref.shape[0] // count * count, count)]
    return jnp.concatenate(slabs, axis=1)


def key_row(ref, rows_here):
    wide = ref[ref.shape[0] - 8 :, :].astype(F32)
    lines = name_lines(rows_here)
    kinds = []
    for kind in range(2):
        parts = [wide[kind * lines + line : kind * lines + line + 1, :] for line in range(lines)]
        kinds.append(jnp.concatenate(parts, axis=1)[:, :rows_here])
    return kinds[0] * 256.0 + kinds[1]


def from_halves(first, second, rows_here):
    half = rows_here // 2
    rows = jnp.concatenate([from_slabs(first, half), from_slabs(second, half)], axis=0)
    return rows, key_row(first, rows_here)


def add_blocks(left, key, scale, blocks, numer, denom):
    scale = 4.0 * scale
    for right_rows, right_key, right_scale in blocks:
        grams = lax.dot_general(
            left, right_rows, (((1,), (1,)), ((), ())), preferred_element_type=F32
        )
        half = jnp.tanh(grams * scale * right_scale - 1.0)
        weight = jnp.where(key == right_key, 0.5 + 0.5 * half, 0.0)
        add = jnp.dot(weight.astype(BF16), right_rows, preferred_element_type=F32)
        add_denom = jnp.sum(weight, axis=1, keepdims=True)
        numer = add if numer is None else numer + add
        denom = add_denom if denom is None else denom + add_denom
    return numer, denom


def left_of(refs, rows_here):
    rows = jnp.concatenate([from_slabs(ref, rows_here) for ref in refs], axis=0)
    key = jnp.concatenate([to_column(key_row(ref, rows_here)) for ref in refs], axis=0)
    return rows, key, scale_column(rows)


def take_blocks(refs, count, rows_here):
    blocks = []
    for _ in range(count):
        rows, key = from_halves(refs.pop(0), refs.pop(0), rows_here)
        blocks.append((rows, key, to_row(scale_column(rows))))
    return blocks


def store_sides(numer, denom, outs):
    rows_here, wide = outs[0].shape
    for side, out in enumerate(outs):
        top = side * rows_here
        out[:, : wide - 128] = numer[top : top + rows_here]
        out[:, wide - 128 :] = jnp.broadcast_to(denom[top : top + rows_here], (rows_here, 128))


def start_kernel(n_blocks, own, other, *refs):
    refs = list(refs)
    rows_here = refs[-1].shape[0]
    left, key, scale = left_of((own, other), rows_here)
    first = (left[:rows_here], key_row(own, rows_here), to_row(scale[:rows_here]))
    blocks = [first] + take_blocks(refs, n_blocks, rows_here)
    store_sides(*add_blocks(left, key, scale, blocks, None, None), refs)


def both_kernel(n_blocks, own, other, *refs):
    refs = list(refs)
    rows_here, wide = refs[-1].shape
    left, key, scale = left_of((own, other), rows_here)
    blocks = take_blocks(refs, n_blocks, rows_here)
    numer = jnp.concatenate([ref[:, : wide - 128] for ref in refs[:2]], axis=0)
    denom = jnp.concatenate([ref[:, wide - 128 : wide - 127] for ref in refs[:2]], axis=0)
    store_sides(*add_blocks(left, key, scale, blocks, numer, denom), refs[2:])


def one_kernel(n_blocks, left, *refs):
    refs = list(refs)
    rows_here, wide = refs[-1].shape
    blocks = take_blocks(refs, n_blocks, rows_here)
    numer = refs[0][:, : wide - 128]
    denom = refs[0][:, wide - 128 : wide - 127]
    store_sides(*add_blocks(*left_of((left,), rows_here), blocks, numer, denom), refs[1:])


def mean_kernel(mine, theirs, out):
    width = out.shape[1]
    denom = mine[:, width : width + 1] + theirs[:, width : width + 1]
    out[...] = ((mine[:, :width] + theirs[:, :width]) / denom).astype(BF16)


def whole_in_vmem(count):
    return [pl.BlockSpec(memory_space=pltpu.VMEM)] * count


def call(kernel, shapes, args, aliases={}):
    return pl.pallas_call(
        kernel,
        out_shape=[jax.ShapeDtypeStruct(shape, dtype) for shape, dtype in shapes],
        in_specs=whole_in_vmem(len(args)),
        out_specs=whole_in_vmem(len(shapes)),
        input_output_aliases=aliases,
        compiler_params=pltpu.CompilerParams(vmem_limit_bytes=VMEM_BYTES),
    )(*args)


def start_both(left, right, shape):
    args = list(left) + [half for block in right for half in block]
    return call(functools.partial(start_kernel, len(right)), [(shape, F32)] * 2, args)


def add_both(left, right, before):
    args = list(left) + [half for block in right for half in block] + list(before)
    at = len(args) - 2
    shapes = [(total.shape, F32) for total in before]
    return call(
        functools.partial(both_kernel, len(right)), shapes, args, {at: 0, at + 1: 1}
    )


def add_one(left, right, before):
    args = [left] + [half for block in right for half in block] + [before]
    shapes = [(before.shape, F32)]
    return call(functools.partial(one_kernel, len(right)), shapes, args, {len(args) - 1: 0})[0]


def folded_ring(size):
    return [0] + list(range(1, size, 2)) + list(range(2, size, 2))[::-1]


def together(*arrays):
    return lax.optimization_barrier(arrays)


def by_block(embeddings, group_of, cluster_id):
    rows_here, width = embeddings.shape
    half = rows_here // 2
    slabs = width // 128
    n_blk = lax.axis_size("blk")
    order = folded_ring(n_blk)
    line = (1, rows_here)

    def along(rows):
        hops = [
            (2 * order[i - 1] + core, 2 * order[i] + 1 - core)
            for i in range(n_blk)
            for core in range(2)
        ]
        return lax.ppermute(rows, ("blk", "pair"), hops)

    def across(rows):
        return lax.ppermute(rows, ("sub", "pair"), [(0, 3), (1, 2), (2, 1), (3, 0)])

    def other_core(rows):
        return lax.ppermute(rows, "pair", [(0, 1), (1, 0)])

    whole, first, second = call(
        pack_kernel,
        [
            ((slabs * rows_here + 8, 128), BF16),
            ((slabs * half + 8, 128), BF16),
            ((slabs * half, 128), BF16),
        ],
        [embeddings, group_of.reshape(line), cluster_id.reshape(line)],
    )
    along_by = [(first, second)]
    across_by = []
    other = other_core(whole)
    for s in range(1, n_blk):
        near, far = along_by[-1]
        if s == 2:
            other, far, *ended = together(other, far, *across_by[-1])
        elif s > 2:
            far, *ended = together(far, *across_by[-1])
        if s > 1:
            along_by[-1], across_by[-1] = (near, far), tuple(ended)
        across_by.append((across(near), across(far)))
        along_by.append((along(near), along(far)))
    left = (whole, other)
    total = start_both(left, across_by[:-1] + along_by[1:-1], (rows_here, width + 128))
    far_first, mine, theirs = together(along_by[-1][0], *total)
    along_by[-1], across_by[-1] = (
        (far_first, along_by[-1][1]),
        together(*across_by[-1], along_by[-1][1])[:2],
    )
    last = (across(far_first), along(across_by[-1][1]))
    mine, theirs = add_both(left, [across_by[-1], along_by[-1]], (mine, theirs))
    theirs = other_core(add_one(left[1], [last], theirs))
    mine = add_one(left[0], [last], mine)
    (out,) = call(mean_kernel, [((rows_here, width), BF16)], [mine, theirs])
    return out


def per_device(embeddings, group_of, cluster_id):
    rows_here, width = embeddings.shape
    devices = lax.axis_size("blk") * lax.axis_size("sub") * lax.axis_size("pair")
    small = devices * rows_here * width * 2 <= GATHER_LIMIT
    fits = width % 128 == 0 and rows_here % 32 == 0 and rows_here <= 512
    if small and fits and lax.axis_size("sub") == 2 and lax.axis_size("pair") == 2:
        return by_block(embeddings, group_of, cluster_id)
    return by_group(embeddings, group_of, cluster_id)


def solution(mesh):
    return jax.shard_map(
        per_device,
        mesh=mesh,
        in_specs=(
            P(("island", "blk", "sub", "pair"), None),
            P(("island", "blk", "sub", "pair"), None),
            P(("island", "blk", "sub", "pair")),
        ),
        out_specs=P(("island", "blk", "sub", "pair"), None),
        check_vma=False,
    )
```

```python
import functools

import jax
import jax.numpy as jnp
from jax import lax
from jax.experimental import pallas as pl
from jax.experimental.pallas import tpu as pltpu
from jax.sharding import PartitionSpec as P

F32 = jnp.float32
BF16 = jnp.bfloat16
VMEM_BYTES = 24 * 1024 * 1024
GATHER_LIMIT = 8 * 1024 * 1024


def unit_scale(rows_in):
    wide = rows_in.astype(F32)
    return lax.rsqrt(jnp.sum(wide * wide, axis=1) + 1e-06)


def tile_weights(left_rows, left_clust, left_scale, right_rows, right_clust, right_scale):
    grams = lax.dot_general(
        left_rows, right_rows, (((1,), (1,)), ((), ())), preferred_element_type=F32
    )
    cosine = grams * left_scale[:, None] * right_scale[None, :]
    same = (left_clust[:, None] == right_clust[None, :]).astype(F32)
    return jax.nn.sigmoid(8.0 * cosine - 2.0) * same


def by_group(embeddings, group_of, cluster_id):
    rows_here, width = embeddings.shape
    groups = lax.axis_size("sub") * lax.axis_size("pair")
    capacity = 2 * rows_here // groups
    slots = groups * capacity
    target = group_of[:, 0]
    onehot = (target[:, None] == jnp.arange(groups, dtype=jnp.int32)[None, :]).astype(jnp.int32)
    position = jnp.sum((jnp.cumsum(onehot, axis=0) - onehot) * onehot, axis=1)
    send_rows = jnp.zeros((groups, capacity, width), BF16).at[target, position].set(embeddings)
    send_clust = jnp.full((groups, capacity), -1, jnp.int32).at[target, position].set(cluster_id)
    recv_rows, recv_clust = (
        lax.all_to_all(send_rows, ("sub", "pair"), split_axis=0, concat_axis=0, tiled=True),
        lax.all_to_all(send_clust, ("sub", "pair"), split_axis=0, concat_axis=0, tiled=True),
    )
    own_rows = recv_rows.reshape(slots, width)
    own_clust = recv_clust.reshape(slots)
    own_scale = unit_scale(own_rows)
    piece_rows = lax.all_gather(own_rows, "blk", axis=0, tiled=True)
    piece_clust = lax.all_gather(own_clust, "blk", axis=0, tiled=True)
    weight = tile_weights(
        own_rows, own_clust, own_scale, piece_rows, piece_clust, unit_scale(piece_rows)
    )
    numer = jnp.dot(weight.astype(BF16), piece_rows, preferred_element_type=F32)
    denom = jnp.sum(weight, axis=1)
    result = (numer / denom[:, None]).astype(BF16).reshape(groups, capacity, width)
    returned = lax.all_to_all(result, ("sub", "pair"), split_axis=0, concat_axis=0, tiled=True)
    return returned[target, position]


def diagonal(size):
    shape = (size, size)
    return lax.broadcasted_iota(jnp.int32, shape, 0) == lax.broadcasted_iota(jnp.int32, shape, 1)


def to_column(row):
    size = row.shape[1]
    return jnp.sum(jnp.where(diagonal(size), row, jnp.zeros_like(row)), axis=1, keepdims=True)


def to_row(column):
    size = column.shape[0]
    return jnp.sum(jnp.where(diagonal(size), column, jnp.zeros_like(column)), axis=0, keepdims=True)


def scale_column(rows):
    wide = rows.astype(F32)
    return lax.rsqrt(jnp.sum(wide * wide, axis=1, keepdims=True) + 1e-06)


def name_lines(rows_here):
    return -(-rows_here // 128)


def pack_kernel(rows, group, cluster, whole, first, second):
    rows_here, width = rows.shape
    slabs = width // 128
    half = rows_here // 2
    for slab in range(slabs):
        columns = rows[:, slab * 128 : (slab + 1) * 128]
        whole[slab * rows_here : (slab + 1) * rows_here, :] = columns
        first[slab * half : (slab + 1) * half, :] = columns[:half]
        second[slab * half : (slab + 1) * half, :] = columns[half:]
    line_at = lax.broadcasted_iota(jnp.int32, (8, 128), 0)
    lines = name_lines(rows_here)
    named = jnp.zeros((8, 128), jnp.int32)
    for kind, ref in enumerate((group, cluster)):
        for line in range(lines):
            part = ref[:, line * 128 : (line + 1) * 128]
            if part.shape[1] < 128:
                rest = jnp.zeros((1, 128 - part.shape[1]), jnp.int32)
                part = jnp.concatenate([part, rest], axis=1)
            named = jnp.where(line_at == kind * lines + line, part, named)
    named = named.astype(F32).astype(BF16)
    whole[slabs * rows_here :, :] = named
    first[slabs * half :, :] = named


def from_slabs(ref, count):
    slabs = [ref[top : top + count, :] for top in range(0, ref.shape[0] // count * count, count)]
    return jnp.concatenate(slabs, axis=1)


def key_row(ref, rows_here):
    wide = ref[ref.shape[0] - 8 :, :].astype(F32)
    lines = name_lines(rows_here)
    kinds = []
    for kind in range(2):
        parts = [wide[kind * lines + line : kind * lines + line + 1, :] for line in range(lines)]
        kinds.append(jnp.concatenate(parts, axis=1)[:, :rows_here])
    return kinds[0] * 256.0 + kinds[1]


def from_halves(first, second, rows_here):
    half = rows_here // 2
    rows = jnp.concatenate([from_slabs(first, half), from_slabs(second, half)], axis=0)
    return rows, key_row(first, rows_here)


def add_blocks(left, key, scale, blocks, numer, denom):
    scale = 4.0 * scale
    for right_rows, right_key, right_scale in blocks:
        grams = lax.dot_general(
            left, right_rows, (((1,), (1,)), ((), ())), preferred_element_type=F32
        )
        half = jnp.tanh(grams * scale * right_scale - 1.0)
        weight = jnp.where(key == right_key, 0.5 + 0.5 * half, 0.0)
        add = jnp.dot(weight.astype(BF16), right_rows, preferred_element_type=F32)
        add_denom = jnp.sum(weight, axis=1, keepdims=True)
        numer = add if numer is None else numer + add
        denom = add_denom if denom is None else denom + add_denom
    return numer, denom


def left_of(refs, rows_here):
    rows = jnp.concatenate([from_slabs(ref, rows_here) for ref in refs], axis=0)
    key = jnp.concatenate([to_column(key_row(ref, rows_here)) for ref in refs], axis=0)
    return rows, key, scale_column(rows)


def take_blocks(refs, count, rows_here):
    blocks = []
    for _ in range(count):
        rows, key = from_halves(refs.pop(0), refs.pop(0), rows_here)
        blocks.append((rows, key, to_row(scale_column(rows))))
    return blocks


def store_sides(numer, denom, outs):
    rows_here, wide = outs[0].shape
    for side, out in enumerate(outs):
        top = side * rows_here
        out[:, : wide - 128] = numer[top : top + rows_here]
        out[:, wide - 128 :] = jnp.broadcast_to(denom[top : top + rows_here], (rows_here, 128))


def start_kernel(n_blocks, own, other, *refs):
    refs = list(refs)
    rows_here = refs[-1].shape[0]
    left, key, scale = left_of((own, other), rows_here)
    first = (left[:rows_here], key_row(own, rows_here), to_row(scale[:rows_here]))
    blocks = [first] + take_blocks(refs, n_blocks, rows_here)
    store_sides(*add_blocks(left, key, scale, blocks, None, None), refs)


def both_kernel(n_blocks, own, other, *refs):
    refs = list(refs)
    rows_here, wide = refs[-1].shape
    left, key, scale = left_of((own, other), rows_here)
    blocks = take_blocks(refs, n_blocks, rows_here)
    numer = jnp.concatenate([ref[:, : wide - 128] for ref in refs[:2]], axis=0)
    denom = jnp.concatenate([ref[:, wide - 128 : wide - 127] for ref in refs[:2]], axis=0)
    store_sides(*add_blocks(left, key, scale, blocks, numer, denom), refs[2:])


def one_kernel(n_blocks, left, *refs):
    refs = list(refs)
    rows_here, wide = refs[-1].shape
    blocks = take_blocks(refs, n_blocks, rows_here)
    numer = refs[0][:, : wide - 128]
    denom = refs[0][:, wide - 128 : wide - 127]
    store_sides(*add_blocks(*left_of((left,), rows_here), blocks, numer, denom), refs[1:])


def mean_kernel(mine, theirs, out):
    width = out.shape[1]
    denom = mine[:, width : width + 1] + theirs[:, width : width + 1]
    out[...] = ((mine[:, :width] + theirs[:, :width]) / denom).astype(BF16)


def whole_in_vmem(count):
    return [pl.BlockSpec(memory_space=pltpu.VMEM)] * count


def call(kernel, shapes, args, aliases={}):
    return pl.pallas_call(
        kernel,
        out_shape=[jax.ShapeDtypeStruct(shape, dtype) for shape, dtype in shapes],
        in_specs=whole_in_vmem(len(args)),
        out_specs=whole_in_vmem(len(shapes)),
        input_output_aliases=aliases,
        compiler_params=pltpu.CompilerParams(vmem_limit_bytes=VMEM_BYTES),
    )(*args)


def start_both(left, right, shape):
    args = list(left) + [half for block in right for half in block]
    return call(functools.partial(start_kernel, len(right)), [(shape, F32)] * 2, args)


def add_both(left, right, before):
    args = list(left) + [half for block in right for half in block] + list(before)
    at = len(args) - 2
    shapes = [(total.shape, F32) for total in before]
    return call(
        functools.partial(both_kernel, len(right)), shapes, args, {at: 0, at + 1: 1}
    )


def add_one(left, right, before):
    args = [left] + [half for block in right for half in block] + [before]
    shapes = [(before.shape, F32)]
    return call(functools.partial(one_kernel, len(right)), shapes, args, {len(args) - 1: 0})[0]


def folded_ring(size):
    return [0] + list(range(1, size, 2)) + list(range(2, size, 2))[::-1]


def together(*arrays):
    return lax.optimization_barrier(arrays)


def by_block(embeddings, group_of, cluster_id):
    rows_here, width = embeddings.shape
    half = rows_here // 2
    slabs = width // 128
    n_blk = lax.axis_size("blk")
    order = folded_ring(n_blk)
    line = (1, rows_here)

    def along(rows):
        hops = [
            (2 * order[i - 1] + core, 2 * order[i] + 1 - core)
            for i in range(n_blk)
            for core in range(2)
        ]
        return lax.ppermute(rows, ("blk", "pair"), hops)

    def across(rows):
        return lax.ppermute(rows, ("sub", "pair"), [(0, 3), (1, 2), (2, 1), (3, 0)])

    def other_core(rows):
        return lax.ppermute(rows, "pair", [(0, 1), (1, 0)])

    whole, first, second = call(
        pack_kernel,
        [
            ((slabs * rows_here + 8, 128), BF16),
            ((slabs * half + 8, 128), BF16),
            ((slabs * half, 128), BF16),
        ],
        [embeddings, group_of.reshape(line), cluster_id.reshape(line)],
    )
    along_by = [(first, second)]
    across_by = []
    for s in range(1, n_blk):
        moved = [along(piece) for piece in along_by[-1]]
        swapped = [across(piece) for piece in along_by[-1]]
        pairs = [together(m, w) for m, w in zip(moved, swapped)]
        along_by.append(tuple(pair[0] for pair in pairs))
        across_by.append(tuple(pair[1] for pair in pairs))
    left = (whole, other_core(whole))
    total = start_both(left, across_by[:-1] + along_by[1:-1], (rows_here, width + 128))
    near_first, _, mine, theirs = together(across_by[-1][0], along_by[-1][0], *total)
    last = (along(near_first), across(along_by[-1][1]))
    mine, theirs = add_both(left, [across_by[-1], along_by[-1]], (mine, theirs))
    theirs = other_core(add_one(left[1], [last], theirs))
    mine = add_one(left[0], [last], mine)
    (out,) = call(mean_kernel, [((rows_here, width), BF16)], [mine, theirs])
    return out


def per_device(embeddings, group_of, cluster_id):
    rows_here, width = embeddings.shape
    devices = lax.axis_size("blk") * lax.axis_size("sub") * lax.axis_size("pair")
    small = devices * rows_here * width * 2 <= GATHER_LIMIT
    fits = width % 128 == 0 and rows_here % 32 == 0 and rows_here <= 512
    if small and fits and lax.axis_size("sub") == 2 and lax.axis_size("pair") == 2:
        return by_block(embeddings, group_of, cluster_id)
    return by_group(embeddings, group_of, cluster_id)


def solution(mesh):
    return jax.shard_map(
        per_device,
        mesh=mesh,
        in_specs=(
            P(("island", "blk", "sub", "pair"), None),
            P(("island", "blk", "sub", "pair"), None),
            P(("island", "blk", "sub", "pair")),
        ),
        out_specs=P(("island", "blk", "sub", "pair"), None),
        check_vma=False,
    )
```

```python
import functools

import jax
import jax.numpy as jnp
from jax import lax
from jax.experimental import pallas as pl
from jax.experimental.pallas import tpu as pltpu
from jax.sharding import PartitionSpec as P

F32 = jnp.float32
BF16 = jnp.bfloat16
VMEM_BYTES = 24 * 1024 * 1024
GATHER_LIMIT = 8 * 1024 * 1024


def unit_scale(rows_in):
    wide = rows_in.astype(F32)
    return lax.rsqrt(jnp.sum(wide * wide, axis=1) + 1e-06)


def tile_weights(left_rows, left_clust, left_scale, right_rows, right_clust, right_scale):
    grams = lax.dot_general(
        left_rows, right_rows, (((1,), (1,)), ((), ())), preferred_element_type=F32
    )
    cosine = grams * left_scale[:, None] * right_scale[None, :]
    same = (left_clust[:, None] == right_clust[None, :]).astype(F32)
    return jax.nn.sigmoid(8.0 * cosine - 2.0) * same


def by_group(embeddings, group_of, cluster_id):
    rows_here, width = embeddings.shape
    groups = lax.axis_size("sub") * lax.axis_size("pair")
    capacity = 2 * rows_here // groups
    slots = groups * capacity
    target = group_of[:, 0]
    onehot = (target[:, None] == jnp.arange(groups, dtype=jnp.int32)[None, :]).astype(jnp.int32)
    position = jnp.sum((jnp.cumsum(onehot, axis=0) - onehot) * onehot, axis=1)
    send_rows = jnp.zeros((groups, capacity, width), BF16).at[target, position].set(embeddings)
    send_clust = jnp.full((groups, capacity), -1, jnp.int32).at[target, position].set(cluster_id)
    recv_rows, recv_clust = (
        lax.all_to_all(send_rows, ("sub", "pair"), split_axis=0, concat_axis=0, tiled=True),
        lax.all_to_all(send_clust, ("sub", "pair"), split_axis=0, concat_axis=0, tiled=True),
    )
    own_rows = recv_rows.reshape(slots, width)
    own_clust = recv_clust.reshape(slots)
    own_scale = unit_scale(own_rows)
    piece_rows = lax.all_gather(own_rows, "blk", axis=0, tiled=True)
    piece_clust = lax.all_gather(own_clust, "blk", axis=0, tiled=True)
    weight = tile_weights(
        own_rows, own_clust, own_scale, piece_rows, piece_clust, unit_scale(piece_rows)
    )
    numer = jnp.dot(weight.astype(BF16), piece_rows, preferred_element_type=F32)
    denom = jnp.sum(weight, axis=1)
    result = (numer / denom[:, None]).astype(BF16).reshape(groups, capacity, width)
    returned = lax.all_to_all(result, ("sub", "pair"), split_axis=0, concat_axis=0, tiled=True)
    return returned[target, position]


def diagonal(size):
    shape = (size, size)
    return lax.broadcasted_iota(jnp.int32, shape, 0) == lax.broadcasted_iota(jnp.int32, shape, 1)


def to_column(row):
    size = row.shape[1]
    return jnp.sum(jnp.where(diagonal(size), row, jnp.zeros_like(row)), axis=1, keepdims=True)


def to_row(column):
    size = column.shape[0]
    return jnp.sum(jnp.where(diagonal(size), column, jnp.zeros_like(column)), axis=0, keepdims=True)


def scale_column(rows):
    wide = rows.astype(F32)
    return lax.rsqrt(jnp.sum(wide * wide, axis=1, keepdims=True) + 1e-06)


def name_lines(rows_here):
    return -(-rows_here // 128)


def pack_kernel(rows, group, cluster, whole, first, second):
    rows_here, width = rows.shape
    slabs = width // 128
    half = rows_here // 2
    for slab in range(slabs):
        columns = rows[:, slab * 128 : (slab + 1) * 128]
        whole[slab * rows_here : (slab + 1) * rows_here, :] = columns
        first[slab * half : (slab + 1) * half, :] = columns[:half]
        second[slab * half : (slab + 1) * half, :] = columns[half:]
    line_at = lax.broadcasted_iota(jnp.int32, (8, 128), 0)
    lines = name_lines(rows_here)
    named = jnp.zeros((8, 128), jnp.int32)
    for kind, ref in enumerate((group, cluster)):
        for line in range(lines):
            part = ref[:, line * 128 : (line + 1) * 128]
            if part.shape[1] < 128:
                rest = jnp.zeros((1, 128 - part.shape[1]), jnp.int32)
                part = jnp.concatenate([part, rest], axis=1)
            named = jnp.where(line_at == kind * lines + line, part, named)
    named = named.astype(F32).astype(BF16)
    whole[slabs * rows_here :, :] = named
    first[slabs * half :, :] = named


def from_slabs(ref, count):
    slabs = [ref[top : top + count, :] for top in range(0, ref.shape[0] // count * count, count)]
    return jnp.concatenate(slabs, axis=1)


def key_row(ref, rows_here):
    wide = ref[ref.shape[0] - 8 :, :].astype(F32)
    lines = name_lines(rows_here)
    kinds = []
    for kind in range(2):
        parts = [wide[kind * lines + line : kind * lines + line + 1, :] for line in range(lines)]
        kinds.append(jnp.concatenate(parts, axis=1)[:, :rows_here])
    return kinds[0] * 256.0 + kinds[1]


def from_halves(first, second, rows_here):
    half = rows_here // 2
    rows = jnp.concatenate([from_slabs(first, half), from_slabs(second, half)], axis=0)
    return rows, key_row(first, rows_here)


def add_blocks(left, key, scale, blocks, numer, denom):
    scale = 4.0 * scale
    for right_rows, right_key, right_scale in blocks:
        grams = lax.dot_general(
            left, right_rows, (((1,), (1,)), ((), ())), preferred_element_type=F32
        )
        half = jnp.tanh(grams * scale * right_scale - 1.0)
        weight = jnp.where(key == right_key, 0.5 + 0.5 * half, 0.0)
        add = jnp.dot(weight.astype(BF16), right_rows, preferred_element_type=F32)
        add_denom = jnp.sum(weight, axis=1, keepdims=True)
        numer = add if numer is None else numer + add
        denom = add_denom if denom is None else denom + add_denom
    return numer, denom


def left_of(refs, rows_here):
    rows = jnp.concatenate([from_slabs(ref, rows_here) for ref in refs], axis=0)
    key = jnp.concatenate([to_column(key_row(ref, rows_here)) for ref in refs], axis=0)
    return rows, key, scale_column(rows)


def take_blocks(refs, count, rows_here):
    blocks = []
    for _ in range(count):
        rows, key = from_halves(refs.pop(0), refs.pop(0), rows_here)
        blocks.append((rows, key, to_row(scale_column(rows))))
    return blocks


def store_sides(numer, denom, outs):
    rows_here, wide = outs[0].shape
    for side, out in enumerate(outs):
        top = side * rows_here
        out[:, : wide - 128] = numer[top : top + rows_here]
        out[:, wide - 128 :] = jnp.broadcast_to(denom[top : top + rows_here], (rows_here, 128))


def start_kernel(n_blocks, own, other, *refs):
    refs = list(refs)
    rows_here = refs[-1].shape[0]
    left, key, scale = left_of((own, other), rows_here)
    first = (left[:rows_here], key_row(own, rows_here), to_row(scale[:rows_here]))
    blocks = [first] + take_blocks(refs, n_blocks, rows_here)
    store_sides(*add_blocks(left, key, scale, blocks, None, None), refs)


def both_kernel(n_blocks, own, other, *refs):
    refs = list(refs)
    rows_here, wide = refs[-1].shape
    left, key, scale = left_of((own, other), rows_here)
    blocks = take_blocks(refs, n_blocks, rows_here)
    numer = jnp.concatenate([ref[:, : wide - 128] for ref in refs[:2]], axis=0)
    denom = jnp.concatenate([ref[:, wide - 128 : wide - 127] for ref in refs[:2]], axis=0)
    store_sides(*add_blocks(left, key, scale, blocks, numer, denom), refs[2:])


def half_of(first, second, rows_here):
    half = rows_here // 2
    rows = from_slabs(first if second is None else second, half)
    top = 0 if second is None else half
    key = to_column(key_row(first, rows_here))[top : top + half]
    return rows, to_row(key), to_row(scale_column(rows))


def first_half_kernel(own, other, first, *refs):
    rows_here, wide = refs[-1].shape
    left, key, scale = left_of((own, other), rows_here)
    blocks = [half_of(first, None, rows_here)]
    numer = jnp.concatenate([ref[:, : wide - 128] for ref in refs[:2]], axis=0)
    denom = jnp.concatenate([ref[:, wide - 128 : wide - 127] for ref in refs[:2]], axis=0)
    store_sides(*add_blocks(left, key, scale, blocks, numer, denom), refs[2:])


def second_half_kernel(left, first, second, before, out):
    rows_here, wide = before.shape
    width = wide - 128
    blocks = [half_of(first, second, rows_here)]
    sides = left_of((left,), rows_here)
    numer, denom = add_blocks(*sides, blocks, before[:, :width], before[:, width : width + 1])
    if out.dtype == F32:
        store_sides(numer, denom, [out])
    else:
        high = denom.astype(BF16).astype(F32)
        lane = lax.broadcasted_iota(jnp.int32, (rows_here, 128), 1)
        out[:, :width] = numer.astype(BF16)
        out[:, width:] = jnp.where(lane == 0, high, denom - high).astype(BF16)


def mean_kernel(mine, theirs, out):
    width = out.shape[1]
    parts = theirs[:, width:].astype(F32)
    denom = mine[:, width : width + 1] + (parts[:, 0:1] + parts[:, 1:2])
    out[...] = ((mine[:, :width] + theirs[:, :width].astype(F32)) / denom).astype(BF16)


def whole_in_vmem(count):
    return [pl.BlockSpec(memory_space=pltpu.VMEM)] * count


def call(kernel, shapes, args, aliases={}):
    return pl.pallas_call(
        kernel,
        out_shape=[jax.ShapeDtypeStruct(shape, dtype) for shape, dtype in shapes],
        in_specs=whole_in_vmem(len(args)),
        out_specs=whole_in_vmem(len(shapes)),
        input_output_aliases=aliases,
        compiler_params=pltpu.CompilerParams(vmem_limit_bytes=VMEM_BYTES),
    )(*args)


def start_both(left, right, shape):
    args = list(left) + [half for block in right for half in block]
    return call(functools.partial(start_kernel, len(right)), [(shape, F32)] * 2, args)


def add_both(left, right, before):
    args = list(left) + [half for block in right for half in block] + list(before)
    at = len(args) - 2
    shapes = [(total.shape, F32) for total in before]
    return call(
        functools.partial(both_kernel, len(right)), shapes, args, {at: 0, at + 1: 1}
    )


def add_first_half(left, first, before):
    shapes = [(total.shape, F32) for total in before]
    return call(first_half_kernel, shapes, [*left, first, *before], {3: 0, 4: 1})


def add_second_half(left, halves, before, dtype):
    return call(second_half_kernel, [(before.shape, dtype)], [left, *halves, before])[0]


def folded_ring(size):
    return [0] + list(range(1, size, 2)) + list(range(2, size, 2))[::-1]


def together(*arrays):
    return lax.optimization_barrier(arrays)


def by_block(embeddings, group_of, cluster_id):
    rows_here, width = embeddings.shape
    half = rows_here // 2
    slabs = width // 128
    n_blk = lax.axis_size("blk")
    order = folded_ring(n_blk)
    line = (1, rows_here)

    def along(rows):
        hops = [
            (2 * order[i - 1] + core, 2 * order[i] + 1 - core)
            for i in range(n_blk)
            for core in range(2)
        ]
        return lax.ppermute(rows, ("blk", "pair"), hops)

    def across(rows):
        return lax.ppermute(rows, ("sub", "pair"), [(0, 3), (1, 2), (2, 1), (3, 0)])

    def other_core(rows):
        return lax.ppermute(rows, "pair", [(0, 1), (1, 0)])

    whole, first, second = call(
        pack_kernel,
        [
            ((slabs * rows_here + 8, 128), BF16),
            ((slabs * half + 8, 128), BF16),
            ((slabs * half, 128), BF16),
        ],
        [embeddings, group_of.reshape(line), cluster_id.reshape(line)],
    )
    along_by = [(first, second)]
    across_by = []
    for s in range(1, n_blk):
        moved = [along(piece) for piece in along_by[-1]]
        swapped = [across(piece) for piece in along_by[-1]]
        pairs = [together(m, w) for m, w in zip(moved, swapped)]
        along_by.append(tuple(pair[0] for pair in pairs))
        across_by.append(tuple(pair[1] for pair in pairs))
    left = (whole, other_core(whole))
    total = start_both(left, across_by[:-1] + along_by[1:-1], (rows_here, width + 128))
    near_first, _, mine, theirs = together(across_by[-1][0], along_by[-1][0], *total)
    last = (along(near_first), across(along_by[-1][1]))
    mine, theirs = add_both(left, [across_by[-1], along_by[-1]], (mine, theirs))
    mine, theirs = add_first_half(left, last[0], (mine, theirs))
    theirs = other_core(add_second_half(left[1], last, theirs, BF16))
    mine = add_second_half(left[0], last, mine, F32)
    (out,) = call(mean_kernel, [((rows_here, width), BF16)], [mine, theirs])
    return out


def per_device(embeddings, group_of, cluster_id):
    rows_here, width = embeddings.shape
    devices = lax.axis_size("blk") * lax.axis_size("sub") * lax.axis_size("pair")
    small = devices * rows_here * width * 2 <= GATHER_LIMIT
    fits = width % 128 == 0 and rows_here % 32 == 0 and rows_here <= 512
    if small and fits and lax.axis_size("sub") == 2 and lax.axis_size("pair") == 2:
        return by_block(embeddings, group_of, cluster_id)
    return by_group(embeddings, group_of, cluster_id)


def solution(mesh):
    return jax.shard_map(
        per_device,
        mesh=mesh,
        in_specs=(
            P(("island", "blk", "sub", "pair"), None),
            P(("island", "blk", "sub", "pair"), None),
            P(("island", "blk", "sub", "pair")),
        ),
        out_specs=P(("island", "blk", "sub", "pair"), None),
        check_vma=False,
    )
```

```python
import functools

import jax
import jax.numpy as jnp
from jax import lax
from jax.experimental import pallas as pl
from jax.experimental.pallas import tpu as pltpu
from jax.sharding import PartitionSpec as P

F32 = jnp.float32
BF16 = jnp.bfloat16
VMEM_BYTES = 24 * 1024 * 1024
PARTS = 3
GATHER_LIMIT = 8 * 1024 * 1024


def unit_scale(rows_in):
    wide = rows_in.astype(F32)
    return lax.rsqrt(jnp.sum(wide * wide, axis=1) + 1e-06)


def tile_weights(left_rows, left_clust, left_scale, right_rows, right_clust, right_scale):
    grams = lax.dot_general(
        left_rows, right_rows, (((1,), (1,)), ((), ())), preferred_element_type=F32
    )
    cosine = grams * left_scale[:, None] * right_scale[None, :]
    same = (left_clust[:, None] == right_clust[None, :]).astype(F32)
    return jax.nn.sigmoid(8.0 * cosine - 2.0) * same


def by_group(embeddings, group_of, cluster_id):
    rows_here, width = embeddings.shape
    groups = lax.axis_size("sub") * lax.axis_size("pair")
    capacity = 2 * rows_here // groups
    slots = groups * capacity
    target = group_of[:, 0]
    onehot = (target[:, None] == jnp.arange(groups, dtype=jnp.int32)[None, :]).astype(jnp.int32)
    position = jnp.sum((jnp.cumsum(onehot, axis=0) - onehot) * onehot, axis=1)
    send_rows = jnp.zeros((groups, capacity, width), BF16).at[target, position].set(embeddings)
    send_clust = jnp.full((groups, capacity), -1, jnp.int32).at[target, position].set(cluster_id)
    recv_rows, recv_clust = (
        lax.all_to_all(send_rows, ("sub", "pair"), split_axis=0, concat_axis=0, tiled=True),
        lax.all_to_all(send_clust, ("sub", "pair"), split_axis=0, concat_axis=0, tiled=True),
    )
    own_rows = recv_rows.reshape(slots, width)
    own_clust = recv_clust.reshape(slots)
    own_scale = unit_scale(own_rows)
    piece_rows = lax.all_gather(own_rows, "blk", axis=0, tiled=True)
    piece_clust = lax.all_gather(own_clust, "blk", axis=0, tiled=True)
    weight = tile_weights(
        own_rows, own_clust, own_scale, piece_rows, piece_clust, unit_scale(piece_rows)
    )
    numer = jnp.dot(weight.astype(BF16), piece_rows, preferred_element_type=F32)
    denom = jnp.sum(weight, axis=1)
    result = (numer / denom[:, None]).astype(BF16).reshape(groups, capacity, width)
    returned = lax.all_to_all(result, ("sub", "pair"), split_axis=0, concat_axis=0, tiled=True)
    return returned[target, position]


def diagonal(size):
    shape = (size, size)
    return lax.broadcasted_iota(jnp.int32, shape, 0) == lax.broadcasted_iota(jnp.int32, shape, 1)


def to_column(row):
    size = row.shape[1]
    return jnp.sum(jnp.where(diagonal(size), row, jnp.zeros_like(row)), axis=1, keepdims=True)


def to_row(column):
    size = column.shape[0]
    return jnp.sum(jnp.where(diagonal(size), column, jnp.zeros_like(column)), axis=0, keepdims=True)


def scale_column(rows):
    wide = rows.astype(F32)
    return lax.rsqrt(jnp.sum(wide * wide, axis=1, keepdims=True) + 1e-06)


def name_lines(rows_here):
    return -(-rows_here // 128)


def pack_kernel(rows, group, cluster, whole, first, second):
    rows_here, width = rows.shape
    slabs = width // 128
    half = rows_here // 2
    for slab in range(slabs):
        columns = rows[:, slab * 128 : (slab + 1) * 128]
        whole[slab * rows_here : (slab + 1) * rows_here, :] = columns
        first[slab * half : (slab + 1) * half, :] = columns[:half]
        second[slab * half : (slab + 1) * half, :] = columns[half:]
    line_at = lax.broadcasted_iota(jnp.int32, (8, 128), 0)
    lines = name_lines(rows_here)
    named = jnp.zeros((8, 128), jnp.int32)
    for kind, ref in enumerate((group, cluster)):
        for line in range(lines):
            part = ref[:, line * 128 : (line + 1) * 128]
            if part.shape[1] < 128:
                rest = jnp.zeros((1, 128 - part.shape[1]), jnp.int32)
                part = jnp.concatenate([part, rest], axis=1)
            named = jnp.where(line_at == kind * lines + line, part, named)
    named = named.astype(F32).astype(BF16)
    whole[slabs * rows_here :, :] = named
    first[slabs * half :, :] = named
    second[slabs * half :, :] = named


def from_slabs(ref, count):
    slabs = [ref[top : top + count, :] for top in range(0, ref.shape[0] // count * count, count)]
    return jnp.concatenate(slabs, axis=1)


def key_row(ref, rows_here):
    wide = ref[ref.shape[0] - 8 :, :].astype(F32)
    lines = name_lines(rows_here)
    kinds = []
    for kind in range(2):
        parts = [wide[kind * lines + line : kind * lines + line + 1, :] for line in range(lines)]
        kinds.append(jnp.concatenate(parts, axis=1)[:, :rows_here])
    return kinds[0] * 256.0 + kinds[1]


def from_halves(first, second, rows_here):
    half = rows_here // 2
    rows = jnp.concatenate([from_slabs(first, half), from_slabs(second, half)], axis=0)
    return rows, key_row(first, rows_here)


def add_blocks(left, info, blocks, numer, denom):
    key = info[: left.shape[0], 0:1]
    scale = info[: left.shape[0], 1:2]
    for right_rows, right_key, right_scale in blocks:
        grams = lax.dot_general(
            left, right_rows, (((1,), (1,)), ((), ())), preferred_element_type=F32
        )
        half = jnp.tanh(grams * scale * right_scale - 1.0)
        weight = jnp.where(key == right_key, 0.5 + 0.5 * half, 0.0)
        add = jnp.dot(weight.astype(BF16), right_rows, preferred_element_type=F32)
        add_denom = jnp.sum(weight, axis=1, keepdims=True)
        numer = add if numer is None else numer + add
        denom = add_denom if denom is None else denom + add_denom
    return numer, denom


def left_rows(refs, rows_here):
    return jnp.concatenate([from_slabs(ref, rows_here) for ref in refs], axis=0)


def take_blocks(refs, count, rows_here):
    blocks = []
    for _ in range(count):
        rows, key = from_halves(refs.pop(0), refs.pop(0), rows_here)
        blocks.append((rows, key, to_row(scale_column(rows))))
    return blocks


def store_sides(numer, denom, outs):
    rows_here, wide = outs[0].shape
    for side, out in enumerate(outs):
        top = side * rows_here
        out[:, : wide - 128] = numer[top : top + rows_here]
        out[:, wide - 128 :] = jnp.broadcast_to(denom[top : top + rows_here], (rows_here, 128))


def start_kernel(n_blocks, own, other, *refs):
    refs = list(refs)
    rows_here = refs[-1].shape[0] // 2
    left = left_rows((own, other), rows_here)
    key = jnp.concatenate([to_column(key_row(ref, rows_here)) for ref in (own, other)], axis=0)
    scale = scale_column(left)
    info = refs.pop()
    lane = lax.broadcasted_iota(jnp.int32, info.shape, 1)
    info[...] = jnp.where(lane == 0, key, 4.0 * scale)
    first = (left[:rows_here], key_row(own, rows_here), to_row(scale[:rows_here]))
    blocks = [first] + take_blocks(refs, n_blocks, rows_here)
    store_sides(*add_blocks(left, info, blocks, None, None), refs)


def both_kernel(n_blocks, own, other, info, *refs):
    refs = list(refs)
    rows_here, wide = refs[-1].shape
    left = left_rows((own, other), rows_here)
    blocks = take_blocks(refs, n_blocks, rows_here)
    numer = jnp.concatenate([ref[:, : wide - 128] for ref in refs[:2]], axis=0)
    denom = jnp.concatenate([ref[:, wide - 128 : wide - 127] for ref in refs[:2]], axis=0)
    store_sides(*add_blocks(left, info, blocks, numer, denom), refs[2:])


def half_of(piece, top, rows_here):
    rows = from_slabs(piece, rows_here // 2)
    key = to_column(key_row(piece, rows_here))[top : top + rows_here // 2]
    return rows, to_row(key), to_row(scale_column(rows))


def first_half_kernel(own, other, info, first, mine_in, theirs_in, mine, *theirs):
    rows_here, wide = mine.shape
    width = wide - 128
    left = left_rows((own, other), rows_here)
    blocks = [half_of(first, 0, rows_here)]
    numer = jnp.concatenate([ref[:, :width] for ref in (mine_in, theirs_in)], axis=0)
    denom = jnp.concatenate([ref[:, width : width + 1] for ref in (mine_in, theirs_in)], axis=0)
    numer, denom = add_blocks(left, info, blocks, numer, denom)
    store_sides(numer[:rows_here], denom[:rows_here], [mine])
    denom = denom[rows_here:]
    high = denom.astype(BF16).astype(F32)
    lane = lax.broadcasted_iota(jnp.int32, (rows_here, 128), 1)
    pair = jnp.where(lane == 0, high, denom - high).astype(BF16)
    count = rows_here // len(theirs)
    for part, out in enumerate(theirs):
        top = part * count
        out[:, :width] = numer[rows_here + top : rows_here + top + count].astype(BF16)
        out[:, width:] = pair[top : top + count]


def last_kernel(own, info, second, second_other, mine, *refs):
    out = refs[-1]
    rows_here, width = out.shape
    theirs = jnp.concatenate([ref[...] for ref in refs[:-1]], axis=0)
    blocks = [half_of(ref, rows_here // 2, rows_here) for ref in (second, second_other)]
    parts = theirs[:, width:].astype(F32)
    numer = mine[:, :width] + theirs[:, :width].astype(F32)
    denom = mine[:, width : width + 1] + (parts[:, 0:1] + parts[:, 1:2])
    numer, denom = add_blocks(left_rows((own,), rows_here), info, blocks, numer, denom)
    out[...] = (numer / denom).astype(BF16)


def whole_in_vmem(count):
    return [pl.BlockSpec(memory_space=pltpu.VMEM)] * count


def call(kernel, shapes, args, aliases={}):
    return pl.pallas_call(
        kernel,
        out_shape=[jax.ShapeDtypeStruct(shape, dtype) for shape, dtype in shapes],
        in_specs=whole_in_vmem(len(args)),
        out_specs=whole_in_vmem(len(shapes)),
        input_output_aliases=aliases,
        compiler_params=pltpu.CompilerParams(vmem_limit_bytes=VMEM_BYTES),
    )(*args)


def start_both(left, right, shape):
    rows_here = shape[0]
    args = list(left) + [half for block in right for half in block]
    shapes = [(shape, F32), (shape, F32), ((2 * rows_here, 128), F32)]
    return call(functools.partial(start_kernel, len(right)), shapes, args)


def add_both(left, right, before):
    args = list(left) + [half for block in right for half in block] + list(before)
    at = len(args) - 2
    shapes = [(total.shape, F32) for total in before]
    return call(
        functools.partial(both_kernel, len(right)), shapes, args, {at: 0, at + 1: 1}
    )


def add_first_half(left, first, before):
    rows_here, wide = before[0].shape
    shapes = [((rows_here, wide), F32)] + [((rows_here // PARTS, wide), BF16)] * PARTS
    return call(first_half_kernel, shapes, [*left, first, *before], {4: 0})


def folded_ring(size):
    return [0] + list(range(1, size, 2)) + list(range(2, size, 2))[::-1]


def together(*arrays):
    return lax.optimization_barrier(arrays)


def by_block(embeddings, group_of, cluster_id):
    rows_here, width = embeddings.shape
    half = rows_here // 2
    slabs = width // 128
    n_blk = lax.axis_size("blk")
    order = folded_ring(n_blk)
    line = (1, rows_here)

    def along(rows):
        hops = [
            (2 * order[i - 1] + core, 2 * order[i] + 1 - core)
            for i in range(n_blk)
            for core in range(2)
        ]
        return lax.ppermute(rows, ("blk", "pair"), hops)

    def across(rows):
        return lax.ppermute(rows, ("sub", "pair"), [(0, 3), (1, 2), (2, 1), (3, 0)])

    def other_core(rows):
        return lax.ppermute(rows, "pair", [(0, 1), (1, 0)])

    whole, first, second = call(
        pack_kernel,
        [
            ((slabs * rows_here + 8, 128), BF16),
            ((slabs * half + 8, 128), BF16),
            ((slabs * half + 8, 128), BF16),
        ],
        [embeddings, group_of.reshape(line), cluster_id.reshape(line)],
    )
    along_by = [(first, second)]
    across_by = []
    for s in range(1, n_blk):
        moved = [along(piece) for piece in along_by[-1]]
        swapped = [across(piece) for piece in along_by[-1]]
        pairs = [together(m, w) for m, w in zip(moved, swapped)]
        along_by.append(tuple(pair[0] for pair in pairs))
        across_by.append(tuple(pair[1] for pair in pairs))
    left = (whole, other_core(whole))
    mine, theirs, info = start_both(
        left, across_by[:-1] + along_by[1:-1], (rows_here, width + 128)
    )
    left = (*left, info)
    near_first, _, mine, theirs = together(across_by[-1][0], along_by[-1][0], mine, theirs)
    last_first, last_second = along(near_first), across(along_by[-1][1])
    mine, theirs = add_both(left, [across_by[-1], along_by[-1]], (mine, theirs))
    mine, *theirs = add_first_half(left, last_first, (mine, theirs))
    last_second, *back = together(last_second, *[other_core(part) for part in theirs])
    (out,) = call(
        last_kernel,
        [((rows_here, width), BF16)],
        [whole, info, last_second, other_core(last_second), mine, *back],
    )
    return out


def per_device(embeddings, group_of, cluster_id):
    rows_here, width = embeddings.shape
    devices = lax.axis_size("blk") * lax.axis_size("sub") * lax.axis_size("pair")
    small = devices * rows_here * width * 2 <= GATHER_LIMIT
    fits = width % 128 == 0 and rows_here % (32 * PARTS) == 0 and rows_here <= 512
    if small and fits and lax.axis_size("sub") == 2 and lax.axis_size("pair") == 2:
        return by_block(embeddings, group_of, cluster_id)
    return by_group(embeddings, group_of, cluster_id)


def solution(mesh):
    return jax.shard_map(
        per_device,
        mesh=mesh,
        in_specs=(
            P(("island", "blk", "sub", "pair"), None),
            P(("island", "blk", "sub", "pair"), None),
            P(("island", "blk", "sub", "pair")),
        ),
        out_specs=P(("island", "blk", "sub", "pair"), None),
        check_vma=False,
    )
```

```python
import functools

import jax
import jax.numpy as jnp
from jax import lax
from jax.experimental import pallas as pl
from jax.experimental.pallas import tpu as pltpu
from jax.sharding import PartitionSpec as P

F32 = jnp.float32
BF16 = jnp.bfloat16
VMEM_BYTES = 24 * 1024 * 1024
PARTS = 3
GATHER_LIMIT = 8 * 1024 * 1024


def unit_scale(rows_in):
    wide = rows_in.astype(F32)
    return lax.rsqrt(jnp.sum(wide * wide, axis=1) + 1e-06)


def tile_weights(left_rows, left_clust, left_scale, right_rows, right_clust, right_scale):
    grams = lax.dot_general(
        left_rows, right_rows, (((1,), (1,)), ((), ())), preferred_element_type=F32
    )
    cosine = grams * left_scale[:, None] * right_scale[None, :]
    same = (left_clust[:, None] == right_clust[None, :]).astype(F32)
    return jax.nn.sigmoid(8.0 * cosine - 2.0) * same


def by_group(embeddings, group_of, cluster_id):
    rows_here, width = embeddings.shape
    groups = lax.axis_size("sub") * lax.axis_size("pair")
    capacity = 2 * rows_here // groups
    slots = groups * capacity
    target = group_of[:, 0]
    onehot = (target[:, None] == jnp.arange(groups, dtype=jnp.int32)[None, :]).astype(jnp.int32)
    position = jnp.sum((jnp.cumsum(onehot, axis=0) - onehot) * onehot, axis=1)
    send_rows = jnp.zeros((groups, capacity, width), BF16).at[target, position].set(embeddings)
    send_clust = jnp.full((groups, capacity), -1, jnp.int32).at[target, position].set(cluster_id)
    recv_rows, recv_clust = (
        lax.all_to_all(send_rows, ("sub", "pair"), split_axis=0, concat_axis=0, tiled=True),
        lax.all_to_all(send_clust, ("sub", "pair"), split_axis=0, concat_axis=0, tiled=True),
    )
    own_rows = recv_rows.reshape(slots, width)
    own_clust = recv_clust.reshape(slots)
    own_scale = unit_scale(own_rows)
    piece_rows = lax.all_gather(own_rows, "blk", axis=0, tiled=True)
    piece_clust = lax.all_gather(own_clust, "blk", axis=0, tiled=True)
    weight = tile_weights(
        own_rows, own_clust, own_scale, piece_rows, piece_clust, unit_scale(piece_rows)
    )
    numer = jnp.dot(weight.astype(BF16), piece_rows, preferred_element_type=F32)
    denom = jnp.sum(weight, axis=1)
    result = (numer / denom[:, None]).astype(BF16).reshape(groups, capacity, width)
    returned = lax.all_to_all(result, ("sub", "pair"), split_axis=0, concat_axis=0, tiled=True)
    return returned[target, position]


def diagonal(size):
    shape = (size, size)
    return lax.broadcasted_iota(jnp.int32, shape, 0) == lax.broadcasted_iota(jnp.int32, shape, 1)


def to_column(row):
    size = row.shape[1]
    return jnp.sum(jnp.where(diagonal(size), row, jnp.zeros_like(row)), axis=1, keepdims=True)


def to_row(column):
    size = column.shape[0]
    return jnp.sum(jnp.where(diagonal(size), column, jnp.zeros_like(column)), axis=0, keepdims=True)


def scale_column(rows):
    wide = rows.astype(F32)
    return lax.rsqrt(jnp.sum(wide * wide, axis=1, keepdims=True) + 1e-06)


def first_pack_kernel(rows, first):
    width = rows.shape[1]
    slabs = width // 128
    half = rows.shape[0] // 2
    for slab in range(slabs):
        first[slab * half : (slab + 1) * half, :] = rows[:half, slab * 128 : (slab + 1) * 128]
    first[slabs * half :, :] = jnp.zeros((8, 128), BF16)


def pack_kernel(rows, group, cluster, whole, second):
    rows_here, width = rows.shape
    slabs = width // 128
    half = rows_here // 2
    for slab in range(slabs):
        columns = rows[:, slab * 128 : (slab + 1) * 128]
        whole[slab * rows_here : (slab + 1) * rows_here, :] = columns
        second[slab * half : (slab + 1) * half, :] = columns[half:]
    line_at = lax.broadcasted_iota(jnp.int32, (8, 128), 0)
    named = jnp.zeros((8, 128), jnp.int32)
    for line in range(4):
        top = line % 2 * half
        part = (group, cluster)[line // 2][:, top : top + half]
        if half < 128:
            part = jnp.concatenate([part, jnp.zeros((1, 128 - half), jnp.int32)], axis=1)
        named = jnp.where(line_at == line, part, named)
    named = named.astype(F32).astype(BF16)
    whole[slabs * rows_here :, :] = named
    second[slabs * half :, :] = named


def from_slabs(ref, count):
    slabs = [ref[top : top + count, :] for top in range(0, ref.shape[0] // count * count, count)]
    return jnp.concatenate(slabs, axis=1)


def key_rows(ref, half):
    wide = ref[ref.shape[0] - 8 :, :].astype(F32)
    return [wide[side : side + 1, :half] * 256.0 + wide[side + 2 : side + 3, :half] for side in range(2)]


def key_row(ref, rows_here):
    return jnp.concatenate(key_rows(ref, rows_here // 2), axis=1)


def from_halves(first, second, rows_here):
    half = rows_here // 2
    rows = jnp.concatenate([from_slabs(first, half), from_slabs(second, half)], axis=0)
    return rows, key_row(second, rows_here)


def add_blocks(left, info, blocks, numer, denom):
    key = info[: left.shape[0], 0:1]
    scale = info[: left.shape[0], 1:2]
    for right_rows, right_key, right_scale in blocks:
        grams = lax.dot_general(
            left, right_rows, (((1,), (1,)), ((), ())), preferred_element_type=F32
        )
        half = jnp.tanh(grams * scale * right_scale - 1.0)
        weight = jnp.where(key == right_key, 0.5 + 0.5 * half, 0.0)
        add = jnp.dot(weight.astype(BF16), right_rows, preferred_element_type=F32)
        add_denom = jnp.sum(weight, axis=1, keepdims=True)
        numer = add if numer is None else numer + add
        denom = add_denom if denom is None else denom + add_denom
    return numer, denom


def left_rows(refs, rows_here):
    return jnp.concatenate([from_slabs(ref, rows_here) for ref in refs], axis=0)


def take_blocks(refs, count, rows_here):
    blocks = []
    for _ in range(count):
        rows, key = from_halves(refs.pop(0), refs.pop(0), rows_here)
        blocks.append((rows, key, to_row(scale_column(rows))))
    return blocks


def store_sides(numer, denom, outs):
    rows_here, wide = outs[0].shape
    for side, out in enumerate(outs):
        top = side * rows_here
        out[:, : wide - 128] = numer[top : top + rows_here]
        out[:, wide - 128 :] = jnp.broadcast_to(denom[top : top + rows_here], (rows_here, 128))


def start_kernel(n_blocks, own, other, *refs):
    refs = list(refs)
    rows_here = refs[-1].shape[0] // 2
    left = left_rows((own, other), rows_here)
    key = jnp.concatenate([to_column(key_row(ref, rows_here)) for ref in (own, other)], axis=0)
    scale = scale_column(left)
    info = refs.pop()
    lane = lax.broadcasted_iota(jnp.int32, info.shape, 1)
    info[...] = jnp.where(lane == 0, key, 4.0 * scale)
    first = (left[:rows_here], key_row(own, rows_here), to_row(scale[:rows_here]))
    blocks = [first] + take_blocks(refs, n_blocks, rows_here)
    store_sides(*add_blocks(left, info, blocks, None, None), refs)


def both_kernel(n_blocks, own, other, info, *refs):
    refs = list(refs)
    rows_here, wide = refs[-1].shape
    left = left_rows((own, other), rows_here)
    blocks = take_blocks(refs, n_blocks, rows_here)
    numer = jnp.concatenate([ref[:, : wide - 128] for ref in refs[:2]], axis=0)
    denom = jnp.concatenate([ref[:, wide - 128 : wide - 127] for ref in refs[:2]], axis=0)
    store_sides(*add_blocks(left, info, blocks, numer, denom), refs[2:])


def first_half_kernel(own, other, info, first, names, mine_in, theirs_in, mine, *theirs):
    rows_here, wide = mine.shape
    width = wide - 128
    left = left_rows((own, other), rows_here)
    rows = from_slabs(first, rows_here // 2)
    blocks = [(rows, key_rows(names, rows_here // 2)[0], to_row(scale_column(rows)))]
    numer = jnp.concatenate([ref[:, :width] for ref in (mine_in, theirs_in)], axis=0)
    denom = jnp.concatenate([ref[:, width : width + 1] for ref in (mine_in, theirs_in)], axis=0)
    numer, denom = add_blocks(left, info, blocks, numer, denom)
    store_sides(numer[:rows_here], denom[:rows_here], [mine])
    denom = denom[rows_here:]
    high = denom.astype(BF16).astype(F32)
    lane = lax.broadcasted_iota(jnp.int32, (rows_here, 128), 1)
    pair = jnp.where(lane == 0, high, denom - high).astype(BF16)
    count = rows_here // len(theirs)
    for part, out in enumerate(theirs):
        top = part * count
        out[:, :width] = numer[rows_here + top : rows_here + top + count].astype(BF16)
        out[:, width:] = pair[top : top + count]


def last_kernel(own, info, second, second_other, mine, *refs):
    out = refs[-1]
    rows_here, width = out.shape
    theirs = jnp.concatenate([ref[...] for ref in refs[:-1]], axis=0)
    half = rows_here // 2
    pieces = (second, second_other)
    rows = jnp.concatenate([from_slabs(ref, half) for ref in pieces], axis=0)
    key = jnp.concatenate([key_rows(ref, half)[1] for ref in pieces], axis=1)
    blocks = [(rows, key, to_row(scale_column(rows)))]
    parts = theirs[:, width:].astype(F32)
    numer = mine[:, :width] + theirs[:, :width].astype(F32)
    denom = mine[:, width : width + 1] + (parts[:, 0:1] + parts[:, 1:2])
    numer, denom = add_blocks(left_rows((own,), rows_here), info, blocks, numer, denom)
    out[...] = (numer * (1.0 / denom)).astype(BF16)


def whole_in_vmem(count):
    return [pl.BlockSpec(memory_space=pltpu.VMEM)] * count


def call(kernel, shapes, args, aliases={}):
    return pl.pallas_call(
        kernel,
        out_shape=[jax.ShapeDtypeStruct(shape, dtype) for shape, dtype in shapes],
        in_specs=whole_in_vmem(len(args)),
        out_specs=whole_in_vmem(len(shapes)),
        input_output_aliases=aliases,
        compiler_params=pltpu.CompilerParams(vmem_limit_bytes=VMEM_BYTES),
    )(*args)


def start_both(left, right, shape):
    rows_here = shape[0]
    args = list(left) + [half for block in right for half in block]
    shapes = [(shape, F32), (shape, F32), ((2 * rows_here, 128), F32)]
    return call(functools.partial(start_kernel, len(right)), shapes, args)


def add_both(left, right, before):
    args = list(left) + [half for block in right for half in block] + list(before)
    at = len(args) - 2
    shapes = [(total.shape, F32) for total in before]
    return call(
        functools.partial(both_kernel, len(right)), shapes, args, {at: 0, at + 1: 1}
    )


def add_first_half(left, first, names, before):
    rows_here, wide = before[0].shape
    shapes = [((rows_here, wide), F32)] + [((rows_here // PARTS, wide), BF16)] * PARTS
    return call(first_half_kernel, shapes, [*left, first, names, *before], {5: 0})


def folded_ring(size):
    return [0] + list(range(1, size, 2)) + list(range(2, size, 2))[::-1]


def together(*arrays):
    return lax.optimization_barrier(arrays)


def by_block(embeddings, group_of, cluster_id):
    rows_here, width = embeddings.shape
    half = rows_here // 2
    slabs = width // 128
    n_blk = lax.axis_size("blk")
    order = folded_ring(n_blk)
    line = (1, rows_here)

    def along(rows):
        hops = [
            (2 * order[i - 1] + core, 2 * order[i] + 1 - core)
            for i in range(n_blk)
            for core in range(2)
        ]
        return lax.ppermute(rows, ("blk", "pair"), hops)

    def across(rows):
        return lax.ppermute(rows, ("sub", "pair"), [(0, 3), (1, 2), (2, 1), (3, 0)])

    def other_core(rows):
        return lax.ppermute(rows, "pair", [(0, 1), (1, 0)])

    half_shape = ((slabs * half + 8, 128), BF16)
    (first,) = call(first_pack_kernel, [half_shape], [embeddings])
    whole, second = call(
        pack_kernel,
        [((slabs * rows_here + 8, 128), BF16), half_shape],
        [embeddings, group_of.reshape(line), cluster_id.reshape(line)],
    )
    along_by = [(first, second)]
    across_by = []
    for s in range(1, n_blk):
        moved = [along(piece) for piece in along_by[-1]]
        swapped = [across(piece) for piece in along_by[-1]]
        pairs = [together(m, w) for m, w in zip(moved, swapped)]
        along_by.append(tuple(pair[0] for pair in pairs))
        across_by.append(tuple(pair[1] for pair in pairs))
    left = (whole, other_core(whole))
    mine, theirs, info = start_both(
        left, across_by[:-1] + along_by[1:-1], (rows_here, width + 128)
    )
    left = (*left, info)
    near_first, _ = together(across_by[-1][0], along_by[-1][0])
    far_second, mine, theirs = together(along_by[-1][1], mine, theirs)
    last_first, last_second = along(near_first), across(far_second)
    mine, theirs = add_both(left, [across_by[-1], along_by[-1]], (mine, theirs))
    names = along(across_by[-1][1][slabs * half :])
    mine, *theirs = add_first_half(left, last_first, names, (mine, theirs))
    last_second, *back = together(last_second, *[other_core(part) for part in theirs])
    (out,) = call(
        last_kernel,
        [((rows_here, width), BF16)],
        [whole, info, last_second, other_core(last_second), mine, *back],
    )
    return out


def per_device(embeddings, group_of, cluster_id):
    rows_here, width = embeddings.shape
    devices = lax.axis_size("blk") * lax.axis_size("sub") * lax.axis_size("pair")
    small = devices * rows_here * width * 2 <= GATHER_LIMIT
    fits = width % 128 == 0 and rows_here % (32 * PARTS) == 0 and rows_here <= 256
    if small and fits and lax.axis_size("sub") == 2 and lax.axis_size("pair") == 2:
        return by_block(embeddings, group_of, cluster_id)
    return by_group(embeddings, group_of, cluster_id)


def solution(mesh):
    return jax.shard_map(
        per_device,
        mesh=mesh,
        in_specs=(
            P(("island", "blk", "sub", "pair"), None),
            P(("island", "blk", "sub", "pair"), None),
            P(("island", "blk", "sub", "pair")),
        ),
        out_specs=P(("island", "blk", "sub", "pair"), None),
        check_vma=False,
    )
```

```python
import functools

import jax
import jax.numpy as jnp
from jax import lax
from jax.experimental import pallas as pl
from jax.experimental.pallas import tpu as pltpu
from jax.sharding import PartitionSpec as P

F32 = jnp.float32
BF16 = jnp.bfloat16
VMEM_BYTES = 24 * 1024 * 1024
PARTS = 3
GATHER_LIMIT = 8 * 1024 * 1024


def unit_scale(rows_in):
    wide = rows_in.astype(F32)
    return lax.rsqrt(jnp.sum(wide * wide, axis=1) + 1e-06)


def tile_weights(left_rows, left_clust, left_scale, right_rows, right_clust, right_scale):
    grams = lax.dot_general(
        left_rows, right_rows, (((1,), (1,)), ((), ())), preferred_element_type=F32
    )
    cosine = grams * left_scale[:, None] * right_scale[None, :]
    same = (left_clust[:, None] == right_clust[None, :]).astype(F32)
    return jax.nn.sigmoid(8.0 * cosine - 2.0) * same


def by_group(embeddings, group_of, cluster_id):
    rows_here, width = embeddings.shape
    groups = lax.axis_size("sub") * lax.axis_size("pair")
    capacity = 2 * rows_here // groups
    slots = groups * capacity
    target = group_of[:, 0]
    onehot = (target[:, None] == jnp.arange(groups, dtype=jnp.int32)[None, :]).astype(jnp.int32)
    position = jnp.sum((jnp.cumsum(onehot, axis=0) - onehot) * onehot, axis=1)
    send_rows = jnp.zeros((groups, capacity, width), BF16).at[target, position].set(embeddings)
    send_clust = jnp.full((groups, capacity), -1, jnp.int32).at[target, position].set(cluster_id)
    recv_rows, recv_clust = (
        lax.all_to_all(send_rows, ("sub", "pair"), split_axis=0, concat_axis=0, tiled=True),
        lax.all_to_all(send_clust, ("sub", "pair"), split_axis=0, concat_axis=0, tiled=True),
    )
    own_rows = recv_rows.reshape(slots, width)
    own_clust = recv_clust.reshape(slots)
    own_scale = unit_scale(own_rows)
    piece_rows = lax.all_gather(own_rows, "blk", axis=0, tiled=True)
    piece_clust = lax.all_gather(own_clust, "blk", axis=0, tiled=True)
    weight = tile_weights(
        own_rows, own_clust, own_scale, piece_rows, piece_clust, unit_scale(piece_rows)
    )
    numer = jnp.dot(weight.astype(BF16), piece_rows, preferred_element_type=F32)
    denom = jnp.sum(weight, axis=1)
    result = (numer / denom[:, None]).astype(BF16).reshape(groups, capacity, width)
    returned = lax.all_to_all(result, ("sub", "pair"), split_axis=0, concat_axis=0, tiled=True)
    return returned[target, position]


def diagonal(size):
    shape = (size, size)
    return lax.broadcasted_iota(jnp.int32, shape, 0) == lax.broadcasted_iota(jnp.int32, shape, 1)


def to_column(row):
    size = row.shape[1]
    return jnp.sum(jnp.where(diagonal(size), row, jnp.zeros_like(row)), axis=1, keepdims=True)


def to_row(column):
    size = column.shape[0]
    return jnp.sum(jnp.where(diagonal(size), column, jnp.zeros_like(column)), axis=0, keepdims=True)


def scale_column(rows):
    wide = rows.astype(F32)
    return lax.rsqrt(jnp.sum(wide * wide, axis=1, keepdims=True) + 1e-06)


def first_pack_kernel(rows, first):
    width = rows.shape[1]
    slabs = width // 128
    half = rows.shape[0] // 2
    for slab in range(slabs):
        first[slab * half : (slab + 1) * half, :] = rows[:half, slab * 128 : (slab + 1) * 128]
    first[slabs * half :, :] = jnp.zeros((8, 128), BF16)


def pack_kernel(rows, group, cluster, whole, second):
    rows_here, width = rows.shape
    slabs = width // 128
    half = rows_here // 2
    for slab in range(slabs):
        columns = rows[:, slab * 128 : (slab + 1) * 128]
        whole[slab * rows_here : (slab + 1) * rows_here, :] = columns
        second[slab * half : (slab + 1) * half, :] = columns[half:]
    line_at = lax.broadcasted_iota(jnp.int32, (8, 128), 0)
    named = jnp.zeros((8, 128), jnp.int32)
    for line in range(4):
        top = line % 2 * half
        part = (group, cluster)[line // 2][:, top : top + half]
        if half < 128:
            part = jnp.concatenate([part, jnp.zeros((1, 128 - half), jnp.int32)], axis=1)
        named = jnp.where(line_at == line, part, named)
    named = named.astype(F32).astype(BF16)
    whole[slabs * rows_here :, :] = named
    second[slabs * half :, :] = named


def from_slabs(ref, count):
    slabs = [ref[top : top + count, :] for top in range(0, ref.shape[0] // count * count, count)]
    return jnp.concatenate(slabs, axis=1)


def key_rows(ref, half):
    wide = ref[ref.shape[0] - 8 :, :].astype(F32)
    return [wide[side : side + 1, :half] * 256.0 + wide[side + 2 : side + 3, :half] for side in range(2)]


def key_row(ref, rows_here):
    return jnp.concatenate(key_rows(ref, rows_here // 2), axis=1)


def from_halves(first, second, rows_here):
    half = rows_here // 2
    rows = jnp.concatenate([from_slabs(first, half), from_slabs(second, half)], axis=0)
    return rows, key_row(second, rows_here)


def add_blocks(left, info, blocks, numer, denom):
    key = info[: left.shape[0], 0:1]
    scale = info[: left.shape[0], 1:2]
    for right_rows, right_key, right_scale in blocks:
        grams = lax.dot_general(
            left, right_rows, (((1,), (1,)), ((), ())), preferred_element_type=F32
        )
        half = jnp.tanh(grams * scale * right_scale - 1.0)
        weight = jnp.where(key == right_key, 0.5 + 0.5 * half, 0.0)
        add = jnp.dot(weight.astype(BF16), right_rows, preferred_element_type=F32)
        add_denom = jnp.sum(weight, axis=1, keepdims=True)
        numer = add if numer is None else numer + add
        denom = add_denom if denom is None else denom + add_denom
    return numer, denom


def left_rows(refs, rows_here):
    return jnp.concatenate([from_slabs(ref, rows_here) for ref in refs], axis=0)


def take_blocks(refs, count, rows_here):
    blocks = []
    for _ in range(count):
        rows, key = from_halves(refs.pop(0), refs.pop(0), rows_here)
        blocks.append((rows, key, to_row(scale_column(rows))))
    return blocks


def store_sides(numer, denom, outs):
    rows_here, wide = outs[0].shape
    for side, out in enumerate(outs):
        top = side * rows_here
        out[:, : wide - 128] = numer[top : top + rows_here]
        out[:, wide - 128 :] = jnp.broadcast_to(denom[top : top + rows_here], (rows_here, 128))


def start_kernel(n_blocks, own, other, *refs):
    refs = list(refs)
    rows_here = refs[-1].shape[0] // 2
    left = left_rows((own, other), rows_here)
    key = jnp.concatenate([to_column(key_row(ref, rows_here)) for ref in (own, other)], axis=0)
    scale = scale_column(left)
    info = refs.pop()
    lane = lax.broadcasted_iota(jnp.int32, info.shape, 1)
    info[...] = jnp.where(lane == 0, key, 4.0 * scale)
    first = (left[:rows_here], key_row(own, rows_here), to_row(scale[:rows_here]))
    blocks = [first] + take_blocks(refs, n_blocks, rows_here)
    store_sides(*add_blocks(left, info, blocks, None, None), refs)


def both_kernel(n_blocks, own, other, info, *refs):
    refs = list(refs)
    rows_here = refs[2 * n_blocks].shape[0]
    blocks = take_blocks(refs, n_blocks, rows_here)
    mine_in, theirs_in, mine, *theirs = refs
    wide = mine.shape[1]
    width = wide - 128
    left = left_rows((own, other), rows_here)
    numer = jnp.concatenate([ref[:, :width] for ref in (mine_in, theirs_in)], axis=0)
    denom = jnp.concatenate([ref[:, width : width + 1] for ref in (mine_in, theirs_in)], axis=0)
    numer, denom = add_blocks(left, info, blocks, numer, denom)
    store_sides(numer[:rows_here], denom[:rows_here], [mine])
    denom = denom[rows_here:]
    high = denom.astype(BF16).astype(F32)
    lane = lax.broadcasted_iota(jnp.int32, (rows_here, 128), 1)
    pair = jnp.where(lane == 0, high, denom - high).astype(BF16)
    count = rows_here // len(theirs)
    for part, out in enumerate(theirs):
        top = part * count
        out[:, :width] = numer[rows_here + top : rows_here + top + count].astype(BF16)
        out[:, width:] = pair[top : top + count]


def last_kernel(own, info, first, second, first_other, second_other, mine, *refs):
    out = refs[-1]
    rows_here, width = out.shape
    theirs = jnp.concatenate([ref[...] for ref in refs[:-1]], axis=0)
    blocks = take_blocks([first, second, first_other, second_other], 2, rows_here)
    parts = theirs[:, width:].astype(F32)
    numer = mine[:, :width] + theirs[:, :width].astype(F32)
    denom = mine[:, width : width + 1] + (parts[:, 0:1] + parts[:, 1:2])
    numer, denom = add_blocks(left_rows((own,), rows_here), info, blocks, numer, denom)
    out[...] = (numer * (1.0 / denom)).astype(BF16)


def whole_in_vmem(count):
    return [pl.BlockSpec(memory_space=pltpu.VMEM)] * count


def call(kernel, shapes, args, aliases={}):
    return pl.pallas_call(
        kernel,
        out_shape=[jax.ShapeDtypeStruct(shape, dtype) for shape, dtype in shapes],
        in_specs=whole_in_vmem(len(args)),
        out_specs=whole_in_vmem(len(shapes)),
        input_output_aliases=aliases,
        compiler_params=pltpu.CompilerParams(vmem_limit_bytes=VMEM_BYTES),
    )(*args)


def start_both(left, right, shape):
    rows_here = shape[0]
    args = list(left) + [half for block in right for half in block]
    shapes = [(shape, F32), (shape, F32), ((2 * rows_here, 128), F32)]
    return call(functools.partial(start_kernel, len(right)), shapes, args)


def add_both(left, right, before):
    args = list(left) + [half for block in right for half in block] + list(before)
    rows_here, wide = before[0].shape
    shapes = [((rows_here, wide), F32)] + [((rows_here // PARTS, wide), BF16)] * PARTS
    kernel = functools.partial(both_kernel, len(right))
    return call(kernel, shapes, args, {len(args) - 2: 0})


def folded_ring(size):
    return [0] + list(range(1, size, 2)) + list(range(2, size, 2))[::-1]


def together(*arrays):
    return lax.optimization_barrier(arrays)


def by_block(embeddings, group_of, cluster_id):
    rows_here, width = embeddings.shape
    half = rows_here // 2
    slabs = width // 128
    n_blk = lax.axis_size("blk")
    order = folded_ring(n_blk)
    line = (1, rows_here)

    def along(rows):
        hops = [
            (2 * order[i - 1] + core, 2 * order[i] + 1 - core)
            for i in range(n_blk)
            for core in range(2)
        ]
        return lax.ppermute(rows, ("blk", "pair"), hops)

    def across(rows):
        return lax.ppermute(rows, ("sub", "pair"), [(0, 3), (1, 2), (2, 1), (3, 0)])

    def other_core(rows):
        return lax.ppermute(rows, "pair", [(0, 1), (1, 0)])

    half_shape = ((slabs * half + 8, 128), BF16)
    (first,) = call(first_pack_kernel, [half_shape], [embeddings])
    whole, second = call(
        pack_kernel,
        [((slabs * rows_here + 8, 128), BF16), half_shape],
        [embeddings, group_of.reshape(line), cluster_id.reshape(line)],
    )
    along_by = [(first, second)]
    across_by = []
    for s in range(1, n_blk):
        moved = [along(piece) for piece in along_by[-1]]
        swapped = [across(piece) for piece in along_by[-1]]
        moved[0], swapped[0] = together(moved[0], swapped[0])
        moved[1], swapped[1], _ = together(moved[1], swapped[1], moved[0])
        along_by.append(tuple(moved))
        across_by.append(tuple(swapped))
    left = (whole, other_core(whole))
    early = across_by[:-1] + along_by[1:-2]
    mine, theirs, info = start_both(left, early, (rows_here, width + 128))
    left = (*left, info)
    near_first, _ = together(across_by[-1][0], along_by[-1][0])
    far_second, mine, theirs, _ = together(along_by[-1][1], mine, theirs, near_first)
    last_first, last_second = along(near_first), across(far_second)
    late = [along_by[-2], across_by[-1], along_by[-1]]
    mine, *theirs = add_both(left, late, (mine, theirs))
    last_first, *theirs = together(last_first, *theirs)
    last_second, *back = together(last_second, *[other_core(part) for part in theirs])
    last = (last_first, last_second)
    (out,) = call(
        last_kernel,
        [((rows_here, width), BF16)],
        [whole, info, *last, *[other_core(half) for half in last], mine, *back],
    )
    return out


def per_device(embeddings, group_of, cluster_id):
    rows_here, width = embeddings.shape
    devices = lax.axis_size("blk") * lax.axis_size("sub") * lax.axis_size("pair")
    small = devices * rows_here * width * 2 <= GATHER_LIMIT
    fits = width % 128 == 0 and rows_here % (32 * PARTS) == 0 and rows_here <= 256
    if small and fits and lax.axis_size("sub") == 2 and lax.axis_size("pair") == 2:
        return by_block(embeddings, group_of, cluster_id)
    return by_group(embeddings, group_of, cluster_id)


def solution(mesh):
    return jax.shard_map(
        per_device,
        mesh=mesh,
        in_specs=(
            P(("island", "blk", "sub", "pair"), None),
            P(("island", "blk", "sub", "pair"), None),
            P(("island", "blk", "sub", "pair")),
        ),
        out_specs=P(("island", "blk", "sub", "pair"), None),
        check_vma=False,
    )
```

```python
import functools

import jax
import jax.numpy as jnp
from jax import lax
from jax.experimental import pallas as pl
from jax.experimental.pallas import tpu as pltpu
from jax.sharding import PartitionSpec as P

F32 = jnp.float32
BF16 = jnp.bfloat16
VMEM_BYTES = 24 * 1024 * 1024
PARTS = 3
GATHER_LIMIT = 8 * 1024 * 1024


def unit_scale(rows_in):
    wide = rows_in.astype(F32)
    return lax.rsqrt(jnp.sum(wide * wide, axis=1) + 1e-06)


def tile_weights(left_rows, left_clust, left_scale, right_rows, right_clust, right_scale):
    grams = lax.dot_general(
        left_rows, right_rows, (((1,), (1,)), ((), ())), preferred_element_type=F32
    )
    cosine = grams * left_scale[:, None] * right_scale[None, :]
    same = (left_clust[:, None] == right_clust[None, :]).astype(F32)
    return jax.nn.sigmoid(8.0 * cosine - 2.0) * same


def by_group(embeddings, group_of, cluster_id):
    rows_here, width = embeddings.shape
    groups = lax.axis_size("sub") * lax.axis_size("pair")
    capacity = 2 * rows_here // groups
    slots = groups * capacity
    target = group_of[:, 0]
    onehot = (target[:, None] == jnp.arange(groups, dtype=jnp.int32)[None, :]).astype(jnp.int32)
    position = jnp.sum((jnp.cumsum(onehot, axis=0) - onehot) * onehot, axis=1)
    send_rows = jnp.zeros((groups, capacity, width), BF16).at[target, position].set(embeddings)
    send_clust = jnp.full((groups, capacity), -1, jnp.int32).at[target, position].set(cluster_id)
    recv_rows, recv_clust = (
        lax.all_to_all(send_rows, ("sub", "pair"), split_axis=0, concat_axis=0, tiled=True),
        lax.all_to_all(send_clust, ("sub", "pair"), split_axis=0, concat_axis=0, tiled=True),
    )
    own_rows = recv_rows.reshape(slots, width)
    own_clust = recv_clust.reshape(slots)
    own_scale = unit_scale(own_rows)
    piece_rows = lax.all_gather(own_rows, "blk", axis=0, tiled=True)
    piece_clust = lax.all_gather(own_clust, "blk", axis=0, tiled=True)
    weight = tile_weights(
        own_rows, own_clust, own_scale, piece_rows, piece_clust, unit_scale(piece_rows)
    )
    numer = jnp.dot(weight.astype(BF16), piece_rows, preferred_element_type=F32)
    denom = jnp.sum(weight, axis=1)
    result = (numer / denom[:, None]).astype(BF16).reshape(groups, capacity, width)
    returned = lax.all_to_all(result, ("sub", "pair"), split_axis=0, concat_axis=0, tiled=True)
    return returned[target, position]


def diagonal(size):
    shape = (size, size)
    return lax.broadcasted_iota(jnp.int32, shape, 0) == lax.broadcasted_iota(jnp.int32, shape, 1)


def to_column(row):
    size = row.shape[1]
    return jnp.sum(jnp.where(diagonal(size), row, jnp.zeros_like(row)), axis=1, keepdims=True)


def to_row(column):
    size = column.shape[0]
    return jnp.sum(jnp.where(diagonal(size), column, jnp.zeros_like(column)), axis=0, keepdims=True)


def scale_column(rows):
    wide = rows.astype(F32)
    return lax.rsqrt(jnp.sum(wide * wide, axis=1, keepdims=True) + 1e-06)


def first_pack_kernel(rows, first):
    width = rows.shape[1]
    slabs = width // 128
    half = rows.shape[0] // 2
    for slab in range(slabs):
        first[slab * half : (slab + 1) * half, :] = rows[:half, slab * 128 : (slab + 1) * 128]
    first[slabs * half :, :] = jnp.zeros((8, 128), BF16)


def pack_kernel(rows, group, cluster, whole, second):
    rows_here, width = rows.shape
    slabs = width // 128
    half = rows_here // 2
    for slab in range(slabs):
        columns = rows[:, slab * 128 : (slab + 1) * 128]
        whole[slab * rows_here : (slab + 1) * rows_here, :] = columns
        second[slab * half : (slab + 1) * half, :] = columns[half:]
    line_at = lax.broadcasted_iota(jnp.int32, (8, 128), 0)
    named = jnp.zeros((8, 128), jnp.int32)
    for line in range(4):
        top = line % 2 * half
        part = (group, cluster)[line // 2][:, top : top + half]
        if half < 128:
            part = jnp.concatenate([part, jnp.zeros((1, 128 - half), jnp.int32)], axis=1)
        named = jnp.where(line_at == line, part, named)
    named = named.astype(F32).astype(BF16)
    whole[slabs * rows_here :, :] = named
    second[slabs * half :, :] = named


def from_slabs(ref, count):
    slabs = [ref[top : top + count, :] for top in range(0, ref.shape[0] // count * count, count)]
    return jnp.concatenate(slabs, axis=1)


def key_rows(ref, half):
    wide = ref[ref.shape[0] - 8 :, :].astype(F32)
    return [wide[side : side + 1, :half] * 256.0 + wide[side + 2 : side + 3, :half] for side in range(2)]


def key_row(ref, rows_here):
    return jnp.concatenate(key_rows(ref, rows_here // 2), axis=1)


def from_halves(first, second, rows_here):
    half = rows_here // 2
    rows = jnp.concatenate([from_slabs(first, half), from_slabs(second, half)], axis=0)
    return rows, key_row(second, rows_here)


def add_blocks(left, info, blocks, numer, denom):
    key = info[: left.shape[0], 0:1]
    scale = info[: left.shape[0], 1:2]
    for right_rows, right_key, right_scale in blocks:
        grams = lax.dot_general(
            left, right_rows, (((1,), (1,)), ((), ())), preferred_element_type=F32
        )
        half = jnp.tanh(grams * scale * right_scale - 1.0)
        weight = jnp.where(key == right_key, 0.5 + 0.5 * half, 0.0)
        add = jnp.dot(weight.astype(BF16), right_rows, preferred_element_type=F32)
        add_denom = jnp.sum(weight, axis=1, keepdims=True)
        numer = add if numer is None else numer + add
        denom = add_denom if denom is None else denom + add_denom
    return numer, denom


def left_rows(refs, rows_here):
    return jnp.concatenate([from_slabs(ref, rows_here) for ref in refs], axis=0)


def take_blocks(refs, count, rows_here):
    blocks = []
    for _ in range(count):
        rows, key = from_halves(refs.pop(0), refs.pop(0), rows_here)
        blocks.append((rows, key, to_row(scale_column(rows))))
    return blocks


def store_sides(numer, denom, outs):
    rows_here, wide = outs[0].shape
    for side, out in enumerate(outs):
        top = side * rows_here
        out[:, : wide - 128] = numer[top : top + rows_here]
        out[:, wide - 128 :] = jnp.broadcast_to(denom[top : top + rows_here], (rows_here, 128))


def start_kernel(n_blocks, own, other, *refs):
    refs = list(refs)
    rows_here = refs[-1].shape[0] // 2
    left = left_rows((own, other), rows_here)
    key = jnp.concatenate([to_column(key_row(ref, rows_here)) for ref in (own, other)], axis=0)
    scale = scale_column(left)
    info = refs.pop()
    lane = lax.broadcasted_iota(jnp.int32, info.shape, 1)
    info[...] = jnp.where(lane == 0, key, 4.0 * scale)
    first = (left[:rows_here], key_row(own, rows_here), to_row(scale[:rows_here]))
    blocks = [first] + take_blocks(refs, n_blocks, rows_here)
    store_sides(*add_blocks(left, info, blocks, None, None), refs)


def both_kernel(n_blocks, own, other, info, *refs):
    refs = list(refs)
    rows_here = refs[2 * n_blocks].shape[0]
    blocks = take_blocks(refs, n_blocks, rows_here)
    mine_in, theirs_in, mine, *theirs = refs
    wide = mine.shape[1]
    width = wide - 128
    left = left_rows((own, other), rows_here)
    numer = jnp.concatenate([ref[:, :width] for ref in (mine_in, theirs_in)], axis=0)
    denom = jnp.concatenate([ref[:, width : width + 1] for ref in (mine_in, theirs_in)], axis=0)
    numer, denom = add_blocks(left, info, blocks, numer, denom)
    store_sides(numer[:rows_here], denom[:rows_here], [mine])
    denom = denom[rows_here:]
    high = denom.astype(BF16).astype(F32)
    lane = lax.broadcasted_iota(jnp.int32, (rows_here, 128), 1)
    pair = jnp.where(lane == 0, high, denom - high).astype(BF16)
    count = rows_here // len(theirs)
    for part, out in enumerate(theirs):
        top = part * count
        out[:, :width] = numer[rows_here + top : rows_here + top + count].astype(BF16)
        out[:, width:] = pair[top : top + count]


def last_kernel(own, info, first, second, first_other, second_other, mine, *refs):
    out = refs[-1]
    rows_here, width = out.shape
    theirs = jnp.concatenate([ref[...] for ref in refs[:-1]], axis=0)
    blocks = take_blocks([first, second, first_other, second_other], 2, rows_here)
    parts = theirs[:, width:].astype(F32)
    numer = mine[:, :width] + theirs[:, :width].astype(F32)
    denom = mine[:, width : width + 1] + (parts[:, 0:1] + parts[:, 1:2])
    numer, denom = add_blocks(left_rows((own,), rows_here), info, blocks, numer, denom)
    out[...] = (numer * (1.0 / denom)).astype(BF16)


def whole_in_vmem(count):
    return [pl.BlockSpec(memory_space=pltpu.VMEM)] * count


def call(kernel, shapes, args, aliases={}):
    return pl.pallas_call(
        kernel,
        out_shape=[jax.ShapeDtypeStruct(shape, dtype) for shape, dtype in shapes],
        in_specs=whole_in_vmem(len(args)),
        out_specs=whole_in_vmem(len(shapes)),
        input_output_aliases=aliases,
        compiler_params=pltpu.CompilerParams(vmem_limit_bytes=VMEM_BYTES),
    )(*args)


def start_both(left, right, shape):
    rows_here = shape[0]
    args = list(left) + [half for block in right for half in block]
    shapes = [(shape, F32), (shape, F32), ((2 * rows_here, 128), F32)]
    return call(functools.partial(start_kernel, len(right)), shapes, args)


def add_both(left, right, before):
    args = list(left) + [half for block in right for half in block] + list(before)
    rows_here, wide = before[0].shape
    shapes = [((rows_here, wide), F32)] + [((rows_here // PARTS, wide), BF16)] * PARTS
    kernel = functools.partial(both_kernel, len(right))
    return call(kernel, shapes, args, {len(args) - 2: 0})


def folded_ring(size):
    return [0] + list(range(1, size, 2)) + list(range(2, size, 2))[::-1]


def together(*arrays):
    return lax.optimization_barrier(arrays)


def by_block(embeddings, group_of, cluster_id):
    rows_here, width = embeddings.shape
    half = rows_here // 2
    slabs = width // 128
    n_blk = lax.axis_size("blk")
    order = folded_ring(n_blk)
    line = (1, rows_here)

    def along(rows):
        hops = [
            (2 * order[i - 1] + core, 2 * order[i] + 1 - core)
            for i in range(n_blk)
            for core in range(2)
        ]
        return lax.ppermute(rows, ("blk", "pair"), hops)

    def across(rows):
        return lax.ppermute(rows, ("sub", "pair"), [(0, 3), (1, 2), (2, 1), (3, 0)])

    def other_core(rows):
        return lax.ppermute(rows, "pair", [(0, 1), (1, 0)])

    half_shape = ((slabs * half + 8, 128), BF16)
    (first,) = call(first_pack_kernel, [half_shape], [embeddings])
    whole, second = call(
        pack_kernel,
        [((slabs * rows_here + 8, 128), BF16), half_shape],
        [embeddings, group_of.reshape(line), cluster_id.reshape(line)],
    )
    along_by = [(first, second)]
    across_by = []
    for s in range(1, n_blk):
        moved = [along(piece) for piece in along_by[-1]]
        swapped = [across(piece) for piece in along_by[-1]]
        moved[0], swapped[0] = together(moved[0], swapped[0])
        moved[1], swapped[1], _ = together(moved[1], swapped[1], moved[0])
        along_by.append(tuple(moved))
        across_by.append(tuple(swapped))
    left = (whole, other_core(whole))
    early = across_by[:-1] + along_by[1:-2]
    mine, theirs, info = start_both(left, early, (rows_here, width + 128))
    left = (*left, info)
    near_first, _, mine, theirs = together(across_by[-1][0], along_by[-1][0], mine, theirs)
    far_second, _ = together(along_by[-1][1], near_first)
    last_first, last_second = along(near_first), across(far_second)
    late = [along_by[-2], across_by[-1], along_by[-1]]
    mine, *theirs = add_both(left, late, (mine, theirs))
    last_first, *theirs = together(last_first, *theirs)
    last_second, *back = together(last_second, *[other_core(part) for part in theirs])
    last = (last_first, last_second)
    (out,) = call(
        last_kernel,
        [((rows_here, width), BF16)],
        [whole, info, *last, *[other_core(half) for half in last], mine, *back],
    )
    return out


def per_device(embeddings, group_of, cluster_id):
    rows_here, width = embeddings.shape
    devices = lax.axis_size("blk") * lax.axis_size("sub") * lax.axis_size("pair")
    small = devices * rows_here * width * 2 <= GATHER_LIMIT
    fits = width % 128 == 0 and rows_here % (32 * PARTS) == 0 and rows_here <= 256
    if small and fits and lax.axis_size("sub") == 2 and lax.axis_size("pair") == 2:
        return by_block(embeddings, group_of, cluster_id)
    return by_group(embeddings, group_of, cluster_id)


def solution(mesh):
    return jax.shard_map(
        per_device,
        mesh=mesh,
        in_specs=(
            P(("island", "blk", "sub", "pair"), None),
            P(("island", "blk", "sub", "pair"), None),
            P(("island", "blk", "sub", "pair")),
        ),
        out_specs=P(("island", "blk", "sub", "pair"), None),
        check_vma=False,
    )
```

```python
import functools

import jax
import jax.numpy as jnp
from jax import lax
from jax.experimental import pallas as pl
from jax.experimental.pallas import tpu as pltpu
from jax.sharding import PartitionSpec as P

F32 = jnp.float32
BF16 = jnp.bfloat16
VMEM_BYTES = 24 * 1024 * 1024
PARTS = 3
GATHER_LIMIT = 8 * 1024 * 1024


def unit_scale(rows_in):
    wide = rows_in.astype(F32)
    return lax.rsqrt(jnp.sum(wide * wide, axis=1) + 1e-06)


def tile_weights(left_rows, left_clust, left_scale, right_rows, right_clust, right_scale):
    grams = lax.dot_general(
        left_rows, right_rows, (((1,), (1,)), ((), ())), preferred_element_type=F32
    )
    cosine = grams * left_scale[:, None] * right_scale[None, :]
    same = (left_clust[:, None] == right_clust[None, :]).astype(F32)
    return jax.nn.sigmoid(8.0 * cosine - 2.0) * same


def by_group(embeddings, group_of, cluster_id):
    rows_here, width = embeddings.shape
    groups = lax.axis_size("sub") * lax.axis_size("pair")
    capacity = 2 * rows_here // groups
    slots = groups * capacity
    target = group_of[:, 0]
    onehot = (target[:, None] == jnp.arange(groups, dtype=jnp.int32)[None, :]).astype(jnp.int32)
    position = jnp.sum((jnp.cumsum(onehot, axis=0) - onehot) * onehot, axis=1)
    send_rows = jnp.zeros((groups, capacity, width), BF16).at[target, position].set(embeddings)
    send_clust = jnp.full((groups, capacity), -1, jnp.int32).at[target, position].set(cluster_id)
    recv_rows, recv_clust = (
        lax.all_to_all(send_rows, ("sub", "pair"), split_axis=0, concat_axis=0, tiled=True),
        lax.all_to_all(send_clust, ("sub", "pair"), split_axis=0, concat_axis=0, tiled=True),
    )
    own_rows = recv_rows.reshape(slots, width)
    own_clust = recv_clust.reshape(slots)
    own_scale = unit_scale(own_rows)
    piece_rows = lax.all_gather(own_rows, "blk", axis=0, tiled=True)
    piece_clust = lax.all_gather(own_clust, "blk", axis=0, tiled=True)
    weight = tile_weights(
        own_rows, own_clust, own_scale, piece_rows, piece_clust, unit_scale(piece_rows)
    )
    numer = jnp.dot(weight.astype(BF16), piece_rows, preferred_element_type=F32)
    denom = jnp.sum(weight, axis=1)
    result = (numer / denom[:, None]).astype(BF16).reshape(groups, capacity, width)
    returned = lax.all_to_all(result, ("sub", "pair"), split_axis=0, concat_axis=0, tiled=True)
    return returned[target, position]


def diagonal(size):
    shape = (size, size)
    return lax.broadcasted_iota(jnp.int32, shape, 0) == lax.broadcasted_iota(jnp.int32, shape, 1)


def to_column(row):
    size = row.shape[1]
    return jnp.sum(jnp.where(diagonal(size), row, jnp.zeros_like(row)), axis=1, keepdims=True)


def to_row(column):
    size = column.shape[0]
    return jnp.sum(jnp.where(diagonal(size), column, jnp.zeros_like(column)), axis=0, keepdims=True)


def scale_column(rows):
    wide = rows.astype(F32)
    return lax.rsqrt(jnp.sum(wide * wide, axis=1, keepdims=True) + 1e-06)


def first_pack_kernel(rows, first):
    width = rows.shape[1]
    slabs = width // 128
    half = rows.shape[0] // 2
    for slab in range(slabs):
        first[slab * half : (slab + 1) * half, :] = rows[:half, slab * 128 : (slab + 1) * 128]
    first[slabs * half :, :] = jnp.zeros((8, 128), BF16)


def pack_kernel(rows, group, cluster, whole, second):
    rows_here, width = rows.shape
    slabs = width // 128
    half = rows_here // 2
    for slab in range(slabs):
        columns = rows[:, slab * 128 : (slab + 1) * 128]
        whole[slab * rows_here : (slab + 1) * rows_here, :] = columns
        second[slab * half : (slab + 1) * half, :] = columns[half:]
    line_at = lax.broadcasted_iota(jnp.int32, (8, 128), 0)
    named = jnp.zeros((8, 128), jnp.int32)
    for line in range(4):
        top = line % 2 * half
        part = (group, cluster)[line // 2][:, top : top + half]
        if half < 128:
            part = jnp.concatenate([part, jnp.zeros((1, 128 - half), jnp.int32)], axis=1)
        named = jnp.where(line_at == line, part, named)
    named = named.astype(F32).astype(BF16)
    whole[slabs * rows_here :, :] = named
    second[slabs * half :, :] = named


def from_slabs(ref, count):
    slabs = [ref[top : top + count, :] for top in range(0, ref.shape[0] // count * count, count)]
    return jnp.concatenate(slabs, axis=1)


def key_rows(ref, half):
    wide = ref[ref.shape[0] - 8 :, :].astype(F32)
    return [wide[side : side + 1, :half] * 256.0 + wide[side + 2 : side + 3, :half] for side in range(2)]


def key_row(ref, rows_here):
    return jnp.concatenate(key_rows(ref, rows_here // 2), axis=1)


def from_halves(first, second, rows_here):
    half = rows_here // 2
    rows = jnp.concatenate([from_slabs(first, half), from_slabs(second, half)], axis=0)
    return rows, key_row(second, rows_here)


def add_blocks(left, info, blocks, numer, denom):
    key = info[: left.shape[0], 0:1]
    scale = info[: left.shape[0], 1:2]
    for right_rows, right_key, right_scale in blocks:
        grams = lax.dot_general(
            left, right_rows, (((1,), (1,)), ((), ())), preferred_element_type=F32
        )
        half = jnp.tanh(grams * scale * right_scale - 1.0)
        weight = jnp.where(key == right_key, 0.5 + 0.5 * half, 0.0)
        add = jnp.dot(weight.astype(BF16), right_rows, preferred_element_type=F32)
        add_denom = jnp.sum(weight, axis=1, keepdims=True)
        numer = add if numer is None else numer + add
        denom = add_denom if denom is None else denom + add_denom
    return numer, denom


def left_rows(refs, rows_here):
    return jnp.concatenate([from_slabs(ref, rows_here) for ref in refs], axis=0)


def take_blocks(refs, count, rows_here):
    blocks = []
    for _ in range(count):
        rows, key = from_halves(refs.pop(0), refs.pop(0), rows_here)
        blocks.append((rows, key, to_row(scale_column(rows))))
    return blocks


def store_sides(numer, denom, outs):
    rows_here, wide = outs[0].shape
    for side, out in enumerate(outs):
        top = side * rows_here
        out[:, : wide - 128] = numer[top : top + rows_here]
        out[:, wide - 128 :] = jnp.broadcast_to(denom[top : top + rows_here], (rows_here, 128))


def start_kernel(n_blocks, own, other, *refs):
    refs = list(refs)
    rows_here = refs[-1].shape[0] // 2
    left = left_rows((own, other), rows_here)
    key = jnp.concatenate([to_column(key_row(ref, rows_here)) for ref in (own, other)], axis=0)
    scale = scale_column(left)
    info = refs.pop()
    lane = lax.broadcasted_iota(jnp.int32, info.shape, 1)
    info[...] = jnp.where(lane == 0, key, 4.0 * scale)
    first = (left[:rows_here], key_row(own, rows_here), to_row(scale[:rows_here]))
    blocks = [first] + take_blocks(refs, n_blocks, rows_here)
    store_sides(*add_blocks(left, info, blocks, None, None), refs)


def both_kernel(n_blocks, own, other, info, *refs):
    refs = list(refs)
    rows_here = refs[2 * n_blocks].shape[0]
    blocks = take_blocks(refs, n_blocks, rows_here)
    mine_in, theirs_in, mine, *theirs = refs
    wide = mine.shape[1]
    width = wide - 128
    left = left_rows((own, other), rows_here)
    numer = jnp.concatenate([ref[:, :width] for ref in (mine_in, theirs_in)], axis=0)
    denom = jnp.concatenate([ref[:, width : width + 1] for ref in (mine_in, theirs_in)], axis=0)
    numer, denom = add_blocks(left, info, blocks, numer, denom)
    store_sides(numer[:rows_here], denom[:rows_here], [mine])
    denom = denom[rows_here:]
    high = denom.astype(BF16).astype(F32)
    lane = lax.broadcasted_iota(jnp.int32, (rows_here, 128), 1)
    pair = jnp.where(lane == 0, high, denom - high).astype(BF16)
    count = rows_here // len(theirs)
    for part, out in enumerate(theirs):
        top = part * count
        out[:, :width] = numer[rows_here + top : rows_here + top + count].astype(BF16)
        out[:, width:] = pair[top : top + count]


def last_kernel(own, info, first, second, first_other, second_other, mine, *refs):
    out = refs[-1]
    rows_here, width = out.shape
    theirs = jnp.concatenate([ref[...] for ref in refs[:-1]], axis=0)
    blocks = take_blocks([first, second, first_other, second_other], 2, rows_here)
    parts = theirs[:, width:].astype(F32)
    numer = mine[:, :width] + theirs[:, :width].astype(F32)
    denom = mine[:, width : width + 1] + (parts[:, 0:1] + parts[:, 1:2])
    numer, denom = add_blocks(left_rows((own,), rows_here), info, blocks, numer, denom)
    out[...] = (numer * (1.0 / denom)).astype(BF16)


def whole_in_vmem(count):
    return [pl.BlockSpec(memory_space=pltpu.VMEM)] * count


def call(kernel, shapes, args, aliases={}):
    return pl.pallas_call(
        kernel,
        out_shape=[jax.ShapeDtypeStruct(shape, dtype) for shape, dtype in shapes],
        in_specs=whole_in_vmem(len(args)),
        out_specs=whole_in_vmem(len(shapes)),
        input_output_aliases=aliases,
        compiler_params=pltpu.CompilerParams(vmem_limit_bytes=VMEM_BYTES),
    )(*args)


def start_both(left, right, shape):
    rows_here = shape[0]
    args = list(left) + [half for block in right for half in block]
    shapes = [(shape, F32), (shape, F32), ((2 * rows_here, 128), F32)]
    return call(functools.partial(start_kernel, len(right)), shapes, args)


def add_both(left, right, before):
    args = list(left) + [half for block in right for half in block] + list(before)
    rows_here, wide = before[0].shape
    shapes = [((rows_here, wide), F32)] + [((rows_here // PARTS, wide), BF16)] * PARTS
    kernel = functools.partial(both_kernel, len(right))
    return call(kernel, shapes, args, {len(args) - 2: 0})


def folded_ring(size):
    return list(range(0, size, 2)) + list(range(1, size, 2))[::-1]


def together(*arrays):
    return lax.optimization_barrier(arrays)


def by_block(embeddings, group_of, cluster_id):
    rows_here, width = embeddings.shape
    half = rows_here // 2
    slabs = width // 128
    n_blk = lax.axis_size("blk")
    order = folded_ring(n_blk)
    line = (1, rows_here)

    def along(rows):
        hops = [
            (2 * order[i - 1] + core, 2 * order[i] + 1 - core)
            for i in range(n_blk)
            for core in range(2)
        ]
        return lax.ppermute(rows, ("blk", "pair"), hops)

    def across(rows):
        return lax.ppermute(rows, ("sub", "pair"), [(0, 3), (1, 2), (2, 1), (3, 0)])

    def other_core(rows):
        return lax.ppermute(rows, "pair", [(0, 1), (1, 0)])

    half_shape = ((slabs * half + 8, 128), BF16)
    (first,) = call(first_pack_kernel, [half_shape], [embeddings])
    whole, second = call(
        pack_kernel,
        [((slabs * rows_here + 8, 128), BF16), half_shape],
        [embeddings, group_of.reshape(line), cluster_id.reshape(line)],
    )
    along_by = [(first, second)]
    across_by = []
    for s in range(1, n_blk):
        moved = [along(piece) for piece in along_by[-1]]
        swapped = [across(piece) for piece in along_by[-1]]
        moved[0], swapped[0] = together(moved[0], swapped[0])
        moved[1], swapped[1], _ = together(moved[1], swapped[1], moved[0])
        along_by.append(tuple(moved))
        across_by.append(tuple(swapped))
    left = (whole, other_core(whole))
    early = across_by[:-1] + along_by[1:-2]
    mine, theirs, info = start_both(left, early, (rows_here, width + 128))
    left = (*left, info)
    near_first, _, mine, theirs = together(across_by[-1][0], along_by[-1][0], mine, theirs)
    far_second, _ = together(along_by[-1][1], near_first)
    last_first, last_second = along(near_first), across(far_second)
    late = [along_by[-2], across_by[-1], along_by[-1]]
    mine, *theirs = add_both(left, late, (mine, theirs))
    last_first, *theirs = together(last_first, *theirs)
    last_second, *back = together(last_second, *[other_core(part) for part in theirs])
    last = (last_first, last_second)
    (out,) = call(
        last_kernel,
        [((rows_here, width), BF16)],
        [whole, info, *last, *[other_core(half) for half in last], mine, *back],
    )
    return out


def per_device(embeddings, group_of, cluster_id):
    rows_here, width = embeddings.shape
    devices = lax.axis_size("blk") * lax.axis_size("sub") * lax.axis_size("pair")
    small = devices * rows_here * width * 2 <= GATHER_LIMIT
    fits = width % 128 == 0 and rows_here % (32 * PARTS) == 0 and rows_here <= 256
    if small and fits and lax.axis_size("sub") == 2 and lax.axis_size("pair") == 2:
        return by_block(embeddings, group_of, cluster_id)
    return by_group(embeddings, group_of, cluster_id)


def solution(mesh):
    return jax.shard_map(
        per_device,
        mesh=mesh,
        in_specs=(
            P(("island", "blk", "sub", "pair"), None),
            P(("island", "blk", "sub", "pair"), None),
            P(("island", "blk", "sub", "pair")),
        ),
        out_specs=P(("island", "blk", "sub", "pair"), None),
        check_vma=False,
    )
```

```python
import functools

import jax
import jax.numpy as jnp
from jax import lax
from jax.experimental import pallas as pl
from jax.experimental.pallas import tpu as pltpu
from jax.sharding import PartitionSpec as P

F32 = jnp.float32
BF16 = jnp.bfloat16
VMEM_BYTES = 24 * 1024 * 1024
PARTS = 3
GATHER_LIMIT = 8 * 1024 * 1024


def unit_scale(rows_in):
    wide = rows_in.astype(F32)
    return lax.rsqrt(jnp.sum(wide * wide, axis=1) + 1e-06)


def tile_weights(left_rows, left_clust, left_scale, right_rows, right_clust, right_scale):
    grams = lax.dot_general(
        left_rows, right_rows, (((1,), (1,)), ((), ())), preferred_element_type=F32
    )
    cosine = grams * left_scale[:, None] * right_scale[None, :]
    same = (left_clust[:, None] == right_clust[None, :]).astype(F32)
    return jax.nn.sigmoid(8.0 * cosine - 2.0) * same


def by_group(embeddings, group_of, cluster_id):
    rows_here, width = embeddings.shape
    groups = lax.axis_size("sub") * lax.axis_size("pair")
    capacity = 2 * rows_here // groups
    slots = groups * capacity
    target = group_of[:, 0]
    onehot = (target[:, None] == jnp.arange(groups, dtype=jnp.int32)[None, :]).astype(jnp.int32)
    position = jnp.sum((jnp.cumsum(onehot, axis=0) - onehot) * onehot, axis=1)
    send_rows = jnp.zeros((groups, capacity, width), BF16).at[target, position].set(embeddings)
    send_clust = jnp.full((groups, capacity), -1, jnp.int32).at[target, position].set(cluster_id)
    recv_rows, recv_clust = (
        lax.all_to_all(send_rows, ("sub", "pair"), split_axis=0, concat_axis=0, tiled=True),
        lax.all_to_all(send_clust, ("sub", "pair"), split_axis=0, concat_axis=0, tiled=True),
    )
    own_rows = recv_rows.reshape(slots, width)
    own_clust = recv_clust.reshape(slots)
    own_scale = unit_scale(own_rows)
    piece_rows = lax.all_gather(own_rows, "blk", axis=0, tiled=True)
    piece_clust = lax.all_gather(own_clust, "blk", axis=0, tiled=True)
    weight = tile_weights(
        own_rows, own_clust, own_scale, piece_rows, piece_clust, unit_scale(piece_rows)
    )
    numer = jnp.dot(weight.astype(BF16), piece_rows, preferred_element_type=F32)
    denom = jnp.sum(weight, axis=1)
    result = (numer / denom[:, None]).astype(BF16).reshape(groups, capacity, width)
    returned = lax.all_to_all(result, ("sub", "pair"), split_axis=0, concat_axis=0, tiled=True)
    return returned[target, position]


def diagonal(size):
    shape = (size, size)
    return lax.broadcasted_iota(jnp.int32, shape, 0) == lax.broadcasted_iota(jnp.int32, shape, 1)


def to_column(row):
    size = row.shape[1]
    return jnp.sum(jnp.where(diagonal(size), row, jnp.zeros_like(row)), axis=1, keepdims=True)


def to_row(column):
    size = column.shape[0]
    return jnp.sum(jnp.where(diagonal(size), column, jnp.zeros_like(column)), axis=0, keepdims=True)


def scale_column(rows):
    wide = rows.astype(F32)
    return lax.rsqrt(jnp.sum(wide * wide, axis=1, keepdims=True) + 1e-06)


def first_pack_kernel(rows, first):
    width = rows.shape[1]
    slabs = width // 128
    half = rows.shape[0] // 2
    for slab in range(slabs):
        first[slab * half : (slab + 1) * half, :] = rows[:half, slab * 128 : (slab + 1) * 128]
    first[slabs * half :, :] = jnp.zeros((8, 128), BF16)


def pack_kernel(rows, group, cluster, whole, second):
    rows_here, width = rows.shape
    slabs = width // 128
    half = rows_here // 2
    for slab in range(slabs):
        columns = rows[:, slab * 128 : (slab + 1) * 128]
        whole[slab * rows_here : (slab + 1) * rows_here, :] = columns
        second[slab * half : (slab + 1) * half, :] = columns[half:]
    line_at = lax.broadcasted_iota(jnp.int32, (8, 128), 0)
    named = jnp.zeros((8, 128), jnp.int32)
    for line in range(4):
        top = line % 2 * half
        part = (group, cluster)[line // 2][:, top : top + half]
        if half < 128:
            part = jnp.concatenate([part, jnp.zeros((1, 128 - half), jnp.int32)], axis=1)
        named = jnp.where(line_at == line, part, named)
    named = named.astype(F32).astype(BF16)
    whole[slabs * rows_here :, :] = named
    second[slabs * half :, :] = named


def from_slabs(ref, count):
    slabs = [ref[top : top + count, :] for top in range(0, ref.shape[0] // count * count, count)]
    return jnp.concatenate(slabs, axis=1)


def key_rows(ref, half):
    wide = ref[ref.shape[0] - 8 :, :].astype(F32)
    return [wide[side : side + 1, :half] * 256.0 + wide[side + 2 : side + 3, :half] for side in range(2)]


def key_row(ref, rows_here):
    return jnp.concatenate(key_rows(ref, rows_here // 2), axis=1)


def from_halves(first, second, rows_here):
    half = rows_here // 2
    rows = jnp.concatenate([from_slabs(first, half), from_slabs(second, half)], axis=0)
    return rows, key_row(second, rows_here)


def add_blocks(left, info, blocks, numer, denom):
    key = info[: left.shape[0], 0:1]
    scale = info[: left.shape[0], 1:2]
    right_rows = jnp.concatenate([block[0] for block in blocks], axis=0)
    right_key = jnp.concatenate([block[1] for block in blocks], axis=1)
    right_scale = jnp.concatenate([block[2] for block in blocks], axis=1)
    grams = lax.dot_general(
        left, right_rows, (((1,), (1,)), ((), ())), preferred_element_type=F32
    )
    half = jnp.tanh(grams * scale * right_scale - 1.0)
    weight = jnp.where(key == right_key, 0.5 + 0.5 * half, 0.0)
    add = jnp.dot(weight.astype(BF16), right_rows, preferred_element_type=F32)
    add_denom = jnp.sum(weight, axis=1, keepdims=True)
    if numer is None:
        return add, add_denom
    return numer + add, denom + add_denom


def left_rows(refs, rows_here):
    return jnp.concatenate([from_slabs(ref, rows_here) for ref in refs], axis=0)


def take_blocks(refs, count, rows_here):
    blocks = []
    for _ in range(count):
        rows, key = from_halves(refs.pop(0), refs.pop(0), rows_here)
        blocks.append((rows, key, to_row(scale_column(rows))))
    return blocks


def store_sides(numer, denom, outs):
    rows_here, wide = outs[0].shape
    for side, out in enumerate(outs):
        top = side * rows_here
        out[:, : wide - 128] = numer[top : top + rows_here]
        out[:, wide - 128 :] = jnp.broadcast_to(denom[top : top + rows_here], (rows_here, 128))


def start_kernel(n_blocks, own, other, *refs):
    refs = list(refs)
    rows_here = refs[-1].shape[0] // 2
    left = left_rows((own, other), rows_here)
    key = jnp.concatenate([to_column(key_row(ref, rows_here)) for ref in (own, other)], axis=0)
    scale = scale_column(left)
    info = refs.pop()
    lane = lax.broadcasted_iota(jnp.int32, info.shape, 1)
    info[...] = jnp.where(lane == 0, key, 4.0 * scale)
    first = (left[:rows_here], key_row(own, rows_here), to_row(scale[:rows_here]))
    blocks = [first] + take_blocks(refs, n_blocks, rows_here)
    store_sides(*add_blocks(left, info, blocks, None, None), refs)


def both_kernel(n_blocks, own, other, info, *refs):
    refs = list(refs)
    rows_here = refs[2 * n_blocks].shape[0]
    blocks = take_blocks(refs, n_blocks, rows_here)
    mine_in, theirs_in, mine, *theirs = refs
    wide = mine.shape[1]
    width = wide - 128
    left = left_rows((own, other), rows_here)
    numer = jnp.concatenate([ref[:, :width] for ref in (mine_in, theirs_in)], axis=0)
    denom = jnp.concatenate([ref[:, width : width + 1] for ref in (mine_in, theirs_in)], axis=0)
    numer, denom = add_blocks(left, info, blocks, numer, denom)
    store_sides(numer[:rows_here], denom[:rows_here], [mine])
    denom = denom[rows_here:]
    high = denom.astype(BF16).astype(F32)
    lane = lax.broadcasted_iota(jnp.int32, (rows_here, 128), 1)
    pair = jnp.where(lane == 0, high, denom - high).astype(BF16)
    count = rows_here // len(theirs)
    for part, out in enumerate(theirs):
        top = part * count
        out[:, :width] = numer[rows_here + top : rows_here + top + count].astype(BF16)
        out[:, width:] = pair[top : top + count]


def last_kernel(own, info, first, second, first_other, second_other, mine, *refs):
    out = refs[-1]
    rows_here, width = out.shape
    theirs = jnp.concatenate([ref[...] for ref in refs[:-1]], axis=0)
    blocks = take_blocks([first, second, first_other, second_other], 2, rows_here)
    parts = theirs[:, width:].astype(F32)
    numer = mine[:, :width] + theirs[:, :width].astype(F32)
    denom = mine[:, width : width + 1] + (parts[:, 0:1] + parts[:, 1:2])
    numer, denom = add_blocks(left_rows((own,), rows_here), info, blocks, numer, denom)
    out[...] = (numer * (1.0 / denom)).astype(BF16)


def whole_in_vmem(count):
    return [pl.BlockSpec(memory_space=pltpu.VMEM)] * count


def call(kernel, shapes, args, aliases={}):
    return pl.pallas_call(
        kernel,
        out_shape=[jax.ShapeDtypeStruct(shape, dtype) for shape, dtype in shapes],
        in_specs=whole_in_vmem(len(args)),
        out_specs=whole_in_vmem(len(shapes)),
        input_output_aliases=aliases,
        compiler_params=pltpu.CompilerParams(vmem_limit_bytes=VMEM_BYTES),
    )(*args)


def start_both(left, right, shape):
    rows_here = shape[0]
    args = list(left) + [half for block in right for half in block]
    shapes = [(shape, F32), (shape, F32), ((2 * rows_here, 128), F32)]
    return call(functools.partial(start_kernel, len(right)), shapes, args)


def add_both(left, right, before):
    args = list(left) + [half for block in right for half in block] + list(before)
    rows_here, wide = before[0].shape
    shapes = [((rows_here, wide), F32)] + [((rows_here // PARTS, wide), BF16)] * PARTS
    kernel = functools.partial(both_kernel, len(right))
    return call(kernel, shapes, args, {len(args) - 2: 0})


def folded_ring(size):
    return list(range(0, size, 2)) + list(range(1, size, 2))[::-1]


def together(*arrays):
    return lax.optimization_barrier(arrays)


def by_block(embeddings, group_of, cluster_id):
    rows_here, width = embeddings.shape
    half = rows_here // 2
    slabs = width // 128
    n_blk = lax.axis_size("blk")
    order = folded_ring(n_blk)
    line = (1, rows_here)

    def along(rows):
        hops = [
            (2 * order[i - 1] + core, 2 * order[i] + 1 - core)
            for i in range(n_blk)
            for core in range(2)
        ]
        return lax.ppermute(rows, ("blk", "pair"), hops)

    def across(rows):
        return lax.ppermute(rows, ("sub", "pair"), [(0, 3), (1, 2), (2, 1), (3, 0)])

    def other_core(rows):
        return lax.ppermute(rows, "pair", [(0, 1), (1, 0)])

    half_shape = ((slabs * half + 8, 128), BF16)
    (first,) = call(first_pack_kernel, [half_shape], [embeddings])
    whole, second = call(
        pack_kernel,
        [((slabs * rows_here + 8, 128), BF16), half_shape],
        [embeddings, group_of.reshape(line), cluster_id.reshape(line)],
    )
    along_by = [(first, second)]
    across_by = []
    for s in range(1, n_blk):
        moved = [along(piece) for piece in along_by[-1]]
        swapped = [across(piece) for piece in along_by[-1]]
        moved[0], swapped[0] = together(moved[0], swapped[0])
        moved[1], swapped[1], _ = together(moved[1], swapped[1], moved[0])
        along_by.append(tuple(moved))
        across_by.append(tuple(swapped))
    left = (whole, other_core(whole))
    early = across_by[:-1] + along_by[1:-2]
    mine, theirs, info = start_both(left, early, (rows_here, width + 128))
    left = (*left, info)
    near_first, _, mine, theirs = together(across_by[-1][0], along_by[-1][0], mine, theirs)
    far_second, _ = together(along_by[-1][1], near_first)
    last_first, last_second = along(near_first), across(far_second)
    late = [along_by[-2], across_by[-1], along_by[-1]]
    mine, *theirs = add_both(left, late, (mine, theirs))
    back = [other_core(part) for part in theirs[:-1]]
    last_first, theirs[-1] = together(last_first, theirs[-1])
    last_second, *back = together(last_second, *back, other_core(theirs[-1]))
    last = (last_first, last_second)
    (out,) = call(
        last_kernel,
        [((rows_here, width), BF16)],
        [whole, info, *last, *[other_core(half) for half in last], mine, *back],
    )
    return out


def per_device(embeddings, group_of, cluster_id):
    rows_here, width = embeddings.shape
    devices = lax.axis_size("blk") * lax.axis_size("sub") * lax.axis_size("pair")
    small = devices * rows_here * width * 2 <= GATHER_LIMIT
    fits = width % 128 == 0 and rows_here % (32 * PARTS) == 0 and rows_here <= 256
    if small and fits and lax.axis_size("sub") == 2 and lax.axis_size("pair") == 2:
        return by_block(embeddings, group_of, cluster_id)
    return by_group(embeddings, group_of, cluster_id)


def solution(mesh):
    return jax.shard_map(
        per_device,
        mesh=mesh,
        in_specs=(
            P(("island", "blk", "sub", "pair"), None),
            P(("island", "blk", "sub", "pair"), None),
            P(("island", "blk", "sub", "pair")),
        ),
        out_specs=P(("island", "blk", "sub", "pair"), None),
        check_vma=False,
    )
```

```python
import functools

import jax
import jax.numpy as jnp
from jax import lax
from jax.experimental import pallas as pl
from jax.experimental.pallas import tpu as pltpu
from jax.sharding import PartitionSpec as P

F32 = jnp.float32
BF16 = jnp.bfloat16
VMEM_BYTES = 24 * 1024 * 1024
PARTS = 3
GATHER_LIMIT = 8 * 1024 * 1024


def unit_scale(rows_in):
    wide = rows_in.astype(F32)
    return lax.rsqrt(jnp.sum(wide * wide, axis=1) + 1e-06)


def tile_weights(left_rows, left_clust, left_scale, right_rows, right_clust, right_scale):
    grams = lax.dot_general(
        left_rows, right_rows, (((1,), (1,)), ((), ())), preferred_element_type=F32
    )
    cosine = grams * left_scale[:, None] * right_scale[None, :]
    same = (left_clust[:, None] == right_clust[None, :]).astype(F32)
    return jax.nn.sigmoid(8.0 * cosine - 2.0) * same


def by_group(embeddings, group_of, cluster_id):
    rows_here, width = embeddings.shape
    groups = lax.axis_size("sub") * lax.axis_size("pair")
    capacity = 2 * rows_here // groups
    slots = groups * capacity
    target = group_of[:, 0]
    onehot = (target[:, None] == jnp.arange(groups, dtype=jnp.int32)[None, :]).astype(jnp.int32)
    position = jnp.sum((jnp.cumsum(onehot, axis=0) - onehot) * onehot, axis=1)
    send_rows = jnp.zeros((groups, capacity, width), BF16).at[target, position].set(embeddings)
    send_clust = jnp.full((groups, capacity), -1, jnp.int32).at[target, position].set(cluster_id)
    recv_rows, recv_clust = (
        lax.all_to_all(send_rows, ("sub", "pair"), split_axis=0, concat_axis=0, tiled=True),
        lax.all_to_all(send_clust, ("sub", "pair"), split_axis=0, concat_axis=0, tiled=True),
    )
    own_rows = recv_rows.reshape(slots, width)
    own_clust = recv_clust.reshape(slots)
    own_scale = unit_scale(own_rows)
    piece_rows = lax.all_gather(own_rows, "blk", axis=0, tiled=True)
    piece_clust = lax.all_gather(own_clust, "blk", axis=0, tiled=True)
    weight = tile_weights(
        own_rows, own_clust, own_scale, piece_rows, piece_clust, unit_scale(piece_rows)
    )
    numer = jnp.dot(weight.astype(BF16), piece_rows, preferred_element_type=F32)
    denom = jnp.sum(weight, axis=1)
    result = (numer / denom[:, None]).astype(BF16).reshape(groups, capacity, width)
    returned = lax.all_to_all(result, ("sub", "pair"), split_axis=0, concat_axis=0, tiled=True)
    return returned[target, position]


def diagonal(size):
    shape = (size, size)
    return lax.broadcasted_iota(jnp.int32, shape, 0) == lax.broadcasted_iota(jnp.int32, shape, 1)


def to_column(row):
    size = row.shape[1]
    return jnp.sum(jnp.where(diagonal(size), row, jnp.zeros_like(row)), axis=1, keepdims=True)


def to_row(column):
    size = column.shape[0]
    return jnp.sum(jnp.where(diagonal(size), column, jnp.zeros_like(column)), axis=0, keepdims=True)


def scale_column(rows):
    wide = rows.astype(F32)
    return lax.rsqrt(jnp.sum(wide * wide, axis=1, keepdims=True) + 1e-06)


def first_rows(rows_here):
    return rows_here * 7 // 192 * 16


def first_pack_kernel(rows, first):
    cut = first_rows(rows.shape[0])
    for slab in range(rows.shape[1] // 128):
        first[slab * cut : (slab + 1) * cut, :] = rows[:cut, slab * 128 : (slab + 1) * 128]


def pack_kernel(rows, group, cluster, whole, second):
    rows_here, width = rows.shape
    slabs = width // 128
    cut = first_rows(rows_here)
    rest = rows_here - cut
    for slab in range(slabs):
        columns = rows[:, slab * 128 : (slab + 1) * 128]
        whole[slab * rows_here : (slab + 1) * rows_here, :] = columns
        second[slab * rest : (slab + 1) * rest, :] = columns[cut:]
    line_at = lax.broadcasted_iota(jnp.int32, (8, 128), 0)
    named = jnp.zeros((8, 128), jnp.int32)
    for line in range(4):
        top = line % 2 * 128
        part = (group, cluster)[line // 2][:, top : top + 128]
        gap = 128 - part.shape[1]
        if gap:
            part = jnp.concatenate([part, jnp.zeros((1, gap), jnp.int32)], axis=1)
        named = jnp.where(line_at == line, part, named)
    named = named.astype(F32).astype(BF16)
    whole[slabs * rows_here :, :] = named
    second[slabs * rest :, :] = named


def from_slabs(ref, count):
    slabs = [ref[top : top + count, :] for top in range(0, ref.shape[0] // count * count, count)]
    return jnp.concatenate(slabs, axis=1)


def key_row(ref, rows_here):
    wide = ref[ref.shape[0] - 8 :, :].astype(F32)
    kinds = [jnp.concatenate([wide[at : at + 1], wide[at + 1 : at + 2]], axis=1) for at in (0, 2)]
    return (kinds[0] * 256.0 + kinds[1])[:, :rows_here]


def from_pieces(first, second, rows_here):
    cut = first_rows(rows_here)
    pieces = [from_slabs(first, cut), from_slabs(second, rows_here - cut)]
    rows = jnp.concatenate(pieces, axis=0)
    return rows, key_row(second, rows_here)


def add_blocks(left, info, blocks, numer, denom):
    key = info[: left.shape[0], 0:1]
    scale = info[: left.shape[0], 1:2]
    right_rows = jnp.concatenate([block[0] for block in blocks], axis=0)
    right_key = jnp.concatenate([block[1] for block in blocks], axis=1)
    right_scale = jnp.concatenate([block[2] for block in blocks], axis=1)
    grams = lax.dot_general(
        left, right_rows, (((1,), (1,)), ((), ())), preferred_element_type=F32
    )
    half = jnp.tanh(grams * scale * right_scale - 1.0)
    weight = jnp.where(key == right_key, 0.5 + 0.5 * half, 0.0)
    add = jnp.dot(weight.astype(BF16), right_rows, preferred_element_type=F32)
    add_denom = jnp.sum(weight, axis=1, keepdims=True)
    if numer is None:
        return add, add_denom
    return numer + add, denom + add_denom


def left_rows(refs, rows_here):
    return jnp.concatenate([from_slabs(ref, rows_here) for ref in refs], axis=0)


def take_blocks(refs, count, rows_here):
    blocks = []
    for _ in range(count):
        rows, key = from_pieces(refs.pop(0), refs.pop(0), rows_here)
        blocks.append((rows, key, to_row(scale_column(rows))))
    return blocks


def store_sides(numer, denom, outs):
    rows_here, wide = outs[0].shape
    for side, out in enumerate(outs):
        top = side * rows_here
        out[:, : wide - 128] = numer[top : top + rows_here]
        out[:, wide - 128 :] = jnp.broadcast_to(denom[top : top + rows_here], (rows_here, 128))


def start_kernel(n_blocks, own, other, *refs):
    refs = list(refs)
    rows_here = refs[-1].shape[0] // 2
    left = left_rows((own, other), rows_here)
    key = jnp.concatenate([to_column(key_row(ref, rows_here)) for ref in (own, other)], axis=0)
    scale = scale_column(left)
    info = refs.pop()
    lane = lax.broadcasted_iota(jnp.int32, info.shape, 1)
    info[...] = jnp.where(lane == 0, key, 4.0 * scale)
    first = (left[:rows_here], key_row(own, rows_here), to_row(scale[:rows_here]))
    blocks = [first] + take_blocks(refs, n_blocks, rows_here)
    store_sides(*add_blocks(left, info, blocks, None, None), refs)


def both_kernel(n_blocks, own, other, info, *refs):
    refs = list(refs)
    rows_here = refs[2 * n_blocks].shape[0]
    blocks = take_blocks(refs, n_blocks, rows_here)
    mine_in, theirs_in, mine, *theirs = refs
    wide = mine.shape[1]
    width = wide - 128
    left = left_rows((own, other), rows_here)
    numer = jnp.concatenate([ref[:, :width] for ref in (mine_in, theirs_in)], axis=0)
    denom = jnp.concatenate([ref[:, width : width + 1] for ref in (mine_in, theirs_in)], axis=0)
    numer, denom = add_blocks(left, info, blocks, numer, denom)
    store_sides(numer[:rows_here], denom[:rows_here], [mine])
    denom = denom[rows_here:]
    high = denom.astype(BF16).astype(F32)
    lane = lax.broadcasted_iota(jnp.int32, (rows_here, 128), 1)
    pair = jnp.where(lane == 0, high, denom - high).astype(BF16)
    count = rows_here // len(theirs)
    for part, out in enumerate(theirs):
        top = part * count
        out[:, :width] = numer[rows_here + top : rows_here + top + count].astype(BF16)
        out[:, width:] = pair[top : top + count]


def last_kernel(own, info, first, second, first_other, second_other, mine, *refs):
    out = refs[-1]
    rows_here, width = out.shape
    theirs = jnp.concatenate([ref[...] for ref in refs[:-1]], axis=0)
    blocks = take_blocks([first, second, first_other, second_other], 2, rows_here)
    parts = theirs[:, width:].astype(F32)
    numer = mine[:, :width] + theirs[:, :width].astype(F32)
    denom = mine[:, width : width + 1] + (parts[:, 0:1] + parts[:, 1:2])
    numer, denom = add_blocks(left_rows((own,), rows_here), info, blocks, numer, denom)
    out[...] = (numer * (1.0 / denom)).astype(BF16)


def whole_in_vmem(count):
    return [pl.BlockSpec(memory_space=pltpu.VMEM)] * count


def call(kernel, shapes, args, aliases={}, products=0):
    return pl.pallas_call(
        kernel,
        out_shape=[jax.ShapeDtypeStruct(shape, dtype) for shape, dtype in shapes],
        in_specs=whole_in_vmem(len(args)),
        out_specs=whole_in_vmem(len(shapes)),
        input_output_aliases=aliases,
        compiler_params=pltpu.CompilerParams(vmem_limit_bytes=VMEM_BYTES),
        cost_estimate=pl.CostEstimate(
            flops=3 * products, transcendentals=0, bytes_accessed=0
        ),
    )(*args)


def start_both(left, right, shape):
    rows_here = shape[0]
    args = list(left) + [piece for block in right for piece in block]
    shapes = [(shape, F32), (shape, F32), ((2 * rows_here, 128), F32)]
    products = 4 * rows_here * (len(right) + 1) * rows_here * (shape[1] - 128)
    return call(
        functools.partial(start_kernel, len(right)), shapes, args, products=products
    )


def add_both(left, right, before):
    args = list(left) + [piece for block in right for piece in block] + list(before)
    rows_here, wide = before[0].shape
    shapes = [((rows_here, wide), F32)] + [((rows_here // PARTS, wide), BF16)] * PARTS
    kernel = functools.partial(both_kernel, len(right))
    products = 4 * rows_here * len(right) * rows_here * (wide - 128)
    return call(kernel, shapes, args, {len(args) - 2: 0}, products)


def folded_ring(size):
    return list(range(0, size, 2)) + list(range(1, size, 2))[::-1]


def together(*arrays):
    return lax.optimization_barrier(arrays)


def by_block(embeddings, group_of, cluster_id):
    rows_here, width = embeddings.shape
    cut = first_rows(rows_here)
    slabs = width // 128
    n_blk = lax.axis_size("blk")
    order = folded_ring(n_blk)
    line = (1, rows_here)

    def along(rows):
        hops = [
            (2 * order[i - 1] + core, 2 * order[i] + 1 - core)
            for i in range(n_blk)
            for core in range(2)
        ]
        return lax.ppermute(rows, ("blk", "pair"), hops)

    def across(rows):
        return lax.ppermute(rows, ("sub", "pair"), [(0, 3), (1, 2), (2, 1), (3, 0)])

    def other_core(rows):
        return lax.ppermute(rows, "pair", [(0, 1), (1, 0)])

    (first,) = call(first_pack_kernel, [((slabs * cut, 128), BF16)], [embeddings])
    whole, second = call(
        pack_kernel,
        [
            ((slabs * rows_here + 8, 128), BF16),
            ((slabs * (rows_here - cut) + 8, 128), BF16),
        ],
        [embeddings, group_of.reshape(line), cluster_id.reshape(line)],
    )
    along_by = [(first, second)]
    across_by = []
    for s in range(1, n_blk):
        moved = [along(piece) for piece in along_by[-1]]
        swapped = [across(piece) for piece in along_by[-1]]
        moved[0], swapped[0] = together(moved[0], swapped[0])
        moved[1], swapped[1], _ = together(moved[1], swapped[1], moved[0])
        along_by.append(tuple(moved))
        across_by.append(tuple(swapped))
    left = (whole, other_core(whole))
    early = across_by[:-1] + along_by[1:-2]
    mine, theirs, info = start_both(left, early, (rows_here, width + 128))
    left = (*left, info)
    near_first, _, mine, theirs = together(across_by[-1][0], along_by[-1][0], mine, theirs)
    far_second, _ = together(along_by[-1][1], near_first)
    last_first, last_second = along(near_first), across(far_second)
    late = [along_by[-2], across_by[-1], along_by[-1]]
    mine, *theirs = add_both(left, late, (mine, theirs))
    back = [other_core(part) for part in theirs[:-1]]
    last_first, theirs[-1] = together(last_first, theirs[-1])
    last_second, *back = together(last_second, *back, other_core(theirs[-1]))
    last = (last_first, last_second)
    (out,) = call(
        last_kernel,
        [((rows_here, width), BF16)],
        [whole, info, *last, *[other_core(piece) for piece in last], mine, *back],
        products=4 * rows_here * rows_here * width,
    )
    return out


def per_device(embeddings, group_of, cluster_id):
    rows_here, width = embeddings.shape
    devices = lax.axis_size("blk") * lax.axis_size("sub") * lax.axis_size("pair")
    small = devices * rows_here * width * 2 <= GATHER_LIMIT
    fits = width % 128 == 0 and rows_here % (32 * PARTS) == 0 and rows_here <= 256
    if small and fits and lax.axis_size("sub") == 2 and lax.axis_size("pair") == 2:
        return by_block(embeddings, group_of, cluster_id)
    return by_group(embeddings, group_of, cluster_id)


def solution(mesh):
    return jax.shard_map(
        per_device,
        mesh=mesh,
        in_specs=(
            P(("island", "blk", "sub", "pair"), None),
            P(("island", "blk", "sub", "pair"), None),
            P(("island", "blk", "sub", "pair")),
        ),
        out_specs=P(("island", "blk", "sub", "pair"), None),
        check_vma=False,
    )
```

```python
import functools

import jax
import jax.numpy as jnp
from jax import lax
from jax.experimental import pallas as pl
from jax.experimental.pallas import tpu as pltpu
from jax.sharding import PartitionSpec as P

F32 = jnp.float32
BF16 = jnp.bfloat16
VMEM_BYTES = 24 * 1024 * 1024
PARTS = 3
GATHER_LIMIT = 8 * 1024 * 1024


def unit_scale(rows_in):
    wide = rows_in.astype(F32)
    return lax.rsqrt(jnp.sum(wide * wide, axis=1) + 1e-06)


def tile_weights(left_rows, left_clust, left_scale, right_rows, right_clust, right_scale):
    grams = lax.dot_general(
        left_rows, right_rows, (((1,), (1,)), ((), ())), preferred_element_type=F32
    )
    cosine = grams * left_scale[:, None] * right_scale[None, :]
    same = (left_clust[:, None] == right_clust[None, :]).astype(F32)
    return jax.nn.sigmoid(8.0 * cosine - 2.0) * same


def by_group(embeddings, group_of, cluster_id):
    rows_here, width = embeddings.shape
    groups = lax.axis_size("sub") * lax.axis_size("pair")
    capacity = 2 * rows_here // groups
    slots = groups * capacity
    target = group_of[:, 0]
    onehot = (target[:, None] == jnp.arange(groups, dtype=jnp.int32)[None, :]).astype(jnp.int32)
    position = jnp.sum((jnp.cumsum(onehot, axis=0) - onehot) * onehot, axis=1)
    send_rows = jnp.zeros((groups, capacity, width), BF16).at[target, position].set(embeddings)
    send_clust = jnp.full((groups, capacity), -1, jnp.int32).at[target, position].set(cluster_id)
    recv_rows, recv_clust = (
        lax.all_to_all(send_rows, ("sub", "pair"), split_axis=0, concat_axis=0, tiled=True),
        lax.all_to_all(send_clust, ("sub", "pair"), split_axis=0, concat_axis=0, tiled=True),
    )
    own_rows = recv_rows.reshape(slots, width)
    own_clust = recv_clust.reshape(slots)
    own_scale = unit_scale(own_rows)
    piece_rows = lax.all_gather(own_rows, "blk", axis=0, tiled=True)
    piece_clust = lax.all_gather(own_clust, "blk", axis=0, tiled=True)
    weight = tile_weights(
        own_rows, own_clust, own_scale, piece_rows, piece_clust, unit_scale(piece_rows)
    )
    numer = jnp.dot(weight.astype(BF16), piece_rows, preferred_element_type=F32)
    denom = jnp.sum(weight, axis=1)
    result = (numer / denom[:, None]).astype(BF16).reshape(groups, capacity, width)
    returned = lax.all_to_all(result, ("sub", "pair"), split_axis=0, concat_axis=0, tiled=True)
    return returned[target, position]


def diagonal(size):
    shape = (size, size)
    return lax.broadcasted_iota(jnp.int32, shape, 0) == lax.broadcasted_iota(jnp.int32, shape, 1)


def to_column(row):
    size = row.shape[1]
    return jnp.sum(jnp.where(diagonal(size), row, jnp.zeros_like(row)), axis=1, keepdims=True)


def to_row(column):
    size = column.shape[0]
    return jnp.sum(jnp.where(diagonal(size), column, jnp.zeros_like(column)), axis=0, keepdims=True)


def scale_column(rows):
    wide = rows.astype(F32)
    return lax.rsqrt(jnp.sum(wide * wide, axis=1, keepdims=True) + 1e-06)


def first_pack_kernel(rows, first):
    width = rows.shape[1]
    slabs = width // 128
    half = rows.shape[0] // 2
    for slab in range(slabs):
        first[slab * half : (slab + 1) * half, :] = rows[:half, slab * 128 : (slab + 1) * 128]
    first[slabs * half :, :] = jnp.zeros((8, 128), BF16)


def pack_kernel(rows, group, cluster, whole, second):
    rows_here, width = rows.shape
    slabs = width // 128
    half = rows_here // 2
    for slab in range(slabs):
        columns = rows[:, slab * 128 : (slab + 1) * 128]
        whole[slab * rows_here : (slab + 1) * rows_here, :] = columns
        second[slab * half : (slab + 1) * half, :] = columns[half:]
    line_at = lax.broadcasted_iota(jnp.int32, (8, 128), 0)
    named = jnp.zeros((8, 128), jnp.int32)
    for line in range(4):
        top = line % 2 * half
        part = (group, cluster)[line // 2][:, top : top + half]
        if half < 128:
            part = jnp.concatenate([part, jnp.zeros((1, 128 - half), jnp.int32)], axis=1)
        named = jnp.where(line_at == line, part, named)
    named = named.astype(F32).astype(BF16)
    whole[slabs * rows_here :, :] = named
    second[slabs * half :, :] = named


def from_slabs(ref, count):
    slabs = [ref[top : top + count, :] for top in range(0, ref.shape[0] // count * count, count)]
    return jnp.concatenate(slabs, axis=1)


def key_rows(ref, half):
    wide = ref[ref.shape[0] - 8 :, :].astype(F32)
    return [wide[side : side + 1, :half] * 256.0 + wide[side + 2 : side + 3, :half] for side in range(2)]


def key_row(ref, rows_here):
    return jnp.concatenate(key_rows(ref, rows_here // 2), axis=1)


def from_halves(first, second, rows_here):
    half = rows_here // 2
    rows = jnp.concatenate([from_slabs(first, half), from_slabs(second, half)], axis=0)
    return rows, key_row(second, rows_here)


def add_blocks(left, info, blocks, numer, denom):
    key = info[: left.shape[0], 0:1]
    scale = info[: left.shape[0], 1:2]
    right_rows = jnp.concatenate([block[0] for block in blocks], axis=0)
    right_key = jnp.concatenate([block[1] for block in blocks], axis=1)
    right_scale = jnp.concatenate([block[2] for block in blocks], axis=1)
    grams = lax.dot_general(
        left, right_rows, (((1,), (1,)), ((), ())), preferred_element_type=F32
    )
    half = jnp.tanh(grams * scale * right_scale - 1.0)
    weight = jnp.where(key == right_key, 0.5 + 0.5 * half, 0.0)
    add = jnp.dot(weight.astype(BF16), right_rows, preferred_element_type=F32)
    add_denom = jnp.sum(weight, axis=1, keepdims=True)
    if numer is None:
        return add, add_denom
    return numer + add, denom + add_denom


def left_rows(refs, rows_here):
    return jnp.concatenate([from_slabs(ref, rows_here) for ref in refs], axis=0)


def take_blocks(refs, count, rows_here):
    blocks = []
    for _ in range(count):
        rows, key = from_halves(refs.pop(0), refs.pop(0), rows_here)
        blocks.append((rows, key, to_row(scale_column(rows))))
    return blocks


def store_sides(numer, denom, outs):
    rows_here, wide = outs[0].shape
    for side, out in enumerate(outs):
        top = side * rows_here
        out[:, : wide - 128] = numer[top : top + rows_here]
        out[:, wide - 128 :] = jnp.broadcast_to(denom[top : top + rows_here], (rows_here, 128))


def start_kernel(n_blocks, own, other, *refs):
    refs = list(refs)
    rows_here = refs[-1].shape[0] // 2
    left = left_rows((own, other), rows_here)
    key = jnp.concatenate([to_column(key_row(ref, rows_here)) for ref in (own, other)], axis=0)
    scale = scale_column(left)
    info = refs.pop()
    lane = lax.broadcasted_iota(jnp.int32, info.shape, 1)
    info[...] = jnp.where(lane == 0, key, 4.0 * scale)
    first = (left[:rows_here], key_row(own, rows_here), to_row(scale[:rows_here]))
    blocks = [first] + take_blocks(refs, n_blocks, rows_here)
    store_sides(*add_blocks(left, info, blocks, None, None), refs)


def both_kernel(n_blocks, own, other, info, *refs):
    refs = list(refs)
    rows_here = refs[2 * n_blocks].shape[0]
    blocks = take_blocks(refs, n_blocks, rows_here)
    mine_in, theirs_in, mine, *theirs = refs
    wide = mine.shape[1]
    width = wide - 128
    left = left_rows((own, other), rows_here)
    numer = jnp.concatenate([ref[:, :width] for ref in (mine_in, theirs_in)], axis=0)
    denom = jnp.concatenate([ref[:, width : width + 1] for ref in (mine_in, theirs_in)], axis=0)
    numer, denom = add_blocks(left, info, blocks, numer, denom)
    store_sides(numer[:rows_here], denom[:rows_here], [mine])
    denom = denom[rows_here:]
    high = denom.astype(BF16).astype(F32)
    lane = lax.broadcasted_iota(jnp.int32, (rows_here, 128), 1)
    pair = jnp.where(lane == 0, high, denom - high).astype(BF16)
    count = rows_here // len(theirs)
    for part, out in enumerate(theirs):
        top = part * count
        out[:, :width] = numer[rows_here + top : rows_here + top + count].astype(BF16)
        out[:, width:] = pair[top : top + count]


def last_kernel(own, info, first, second, first_other, second_other, mine, *refs):
    out = refs[-1]
    rows_here, width = out.shape
    theirs = jnp.concatenate([ref[...] for ref in refs[:-1]], axis=0)
    blocks = take_blocks([first, second, first_other, second_other], 2, rows_here)
    parts = theirs[:, width:].astype(F32)
    numer = mine[:, :width] + theirs[:, :width].astype(F32)
    denom = mine[:, width : width + 1] + (parts[:, 0:1] + parts[:, 1:2])
    numer, denom = add_blocks(left_rows((own,), rows_here), info, blocks, numer, denom)
    out[...] = (numer * (1.0 / denom)).astype(BF16)


def whole_in_vmem(count):
    return [pl.BlockSpec(memory_space=pltpu.VMEM)] * count


def call(kernel, shapes, args, aliases={}):
    return pl.pallas_call(
        kernel,
        out_shape=[jax.ShapeDtypeStruct(shape, dtype) for shape, dtype in shapes],
        in_specs=whole_in_vmem(len(args)),
        out_specs=whole_in_vmem(len(shapes)),
        input_output_aliases=aliases,
        compiler_params=pltpu.CompilerParams(vmem_limit_bytes=VMEM_BYTES),
    )(*args)


def start_both(left, right, shape):
    rows_here = shape[0]
    args = list(left) + [half for block in right for half in block]
    shapes = [(shape, F32), (shape, F32), ((2 * rows_here, 128), F32)]
    return call(functools.partial(start_kernel, len(right)), shapes, args)


def add_both(left, right, before):
    args = list(left) + [half for block in right for half in block] + list(before)
    rows_here, wide = before[0].shape
    shapes = [((rows_here, wide), F32)] + [((rows_here // PARTS, wide), BF16)] * PARTS
    kernel = functools.partial(both_kernel, len(right))
    return call(kernel, shapes, args, {len(args) - 2: 0})


def folded_ring(size):
    return list(range(0, size, 2)) + list(range(1, size, 2))[::-1]


def together(*arrays):
    return lax.optimization_barrier(arrays)


def by_block(embeddings, group_of, cluster_id):
    rows_here, width = embeddings.shape
    half = rows_here // 2
    slabs = width // 128
    n_blk = lax.axis_size("blk")
    order = folded_ring(n_blk)
    line = (1, rows_here)

    def along(rows):
        hops = [
            (2 * order[i - 1] + core, 2 * order[i] + 1 - core)
            for i in range(n_blk)
            for core in range(2)
        ]
        return lax.ppermute(rows, ("blk", "pair"), hops)

    def across(rows):
        return lax.ppermute(rows, ("sub", "pair"), [(0, 3), (1, 2), (2, 1), (3, 0)])

    def other_core(rows):
        return lax.ppermute(rows, "pair", [(0, 1), (1, 0)])

    half_shape = ((slabs * half + 8, 128), BF16)
    (first,) = call(first_pack_kernel, [half_shape], [embeddings])
    whole, second = call(
        pack_kernel,
        [((slabs * rows_here + 8, 128), BF16), half_shape],
        [embeddings, group_of.reshape(line), cluster_id.reshape(line)],
    )
    along_by = [(first, second)]
    across_by = []
    for s in range(1, n_blk):
        moved = [along(piece) for piece in along_by[-1]]
        swapped = [across(piece) for piece in along_by[-1]]
        moved[0], swapped[0] = together(moved[0], swapped[0])
        if s < n_blk - 1:
            moved[1], swapped[1], _ = together(moved[1], swapped[1], moved[0])
        along_by.append(tuple(moved))
        across_by.append(tuple(swapped))
    left = (whole, other_core(whole))
    early = across_by[:-1] + along_by[1:-2]
    mine, theirs, info = start_both(left, early, (rows_here, width + 128))
    left = (*left, info)
    far_first, _, mine, theirs = together(along_by[-1][0], across_by[-1][0], mine, theirs)
    near_second, _ = together(across_by[-1][1], far_first)
    last_first, last_second = across(far_first), along(near_second)
    late = [along_by[-2], across_by[-1], along_by[-1]]
    mine, *theirs = add_both(left, late, (mine, theirs))
    back = [other_core(part) for part in theirs[:-1]]
    last_first, theirs[-1] = together(last_first, theirs[-1])
    last_second, *back = together(last_second, *back, other_core(theirs[-1]))
    last = (last_first, last_second)
    (out,) = call(
        last_kernel,
        [((rows_here, width), BF16)],
        [whole, info, *last, *[other_core(half) for half in last], mine, *back],
    )
    return out


def per_device(embeddings, group_of, cluster_id):
    rows_here, width = embeddings.shape
    devices = lax.axis_size("blk") * lax.axis_size("sub") * lax.axis_size("pair")
    small = devices * rows_here * width * 2 <= GATHER_LIMIT
    fits = width % 128 == 0 and rows_here % (32 * PARTS) == 0 and rows_here <= 256
    if small and fits and lax.axis_size("sub") == 2 and lax.axis_size("pair") == 2:
        return by_block(embeddings, group_of, cluster_id)
    return by_group(embeddings, group_of, cluster_id)


def solution(mesh):
    return jax.shard_map(
        per_device,
        mesh=mesh,
        in_specs=(
            P(("island", "blk", "sub", "pair"), None),
            P(("island", "blk", "sub", "pair"), None),
            P(("island", "blk", "sub", "pair")),
        ),
        out_specs=P(("island", "blk", "sub", "pair"), None),
        check_vma=False,
    )
```

```python
import functools

import jax
import jax.numpy as jnp
from jax import lax
from jax.experimental import pallas as pl
from jax.experimental.pallas import tpu as pltpu
from jax.sharding import PartitionSpec as P

F32 = jnp.float32
BF16 = jnp.bfloat16
VMEM_BYTES = 24 * 1024 * 1024
PARTS = 3
GATHER_LIMIT = 8 * 1024 * 1024


def unit_scale(rows_in):
    wide = rows_in.astype(F32)
    return lax.rsqrt(jnp.sum(wide * wide, axis=1) + 1e-06)


def tile_weights(left_rows, left_clust, left_scale, right_rows, right_clust, right_scale):
    grams = lax.dot_general(
        left_rows, right_rows, (((1,), (1,)), ((), ())), preferred_element_type=F32
    )
    cosine = grams * left_scale[:, None] * right_scale[None, :]
    same = (left_clust[:, None] == right_clust[None, :]).astype(F32)
    return jax.nn.sigmoid(8.0 * cosine - 2.0) * same


def by_group(embeddings, group_of, cluster_id):
    rows_here, width = embeddings.shape
    groups = lax.axis_size("sub") * lax.axis_size("pair")
    capacity = 2 * rows_here // groups
    slots = groups * capacity
    target = group_of[:, 0]
    onehot = (target[:, None] == jnp.arange(groups, dtype=jnp.int32)[None, :]).astype(jnp.int32)
    position = jnp.sum((jnp.cumsum(onehot, axis=0) - onehot) * onehot, axis=1)
    send_rows = jnp.zeros((groups, capacity, width), BF16).at[target, position].set(embeddings)
    send_clust = jnp.full((groups, capacity), -1, jnp.int32).at[target, position].set(cluster_id)
    recv_rows, recv_clust = (
        lax.all_to_all(send_rows, ("sub", "pair"), split_axis=0, concat_axis=0, tiled=True),
        lax.all_to_all(send_clust, ("sub", "pair"), split_axis=0, concat_axis=0, tiled=True),
    )
    own_rows = recv_rows.reshape(slots, width)
    own_clust = recv_clust.reshape(slots)
    own_scale = unit_scale(own_rows)
    piece_rows = lax.all_gather(own_rows, "blk", axis=0, tiled=True)
    piece_clust = lax.all_gather(own_clust, "blk", axis=0, tiled=True)
    weight = tile_weights(
        own_rows, own_clust, own_scale, piece_rows, piece_clust, unit_scale(piece_rows)
    )
    numer = jnp.dot(weight.astype(BF16), piece_rows, preferred_element_type=F32)
    denom = jnp.sum(weight, axis=1)
    result = (numer / denom[:, None]).astype(BF16).reshape(groups, capacity, width)
    returned = lax.all_to_all(result, ("sub", "pair"), split_axis=0, concat_axis=0, tiled=True)
    return returned[target, position]


def diagonal(size):
    shape = (size, size)
    return lax.broadcasted_iota(jnp.int32, shape, 0) == lax.broadcasted_iota(jnp.int32, shape, 1)


def to_column(row):
    size = row.shape[1]
    return jnp.sum(jnp.where(diagonal(size), row, jnp.zeros_like(row)), axis=1, keepdims=True)


def to_row(column):
    size = column.shape[0]
    return jnp.sum(jnp.where(diagonal(size), column, jnp.zeros_like(column)), axis=0, keepdims=True)


def scale_column(rows):
    wide = rows.astype(F32)
    return lax.rsqrt(jnp.sum(wide * wide, axis=1, keepdims=True) + 1e-06)


def first_pack_kernel(rows, first):
    width = rows.shape[1]
    slabs = width // 128
    half = rows.shape[0] // 2
    for slab in range(slabs):
        first[slab * half : (slab + 1) * half, :] = rows[:half, slab * 128 : (slab + 1) * 128]
    first[slabs * half :, :] = jnp.zeros((8, 128), BF16)


def pack_kernel(rows, group, cluster, whole, second):
    rows_here, width = rows.shape
    slabs = width // 128
    half = rows_here // 2
    for slab in range(slabs):
        columns = rows[:, slab * 128 : (slab + 1) * 128]
        whole[slab * rows_here : (slab + 1) * rows_here, :] = columns
        second[slab * half : (slab + 1) * half, :] = columns[half:]
    line_at = lax.broadcasted_iota(jnp.int32, (8, 128), 0)
    named = jnp.zeros((8, 128), jnp.int32)
    for line in range(4):
        top = line % 2 * half
        part = (group, cluster)[line // 2][:, top : top + half]
        if half < 128:
            part = jnp.concatenate([part, jnp.zeros((1, 128 - half), jnp.int32)], axis=1)
        named = jnp.where(line_at == line, part, named)
    named = named.astype(F32).astype(BF16)
    whole[slabs * rows_here :, :] = named
    second[slabs * half :, :] = named


def from_slabs(ref, count):
    slabs = [ref[top : top + count, :] for top in range(0, ref.shape[0] // count * count, count)]
    return jnp.concatenate(slabs, axis=1)


def key_row(ref, rows_here, line=0):
    half = rows_here // 2
    wide = ref[ref.shape[0] - 8 :, :].astype(F32)[line : line + 4, :half]
    return jnp.concatenate([wide[0:1] * 256.0 + wide[2:3], wide[1:2] * 256.0 + wide[3:4]], axis=1)


def add_names_kernel(piece, whole, out):
    top = piece.shape[0] - 8
    out[:top, :] = piece[:top, :]
    lines = piece[top:, :].astype(F32)
    own = whole[whole.shape[0] - 8 :, :].astype(F32)
    out[top:, :] = jnp.concatenate([lines[:4], own[:4]], axis=0).astype(BF16)


def from_halves(first, second, rows_here):
    half = rows_here // 2
    rows = jnp.concatenate([from_slabs(first, half), from_slabs(second, half)], axis=0)
    return rows, key_row(second, rows_here)


def add_blocks(left, info, blocks, numer, denom):
    key = info[: left.shape[0], 0:1]
    scale = info[: left.shape[0], 1:2]
    right_rows = jnp.concatenate([block[0] for block in blocks], axis=0)
    right_key = jnp.concatenate([block[1] for block in blocks], axis=1)
    right_scale = jnp.concatenate([block[2] for block in blocks], axis=1)
    grams = lax.dot_general(
        left, right_rows, (((1,), (1,)), ((), ())), preferred_element_type=F32
    )
    half = jnp.tanh(grams * scale * right_scale - 1.0)
    weight = jnp.where(key == right_key, 0.5 + 0.5 * half, 0.0)
    add = jnp.dot(weight.astype(BF16), right_rows, preferred_element_type=F32)
    add_denom = jnp.sum(weight, axis=1, keepdims=True)
    if numer is None:
        return add, add_denom
    return numer + add, denom + add_denom


def left_rows(refs, rows_here):
    return jnp.concatenate([from_slabs(ref, rows_here) for ref in refs], axis=0)


def take_blocks(refs, count, rows_here):
    blocks = []
    for _ in range(count):
        rows, key = from_halves(refs.pop(0), refs.pop(0), rows_here)
        blocks.append((rows, key, to_row(scale_column(rows))))
    return blocks


def store_sides(numer, denom, outs):
    rows_here, wide = outs[0].shape
    for side, out in enumerate(outs):
        top = side * rows_here
        out[:, : wide - 128] = numer[top : top + rows_here]
        out[:, wide - 128 :] = jnp.broadcast_to(denom[top : top + rows_here], (rows_here, 128))


def start_kernel(n_blocks, own, other, crossed, *refs):
    refs = list(refs)
    rows_here = refs[-1].shape[0] // 2
    raw = crossed[...]
    crossed = (raw, key_row(refs[1], rows_here, 4), to_row(scale_column(raw)))
    left = left_rows((own, other), rows_here)
    key = jnp.concatenate([to_column(key_row(ref, rows_here)) for ref in (own, other)], axis=0)
    scale = scale_column(left)
    info = refs.pop()
    lane = lax.broadcasted_iota(jnp.int32, info.shape, 1)
    info[...] = jnp.where(lane == 0, key, 4.0 * scale)
    first = (left[:rows_here], key_row(own, rows_here), to_row(scale[:rows_here]))
    blocks = [first, crossed] + take_blocks(refs, n_blocks, rows_here)
    store_sides(*add_blocks(left, info, blocks, None, None), refs)


def both_kernel(n_blocks, own, other, info, *refs):
    refs = list(refs)
    rows_here = refs[2 * n_blocks].shape[0]
    blocks = take_blocks(refs, n_blocks, rows_here)
    mine_in, theirs_in, mine, *theirs = refs
    wide = mine.shape[1]
    width = wide - 128
    left = left_rows((own, other), rows_here)
    numer = jnp.concatenate([ref[:, :width] for ref in (mine_in, theirs_in)], axis=0)
    denom = jnp.concatenate([ref[:, width : width + 1] for ref in (mine_in, theirs_in)], axis=0)
    numer, denom = add_blocks(left, info, blocks, numer, denom)
    store_sides(numer[:rows_here], denom[:rows_here], [mine])
    denom = denom[rows_here:]
    high = denom.astype(BF16).astype(F32)
    lane = lax.broadcasted_iota(jnp.int32, (rows_here, 128), 1)
    pair = jnp.where(lane == 0, high, denom - high).astype(BF16)
    count = rows_here // len(theirs)
    for part, out in enumerate(theirs):
        top = part * count
        out[:, :width] = numer[rows_here + top : rows_here + top + count].astype(BF16)
        out[:, width:] = pair[top : top + count]


def last_kernel(own, info, first, second, first_other, second_other, mine, *refs):
    out = refs[-1]
    rows_here, width = out.shape
    theirs = jnp.concatenate([ref[...] for ref in refs[:-1]], axis=0)
    blocks = take_blocks([first, second, first_other, second_other], 2, rows_here)
    parts = theirs[:, width:].astype(F32)
    numer = mine[:, :width] + theirs[:, :width].astype(F32)
    denom = mine[:, width : width + 1] + (parts[:, 0:1] + parts[:, 1:2])
    numer, denom = add_blocks(left_rows((own,), rows_here), info, blocks, numer, denom)
    out[...] = (numer * (1.0 / denom)).astype(BF16)


def whole_in_vmem(count):
    return [pl.BlockSpec(memory_space=pltpu.VMEM)] * count


def call(kernel, shapes, args, aliases={}):
    return pl.pallas_call(
        kernel,
        out_shape=[jax.ShapeDtypeStruct(shape, dtype) for shape, dtype in shapes],
        in_specs=whole_in_vmem(len(args)),
        out_specs=whole_in_vmem(len(shapes)),
        input_output_aliases=aliases,
        compiler_params=pltpu.CompilerParams(vmem_limit_bytes=VMEM_BYTES),
    )(*args)


def start_both(left, crossed, right, shape):
    rows_here = shape[0]
    args = [*left, crossed] + [half for block in right for half in block]
    shapes = [(shape, F32), (shape, F32), ((2 * rows_here, 128), F32)]
    return call(functools.partial(start_kernel, len(right)), shapes, args)


def add_both(left, right, before):
    args = list(left) + [half for block in right for half in block] + list(before)
    rows_here, wide = before[0].shape
    shapes = [((rows_here, wide), F32)] + [((rows_here // PARTS, wide), BF16)] * PARTS
    kernel = functools.partial(both_kernel, len(right))
    return call(kernel, shapes, args, {len(args) - 2: 0})


def folded_ring(size):
    return list(range(0, size, 2)) + list(range(1, size, 2))[::-1]


def together(*arrays):
    return lax.optimization_barrier(arrays)


def by_block(embeddings, group_of, cluster_id):
    rows_here, width = embeddings.shape
    half = rows_here // 2
    slabs = width // 128
    n_blk = lax.axis_size("blk")
    order = folded_ring(n_blk)
    line = (1, rows_here)

    def along(rows):
        hops = [
            (2 * order[i - 1] + core, 2 * order[i] + 1 - core)
            for i in range(n_blk)
            for core in range(2)
        ]
        return lax.ppermute(rows, ("blk", "pair"), hops)

    def across(rows):
        return lax.ppermute(rows, ("sub", "pair"), [(0, 3), (1, 2), (2, 1), (3, 0)])

    def other_core(rows):
        return lax.ppermute(rows, "pair", [(0, 1), (1, 0)])

    half_shape = ((slabs * half + 8, 128), BF16)
    (first,) = call(first_pack_kernel, [half_shape], [embeddings])
    whole, second = call(
        pack_kernel,
        [((slabs * rows_here + 8, 128), BF16), half_shape],
        [embeddings, group_of.reshape(line), cluster_id.reshape(line)],
    )
    crossed = across(embeddings)
    moved = [along(first), along(second)]
    moved[1], crossed, _ = together(moved[1], crossed, moved[0])
    (named,) = call(add_names_kernel, [half_shape], [moved[1], whole])
    along_by = [(first, second), (moved[0], named)]
    across_by = [crossed]
    for s in range(2, n_blk):
        moved = [along(piece) for piece in along_by[-1]]
        swapped = [across(piece) for piece in along_by[-1]]
        moved[0], swapped[0] = together(moved[0], swapped[0])
        if s < n_blk - 1:
            moved[1], swapped[1], _ = together(moved[1], swapped[1], moved[0])
        along_by.append(tuple(moved))
        across_by.append(tuple(swapped))
    left = (whole, other_core(whole))
    early = across_by[1:-1] + along_by[1:-2]
    mine, theirs, info = start_both(left, crossed, early, (rows_here, width + 128))
    left = (*left, info)
    far_first, _, mine, theirs = together(along_by[-1][0], across_by[-1][0], mine, theirs)
    near_second, _ = together(across_by[-1][1], far_first)
    last_first, last_second = across(far_first), along(near_second)
    late = [along_by[-2], across_by[-1], along_by[-1]]
    mine, *theirs = add_both(left, late, (mine, theirs))
    back = [other_core(part) for part in theirs[:-1]]
    last_first, theirs[-1] = together(last_first, theirs[-1])
    last_second, *back = together(last_second, *back, other_core(theirs[-1]))
    last = (last_first, last_second)
    (out,) = call(
        last_kernel,
        [((rows_here, width), BF16)],
        [whole, info, *last, *[other_core(half) for half in last], mine, *back],
    )
    return out


def per_device(embeddings, group_of, cluster_id):
    rows_here, width = embeddings.shape
    devices = lax.axis_size("blk") * lax.axis_size("sub") * lax.axis_size("pair")
    small = devices * rows_here * width * 2 <= GATHER_LIMIT and lax.axis_size("blk") > 3
    fits = width % 128 == 0 and rows_here % (32 * PARTS) == 0 and rows_here <= 256
    if small and fits and lax.axis_size("sub") == 2 and lax.axis_size("pair") == 2:
        return by_block(embeddings, group_of, cluster_id)
    return by_group(embeddings, group_of, cluster_id)


def solution(mesh):
    return jax.shard_map(
        per_device,
        mesh=mesh,
        in_specs=(
            P(("island", "blk", "sub", "pair"), None),
            P(("island", "blk", "sub", "pair"), None),
            P(("island", "blk", "sub", "pair")),
        ),
        out_specs=P(("island", "blk", "sub", "pair"), None),
        check_vma=False,
    )
```

```python
import functools

import jax
import jax.numpy as jnp
from jax import lax
from jax.experimental import pallas as pl
from jax.experimental.pallas import tpu as pltpu
from jax.sharding import PartitionSpec as P

F32 = jnp.float32
BF16 = jnp.bfloat16
VMEM_BYTES = 24 * 1024 * 1024
PARTS = 3
GATHER_LIMIT = 8 * 1024 * 1024


def unit_scale(rows_in):
    wide = rows_in.astype(F32)
    return lax.rsqrt(jnp.sum(wide * wide, axis=1) + 1e-06)


def tile_weights(left_rows, left_clust, left_scale, right_rows, right_clust, right_scale):
    grams = lax.dot_general(
        left_rows, right_rows, (((1,), (1,)), ((), ())), preferred_element_type=F32
    )
    cosine = grams * left_scale[:, None] * right_scale[None, :]
    same = (left_clust[:, None] == right_clust[None, :]).astype(F32)
    return jax.nn.sigmoid(8.0 * cosine - 2.0) * same


def by_group(embeddings, group_of, cluster_id):
    rows_here, width = embeddings.shape
    groups = lax.axis_size("sub") * lax.axis_size("pair")
    capacity = 2 * rows_here // groups
    slots = groups * capacity
    target = group_of[:, 0]
    onehot = (target[:, None] == jnp.arange(groups, dtype=jnp.int32)[None, :]).astype(jnp.int32)
    position = jnp.sum((jnp.cumsum(onehot, axis=0) - onehot) * onehot, axis=1)
    send_rows = jnp.zeros((groups, capacity, width), BF16).at[target, position].set(embeddings)
    send_clust = jnp.full((groups, capacity), -1, jnp.int32).at[target, position].set(cluster_id)
    recv_rows, recv_clust = (
        lax.all_to_all(send_rows, ("sub", "pair"), split_axis=0, concat_axis=0, tiled=True),
        lax.all_to_all(send_clust, ("sub", "pair"), split_axis=0, concat_axis=0, tiled=True),
    )
    own_rows = recv_rows.reshape(slots, width)
    own_clust = recv_clust.reshape(slots)
    own_scale = unit_scale(own_rows)
    piece_rows = lax.all_gather(own_rows, "blk", axis=0, tiled=True)
    piece_clust = lax.all_gather(own_clust, "blk", axis=0, tiled=True)
    weight = tile_weights(
        own_rows, own_clust, own_scale, piece_rows, piece_clust, unit_scale(piece_rows)
    )
    numer = jnp.dot(weight.astype(BF16), piece_rows, preferred_element_type=F32)
    denom = jnp.sum(weight, axis=1)
    result = (numer / denom[:, None]).astype(BF16).reshape(groups, capacity, width)
    returned = lax.all_to_all(result, ("sub", "pair"), split_axis=0, concat_axis=0, tiled=True)
    return returned[target, position]


def diagonal(size):
    shape = (size, size)
    return lax.broadcasted_iota(jnp.int32, shape, 0) == lax.broadcasted_iota(jnp.int32, shape, 1)


def to_column(row):
    size = row.shape[1]
    return jnp.sum(jnp.where(diagonal(size), row, jnp.zeros_like(row)), axis=1, keepdims=True)


def to_row(column):
    size = column.shape[0]
    return jnp.sum(jnp.where(diagonal(size), column, jnp.zeros_like(column)), axis=0, keepdims=True)


def scale_column(rows):
    wide = rows.astype(F32)
    return lax.rsqrt(jnp.sum(wide * wide, axis=1, keepdims=True) + 1e-06)


def first_pack_kernel(rows, first):
    width = rows.shape[1]
    slabs = width // 128
    half = rows.shape[0] // 2
    for slab in range(slabs):
        first[slab * half : (slab + 1) * half, :] = rows[:half, slab * 128 : (slab + 1) * 128]
    first[slabs * half :, :] = jnp.zeros((8, 128), BF16)


def pack_kernel(rows, group, cluster, whole, second):
    rows_here, width = rows.shape
    slabs = width // 128
    half = rows_here // 2
    for slab in range(slabs):
        columns = rows[:, slab * 128 : (slab + 1) * 128]
        whole[slab * rows_here : (slab + 1) * rows_here, :] = columns
        second[slab * half : (slab + 1) * half, :] = columns[half:]
    line_at = lax.broadcasted_iota(jnp.int32, (8, 128), 0)
    named = jnp.zeros((8, 128), jnp.int32)
    for line in range(4):
        top = line % 2 * half
        part = (group, cluster)[line // 2][:, top : top + half]
        if half < 128:
            part = jnp.concatenate([part, jnp.zeros((1, 128 - half), jnp.int32)], axis=1)
        named = jnp.where(line_at == line, part, named)
    named = named.astype(F32).astype(BF16)
    whole[slabs * rows_here :, :] = named
    second[slabs * half :, :] = named


def from_slabs(ref, count):
    slabs = [ref[top : top + count, :] for top in range(0, ref.shape[0] // count * count, count)]
    return jnp.concatenate(slabs, axis=1)


def key_rows(ref, half):
    wide = ref[ref.shape[0] - 8 :, :].astype(F32)
    return [wide[side : side + 1, :half] * 256.0 + wide[side + 2 : side + 3, :half] for side in range(2)]


def key_row(ref, rows_here):
    return jnp.concatenate(key_rows(ref, rows_here // 2), axis=1)


def from_halves(first, second, rows_here):
    half = rows_here // 2
    rows = jnp.concatenate([from_slabs(first, half), from_slabs(second, half)], axis=0)
    return rows, key_row(second, rows_here)


def add_blocks(left, info, blocks, numer, denom):
    key = info[: left.shape[0], 0:1]
    scale = info[: left.shape[0], 1:2]
    right_rows = jnp.concatenate([block[0] for block in blocks], axis=0)
    right_key = jnp.concatenate([block[1] for block in blocks], axis=1)
    right_scale = jnp.concatenate([block[2] for block in blocks], axis=1)
    grams = lax.dot_general(
        left, right_rows, (((1,), (1,)), ((), ())), preferred_element_type=F32
    )
    half = jnp.tanh(grams * scale * right_scale - 1.0)
    weight = jnp.where(key == right_key, 0.5 + 0.5 * half, 0.0)
    add = jnp.dot(weight.astype(BF16), right_rows, preferred_element_type=F32)
    add_denom = jnp.sum(weight, axis=1, keepdims=True)
    if numer is None:
        return add, add_denom
    return numer + add, denom + add_denom


def left_rows(refs, rows_here):
    return jnp.concatenate([from_slabs(ref, rows_here) for ref in refs], axis=0)


def take_blocks(refs, count, rows_here):
    blocks = []
    for _ in range(count):
        rows, key = from_halves(refs.pop(0), refs.pop(0), rows_here)
        blocks.append((rows, key, to_row(scale_column(rows))))
    return blocks


def store_sides(numer, denom, outs):
    rows_here, wide = outs[0].shape
    for side, out in enumerate(outs):
        top = side * rows_here
        out[:, : wide - 128] = numer[top : top + rows_here]
        out[:, wide - 128 :] = jnp.broadcast_to(denom[top : top + rows_here], (rows_here, 128))


def start_kernel(n_blocks, own, other, *refs):
    refs = list(refs)
    rows_here = refs[-1].shape[0] // 2
    left = left_rows((own, other), rows_here)
    key = jnp.concatenate([to_column(key_row(ref, rows_here)) for ref in (own, other)], axis=0)
    scale = scale_column(left)
    info = refs.pop()
    lane = lax.broadcasted_iota(jnp.int32, info.shape, 1)
    info[...] = jnp.where(lane == 0, key, 4.0 * scale)
    first = (left[:rows_here], key_row(own, rows_here), to_row(scale[:rows_here]))
    blocks = [first] + take_blocks(refs, n_blocks, rows_here)
    store_sides(*add_blocks(left, info, blocks, None, None), refs)


def both_kernel(n_blocks, own, other, info, *refs):
    refs = list(refs)
    rows_here = refs[2 * n_blocks].shape[0]
    blocks = take_blocks(refs, n_blocks, rows_here)
    mine_in, theirs_in, mine, *theirs = refs
    wide = mine.shape[1]
    width = wide - 128
    left = left_rows((own, other), rows_here)
    numer = jnp.concatenate([ref[:, :width] for ref in (mine_in, theirs_in)], axis=0)
    denom = jnp.concatenate([ref[:, width : width + 1] for ref in (mine_in, theirs_in)], axis=0)
    numer, denom = add_blocks(left, info, blocks, numer, denom)
    store_sides(numer[:rows_here], denom[:rows_here], [mine])
    denom = denom[rows_here:]
    high = denom.astype(BF16).astype(F32)
    lane = lax.broadcasted_iota(jnp.int32, (rows_here, 128), 1)
    pair = jnp.where(lane == 0, high, denom - high).astype(BF16)
    count = rows_here // len(theirs)
    for part, out in enumerate(theirs):
        top = part * count
        out[:, :width] = numer[rows_here + top : rows_here + top + count].astype(BF16)
        out[:, width:] = pair[top : top + count]


def last_kernel(own, info, first, second, first_other, second_other, mine, *refs):
    out = refs[-1]
    rows_here, width = out.shape
    theirs = jnp.concatenate([ref[...] for ref in refs[:-1]], axis=0)
    blocks = take_blocks([first, second, first_other, second_other], 2, rows_here)
    parts = theirs[:, width:].astype(F32)
    numer = mine[:, :width] + theirs[:, :width].astype(F32)
    denom = mine[:, width : width + 1] + (parts[:, 0:1] + parts[:, 1:2])
    numer, denom = add_blocks(left_rows((own,), rows_here), info, blocks, numer, denom)
    out[...] = (numer * (1.0 / denom)).astype(BF16)


def whole_in_vmem(count):
    return [pl.BlockSpec(memory_space=pltpu.VMEM)] * count


def call(kernel, shapes, args, aliases={}):
    return pl.pallas_call(
        kernel,
        out_shape=[jax.ShapeDtypeStruct(shape, dtype) for shape, dtype in shapes],
        in_specs=whole_in_vmem(len(args)),
        out_specs=whole_in_vmem(len(shapes)),
        input_output_aliases=aliases,
        compiler_params=pltpu.CompilerParams(vmem_limit_bytes=VMEM_BYTES),
    )(*args)


def start_both(left, right, shape):
    rows_here = shape[0]
    args = list(left) + [half for block in right for half in block]
    shapes = [(shape, F32), (shape, F32), ((2 * rows_here, 128), F32)]
    return call(functools.partial(start_kernel, len(right)), shapes, args)


def add_both(left, right, before):
    args = list(left) + [half for block in right for half in block] + list(before)
    rows_here, wide = before[0].shape
    shapes = [((rows_here, wide), F32)] + [((rows_here // PARTS, wide), BF16)] * PARTS
    kernel = functools.partial(both_kernel, len(right))
    return call(kernel, shapes, args, {len(args) - 2: 0})


def folded_ring(size):
    return list(range(0, size, 2)) + list(range(1, size, 2))[::-1]


def together(*arrays):
    return lax.optimization_barrier(arrays)


def by_block(embeddings, group_of, cluster_id):
    rows_here, width = embeddings.shape
    half = rows_here // 2
    slabs = width // 128
    n_blk = lax.axis_size("blk")
    order = folded_ring(n_blk)
    line = (1, rows_here)

    def along(rows):
        hops = [
            (2 * order[i - 1] + core, 2 * order[i] + 1 - core)
            for i in range(n_blk)
            for core in range(2)
        ]
        return lax.ppermute(rows, ("blk", "pair"), hops)

    def across(rows):
        return lax.ppermute(rows, ("sub", "pair"), [(0, 3), (1, 2), (2, 1), (3, 0)])

    def other_core(rows):
        return lax.ppermute(rows, "pair", [(0, 1), (1, 0)])

    half_shape = ((slabs * half + 8, 128), BF16)
    (first,) = call(first_pack_kernel, [half_shape], [embeddings])
    whole, second = call(
        pack_kernel,
        [((slabs * rows_here + 8, 128), BF16), half_shape],
        [embeddings, group_of.reshape(line), cluster_id.reshape(line)],
    )
    along_by = [(first, second)]
    across_by = []
    for s in range(1, n_blk):
        moved = [along(piece) for piece in along_by[-1]]
        swapped = [across(piece) for piece in (along_by[-1] if s > 1 else together(first, second))]
        moved[0], swapped[0] = together(moved[0], swapped[0])
        if s < n_blk - 1:
            moved[1], swapped[1], _ = together(moved[1], swapped[1], moved[0])
        along_by.append(tuple(moved))
        across_by.append(tuple(swapped))
    left = (whole, other_core(whole))
    early = across_by[:-1] + along_by[1:-2]
    mine, theirs, info = start_both(left, early, (rows_here, width + 128))
    left = (*left, info)
    far_first, _, mine, theirs = together(along_by[-1][0], across_by[-1][0], mine, theirs)
    near_second, _ = together(across_by[-1][1], far_first)
    last_first, last_second = across(far_first), along(near_second)
    late = [along_by[-2], across_by[-1], along_by[-1]]
    mine, *theirs = add_both(left, late, (mine, theirs))
    back = [other_core(part) for part in theirs[:-1]]
    last_first, theirs[-1] = together(last_first, theirs[-1])
    last_second, *back = together(last_second, *back, other_core(theirs[-1]))
    last = (last_first, last_second)
    (out,) = call(
        last_kernel,
        [((rows_here, width), BF16)],
        [whole, info, *last, *[other_core(half) for half in last], mine, *back],
    )
    return out


def per_device(embeddings, group_of, cluster_id):
    rows_here, width = embeddings.shape
    devices = lax.axis_size("blk") * lax.axis_size("sub") * lax.axis_size("pair")
    small = devices * rows_here * width * 2 <= GATHER_LIMIT
    fits = width % 128 == 0 and rows_here % (32 * PARTS) == 0 and rows_here <= 256
    if small and fits and lax.axis_size("sub") == 2 and lax.axis_size("pair") == 2:
        return by_block(embeddings, group_of, cluster_id)
    return by_group(embeddings, group_of, cluster_id)


def solution(mesh):
    return jax.shard_map(
        per_device,
        mesh=mesh,
        in_specs=(
            P(("island", "blk", "sub", "pair"), None),
            P(("island", "blk", "sub", "pair"), None),
            P(("island", "blk", "sub", "pair")),
        ),
        out_specs=P(("island", "blk", "sub", "pair"), None),
        check_vma=False,
    )
```

```python
import functools

import jax
import jax.numpy as jnp
from jax import lax
from jax.experimental import pallas as pl
from jax.experimental.pallas import tpu as pltpu
from jax.sharding import PartitionSpec as P

F32 = jnp.float32
BF16 = jnp.bfloat16
VMEM_BYTES = 24 * 1024 * 1024
PARTS = 3
GATHER_LIMIT = 8 * 1024 * 1024


def unit_scale(rows_in):
    wide = rows_in.astype(F32)
    return lax.rsqrt(jnp.sum(wide * wide, axis=1) + 1e-06)


def tile_weights(left_rows, left_clust, left_scale, right_rows, right_clust, right_scale):
    grams = lax.dot_general(
        left_rows, right_rows, (((1,), (1,)), ((), ())), preferred_element_type=F32
    )
    cosine = grams * left_scale[:, None] * right_scale[None, :]
    same = (left_clust[:, None] == right_clust[None, :]).astype(F32)
    return jax.nn.sigmoid(8.0 * cosine - 2.0) * same


def by_group(embeddings, group_of, cluster_id):
    rows_here, width = embeddings.shape
    groups = lax.axis_size("sub") * lax.axis_size("pair")
    capacity = 2 * rows_here // groups
    slots = groups * capacity
    target = group_of[:, 0]
    onehot = (target[:, None] == jnp.arange(groups, dtype=jnp.int32)[None, :]).astype(jnp.int32)
    position = jnp.sum((jnp.cumsum(onehot, axis=0) - onehot) * onehot, axis=1)
    send_rows = jnp.zeros((groups, capacity, width), BF16).at[target, position].set(embeddings)
    send_clust = jnp.full((groups, capacity), -1, jnp.int32).at[target, position].set(cluster_id)
    recv_rows, recv_clust = (
        lax.all_to_all(send_rows, ("sub", "pair"), split_axis=0, concat_axis=0, tiled=True),
        lax.all_to_all(send_clust, ("sub", "pair"), split_axis=0, concat_axis=0, tiled=True),
    )
    own_rows = recv_rows.reshape(slots, width)
    own_clust = recv_clust.reshape(slots)
    own_scale = unit_scale(own_rows)
    piece_rows = lax.all_gather(own_rows, "blk", axis=0, tiled=True)
    piece_clust = lax.all_gather(own_clust, "blk", axis=0, tiled=True)
    weight = tile_weights(
        own_rows, own_clust, own_scale, piece_rows, piece_clust, unit_scale(piece_rows)
    )
    numer = jnp.dot(weight.astype(BF16), piece_rows, preferred_element_type=F32)
    denom = jnp.sum(weight, axis=1)
    result = (numer / denom[:, None]).astype(BF16).reshape(groups, capacity, width)
    returned = lax.all_to_all(result, ("sub", "pair"), split_axis=0, concat_axis=0, tiled=True)
    return returned[target, position]


def diagonal(size):
    shape = (size, size)
    return lax.broadcasted_iota(jnp.int32, shape, 0) == lax.broadcasted_iota(jnp.int32, shape, 1)


def to_column(row):
    size = row.shape[1]
    return jnp.sum(jnp.where(diagonal(size), row, jnp.zeros_like(row)), axis=1, keepdims=True)


def to_row(column):
    size = column.shape[0]
    return jnp.sum(jnp.where(diagonal(size), column, jnp.zeros_like(column)), axis=0, keepdims=True)


def scale_column(rows):
    wide = rows.astype(F32)
    return lax.rsqrt(jnp.sum(wide * wide, axis=1, keepdims=True) + 1e-06)


def first_pack_kernel(rows, first):
    width = rows.shape[1]
    slabs = width // 128
    half = rows.shape[0] // 2
    for slab in range(slabs):
        first[slab * half : (slab + 1) * half, :] = rows[:half, slab * 128 : (slab + 1) * 128]
    first[slabs * half :, :] = jnp.zeros((8, 128), BF16)


def pack_kernel(rows, group, cluster, whole, second):
    rows_here, width = rows.shape
    slabs = width // 128
    half = rows_here // 2
    for slab in range(slabs):
        columns = rows[:, slab * 128 : (slab + 1) * 128]
        whole[slab * rows_here : (slab + 1) * rows_here, :] = columns
        second[slab * half : (slab + 1) * half, :] = columns[half:]
    line_at = lax.broadcasted_iota(jnp.int32, (8, 128), 0)
    named = jnp.zeros((8, 128), jnp.int32)
    for line in range(4):
        top = line % 2 * half
        part = (group, cluster)[line // 2][:, top : top + half]
        if half < 128:
            part = jnp.concatenate([part, jnp.zeros((1, 128 - half), jnp.int32)], axis=1)
        named = jnp.where(line_at == line, part, named)
    named = named.astype(F32).astype(BF16)
    whole[slabs * rows_here :, :] = named
    second[slabs * half :, :] = named


def from_slabs(ref, count):
    slabs = [ref[top : top + count, :] for top in range(0, ref.shape[0] // count * count, count)]
    return jnp.concatenate(slabs, axis=1)


def key_rows(ref, half):
    wide = ref[ref.shape[0] - 8 :, :].astype(F32)
    return [wide[side : side + 1, :half] * 256.0 + wide[side + 2 : side + 3, :half] for side in range(2)]


def key_row(ref, rows_here):
    return jnp.concatenate(key_rows(ref, rows_here // 2), axis=1)


def from_halves(first, second, rows_here):
    half = rows_here // 2
    rows = jnp.concatenate([from_slabs(first, half), from_slabs(second, half)], axis=0)
    return rows, key_row(second, rows_here)


def add_blocks(left, info, blocks, numer, denom):
    key = info[: left.shape[0], 0:1]
    scale = info[: left.shape[0], 1:2]
    right_rows = jnp.concatenate([block[0] for block in blocks], axis=0)
    right_key = jnp.concatenate([block[1] for block in blocks], axis=1)
    right_scale = jnp.concatenate([block[2] for block in blocks], axis=1)
    grams = lax.dot_general(
        left, right_rows, (((1,), (1,)), ((), ())), preferred_element_type=F32
    )
    half = jnp.tanh(grams * scale * right_scale - 1.0)
    weight = jnp.where(key == right_key, 0.5 + 0.5 * half, 0.0)
    add = jnp.dot(weight.astype(BF16), right_rows, preferred_element_type=F32)
    add_denom = jnp.sum(weight, axis=1, keepdims=True)
    if numer is None:
        return add, add_denom
    return numer + add, denom + add_denom


def left_rows(refs, rows_here):
    return jnp.concatenate([from_slabs(ref, rows_here) for ref in refs], axis=0)


def take_blocks(refs, count, rows_here):
    blocks = []
    for _ in range(count):
        rows, key = from_halves(refs.pop(0), refs.pop(0), rows_here)
        blocks.append((rows, key, to_row(scale_column(rows))))
    return blocks


def store_sides(numer, denom, outs):
    rows_here, wide = outs[0].shape
    for side, out in enumerate(outs):
        top = side * rows_here
        out[:, : wide - 128] = numer[top : top + rows_here]
        out[:, wide - 128 :] = jnp.broadcast_to(denom[top : top + rows_here], (rows_here, 128))


def start_kernel(n_blocks, own, other, *refs):
    refs = list(refs)
    rows_here = refs[-1].shape[0] // 2
    left = left_rows((own, other), rows_here)
    key = jnp.concatenate([to_column(key_row(ref, rows_here)) for ref in (own, other)], axis=0)
    scale = scale_column(left)
    info = refs.pop()
    lane = lax.broadcasted_iota(jnp.int32, info.shape, 1)
    info[...] = jnp.where(lane == 0, key, 4.0 * scale)
    first = (left[:rows_here], key_row(own, rows_here), to_row(scale[:rows_here]))
    blocks = [first] + take_blocks(refs, n_blocks, rows_here)
    store_sides(*add_blocks(left, info, blocks, None, None), refs)


def both_kernel(n_blocks, own, other, info, *refs):
    refs = list(refs)
    rows_here = refs[2 * n_blocks].shape[0]
    blocks = take_blocks(refs, n_blocks, rows_here)
    mine_in, theirs_in, mine, *theirs = refs
    wide = mine.shape[1]
    width = wide - 128
    left = left_rows((own, other), rows_here)
    numer = jnp.concatenate([ref[:, :width] for ref in (mine_in, theirs_in)], axis=0)
    denom = jnp.concatenate([ref[:, width : width + 1] for ref in (mine_in, theirs_in)], axis=0)
    numer, denom = add_blocks(left, info, blocks, numer, denom)
    store_sides(numer[:rows_here], denom[:rows_here], [mine])
    denom = denom[rows_here:]
    high = denom.astype(BF16).astype(F32)
    lane = lax.broadcasted_iota(jnp.int32, (rows_here, 128), 1)
    pair = jnp.where(lane == 0, high, denom - high).astype(BF16)
    count = rows_here // len(theirs)
    for part, out in enumerate(theirs):
        top = part * count
        out[:, :width] = numer[rows_here + top : rows_here + top + count].astype(BF16)
        out[:, width:] = pair[top : top + count]


def join_kernel(own, info, first, second, mine, *refs):
    *parts, out = refs
    rows_here, wide = out.shape
    width = wide - 128
    theirs = jnp.concatenate([ref[...] for ref in parts], axis=0)
    pair = theirs[:, width:].astype(F32)
    numer = mine[:, :width] + theirs[:, :width].astype(F32)
    denom = mine[:, width : width + 1] + (pair[:, 0:1] + pair[:, 1:2])
    blocks = take_blocks([first, second], 1, rows_here)
    left = left_rows((own,), rows_here)
    store_sides(*add_blocks(left, info, blocks, numer, denom), [out])


def last_kernel(own, info, first, second, total, out, staged, sems):
    rows_here, width = out.shape
    blocks = take_blocks([first, second], 1, rows_here)
    left = left_rows((own,), rows_here)
    numer, denom = total[:, :width], total[:, width : width + 1]
    numer, denom = add_blocks(left, info, blocks, numer, denom)
    share = 1.0 / denom
    count = rows_here // 4
    copies = []
    for part in range(4):
        rows = slice(part * count, (part + 1) * count)
        staged[rows, :] = (numer[rows] * share[rows]).astype(BF16)
        copies.append(pltpu.make_async_copy(staged.at[rows, :], out.at[rows, :], sems.at[part]))
        copies[-1].start()
    for copy in copies:
        copy.wait()


def whole_in_vmem(count):
    return [pl.BlockSpec(memory_space=pltpu.VMEM)] * count


def call(kernel, shapes, args, aliases={}):
    return pl.pallas_call(
        kernel,
        out_shape=[jax.ShapeDtypeStruct(shape, dtype) for shape, dtype in shapes],
        in_specs=whole_in_vmem(len(args)),
        out_specs=whole_in_vmem(len(shapes)),
        input_output_aliases=aliases,
        compiler_params=pltpu.CompilerParams(vmem_limit_bytes=VMEM_BYTES),
    )(*args)


def start_both(left, right, shape):
    rows_here = shape[0]
    args = list(left) + [half for block in right for half in block]
    shapes = [(shape, F32), (shape, F32), ((2 * rows_here, 128), F32)]
    return call(functools.partial(start_kernel, len(right)), shapes, args)


def add_both(left, right, before):
    args = list(left) + [half for block in right for half in block] + list(before)
    rows_here, wide = before[0].shape
    shapes = [((rows_here, wide), F32)] + [((rows_here // PARTS, wide), BF16)] * PARTS
    kernel = functools.partial(both_kernel, len(right))
    return call(kernel, shapes, args, {len(args) - 2: 0})


def finish(shape, args):
    return pl.pallas_call(
        last_kernel,
        out_shape=jax.ShapeDtypeStruct(shape, BF16),
        in_specs=whole_in_vmem(len(args)),
        out_specs=pl.BlockSpec(memory_space=pl.ANY),
        scratch_shapes=[pltpu.VMEM(shape, BF16), pltpu.SemaphoreType.DMA((4,))],
        compiler_params=pltpu.CompilerParams(vmem_limit_bytes=VMEM_BYTES),
    )(*args)


def folded_ring(size):
    return list(range(0, size, 2)) + list(range(1, size, 2))[::-1]


def together(*arrays):
    return lax.optimization_barrier(arrays)


def by_block(embeddings, group_of, cluster_id):
    rows_here, width = embeddings.shape
    half = rows_here // 2
    slabs = width // 128
    n_blk = lax.axis_size("blk")
    order = folded_ring(n_blk)
    line = (1, rows_here)

    def along(rows):
        hops = [
            (2 * order[i - 1] + core, 2 * order[i] + 1 - core)
            for i in range(n_blk)
            for core in range(2)
        ]
        return lax.ppermute(rows, ("blk", "pair"), hops)

    def across(rows):
        return lax.ppermute(rows, ("sub", "pair"), [(0, 3), (1, 2), (2, 1), (3, 0)])

    def other_core(rows):
        return lax.ppermute(rows, "pair", [(0, 1), (1, 0)])

    half_shape = ((slabs * half + 8, 128), BF16)
    (first,) = call(first_pack_kernel, [half_shape], [embeddings])
    whole, second = call(
        pack_kernel,
        [((slabs * rows_here + 8, 128), BF16), half_shape],
        [embeddings, group_of.reshape(line), cluster_id.reshape(line)],
    )
    along_by = [(first, second)]
    across_by = []
    for s in range(1, n_blk):
        moved = [along(piece) for piece in along_by[-1]]
        swapped = [across(piece) for piece in along_by[-1]]
        moved[0], swapped[0] = together(moved[0], swapped[0])
        if s < n_blk - 1:
            moved[1], swapped[1], _ = together(moved[1], swapped[1], moved[0])
        along_by.append(tuple(moved))
        across_by.append(tuple(swapped))
    left = (whole, other_core(whole))
    early = across_by[:-1] + along_by[1:-2]
    mine, theirs, info = start_both(left, early, (rows_here, width + 128))
    left = (*left, info)
    far_first, _, mine, theirs = together(along_by[-1][0], across_by[-1][0], mine, theirs)
    near_second, _ = together(across_by[-1][1], far_first)
    last_first, last_second = across(far_first), along(near_second)
    late = [along_by[-2], across_by[-1], along_by[-1]]
    mine, *theirs = add_both(left, late, (mine, theirs))
    back = [other_core(part) for part in theirs[:-1]]
    last_first, theirs[-1] = together(last_first, theirs[-1])
    last_second, *back = together(last_second, *back, other_core(theirs[-1]))
    last = [other_core(last_first), other_core(last_second)]
    (total,) = call(
        join_kernel,
        [((rows_here, width + 128), F32)],
        [whole, info, last_first, last_second, mine, *back],
        {4: 0},
    )
    out = finish((rows_here, width), [whole, info, *last, total])
    return out


def per_device(embeddings, group_of, cluster_id):
    rows_here, width = embeddings.shape
    devices = lax.axis_size("blk") * lax.axis_size("sub") * lax.axis_size("pair")
    small = devices * rows_here * width * 2 <= GATHER_LIMIT
    fits = width % 128 == 0 and rows_here % (64 * PARTS) == 0 and rows_here <= 256
    if small and fits and lax.axis_size("sub") == 2 and lax.axis_size("pair") == 2:
        return by_block(embeddings, group_of, cluster_id)
    return by_group(embeddings, group_of, cluster_id)


def solution(mesh):
    return jax.shard_map(
        per_device,
        mesh=mesh,
        in_specs=(
            P(("island", "blk", "sub", "pair"), None),
            P(("island", "blk", "sub", "pair"), None),
            P(("island", "blk", "sub", "pair")),
        ),
        out_specs=P(("island", "blk", "sub", "pair"), None),
        check_vma=False,
    )
```

```python
import functools

import jax
import jax.numpy as jnp
from jax import lax
from jax.experimental import pallas as pl
from jax.experimental.pallas import tpu as pltpu
from jax.sharding import PartitionSpec as P

F32 = jnp.float32
BF16 = jnp.bfloat16
VMEM_BYTES = 24 * 1024 * 1024
PARTS = 3
GATHER_LIMIT = 8 * 1024 * 1024


def unit_scale(rows_in):
    wide = rows_in.astype(F32)
    return lax.rsqrt(jnp.sum(wide * wide, axis=1) + 1e-06)


def tile_weights(left_rows, left_clust, left_scale, right_rows, right_clust, right_scale):
    grams = lax.dot_general(
        left_rows, right_rows, (((1,), (1,)), ((), ())), preferred_element_type=F32
    )
    cosine = grams * left_scale[:, None] * right_scale[None, :]
    same = (left_clust[:, None] == right_clust[None, :]).astype(F32)
    return jax.nn.sigmoid(8.0 * cosine - 2.0) * same


def by_group(embeddings, group_of, cluster_id):
    rows_here, width = embeddings.shape
    groups = lax.axis_size("sub") * lax.axis_size("pair")
    capacity = 2 * rows_here // groups
    slots = groups * capacity
    target = group_of[:, 0]
    onehot = (target[:, None] == jnp.arange(groups, dtype=jnp.int32)[None, :]).astype(jnp.int32)
    position = jnp.sum((jnp.cumsum(onehot, axis=0) - onehot) * onehot, axis=1)
    send_rows = jnp.zeros((groups, capacity, width), BF16).at[target, position].set(embeddings)
    send_clust = jnp.full((groups, capacity), -1, jnp.int32).at[target, position].set(cluster_id)
    recv_rows, recv_clust = (
        lax.all_to_all(send_rows, ("sub", "pair"), split_axis=0, concat_axis=0, tiled=True),
        lax.all_to_all(send_clust, ("sub", "pair"), split_axis=0, concat_axis=0, tiled=True),
    )
    own_rows = recv_rows.reshape(slots, width)
    own_clust = recv_clust.reshape(slots)
    own_scale = unit_scale(own_rows)
    piece_rows = lax.all_gather(own_rows, "blk", axis=0, tiled=True)
    piece_clust = lax.all_gather(own_clust, "blk", axis=0, tiled=True)
    weight = tile_weights(
        own_rows, own_clust, own_scale, piece_rows, piece_clust, unit_scale(piece_rows)
    )
    numer = jnp.dot(weight.astype(BF16), piece_rows, preferred_element_type=F32)
    denom = jnp.sum(weight, axis=1)
    result = (numer / denom[:, None]).astype(BF16).reshape(groups, capacity, width)
    returned = lax.all_to_all(result, ("sub", "pair"), split_axis=0, concat_axis=0, tiled=True)
    return returned[target, position]


def diagonal(size):
    shape = (size, size)
    return lax.broadcasted_iota(jnp.int32, shape, 0) == lax.broadcasted_iota(jnp.int32, shape, 1)


def to_column(row):
    size = row.shape[1]
    return jnp.sum(jnp.where(diagonal(size), row, jnp.zeros_like(row)), axis=1, keepdims=True)


def to_row(column):
    size = column.shape[0]
    return jnp.sum(jnp.where(diagonal(size), column, jnp.zeros_like(column)), axis=0, keepdims=True)


def scale_column(rows):
    wide = rows.astype(F32)
    return lax.rsqrt(jnp.sum(wide * wide, axis=1, keepdims=True) + 1e-06)


def first_pack_kernel(rows, first):
    width = rows.shape[1]
    slabs = width // 128
    half = rows.shape[0] // 2
    for slab in range(slabs):
        first[slab * half : (slab + 1) * half, :] = rows[:half, slab * 128 : (slab + 1) * 128]
    first[slabs * half :, :] = jnp.zeros((8, 128), BF16)


def pack_kernel(rows, group, cluster, whole, second):
    rows_here, width = rows.shape
    slabs = width // 128
    half = rows_here // 2
    for slab in range(slabs):
        columns = rows[:, slab * 128 : (slab + 1) * 128]
        whole[slab * rows_here : (slab + 1) * rows_here, :] = columns
        second[slab * half : (slab + 1) * half, :] = columns[half:]
    line_at = lax.broadcasted_iota(jnp.int32, (8, 128), 0)
    named = jnp.zeros((8, 128), jnp.int32)
    for line in range(4):
        top = line % 2 * half
        part = (group, cluster)[line // 2][:, top : top + half]
        if half < 128:
            part = jnp.concatenate([part, jnp.zeros((1, 128 - half), jnp.int32)], axis=1)
        named = jnp.where(line_at == line, part, named)
    named = named.astype(F32).astype(BF16)
    whole[slabs * rows_here :, :] = named
    second[slabs * half :, :] = named


def from_slabs(ref, count):
    slabs = [ref[top : top + count, :] for top in range(0, ref.shape[0] // count * count, count)]
    return jnp.concatenate(slabs, axis=1)


def key_rows(ref, half):
    wide = ref[ref.shape[0] - 8 :, :].astype(F32)
    return [wide[side : side + 1, :half] * 256.0 + wide[side + 2 : side + 3, :half] for side in range(2)]


def key_row(ref, rows_here):
    return jnp.concatenate(key_rows(ref, rows_here // 2), axis=1)


def from_halves(first, second, rows_here):
    half = rows_here // 2
    rows = jnp.concatenate([from_slabs(first, half), from_slabs(second, half)], axis=0)
    return rows, key_row(second, rows_here)


def add_blocks(left, info, blocks, numer, denom):
    key = info[: left.shape[0], 0:1]
    scale = info[: left.shape[0], 1:2]
    right_rows = jnp.concatenate([block[0] for block in blocks], axis=0)
    right_key = jnp.concatenate([block[1] for block in blocks], axis=1)
    right_scale = jnp.concatenate([block[2] for block in blocks], axis=1)
    grams = lax.dot_general(
        left, right_rows, (((1,), (1,)), ((), ())), preferred_element_type=F32
    )
    half = jnp.tanh(grams * scale * right_scale - 1.0)
    weight = jnp.where(key == right_key, 0.5 + 0.5 * half, 0.0)
    add = jnp.dot(weight.astype(BF16), right_rows, preferred_element_type=F32)
    add_denom = jnp.sum(weight, axis=1, keepdims=True)
    if numer is None:
        return add, add_denom
    return numer + add, denom + add_denom


def left_rows(refs, rows_here):
    return jnp.concatenate([from_slabs(ref, rows_here) for ref in refs], axis=0)


def take_blocks(refs, count, rows_here):
    blocks = []
    for _ in range(count):
        rows, key = from_halves(refs.pop(0), refs.pop(0), rows_here)
        blocks.append((rows, key, to_row(scale_column(rows))))
    return blocks


def store_sides(numer, denom, outs):
    rows_here, wide = outs[0].shape
    for side, out in enumerate(outs):
        top = side * rows_here
        out[:, : wide - 128] = numer[top : top + rows_here]
        out[:, wide - 128 :] = jnp.broadcast_to(denom[top : top + rows_here], (rows_here, 128))


def start_kernel(n_blocks, own, other, *refs):
    refs = list(refs)
    rows_here = refs[-1].shape[0] // 2
    left = left_rows((own, other), rows_here)
    key = jnp.concatenate([to_column(key_row(ref, rows_here)) for ref in (own, other)], axis=0)
    scale = scale_column(left)
    info = refs.pop()
    lane = lax.broadcasted_iota(jnp.int32, info.shape, 1)
    info[...] = jnp.where(lane == 0, key, 4.0 * scale)
    first = (left[:rows_here], key_row(own, rows_here), to_row(scale[:rows_here]))
    blocks = [first] + take_blocks(refs, n_blocks, rows_here)
    store_sides(*add_blocks(left, info, blocks, None, None), refs)


def both_kernel(n_blocks, own, other, info, *refs):
    refs = list(refs)
    rows_here = refs[2 * n_blocks].shape[0]
    blocks = take_blocks(refs, n_blocks, rows_here)
    mine_in, theirs_in, mine, *theirs = refs
    wide = mine.shape[1]
    width = wide - 128
    left = left_rows((own, other), rows_here)
    numer = jnp.concatenate([ref[:, :width] for ref in (mine_in, theirs_in)], axis=0)
    denom = jnp.concatenate([ref[:, width : width + 1] for ref in (mine_in, theirs_in)], axis=0)
    numer, denom = add_blocks(left, info, blocks, numer, denom)
    store_sides(numer[:rows_here], denom[:rows_here], [mine])
    denom = denom[rows_here:]
    high = denom.astype(BF16).astype(F32)
    lane = lax.broadcasted_iota(jnp.int32, (rows_here, 128), 1)
    pair = jnp.where(lane == 0, high, denom - high).astype(BF16)
    count = rows_here // len(theirs)
    for part, out in enumerate(theirs):
        top = part * count
        out[:, :width] = numer[rows_here + top : rows_here + top + count].astype(BF16)
        out[:, width:] = pair[top : top + count]


def join_kernel(own, info, first, second, mine, *refs):
    *parts, out = refs
    rows_here, wide = out.shape
    width = wide - 128
    theirs = jnp.concatenate([ref[...] for ref in parts], axis=0)
    pair = theirs[:, width:].astype(F32)
    numer = mine[:, :width] + theirs[:, :width].astype(F32)
    denom = mine[:, width : width + 1] + (pair[:, 0:1] + pair[:, 1:2])
    blocks = take_blocks([first, second], 1, rows_here)
    left = left_rows((own,), rows_here)
    store_sides(*add_blocks(left, info, blocks, numer, denom), [out])


def last_kernel(own, info, first, second, total, out, staged, sems):
    rows_here, width = out.shape
    blocks = take_blocks([first, second], 1, rows_here)
    left = left_rows((own,), rows_here)
    numer, denom = total[:, :width], total[:, width : width + 1]
    numer, denom = add_blocks(left, info, blocks, numer, denom)
    share = 1.0 / denom
    count = rows_here // 4
    copies = []
    for part in range(4):
        rows = slice(part * count, (part + 1) * count)
        staged[rows, :] = (numer[rows] * share[rows]).astype(BF16)
        copies.append(pltpu.make_async_copy(staged.at[rows, :], out.at[rows, :], sems.at[part]))
        copies[-1].start()
    for copy in copies:
        copy.wait()


def whole_in_vmem(count):
    return [pl.BlockSpec(memory_space=pltpu.VMEM)] * count


def call(kernel, shapes, args, aliases={}):
    return pl.pallas_call(
        kernel,
        out_shape=[jax.ShapeDtypeStruct(shape, dtype) for shape, dtype in shapes],
        in_specs=whole_in_vmem(len(args)),
        out_specs=whole_in_vmem(len(shapes)),
        input_output_aliases=aliases,
        compiler_params=pltpu.CompilerParams(vmem_limit_bytes=VMEM_BYTES),
    )(*args)


def start_both(left, right, shape):
    rows_here = shape[0]
    args = list(left) + [half for block in right for half in block]
    shapes = [(shape, F32), (shape, F32), ((2 * rows_here, 128), F32)]
    return call(functools.partial(start_kernel, len(right)), shapes, args)


def add_both(left, right, before):
    args = list(left) + [half for block in right for half in block] + list(before)
    rows_here, wide = before[0].shape
    shapes = [((rows_here, wide), F32)] + [((rows_here // PARTS, wide), BF16)] * PARTS
    kernel = functools.partial(both_kernel, len(right))
    return call(kernel, shapes, args, {len(args) - 2: 0})


def finish(shape, args):
    return pl.pallas_call(
        last_kernel,
        out_shape=jax.ShapeDtypeStruct(shape, BF16),
        in_specs=whole_in_vmem(len(args)),
        out_specs=pl.BlockSpec(memory_space=pl.ANY),
        scratch_shapes=[pltpu.VMEM(shape, BF16), pltpu.SemaphoreType.DMA((4,))],
        compiler_params=pltpu.CompilerParams(vmem_limit_bytes=VMEM_BYTES),
    )(*args)


def folded_ring(size):
    return list(range(0, size, 2)) + list(range(1, size, 2))[::-1]


def together(*arrays):
    return lax.optimization_barrier(arrays)


def by_block(embeddings, group_of, cluster_id):
    rows_here, width = embeddings.shape
    half = rows_here // 2
    slabs = width // 128
    n_blk = lax.axis_size("blk")
    order = folded_ring(n_blk)
    line = (1, rows_here)

    def along(rows):
        hops = [
            (2 * order[i - 1] + core, 2 * order[i] + 1 - core)
            for i in range(n_blk)
            for core in range(2)
        ]
        return lax.ppermute(rows, ("blk", "pair"), hops)

    def across(rows):
        return lax.ppermute(rows, ("sub", "pair"), [(0, 3), (1, 2), (2, 1), (3, 0)])

    def other_core(rows):
        return lax.ppermute(rows, "pair", [(0, 1), (1, 0)])

    half_shape = ((slabs * half + 8, 128), BF16)
    (first,) = call(first_pack_kernel, [half_shape], [embeddings])
    whole, second = call(
        pack_kernel,
        [((slabs * rows_here + 8, 128), BF16), half_shape],
        [embeddings, group_of.reshape(line), cluster_id.reshape(line)],
    )
    along_by = [(first, second)]
    across_by = []
    for s in range(1, n_blk):
        moved = [along(piece) for piece in along_by[-1]]
        if s == 1:
            swapped = [across(piece) for piece in together(first, second)]
            moved[1], *swapped, _ = together(moved[1], *swapped, moved[0])
        else:
            swapped = [across(piece) for piece in along_by[-1]]
            moved[0], swapped[0] = together(moved[0], swapped[0])
            if s < n_blk - 1:
                moved[1], swapped[1], _ = together(moved[1], swapped[1], moved[0])
        along_by.append(tuple(moved))
        across_by.append(tuple(swapped))
    left = (whole, other_core(whole))
    early = across_by[:-1] + along_by[1:-2]
    mine, theirs, info = start_both(left, early, (rows_here, width + 128))
    left = (*left, info)
    far_first, _, mine, theirs = together(along_by[-1][0], across_by[-1][0], mine, theirs)
    near_second, _ = together(across_by[-1][1], far_first)
    last_first, last_second = across(far_first), along(near_second)
    late = [along_by[-2], across_by[-1], along_by[-1]]
    mine, *theirs = add_both(left, late, (mine, theirs))
    back = [other_core(part) for part in theirs[:-1]]
    last_first, theirs[-1] = together(last_first, theirs[-1])
    last_second, *back = together(last_second, *back, other_core(theirs[-1]))
    last = [other_core(last_first), other_core(last_second)]
    (total,) = call(
        join_kernel,
        [((rows_here, width + 128), F32)],
        [whole, info, last_first, last_second, mine, *back],
        {4: 0},
    )
    out = finish((rows_here, width), [whole, info, *last, total])
    return out


def per_device(embeddings, group_of, cluster_id):
    rows_here, width = embeddings.shape
    devices = lax.axis_size("blk") * lax.axis_size("sub") * lax.axis_size("pair")
    small = devices * rows_here * width * 2 <= GATHER_LIMIT
    fits = width % 128 == 0 and rows_here % (64 * PARTS) == 0 and rows_here <= 256
    if small and fits and lax.axis_size("sub") == 2 and lax.axis_size("pair") == 2:
        return by_block(embeddings, group_of, cluster_id)
    return by_group(embeddings, group_of, cluster_id)


def solution(mesh):
    return jax.shard_map(
        per_device,
        mesh=mesh,
        in_specs=(
            P(("island", "blk", "sub", "pair"), None),
            P(("island", "blk", "sub", "pair"), None),
            P(("island", "blk", "sub", "pair")),
        ),
        out_specs=P(("island", "blk", "sub", "pair"), None),
        check_vma=False,
    )
```

```python
import functools

import jax
import jax.numpy as jnp
from jax import lax
from jax.experimental import pallas as pl
from jax.experimental.pallas import tpu as pltpu
from jax.sharding import PartitionSpec as P

F32 = jnp.float32
BF16 = jnp.bfloat16
VMEM_BYTES = 24 * 1024 * 1024
PARTS = 3
GATHER_LIMIT = 8 * 1024 * 1024


def unit_scale(rows_in):
    wide = rows_in.astype(F32)
    return lax.rsqrt(jnp.sum(wide * wide, axis=1) + 1e-06)


def tile_weights(left_rows, left_clust, left_scale, right_rows, right_clust, right_scale):
    grams = lax.dot_general(
        left_rows, right_rows, (((1,), (1,)), ((), ())), preferred_element_type=F32
    )
    cosine = grams * left_scale[:, None] * right_scale[None, :]
    same = (left_clust[:, None] == right_clust[None, :]).astype(F32)
    return jax.nn.sigmoid(8.0 * cosine - 2.0) * same


def by_group(embeddings, group_of, cluster_id):
    rows_here, width = embeddings.shape
    groups = lax.axis_size("sub") * lax.axis_size("pair")
    capacity = 2 * rows_here // groups
    slots = groups * capacity
    target = group_of[:, 0]
    onehot = (target[:, None] == jnp.arange(groups, dtype=jnp.int32)[None, :]).astype(jnp.int32)
    position = jnp.sum((jnp.cumsum(onehot, axis=0) - onehot) * onehot, axis=1)
    send_rows = jnp.zeros((groups, capacity, width), BF16).at[target, position].set(embeddings)
    send_clust = jnp.full((groups, capacity), -1, jnp.int32).at[target, position].set(cluster_id)
    recv_rows, recv_clust = (
        lax.all_to_all(send_rows, ("sub", "pair"), split_axis=0, concat_axis=0, tiled=True),
        lax.all_to_all(send_clust, ("sub", "pair"), split_axis=0, concat_axis=0, tiled=True),
    )
    own_rows = recv_rows.reshape(slots, width)
    own_clust = recv_clust.reshape(slots)
    own_scale = unit_scale(own_rows)
    piece_rows = lax.all_gather(own_rows, "blk", axis=0, tiled=True)
    piece_clust = lax.all_gather(own_clust, "blk", axis=0, tiled=True)
    weight = tile_weights(
        own_rows, own_clust, own_scale, piece_rows, piece_clust, unit_scale(piece_rows)
    )
    numer = jnp.dot(weight.astype(BF16), piece_rows, preferred_element_type=F32)
    denom = jnp.sum(weight, axis=1)
    result = (numer / denom[:, None]).astype(BF16).reshape(groups, capacity, width)
    returned = lax.all_to_all(result, ("sub", "pair"), split_axis=0, concat_axis=0, tiled=True)
    return returned[target, position]


def diagonal(size):
    shape = (size, size)
    return lax.broadcasted_iota(jnp.int32, shape, 0) == lax.broadcasted_iota(jnp.int32, shape, 1)


def to_column(row):
    size = row.shape[1]
    return jnp.sum(jnp.where(diagonal(size), row, jnp.zeros_like(row)), axis=1, keepdims=True)


def to_row(column):
    size = column.shape[0]
    return jnp.sum(jnp.where(diagonal(size), column, jnp.zeros_like(column)), axis=0, keepdims=True)


def scale_column(rows):
    wide = rows.astype(F32)
    return lax.rsqrt(jnp.sum(wide * wide, axis=1, keepdims=True) + 1e-06)


def first_rows(rows_here):
    return rows_here * 7 // 192 * 16


def first_pack_kernel(rows, first):
    cut = first_rows(rows.shape[0])
    for slab in range(rows.shape[1] // 128):
        first[slab * cut : (slab + 1) * cut, :] = rows[:cut, slab * 128 : (slab + 1) * 128]


def pack_kernel(rows, group, cluster, whole, second):
    rows_here, width = rows.shape
    slabs = width // 128
    cut = first_rows(rows_here)
    rest = rows_here - cut
    for slab in range(slabs):
        columns = rows[:, slab * 128 : (slab + 1) * 128]
        whole[slab * rows_here : (slab + 1) * rows_here, :] = columns
        second[slab * rest : (slab + 1) * rest, :] = columns[cut:]
    line_at = lax.broadcasted_iota(jnp.int32, (8, 128), 0)
    named = jnp.zeros((8, 128), jnp.int32)
    for line in range(4):
        top = line % 2 * 128
        part = (group, cluster)[line // 2][:, top : top + 128]
        gap = 128 - part.shape[1]
        if gap:
            part = jnp.concatenate([part, jnp.zeros((1, gap), jnp.int32)], axis=1)
        named = jnp.where(line_at == line, part, named)
    named = named.astype(F32).astype(BF16)
    whole[slabs * rows_here :, :] = named
    second[slabs * rest :, :] = named


def from_slabs(ref, count):
    slabs = [ref[top : top + count, :] for top in range(0, ref.shape[0] // count * count, count)]
    return jnp.concatenate(slabs, axis=1)


def key_row(ref, rows_here):
    wide = ref[ref.shape[0] - 8 :, :].astype(F32)
    kinds = [jnp.concatenate([wide[at : at + 1], wide[at + 1 : at + 2]], axis=1) for at in (0, 2)]
    return (kinds[0] * 256.0 + kinds[1])[:, :rows_here]


def from_pieces(first, second, rows_here):
    cut = first_rows(rows_here)
    pieces = [from_slabs(first, cut), from_slabs(second, rows_here - cut)]
    rows = jnp.concatenate(pieces, axis=0)
    return rows, key_row(second, rows_here)


def add_blocks(left, info, blocks, numer, denom):
    key = info[: left.shape[0], 0:1]
    scale = info[: left.shape[0], 1:2]
    right_rows = jnp.concatenate([block[0] for block in blocks], axis=0)
    right_key = jnp.concatenate([block[1] for block in blocks], axis=1)
    right_scale = jnp.concatenate([block[2] for block in blocks], axis=1)
    grams = lax.dot_general(
        left, right_rows, (((1,), (1,)), ((), ())), preferred_element_type=F32
    )
    half = jnp.tanh(grams * scale * right_scale - 1.0)
    weight = jnp.where(key == right_key, 0.5 + 0.5 * half, 0.0)
    add = jnp.dot(weight.astype(BF16), right_rows, preferred_element_type=F32)
    add_denom = jnp.sum(weight, axis=1, keepdims=True)
    if numer is None:
        return add, add_denom
    return numer + add, denom + add_denom


def left_rows(refs, rows_here):
    return jnp.concatenate([from_slabs(ref, rows_here) for ref in refs], axis=0)


def take_blocks(refs, count, rows_here):
    blocks = []
    for _ in range(count):
        rows, key = from_pieces(refs.pop(0), refs.pop(0), rows_here)
        blocks.append((rows, key, to_row(scale_column(rows))))
    return blocks


def store_sides(numer, denom, outs):
    rows_here, wide = outs[0].shape
    for side, out in enumerate(outs):
        top = side * rows_here
        out[:, : wide - 128] = numer[top : top + rows_here]
        out[:, wide - 128 :] = jnp.broadcast_to(denom[top : top + rows_here], (rows_here, 128))


def start_kernel(n_blocks, own, other, *refs):
    refs = list(refs)
    rows_here = refs[-1].shape[0] // 2
    left = left_rows((own, other), rows_here)
    key = jnp.concatenate([to_column(key_row(ref, rows_here)) for ref in (own, other)], axis=0)
    scale = scale_column(left)
    info = refs.pop()
    lane = lax.broadcasted_iota(jnp.int32, info.shape, 1)
    info[...] = jnp.where(lane == 0, key, 4.0 * scale)
    first = (left[:rows_here], key_row(own, rows_here), to_row(scale[:rows_here]))
    blocks = [first] + take_blocks(refs, n_blocks, rows_here)
    store_sides(*add_blocks(left, info, blocks, None, None), refs)


def both_kernel(n_blocks, own, other, info, *refs):
    refs = list(refs)
    rows_here = refs[2 * n_blocks].shape[0]
    blocks = take_blocks(refs, n_blocks, rows_here)
    mine_in, theirs_in, mine, *theirs = refs
    wide = mine.shape[1]
    width = wide - 128
    left = left_rows((own, other), rows_here)
    numer = jnp.concatenate([ref[:, :width] for ref in (mine_in, theirs_in)], axis=0)
    denom = jnp.concatenate([ref[:, width : width + 1] for ref in (mine_in, theirs_in)], axis=0)
    numer, denom = add_blocks(left, info, blocks, numer, denom)
    store_sides(numer[:rows_here], denom[:rows_here], [mine])
    denom = denom[rows_here:]
    high = denom.astype(BF16).astype(F32)
    lane = lax.broadcasted_iota(jnp.int32, (rows_here, 128), 1)
    pair = jnp.where(lane == 0, high, denom - high).astype(BF16)
    count = rows_here // len(theirs)
    for part, out in enumerate(theirs):
        top = part * count
        out[:, :width] = numer[rows_here + top : rows_here + top + count].astype(BF16)
        out[:, width:] = pair[top : top + count]


def join_kernel(own, info, first, second, mine, *refs):
    *parts, out = refs
    rows_here, wide = out.shape
    width = wide - 128
    theirs = jnp.concatenate([ref[...] for ref in parts], axis=0)
    pair = theirs[:, width:].astype(F32)
    numer = mine[:, :width] + theirs[:, :width].astype(F32)
    denom = mine[:, width : width + 1] + (pair[:, 0:1] + pair[:, 1:2])
    blocks = take_blocks([first, second], 1, rows_here)
    left = left_rows((own,), rows_here)
    store_sides(*add_blocks(left, info, blocks, numer, denom), [out])


def last_kernel(own, info, first, second, total, out, staged, sems):
    rows_here, width = out.shape
    blocks = take_blocks([first, second], 1, rows_here)
    left = left_rows((own,), rows_here)
    numer, denom = total[:, :width], total[:, width : width + 1]
    numer, denom = add_blocks(left, info, blocks, numer, denom)
    share = 1.0 / denom
    count = rows_here // 4
    copies = []
    for part in range(4):
        rows = slice(part * count, (part + 1) * count)
        staged[rows, :] = (numer[rows] * share[rows]).astype(BF16)
        copies.append(pltpu.make_async_copy(staged.at[rows, :], out.at[rows, :], sems.at[part]))
        copies[-1].start()
    for copy in copies:
        copy.wait()


def whole_in_vmem(count):
    return [pl.BlockSpec(memory_space=pltpu.VMEM)] * count


def call(kernel, shapes, args, aliases={}, products=0):
    return pl.pallas_call(
        kernel,
        out_shape=[jax.ShapeDtypeStruct(shape, dtype) for shape, dtype in shapes],
        in_specs=whole_in_vmem(len(args)),
        out_specs=whole_in_vmem(len(shapes)),
        input_output_aliases=aliases,
        compiler_params=pltpu.CompilerParams(vmem_limit_bytes=VMEM_BYTES),
        cost_estimate=pl.CostEstimate(
            flops=3 * products, transcendentals=0, bytes_accessed=0
        ),
    )(*args)


def start_both(left, right, shape):
    rows_here = shape[0]
    args = list(left) + [piece for block in right for piece in block]
    shapes = [(shape, F32), (shape, F32), ((2 * rows_here, 128), F32)]
    products = 4 * rows_here * (len(right) + 1) * rows_here * (shape[1] - 128)
    return call(
        functools.partial(start_kernel, len(right)), shapes, args, products=products
    )


def add_both(left, right, before):
    args = list(left) + [piece for block in right for piece in block] + list(before)
    rows_here, wide = before[0].shape
    shapes = [((rows_here, wide), F32)] + [((rows_here // PARTS, wide), BF16)] * PARTS
    kernel = functools.partial(both_kernel, len(right))
    products = 4 * rows_here * len(right) * rows_here * (wide - 128)
    return call(kernel, shapes, args, {len(args) - 2: 0}, products)


def finish(shape, args):
    return pl.pallas_call(
        last_kernel,
        out_shape=jax.ShapeDtypeStruct(shape, BF16),
        in_specs=whole_in_vmem(len(args)),
        out_specs=pl.BlockSpec(memory_space=pl.ANY),
        scratch_shapes=[pltpu.VMEM(shape, BF16), pltpu.SemaphoreType.DMA((4,))],
        compiler_params=pltpu.CompilerParams(vmem_limit_bytes=VMEM_BYTES),
    )(*args)


def folded_ring(size):
    return list(range(0, size, 2)) + list(range(1, size, 2))[::-1]


def together(*arrays):
    return lax.optimization_barrier(arrays)


def by_block(embeddings, group_of, cluster_id):
    rows_here, width = embeddings.shape
    cut = first_rows(rows_here)
    slabs = width // 128
    n_blk = lax.axis_size("blk")
    order = folded_ring(n_blk)
    line = (1, rows_here)

    def along(rows):
        hops = [
            (2 * order[i - 1] + core, 2 * order[i] + 1 - core)
            for i in range(n_blk)
            for core in range(2)
        ]
        return lax.ppermute(rows, ("blk", "pair"), hops)

    def across(rows):
        return lax.ppermute(rows, ("sub", "pair"), [(0, 3), (1, 2), (2, 1), (3, 0)])

    def other_core(rows):
        return lax.ppermute(rows, "pair", [(0, 1), (1, 0)])

    (first,) = call(first_pack_kernel, [((slabs * cut, 128), BF16)], [embeddings])
    whole, second = call(
        pack_kernel,
        [
            ((slabs * rows_here + 8, 128), BF16),
            ((slabs * (rows_here - cut) + 8, 128), BF16),
        ],
        [embeddings, group_of.reshape(line), cluster_id.reshape(line)],
    )
    along_by = [(first, second)]
    across_by = []
    for s in range(1, n_blk):
        moved = [along(piece) for piece in along_by[-1]]
        swapped = [across(piece) for piece in along_by[-1]]
        moved[0], swapped[0] = together(moved[0], swapped[0])
        if s < n_blk - 1:
            moved[1], swapped[1], _ = together(moved[1], swapped[1], moved[0])
        along_by.append(tuple(moved))
        across_by.append(tuple(swapped))
    left = (whole, other_core(whole))
    early = across_by[:-1] + along_by[1:-2]
    mine, theirs, info = start_both(left, early, (rows_here, width + 128))
    left = (*left, info)
    far_first, _, mine, theirs = together(along_by[-1][0], across_by[-1][0], mine, theirs)
    near_second, _ = together(across_by[-1][1], far_first)
    last_first, last_second = across(far_first), along(near_second)
    late = [along_by[-2], across_by[-1], along_by[-1]]
    mine, *theirs = add_both(left, late, (mine, theirs))
    back = [other_core(part) for part in theirs[:-1]]
    last_first, theirs[-1] = together(last_first, theirs[-1])
    last_second, *back = together(last_second, *back, other_core(theirs[-1]))
    last = [other_core(last_first), other_core(last_second)]
    (total,) = call(
        join_kernel,
        [((rows_here, width + 128), F32)],
        [whole, info, last_first, last_second, mine, *back],
        {4: 0},
    )
    out = finish((rows_here, width), [whole, info, *last, total])
    return out


def per_device(embeddings, group_of, cluster_id):
    rows_here, width = embeddings.shape
    devices = lax.axis_size("blk") * lax.axis_size("sub") * lax.axis_size("pair")
    small = devices * rows_here * width * 2 <= GATHER_LIMIT
    fits = width % 128 == 0 and rows_here % (64 * PARTS) == 0 and rows_here <= 256
    if small and fits and lax.axis_size("sub") == 2 and lax.axis_size("pair") == 2:
        return by_block(embeddings, group_of, cluster_id)
    return by_group(embeddings, group_of, cluster_id)


def solution(mesh):
    return jax.shard_map(
        per_device,
        mesh=mesh,
        in_specs=(
            P(("island", "blk", "sub", "pair"), None),
            P(("island", "blk", "sub", "pair"), None),
            P(("island", "blk", "sub", "pair")),
        ),
        out_specs=P(("island", "blk", "sub", "pair"), None),
        check_vma=False,
    )
```

```python
import functools

import jax
import jax.numpy as jnp
from jax import lax
from jax.experimental import pallas as pl
from jax.experimental.pallas import tpu as pltpu
from jax.sharding import PartitionSpec as P

F32 = jnp.float32
BF16 = jnp.bfloat16
VMEM_BYTES = 24 * 1024 * 1024
PARTS = 3
LINES = 16
GATHER_LIMIT = 8 * 1024 * 1024


def unit_scale(rows_in):
    wide = rows_in.astype(F32)
    return lax.rsqrt(jnp.sum(wide * wide, axis=1) + 1e-06)


def tile_weights(left_rows, left_clust, left_scale, right_rows, right_clust, right_scale):
    grams = lax.dot_general(
        left_rows, right_rows, (((1,), (1,)), ((), ())), preferred_element_type=F32
    )
    cosine = grams * left_scale[:, None] * right_scale[None, :]
    same = (left_clust[:, None] == right_clust[None, :]).astype(F32)
    return jax.nn.sigmoid(8.0 * cosine - 2.0) * same


def by_group(embeddings, group_of, cluster_id):
    rows_here, width = embeddings.shape
    groups = lax.axis_size("sub") * lax.axis_size("pair")
    capacity = 2 * rows_here // groups
    slots = groups * capacity
    target = group_of[:, 0]
    onehot = (target[:, None] == jnp.arange(groups, dtype=jnp.int32)[None, :]).astype(jnp.int32)
    position = jnp.sum((jnp.cumsum(onehot, axis=0) - onehot) * onehot, axis=1)
    send_rows = jnp.zeros((groups, capacity, width), BF16).at[target, position].set(embeddings)
    send_clust = jnp.full((groups, capacity), -1, jnp.int32).at[target, position].set(cluster_id)
    recv_rows, recv_clust = (
        lax.all_to_all(send_rows, ("sub", "pair"), split_axis=0, concat_axis=0, tiled=True),
        lax.all_to_all(send_clust, ("sub", "pair"), split_axis=0, concat_axis=0, tiled=True),
    )
    own_rows = recv_rows.reshape(slots, width)
    own_clust = recv_clust.reshape(slots)
    own_scale = unit_scale(own_rows)
    piece_rows = lax.all_gather(own_rows, "blk", axis=0, tiled=True)
    piece_clust = lax.all_gather(own_clust, "blk", axis=0, tiled=True)
    weight = tile_weights(
        own_rows, own_clust, own_scale, piece_rows, piece_clust, unit_scale(piece_rows)
    )
    numer = jnp.dot(weight.astype(BF16), piece_rows, preferred_element_type=F32)
    denom = jnp.sum(weight, axis=1)
    result = (numer / denom[:, None]).astype(BF16).reshape(groups, capacity, width)
    returned = lax.all_to_all(result, ("sub", "pair"), split_axis=0, concat_axis=0, tiled=True)
    return returned[target, position]


def diagonal(size):
    shape = (size, size)
    return lax.broadcasted_iota(jnp.int32, shape, 0) == lax.broadcasted_iota(jnp.int32, shape, 1)


def to_column(row):
    size = row.shape[1]
    return jnp.sum(jnp.where(diagonal(size), row, jnp.zeros_like(row)), axis=1, keepdims=True)


def to_row(column):
    size = column.shape[0]
    return jnp.sum(jnp.where(diagonal(size), column, jnp.zeros_like(column)), axis=0, keepdims=True)


def scale_column(rows):
    wide = rows.astype(F32)
    return lax.rsqrt(jnp.sum(wide * wide, axis=1, keepdims=True) + 1e-06)


def first_pack_kernel(rows, first):
    width = rows.shape[1]
    slabs = width // 128
    half = rows.shape[0] // 2
    for slab in range(slabs):
        first[slab * half : (slab + 1) * half, :] = rows[:half, slab * 128 : (slab + 1) * 128]
    first[slabs * half :, :] = jnp.zeros((LINES, 128), BF16)


def pack_kernel(rows, group, cluster, whole, second):
    rows_here, width = rows.shape
    slabs = width // 128
    half = rows_here // 2
    for slab in range(slabs):
        columns = rows[:, slab * 128 : (slab + 1) * 128]
        whole[slab * rows_here : (slab + 1) * rows_here, :] = columns
        second[slab * half : (slab + 1) * half, :] = columns[half:]
    line_at = lax.broadcasted_iota(jnp.int32, (LINES, 128), 0)
    named = jnp.zeros((LINES, 128), jnp.int32)
    for line in range(4):
        top = line % 2 * half
        part = (group, cluster)[line // 2][:, top : top + half]
        if half < 128:
            part = jnp.concatenate([part, jnp.zeros((1, 128 - half), jnp.int32)], axis=1)
        named = jnp.where(line_at == line, part, named)
    named = named.astype(F32).astype(BF16)
    whole[slabs * rows_here :, :] = named
    second[slabs * half :, :] = named


def from_slabs(ref, count):
    slabs = [ref[top : top + count, :] for top in range(0, ref.shape[0] // count * count, count)]
    return jnp.concatenate(slabs, axis=1)


def key_rows(ref, half):
    wide = ref[ref.shape[0] - LINES :, :].astype(F32)
    return [
        wide[side : side + 1, :half] * 256.0 + wide[side + 2 : side + 3, :half]
        for side in range(2)
    ]


def key_row(ref, rows_here):
    return jnp.concatenate(key_rows(ref, rows_here // 2), axis=1)


def from_halves(first, second, rows_here):
    half = rows_here // 2
    rows = jnp.concatenate([from_slabs(first, half), from_slabs(second, half)], axis=0)
    return rows, key_row(second, rows_here)


def add_blocks(left, info, blocks, numer, denom):
    key = info[: left.shape[0], 0:1]
    scale = info[: left.shape[0], 1:2]
    right_rows = jnp.concatenate([block[0] for block in blocks], axis=0)
    right_key = jnp.concatenate([block[1] for block in blocks], axis=1)
    right_scale = jnp.concatenate([block[2] for block in blocks], axis=1)
    grams = lax.dot_general(
        left, right_rows, (((1,), (1,)), ((), ())), preferred_element_type=F32
    )
    half = jnp.tanh(grams * scale * right_scale - 1.0)
    weight = jnp.where(key == right_key, 0.5 + 0.5 * half, 0.0)
    add = jnp.dot(weight.astype(BF16), right_rows, preferred_element_type=F32)
    add_denom = jnp.sum(weight, axis=1, keepdims=True)
    if numer is None:
        return add, add_denom
    return numer + add, denom + add_denom


def left_rows(refs, rows_here):
    return jnp.concatenate([from_slabs(ref, rows_here) for ref in refs], axis=0)


def take_blocks(refs, count, rows_here):
    blocks = []
    for _ in range(count):
        rows, key = from_halves(refs.pop(0), refs.pop(0), rows_here)
        blocks.append((rows, key, to_row(scale_column(rows))))
    return blocks


def store_sides(numer, denom, outs):
    rows_here, wide = outs[0].shape
    for side, out in enumerate(outs):
        top = side * rows_here
        out[:, : wide - 128] = numer[top : top + rows_here]
        out[:, wide - 128 :] = jnp.broadcast_to(denom[top : top + rows_here], (rows_here, 128))


def start_kernel(n_blocks, own, other, *refs):
    refs = list(refs)
    rows_here = refs[-1].shape[0] // 2
    left = left_rows((own, other), rows_here)
    key = jnp.concatenate([to_column(key_row(ref, rows_here)) for ref in (own, other)], axis=0)
    scale = scale_column(left)
    info = refs.pop()
    lane = lax.broadcasted_iota(jnp.int32, info.shape, 1)
    info[...] = jnp.where(lane == 0, key, 4.0 * scale)
    first = (left[:rows_here], key_row(own, rows_here), to_row(scale[:rows_here]))
    blocks = [first] + take_blocks(refs, n_blocks, rows_here)
    store_sides(*add_blocks(left, info, blocks, None, None), refs)


def both_kernel(n_blocks, own, other, info, *refs):
    refs = list(refs)
    rows_here = refs[2 * n_blocks].shape[0]
    blocks = take_blocks(refs, n_blocks, rows_here)
    mine_in, theirs_in, mine, *theirs = refs
    wide = mine.shape[1]
    width = wide - 128
    left = left_rows((own, other), rows_here)
    numer = jnp.concatenate([ref[:, :width] for ref in (mine_in, theirs_in)], axis=0)
    denom = jnp.concatenate([ref[:, width : width + 1] for ref in (mine_in, theirs_in)], axis=0)
    numer, denom = add_blocks(left, info, blocks, numer, denom)
    store_sides(numer[:rows_here], denom[:rows_here], [mine])
    denom = denom[rows_here:]
    high = denom.astype(BF16).astype(F32)
    lane = lax.broadcasted_iota(jnp.int32, (rows_here, 128), 1)
    pair = jnp.where(lane == 0, high, denom - high).astype(BF16)
    count = rows_here // len(theirs)
    for part, out in enumerate(theirs):
        top = part * count
        out[:, :width] = numer[rows_here + top : rows_here + top + count].astype(BF16)
        out[:, width:] = pair[top : top + count]


def join_kernel(own, info, first, second, mine, *refs):
    *parts, out = refs
    rows_here, wide = out.shape
    width = wide - 128
    theirs = jnp.concatenate([ref[...] for ref in parts], axis=0)
    pair = theirs[:, width:].astype(F32)
    numer = mine[:, :width] + theirs[:, :width].astype(F32)
    denom = mine[:, width : width + 1] + (pair[:, 0:1] + pair[:, 1:2])
    blocks = take_blocks([first, second], 1, rows_here)
    left = left_rows((own,), rows_here)
    store_sides(*add_blocks(left, info, blocks, numer, denom), [out])


def last_kernel(own, info, first, second, total, out, staged, sems):
    rows_here, width = out.shape
    blocks = take_blocks([first, second], 1, rows_here)
    left = left_rows((own,), rows_here)
    numer, denom = total[:, :width], total[:, width : width + 1]
    numer, denom = add_blocks(left, info, blocks, numer, denom)
    share = 1.0 / denom
    count = rows_here // 4
    copies = []
    for part in range(4):
        rows = slice(part * count, (part + 1) * count)
        staged[rows, :] = (numer[rows] * share[rows]).astype(BF16)
        copies.append(pltpu.make_async_copy(staged.at[rows, :], out.at[rows, :], sems.at[part]))
        copies[-1].start()
    for copy in copies:
        copy.wait()


def whole_in_vmem(count):
    return [pl.BlockSpec(memory_space=pltpu.VMEM)] * count


def call(kernel, shapes, args, aliases={}):
    return pl.pallas_call(
        kernel,
        out_shape=[jax.ShapeDtypeStruct(shape, dtype) for shape, dtype in shapes],
        in_specs=whole_in_vmem(len(args)),
        out_specs=whole_in_vmem(len(shapes)),
        input_output_aliases=aliases,
        compiler_params=pltpu.CompilerParams(vmem_limit_bytes=VMEM_BYTES),
    )(*args)


def start_both(left, right, shape):
    rows_here = shape[0]
    args = list(left) + [half for block in right for half in block]
    shapes = [(shape, F32), (shape, F32), ((2 * rows_here, 128), F32)]
    return call(functools.partial(start_kernel, len(right)), shapes, args)


def add_both(left, right, before):
    args = list(left) + [half for block in right for half in block] + list(before)
    rows_here, wide = before[0].shape
    shapes = [((rows_here, wide), F32)] + [((rows_here // PARTS, wide), BF16)] * PARTS
    kernel = functools.partial(both_kernel, len(right))
    return call(kernel, shapes, args, {len(args) - 2: 0})


def finish(shape, args):
    return pl.pallas_call(
        last_kernel,
        out_shape=jax.ShapeDtypeStruct(shape, BF16),
        in_specs=whole_in_vmem(len(args)),
        out_specs=pl.BlockSpec(memory_space=pl.ANY),
        scratch_shapes=[pltpu.VMEM(shape, BF16), pltpu.SemaphoreType.DMA((4,))],
        compiler_params=pltpu.CompilerParams(vmem_limit_bytes=VMEM_BYTES),
    )(*args)


def folded_ring(size):
    return list(range(0, size, 2)) + list(range(1, size, 2))[::-1]


def together(*arrays):
    return lax.optimization_barrier(arrays)


def by_block(embeddings, group_of, cluster_id):
    rows_here, width = embeddings.shape
    half = rows_here // 2
    slabs = width // 128
    n_blk = lax.axis_size("blk")
    order = folded_ring(n_blk)
    line = (1, rows_here)

    def along(rows):
        hops = [
            (2 * order[i - 1] + core, 2 * order[i] + 1 - core)
            for i in range(n_blk)
            for core in range(2)
        ]
        return lax.ppermute(rows, ("blk", "pair"), hops)

    def across(rows):
        return lax.ppermute(rows, ("sub", "pair"), [(0, 3), (1, 2), (2, 1), (3, 0)])

    def other_core(rows):
        return lax.ppermute(rows, "pair", [(0, 1), (1, 0)])

    half_shape = ((slabs * half + LINES, 128), BF16)
    (first,) = call(first_pack_kernel, [half_shape], [embeddings])
    whole, second = call(
        pack_kernel,
        [((slabs * rows_here + LINES, 128), BF16), half_shape],
        [embeddings, group_of.reshape(line), cluster_id.reshape(line)],
    )
    along_by = [(first, second)]
    across_by = []
    for s in range(1, n_blk):
        moved = [along(piece) for piece in along_by[-1]]
        swapped = [across(piece) for piece in along_by[-1]]
        moved[0], swapped[0] = together(moved[0], swapped[0])
        if s < n_blk - 1:
            moved[1], swapped[1], _ = together(moved[1], swapped[1], moved[0])
        along_by.append(tuple(moved))
        across_by.append(tuple(swapped))
    left = (whole, other_core(whole))
    early = across_by[:-1] + along_by[1:-2]
    mine, theirs, info = start_both(left, early, (rows_here, width + 128))
    left = (*left, info)
    far_first, _, mine, theirs = together(along_by[-1][0], across_by[-1][0], mine, theirs)
    near_second, _ = together(across_by[-1][1], far_first)
    last_first, last_second = across(far_first), along(near_second)
    late = [along_by[-2], across_by[-1], along_by[-1]]
    mine, *theirs = add_both(left, late, (mine, theirs))
    back = [other_core(part) for part in theirs[:-1]]
    last_first, theirs[-1] = together(last_first, theirs[-1])
    last_second, *back = together(last_second, *back, other_core(theirs[-1]))
    last = [other_core(last_first), other_core(last_second)]
    (total,) = call(
        join_kernel,
        [((rows_here, width + 128), F32)],
        [whole, info, last_first, last_second, mine, *back],
        {4: 0},
    )
    out = finish((rows_here, width), [whole, info, *last, total])
    return out


def per_device(embeddings, group_of, cluster_id):
    rows_here, width = embeddings.shape
    devices = lax.axis_size("blk") * lax.axis_size("sub") * lax.axis_size("pair")
    small = devices * rows_here * width * 2 <= GATHER_LIMIT
    fits = width % 128 == 0 and rows_here % (64 * PARTS) == 0 and rows_here <= 256
    if small and fits and lax.axis_size("sub") == 2 and lax.axis_size("pair") == 2:
        return by_block(embeddings, group_of, cluster_id)
    return by_group(embeddings, group_of, cluster_id)


def solution(mesh):
    return jax.shard_map(
        per_device,
        mesh=mesh,
        in_specs=(
            P(("island", "blk", "sub", "pair"), None),
            P(("island", "blk", "sub", "pair"), None),
            P(("island", "blk", "sub", "pair")),
        ),
        out_specs=P(("island", "blk", "sub", "pair"), None),
        check_vma=False,
    )
```

```python
import functools

import jax
import jax.numpy as jnp
from jax import lax
from jax.experimental import pallas as pl
from jax.experimental.pallas import tpu as pltpu
from jax.sharding import PartitionSpec as P

F32 = jnp.float32
BF16 = jnp.bfloat16
VMEM_BYTES = 24 * 1024 * 1024
PARTS = 3
LINES = 16
GATHER_LIMIT = 8 * 1024 * 1024


def unit_scale(rows_in):
    wide = rows_in.astype(F32)
    return lax.rsqrt(jnp.sum(wide * wide, axis=1) + 1e-06)


def tile_weights(left_rows, left_clust, left_scale, right_rows, right_clust, right_scale):
    grams = lax.dot_general(
        left_rows, right_rows, (((1,), (1,)), ((), ())), preferred_element_type=F32
    )
    cosine = grams * left_scale[:, None] * right_scale[None, :]
    same = (left_clust[:, None] == right_clust[None, :]).astype(F32)
    return jax.nn.sigmoid(8.0 * cosine - 2.0) * same


def by_group(embeddings, group_of, cluster_id):
    rows_here, width = embeddings.shape
    groups = lax.axis_size("sub") * lax.axis_size("pair")
    capacity = 2 * rows_here // groups
    slots = groups * capacity
    target = group_of[:, 0]
    onehot = (target[:, None] == jnp.arange(groups, dtype=jnp.int32)[None, :]).astype(jnp.int32)
    position = jnp.sum((jnp.cumsum(onehot, axis=0) - onehot) * onehot, axis=1)
    send_rows = jnp.zeros((groups, capacity, width), BF16).at[target, position].set(embeddings)
    send_clust = jnp.full((groups, capacity), -1, jnp.int32).at[target, position].set(cluster_id)
    recv_rows, recv_clust = (
        lax.all_to_all(send_rows, ("sub", "pair"), split_axis=0, concat_axis=0, tiled=True),
        lax.all_to_all(send_clust, ("sub", "pair"), split_axis=0, concat_axis=0, tiled=True),
    )
    own_rows = recv_rows.reshape(slots, width)
    own_clust = recv_clust.reshape(slots)
    own_scale = unit_scale(own_rows)
    piece_rows = lax.all_gather(own_rows, "blk", axis=0, tiled=True)
    piece_clust = lax.all_gather(own_clust, "blk", axis=0, tiled=True)
    weight = tile_weights(
        own_rows, own_clust, own_scale, piece_rows, piece_clust, unit_scale(piece_rows)
    )
    numer = jnp.dot(weight.astype(BF16), piece_rows, preferred_element_type=F32)
    denom = jnp.sum(weight, axis=1)
    result = (numer / denom[:, None]).astype(BF16).reshape(groups, capacity, width)
    returned = lax.all_to_all(result, ("sub", "pair"), split_axis=0, concat_axis=0, tiled=True)
    return returned[target, position]


def diagonal(size):
    shape = (size, size)
    return lax.broadcasted_iota(jnp.int32, shape, 0) == lax.broadcasted_iota(jnp.int32, shape, 1)


def to_column(row):
    size = row.shape[1]
    return jnp.sum(jnp.where(diagonal(size), row, jnp.zeros_like(row)), axis=1, keepdims=True)


def to_row(column):
    size = column.shape[0]
    return jnp.sum(jnp.where(diagonal(size), column, jnp.zeros_like(column)), axis=0, keepdims=True)


def scale_column(rows):
    wide = rows.astype(F32)
    return lax.rsqrt(jnp.sum(wide * wide, axis=1, keepdims=True) + 1e-06)


def first_pack_kernel(rows, first):
    half = rows.shape[0] // 2
    for slab in range(rows.shape[1] // 128):
        first[slab * half : (slab + 1) * half, :] = rows[:half, slab * 128 : (slab + 1) * 128]


def pack_kernel(rows, group, cluster, whole, second):
    rows_here, width = rows.shape
    slabs = width // 128
    half = rows_here // 2
    for slab in range(slabs):
        columns = rows[:, slab * 128 : (slab + 1) * 128]
        whole[slab * rows_here : (slab + 1) * rows_here, :] = columns
        second[slab * half : (slab + 1) * half, :] = columns[half:]
    line_at = lax.broadcasted_iota(jnp.int32, (LINES, 128), 0)
    named = jnp.zeros((LINES, 128), jnp.int32)
    for line in range(4):
        top = line % 2 * half
        part = (group, cluster)[line // 2][:, top : top + half]
        if half < 128:
            part = jnp.concatenate([part, jnp.zeros((1, 128 - half), jnp.int32)], axis=1)
        named = jnp.where(line_at == line, part, named)
    named = named.astype(F32).astype(BF16)
    whole[slabs * rows_here :, :] = named
    second[slabs * half :, :] = named


def from_slabs(ref, count):
    slabs = [ref[top : top + count, :] for top in range(0, ref.shape[0] // count * count, count)]
    return jnp.concatenate(slabs, axis=1)


def key_rows(ref, half):
    wide = ref[ref.shape[0] - LINES :, :].astype(F32)
    return [
        wide[side : side + 1, :half] * 256.0 + wide[side + 2 : side + 3, :half]
        for side in range(2)
    ]


def key_row(ref, rows_here):
    return jnp.concatenate(key_rows(ref, rows_here // 2), axis=1)


def from_halves(first, second, rows_here):
    half = rows_here // 2
    rows = jnp.concatenate([from_slabs(first, half), from_slabs(second, half)], axis=0)
    return rows, key_row(second, rows_here)


def add_blocks(left, info, blocks, numer, denom):
    key = info[: left.shape[0], 0:1]
    scale = info[: left.shape[0], 1:2]
    right_rows = jnp.concatenate([block[0] for block in blocks], axis=0)
    right_key = jnp.concatenate([block[1] for block in blocks], axis=1)
    right_scale = jnp.concatenate([block[2] for block in blocks], axis=1)
    grams = lax.dot_general(
        left, right_rows, (((1,), (1,)), ((), ())), preferred_element_type=F32
    )
    half = jnp.tanh(grams * scale * right_scale - 1.0)
    weight = jnp.where(key == right_key, 0.5 + 0.5 * half, 0.0)
    add = jnp.dot(weight.astype(BF16), right_rows, preferred_element_type=F32)
    add_denom = jnp.sum(weight, axis=1, keepdims=True)
    if numer is None:
        return add, add_denom
    return numer + add, denom + add_denom


def left_rows(refs, rows_here):
    return jnp.concatenate([from_slabs(ref, rows_here) for ref in refs], axis=0)


def take_blocks(refs, count, rows_here):
    blocks = []
    for _ in range(count):
        rows, key = from_halves(refs.pop(0), refs.pop(0), rows_here)
        blocks.append((rows, key, to_row(scale_column(rows))))
    return blocks


def store_sides(numer, denom, outs):
    rows_here, wide = outs[0].shape
    for side, out in enumerate(outs):
        top = side * rows_here
        out[:, : wide - 128] = numer[top : top + rows_here]
        out[:, wide - 128 :] = jnp.broadcast_to(denom[top : top + rows_here], (rows_here, 128))


def start_kernel(n_blocks, own, other, *refs):
    refs = list(refs)
    rows_here = refs[-1].shape[0] // 2
    left = left_rows((own, other), rows_here)
    key = jnp.concatenate([to_column(key_row(ref, rows_here)) for ref in (own, other)], axis=0)
    scale = scale_column(left)
    info = refs.pop()
    lane = lax.broadcasted_iota(jnp.int32, info.shape, 1)
    info[...] = jnp.where(lane == 0, key, 4.0 * scale)
    first = (left[:rows_here], key_row(own, rows_here), to_row(scale[:rows_here]))
    blocks = [first] + take_blocks(refs, n_blocks, rows_here)
    store_sides(*add_blocks(left, info, blocks, None, None), refs)


def both_kernel(n_blocks, own, other, info, *refs):
    refs = list(refs)
    rows_here = refs[2 * n_blocks].shape[0]
    blocks = take_blocks(refs, n_blocks, rows_here)
    mine_in, theirs_in, mine, *theirs = refs
    wide = mine.shape[1]
    width = wide - 128
    left = left_rows((own, other), rows_here)
    numer = jnp.concatenate([ref[:, :width] for ref in (mine_in, theirs_in)], axis=0)
    denom = jnp.concatenate([ref[:, width : width + 1] for ref in (mine_in, theirs_in)], axis=0)
    numer, denom = add_blocks(left, info, blocks, numer, denom)
    store_sides(numer[:rows_here], denom[:rows_here], [mine])
    denom = denom[rows_here:]
    high = denom.astype(BF16).astype(F32)
    lane = lax.broadcasted_iota(jnp.int32, (rows_here, 128), 1)
    pair = jnp.where(lane == 0, high, denom - high).astype(BF16)
    count = rows_here // len(theirs)
    for part, out in enumerate(theirs):
        top = part * count
        out[:, :width] = numer[rows_here + top : rows_here + top + count].astype(BF16)
        out[:, width:] = pair[top : top + count]


def join_kernel(own, info, first, second, mine, *refs):
    *parts, out = refs
    rows_here, wide = out.shape
    width = wide - 128
    theirs = jnp.concatenate([ref[...] for ref in parts], axis=0)
    pair = theirs[:, width:].astype(F32)
    numer = mine[:, :width] + theirs[:, :width].astype(F32)
    denom = mine[:, width : width + 1] + (pair[:, 0:1] + pair[:, 1:2])
    blocks = take_blocks([first, second], 1, rows_here)
    left = left_rows((own,), rows_here)
    store_sides(*add_blocks(left, info, blocks, numer, denom), [out])


def last_kernel(own, info, first, second, total, out, staged, sems):
    rows_here, width = out.shape
    blocks = take_blocks([first, second], 1, rows_here)
    left = left_rows((own,), rows_here)
    numer, denom = total[:, :width], total[:, width : width + 1]
    numer, denom = add_blocks(left, info, blocks, numer, denom)
    share = 1.0 / denom
    count = rows_here // 4
    copies = []
    for part in range(4):
        rows = slice(part * count, (part + 1) * count)
        staged[rows, :] = (numer[rows] * share[rows]).astype(BF16)
        copies.append(pltpu.make_async_copy(staged.at[rows, :], out.at[rows, :], sems.at[part]))
        copies[-1].start()
    for copy in copies:
        copy.wait()


def whole_in_vmem(count):
    return [pl.BlockSpec(memory_space=pltpu.VMEM)] * count


def call(kernel, shapes, args, aliases={}):
    return pl.pallas_call(
        kernel,
        out_shape=[jax.ShapeDtypeStruct(shape, dtype) for shape, dtype in shapes],
        in_specs=whole_in_vmem(len(args)),
        out_specs=whole_in_vmem(len(shapes)),
        input_output_aliases=aliases,
        compiler_params=pltpu.CompilerParams(vmem_limit_bytes=VMEM_BYTES),
    )(*args)


def start_both(left, right, shape):
    rows_here = shape[0]
    args = list(left) + [half for block in right for half in block]
    shapes = [(shape, F32), (shape, F32), ((2 * rows_here, 128), F32)]
    return call(functools.partial(start_kernel, len(right)), shapes, args)


def add_both(left, right, before):
    args = list(left) + [half for block in right for half in block] + list(before)
    rows_here, wide = before[0].shape
    shapes = [((rows_here, wide), F32)] + [((rows_here // PARTS, wide), BF16)] * PARTS
    kernel = functools.partial(both_kernel, len(right))
    return call(kernel, shapes, args, {len(args) - 2: 0})


def finish(shape, args):
    return pl.pallas_call(
        last_kernel,
        out_shape=jax.ShapeDtypeStruct(shape, BF16),
        in_specs=whole_in_vmem(len(args)),
        out_specs=pl.BlockSpec(memory_space=pl.ANY),
        scratch_shapes=[pltpu.VMEM(shape, BF16), pltpu.SemaphoreType.DMA((4,))],
        compiler_params=pltpu.CompilerParams(vmem_limit_bytes=VMEM_BYTES),
    )(*args)


def folded_ring(size):
    return list(range(0, size, 2)) + list(range(1, size, 2))[::-1]


def together(*arrays):
    return lax.optimization_barrier(arrays)


def by_block(embeddings, group_of, cluster_id):
    rows_here, width = embeddings.shape
    half = rows_here // 2
    slabs = width // 128
    n_blk = lax.axis_size("blk")
    order = folded_ring(n_blk)
    line = (1, rows_here)

    def along(rows):
        hops = [
            (2 * order[i - 1] + core, 2 * order[i] + 1 - core)
            for i in range(n_blk)
            for core in range(2)
        ]
        return lax.ppermute(rows, ("blk", "pair"), hops)

    def across(rows):
        return lax.ppermute(rows, ("sub", "pair"), [(0, 3), (1, 2), (2, 1), (3, 0)])

    def other_core(rows):
        return lax.ppermute(rows, "pair", [(0, 1), (1, 0)])

    (first,) = call(first_pack_kernel, [((slabs * half, 128), BF16)], [embeddings])
    whole, second = call(
        pack_kernel,
        [((slabs * count + LINES, 128), BF16) for count in (rows_here, half)],
        [embeddings, group_of.reshape(line), cluster_id.reshape(line)],
    )
    along_by = [(first, second)]
    across_by = []
    for s in range(1, n_blk):
        moved = [along(piece) for piece in along_by[-1]]
        swapped = [across(piece) for piece in along_by[-1]]
        moved[0], swapped[0] = together(moved[0], swapped[0])
        if s < n_blk - 1:
            moved[1], swapped[1], _ = together(moved[1], swapped[1], moved[0])
        along_by.append(tuple(moved))
        across_by.append(tuple(swapped))
    left = (whole, other_core(whole))
    early = across_by[:-1] + along_by[1:-2]
    mine, theirs, info = start_both(left, early, (rows_here, width + 128))
    left = (*left, info)
    far_first, _, mine, theirs = together(along_by[-1][0], across_by[-1][0], mine, theirs)
    near_second, _ = together(across_by[-1][1], far_first)
    last_first, last_second = across(far_first), along(near_second)
    late = [along_by[-2], across_by[-1], along_by[-1]]
    mine, *theirs = add_both(left, late, (mine, theirs))
    back = [other_core(part) for part in theirs[:-1]]
    last_first, theirs[-1] = together(last_first, theirs[-1])
    last_second, *back = together(last_second, *back, other_core(theirs[-1]))
    last = [other_core(last_first), other_core(last_second)]
    (total,) = call(
        join_kernel,
        [((rows_here, width + 128), F32)],
        [whole, info, last_first, last_second, mine, *back],
        {4: 0},
    )
    out = finish((rows_here, width), [whole, info, *last, total])
    return out


def per_device(embeddings, group_of, cluster_id):
    rows_here, width = embeddings.shape
    devices = lax.axis_size("blk") * lax.axis_size("sub") * lax.axis_size("pair")
    small = devices * rows_here * width * 2 <= GATHER_LIMIT
    fits = width % 128 == 0 and rows_here % (64 * PARTS) == 0 and rows_here <= 256
    if small and fits and lax.axis_size("sub") == 2 and lax.axis_size("pair") == 2:
        return by_block(embeddings, group_of, cluster_id)
    return by_group(embeddings, group_of, cluster_id)


def solution(mesh):
    return jax.shard_map(
        per_device,
        mesh=mesh,
        in_specs=(
            P(("island", "blk", "sub", "pair"), None),
            P(("island", "blk", "sub", "pair"), None),
            P(("island", "blk", "sub", "pair")),
        ),
        out_specs=P(("island", "blk", "sub", "pair"), None),
        check_vma=False,
    )
```

```python
import functools

import jax
import jax.numpy as jnp
from jax import lax
from jax.experimental import pallas as pl
from jax.experimental.pallas import tpu as pltpu
from jax.sharding import PartitionSpec as P

F32 = jnp.float32
BF16 = jnp.bfloat16
VMEM_BYTES = 24 * 1024 * 1024
PARTS = 3
LINES = 16
GATHER_LIMIT = 8 * 1024 * 1024


def unit_scale(rows_in):
    wide = rows_in.astype(F32)
    return lax.rsqrt(jnp.sum(wide * wide, axis=1) + 1e-06)


def tile_weights(left_rows, left_clust, left_scale, right_rows, right_clust, right_scale):
    grams = lax.dot_general(
        left_rows, right_rows, (((1,), (1,)), ((), ())), preferred_element_type=F32
    )
    cosine = grams * left_scale[:, None] * right_scale[None, :]
    same = (left_clust[:, None] == right_clust[None, :]).astype(F32)
    return jax.nn.sigmoid(8.0 * cosine - 2.0) * same


def by_group(embeddings, group_of, cluster_id):
    rows_here, width = embeddings.shape
    groups = lax.axis_size("sub") * lax.axis_size("pair")
    capacity = 2 * rows_here // groups
    slots = groups * capacity
    target = group_of[:, 0]
    onehot = (target[:, None] == jnp.arange(groups, dtype=jnp.int32)[None, :]).astype(jnp.int32)
    position = jnp.sum((jnp.cumsum(onehot, axis=0) - onehot) * onehot, axis=1)
    send_rows = jnp.zeros((groups, capacity, width), BF16).at[target, position].set(embeddings)
    send_clust = jnp.full((groups, capacity), -1, jnp.int32).at[target, position].set(cluster_id)
    recv_rows, recv_clust = (
        lax.all_to_all(send_rows, ("sub", "pair"), split_axis=0, concat_axis=0, tiled=True),
        lax.all_to_all(send_clust, ("sub", "pair"), split_axis=0, concat_axis=0, tiled=True),
    )
    own_rows = recv_rows.reshape(slots, width)
    own_clust = recv_clust.reshape(slots)
    own_scale = unit_scale(own_rows)
    piece_rows = lax.all_gather(own_rows, "blk", axis=0, tiled=True)
    piece_clust = lax.all_gather(own_clust, "blk", axis=0, tiled=True)
    weight = tile_weights(
        own_rows, own_clust, own_scale, piece_rows, piece_clust, unit_scale(piece_rows)
    )
    numer = jnp.dot(weight.astype(BF16), piece_rows, preferred_element_type=F32)
    denom = jnp.sum(weight, axis=1)
    result = (numer / denom[:, None]).astype(BF16).reshape(groups, capacity, width)
    returned = lax.all_to_all(result, ("sub", "pair"), split_axis=0, concat_axis=0, tiled=True)
    return returned[target, position]


def diagonal(size):
    shape = (size, size)
    return lax.broadcasted_iota(jnp.int32, shape, 0) == lax.broadcasted_iota(jnp.int32, shape, 1)


def to_column(row):
    size = row.shape[1]
    return jnp.sum(jnp.where(diagonal(size), row, jnp.zeros_like(row)), axis=1, keepdims=True)


def to_row(column):
    size = column.shape[0]
    return jnp.sum(jnp.where(diagonal(size), column, jnp.zeros_like(column)), axis=0, keepdims=True)


def scale_column(rows):
    wide = rows.astype(F32)
    return lax.rsqrt(jnp.sum(wide * wide, axis=1, keepdims=True) + 1e-06)


def first_pack_kernel(rows, first):
    half = rows.shape[0] // 2
    for slab in range(rows.shape[1] // 128):
        first[slab * half : (slab + 1) * half, :] = rows[:half, slab * 128 : (slab + 1) * 128]


def pack_kernel(rows, group, cluster, whole, second):
    rows_here, width = rows.shape
    slabs = width // 128
    half = rows_here // 2
    for slab in range(slabs):
        columns = rows[:, slab * 128 : (slab + 1) * 128]
        whole[slab * rows_here : (slab + 1) * rows_here, :] = columns
        second[slab * half : (slab + 1) * half, :] = columns[half:]
    line_at = lax.broadcasted_iota(jnp.int32, (LINES, 128), 0)
    named = jnp.zeros((LINES, 128), jnp.int32)
    for line in range(4):
        top = line % 2 * half
        part = (group, cluster)[line // 2][:, top : top + half]
        if half < 128:
            part = jnp.concatenate([part, jnp.zeros((1, 128 - half), jnp.int32)], axis=1)
        named = jnp.where(line_at == line, part, named)
    named = named.astype(F32).astype(BF16)
    whole[slabs * rows_here :, :] = named
    second[slabs * half :, :] = named


def pad_kernel(first, out):
    top = first.shape[0]
    out[:top, :] = first[...]
    out[top:, :] = jnp.zeros((out.shape[0] - top, 128), BF16)


def from_slabs(ref, count):
    slabs = [ref[top : top + count, :] for top in range(0, ref.shape[0] // count * count, count)]
    return jnp.concatenate(slabs, axis=1)


def key_rows(ref, half):
    wide = ref[ref.shape[0] - LINES :, :].astype(F32)
    return [
        wide[side : side + 1, :half] * 256.0 + wide[side + 2 : side + 3, :half]
        for side in range(2)
    ]


def key_row(ref, rows_here):
    return jnp.concatenate(key_rows(ref, rows_here // 2), axis=1)


def from_halves(first, second, rows_here):
    half = rows_here // 2
    rows = jnp.concatenate([from_slabs(first, half), from_slabs(second, half)], axis=0)
    return rows, key_row(second, rows_here)


def add_blocks(left, info, blocks, numer, denom):
    key = info[: left.shape[0], 0:1]
    scale = info[: left.shape[0], 1:2]
    right_rows = jnp.concatenate([block[0] for block in blocks], axis=0)
    right_key = jnp.concatenate([block[1] for block in blocks], axis=1)
    right_scale = jnp.concatenate([block[2] for block in blocks], axis=1)
    grams = lax.dot_general(
        left, right_rows, (((1,), (1,)), ((), ())), preferred_element_type=F32
    )
    half = jnp.tanh(grams * scale * right_scale - 1.0)
    weight = jnp.where(key == right_key, 0.5 + 0.5 * half, 0.0)
    add = jnp.dot(weight.astype(BF16), right_rows, preferred_element_type=F32)
    add_denom = jnp.sum(weight, axis=1, keepdims=True)
    if numer is None:
        return add, add_denom
    return numer + add, denom + add_denom


def left_rows(refs, rows_here):
    return jnp.concatenate([from_slabs(ref, rows_here) for ref in refs], axis=0)


def take_blocks(refs, count, rows_here):
    blocks = []
    for _ in range(count):
        rows, key = from_halves(refs.pop(0), refs.pop(0), rows_here)
        blocks.append((rows, key, to_row(scale_column(rows))))
    return blocks


def store_sides(numer, denom, outs):
    rows_here, wide = outs[0].shape
    for side, out in enumerate(outs):
        top = side * rows_here
        out[:, : wide - 128] = numer[top : top + rows_here]
        out[:, wide - 128 :] = jnp.broadcast_to(denom[top : top + rows_here], (rows_here, 128))


def start_kernel(n_blocks, own, other, *refs):
    refs = list(refs)
    rows_here = refs[-1].shape[0] // 2
    left = left_rows((own, other), rows_here)
    key = jnp.concatenate([to_column(key_row(ref, rows_here)) for ref in (own, other)], axis=0)
    scale = scale_column(left)
    info = refs.pop()
    lane = lax.broadcasted_iota(jnp.int32, info.shape, 1)
    info[...] = jnp.where(lane == 0, key, 4.0 * scale)
    first = (left[:rows_here], key_row(own, rows_here), to_row(scale[:rows_here]))
    blocks = [first] + take_blocks(refs, n_blocks, rows_here)
    store_sides(*add_blocks(left, info, blocks, None, None), refs)


def both_kernel(n_blocks, own, other, info, *refs):
    refs = list(refs)
    rows_here = refs[2 * n_blocks].shape[0]
    blocks = take_blocks(refs, n_blocks, rows_here)
    mine_in, theirs_in, mine, *theirs = refs
    wide = mine.shape[1]
    width = wide - 128
    left = left_rows((own, other), rows_here)
    numer = jnp.concatenate([ref[:, :width] for ref in (mine_in, theirs_in)], axis=0)
    denom = jnp.concatenate([ref[:, width : width + 1] for ref in (mine_in, theirs_in)], axis=0)
    numer, denom = add_blocks(left, info, blocks, numer, denom)
    store_sides(numer[:rows_here], denom[:rows_here], [mine])
    denom = denom[rows_here:]
    high = denom.astype(BF16).astype(F32)
    lane = lax.broadcasted_iota(jnp.int32, (rows_here, 128), 1)
    pair = jnp.where(lane == 0, high, denom - high).astype(BF16)
    count = rows_here // len(theirs)
    for part, out in enumerate(theirs):
        top = part * count
        out[:, :width] = numer[rows_here + top : rows_here + top + count].astype(BF16)
        out[:, width:] = pair[top : top + count]


def join_kernel(own, info, first, second, mine, *refs):
    *parts, out = refs
    rows_here, wide = out.shape
    width = wide - 128
    theirs = jnp.concatenate([ref[...] for ref in parts], axis=0)
    pair = theirs[:, width:].astype(F32)
    numer = mine[:, :width] + theirs[:, :width].astype(F32)
    denom = mine[:, width : width + 1] + (pair[:, 0:1] + pair[:, 1:2])
    blocks = take_blocks([first, second], 1, rows_here)
    left = left_rows((own,), rows_here)
    store_sides(*add_blocks(left, info, blocks, numer, denom), [out])


def last_kernel(own, info, first, second, total, out, staged, sems):
    rows_here, width = out.shape
    blocks = take_blocks([first, second], 1, rows_here)
    left = left_rows((own,), rows_here)
    numer, denom = total[:, :width], total[:, width : width + 1]
    numer, denom = add_blocks(left, info, blocks, numer, denom)
    share = 1.0 / denom
    count = rows_here // 4
    copies = []
    for part in range(4):
        rows = slice(part * count, (part + 1) * count)
        staged[rows, :] = (numer[rows] * share[rows]).astype(BF16)
        copies.append(pltpu.make_async_copy(staged.at[rows, :], out.at[rows, :], sems.at[part]))
        copies[-1].start()
    for copy in copies:
        copy.wait()


def whole_in_vmem(count):
    return [pl.BlockSpec(memory_space=pltpu.VMEM)] * count


def call(kernel, shapes, args, aliases={}):
    return pl.pallas_call(
        kernel,
        out_shape=[jax.ShapeDtypeStruct(shape, dtype) for shape, dtype in shapes],
        in_specs=whole_in_vmem(len(args)),
        out_specs=whole_in_vmem(len(shapes)),
        input_output_aliases=aliases,
        compiler_params=pltpu.CompilerParams(vmem_limit_bytes=VMEM_BYTES),
    )(*args)


def start_both(left, right, shape):
    rows_here = shape[0]
    args = list(left) + [half for block in right for half in block]
    shapes = [(shape, F32), (shape, F32), ((2 * rows_here, 128), F32)]
    return call(functools.partial(start_kernel, len(right)), shapes, args)


def add_both(left, right, before):
    args = list(left) + [half for block in right for half in block] + list(before)
    rows_here, wide = before[0].shape
    shapes = [((rows_here, wide), F32)] + [((rows_here // PARTS, wide), BF16)] * PARTS
    kernel = functools.partial(both_kernel, len(right))
    return call(kernel, shapes, args, {len(args) - 2: 0})


def finish(shape, args):
    return pl.pallas_call(
        last_kernel,
        out_shape=jax.ShapeDtypeStruct(shape, BF16),
        in_specs=whole_in_vmem(len(args)),
        out_specs=pl.BlockSpec(memory_space=pl.ANY),
        scratch_shapes=[pltpu.VMEM(shape, BF16), pltpu.SemaphoreType.DMA((4,))],
        compiler_params=pltpu.CompilerParams(vmem_limit_bytes=VMEM_BYTES),
    )(*args)


def folded_ring(size):
    return list(range(0, size, 2)) + list(range(1, size, 2))[::-1]


def together(*arrays):
    return lax.optimization_barrier(arrays)


def by_block(embeddings, group_of, cluster_id):
    rows_here, width = embeddings.shape
    half = rows_here // 2
    slabs = width // 128
    n_blk = lax.axis_size("blk")
    order = folded_ring(n_blk)
    line = (1, rows_here)

    def along(rows):
        hops = [
            (2 * order[i - 1] + core, 2 * order[i] + 1 - core)
            for i in range(n_blk)
            for core in range(2)
        ]
        return lax.ppermute(rows, ("blk", "pair"), hops)

    def across(rows):
        return lax.ppermute(rows, ("sub", "pair"), [(0, 3), (1, 2), (2, 1), (3, 0)])

    def other_core(rows):
        return lax.ppermute(rows, "pair", [(0, 1), (1, 0)])

    (first,) = call(first_pack_kernel, [((slabs * half, 128), BF16)], [embeddings])
    whole, second = call(
        pack_kernel,
        [((slabs * count + LINES, 128), BF16) for count in (rows_here, half)],
        [embeddings, group_of.reshape(line), cluster_id.reshape(line)],
    )
    along_by = [(first, second)]
    across_by = []
    for s in range(1, n_blk):
        moved = [along(piece) for piece in along_by[-1]]
        swapped = [across(piece) for piece in along_by[-1]]
        moved[0], swapped[0] = together(moved[0], swapped[0])
        if s < n_blk - 1:
            moved[1], swapped[1], _ = together(moved[1], swapped[1], moved[0])
        along_by.append(tuple(moved))
        across_by.append(tuple(swapped))
    left = (whole, other_core(whole))
    early = across_by[:-1] + along_by[1:-2]
    mine, theirs, info = start_both(left, early, (rows_here, width + 128))
    left = (*left, info)
    far_first, _, mine, theirs = together(along_by[-1][0], across_by[-1][0], mine, theirs)
    near_second, _ = together(across_by[-1][1], far_first)
    last_first, last_second = across(far_first), along(near_second)
    late = [along_by[-2], across_by[-1], along_by[-1]]
    mine, *theirs = add_both(left, late, (mine, theirs))
    back = [other_core(part) for part in theirs[:-1]]
    last_first, theirs[-1] = together(last_first, theirs[-1])
    last_second, *back = together(last_second, *back, other_core(theirs[-1]))
    (padded,) = call(pad_kernel, [(last_second.shape, BF16)], [last_first])
    last = [other_core(padded), other_core(last_second)]
    (total,) = call(
        join_kernel,
        [((rows_here, width + 128), F32)],
        [whole, info, last_first, last_second, mine, *back],
        {4: 0},
    )
    out = finish((rows_here, width), [whole, info, *last, total])
    return out


def per_device(embeddings, group_of, cluster_id):
    rows_here, width = embeddings.shape
    devices = lax.axis_size("blk") * lax.axis_size("sub") * lax.axis_size("pair")
    small = devices * rows_here * width * 2 <= GATHER_LIMIT
    fits = width % 128 == 0 and rows_here % (64 * PARTS) == 0 and rows_here <= 256
    if small and fits and lax.axis_size("sub") == 2 and lax.axis_size("pair") == 2:
        return by_block(embeddings, group_of, cluster_id)
    return by_group(embeddings, group_of, cluster_id)


def solution(mesh):
    return jax.shard_map(
        per_device,
        mesh=mesh,
        in_specs=(
            P(("island", "blk", "sub", "pair"), None),
            P(("island", "blk", "sub", "pair"), None),
            P(("island", "blk", "sub", "pair")),
        ),
        out_specs=P(("island", "blk", "sub", "pair"), None),
        check_vma=False,
    )
```

```python
import functools

import jax
import jax.numpy as jnp
from jax import lax
from jax.experimental import pallas as pl
from jax.experimental.pallas import tpu as pltpu
from jax.sharding import PartitionSpec as P

F32 = jnp.float32
BF16 = jnp.bfloat16
VMEM_BYTES = 24 * 1024 * 1024
PARTS = 3
LINES = 16
GATHER_LIMIT = 8 * 1024 * 1024


def unit_scale(rows_in):
    wide = rows_in.astype(F32)
    return lax.rsqrt(jnp.sum(wide * wide, axis=1) + 1e-06)


def tile_weights(left_rows, left_clust, left_scale, right_rows, right_clust, right_scale):
    grams = lax.dot_general(
        left_rows, right_rows, (((1,), (1,)), ((), ())), preferred_element_type=F32
    )
    cosine = grams * left_scale[:, None] * right_scale[None, :]
    same = (left_clust[:, None] == right_clust[None, :]).astype(F32)
    return jax.nn.sigmoid(8.0 * cosine - 2.0) * same


def by_group(embeddings, group_of, cluster_id):
    rows_here, width = embeddings.shape
    groups = lax.axis_size("sub") * lax.axis_size("pair")
    capacity = 2 * rows_here // groups
    slots = groups * capacity
    target = group_of[:, 0]
    onehot = (target[:, None] == jnp.arange(groups, dtype=jnp.int32)[None, :]).astype(jnp.int32)
    position = jnp.sum((jnp.cumsum(onehot, axis=0) - onehot) * onehot, axis=1)
    send_rows = jnp.zeros((groups, capacity, width), BF16).at[target, position].set(embeddings)
    send_clust = jnp.full((groups, capacity), -1, jnp.int32).at[target, position].set(cluster_id)
    recv_rows, recv_clust = (
        lax.all_to_all(send_rows, ("sub", "pair"), split_axis=0, concat_axis=0, tiled=True),
        lax.all_to_all(send_clust, ("sub", "pair"), split_axis=0, concat_axis=0, tiled=True),
    )
    own_rows = recv_rows.reshape(slots, width)
    own_clust = recv_clust.reshape(slots)
    own_scale = unit_scale(own_rows)
    piece_rows = lax.all_gather(own_rows, "blk", axis=0, tiled=True)
    piece_clust = lax.all_gather(own_clust, "blk", axis=0, tiled=True)
    weight = tile_weights(
        own_rows, own_clust, own_scale, piece_rows, piece_clust, unit_scale(piece_rows)
    )
    numer = jnp.dot(weight.astype(BF16), piece_rows, preferred_element_type=F32)
    denom = jnp.sum(weight, axis=1)
    result = (numer / denom[:, None]).astype(BF16).reshape(groups, capacity, width)
    returned = lax.all_to_all(result, ("sub", "pair"), split_axis=0, concat_axis=0, tiled=True)
    return returned[target, position]


def diagonal(size):
    shape = (size, size)
    return lax.broadcasted_iota(jnp.int32, shape, 0) == lax.broadcasted_iota(jnp.int32, shape, 1)


def to_column(row):
    size = row.shape[1]
    return jnp.sum(jnp.where(diagonal(size), row, jnp.zeros_like(row)), axis=1, keepdims=True)


def to_row(column):
    size = column.shape[0]
    return jnp.sum(jnp.where(diagonal(size), column, jnp.zeros_like(column)), axis=0, keepdims=True)


def scale_column(rows):
    wide = rows.astype(F32)
    return lax.rsqrt(jnp.sum(wide * wide, axis=1, keepdims=True) + 1e-06)


def first_pack_kernel(rows, first):
    half = rows.shape[0] // 2
    for slab in range(rows.shape[1] // 128):
        first[slab * half : (slab + 1) * half, :] = rows[:half, slab * 128 : (slab + 1) * 128]


def pack_kernel(rows, group, cluster, whole, second):
    rows_here, width = rows.shape
    slabs = width // 128
    half = rows_here // 2
    for slab in range(slabs):
        columns = rows[:, slab * 128 : (slab + 1) * 128]
        whole[slab * rows_here : (slab + 1) * rows_here, :] = columns
        second[slab * half : (slab + 1) * half, :] = columns[half:]
    line_at = lax.broadcasted_iota(jnp.int32, (LINES, 128), 0)
    named = jnp.zeros((LINES, 128), jnp.int32)
    for line in range(4):
        top = line % 2 * half
        part = (group, cluster)[line // 2][:, top : top + half]
        if half < 128:
            part = jnp.concatenate([part, jnp.zeros((1, 128 - half), jnp.int32)], axis=1)
        named = jnp.where(line_at == line, part, named)
    named = named.astype(F32).astype(BF16)
    whole[slabs * rows_here :, :] = named
    second[slabs * half :, :] = named


def pad_kernel(first, out):
    top = first.shape[0]
    out[:top, :] = first[...]
    out[top:, :] = jnp.zeros((out.shape[0] - top, 128), BF16)


def from_slabs(ref, count):
    slabs = [ref[top : top + count, :] for top in range(0, ref.shape[0] // count * count, count)]
    return jnp.concatenate(slabs, axis=1)


def key_rows(ref, half):
    wide = ref[ref.shape[0] - LINES :, :].astype(F32)
    return [
        wide[side : side + 1, :half] * 256.0 + wide[side + 2 : side + 3, :half]
        for side in range(2)
    ]


def key_row(ref, rows_here):
    return jnp.concatenate(key_rows(ref, rows_here // 2), axis=1)


def from_halves(first, second, rows_here):
    half = rows_here // 2
    rows = jnp.concatenate([from_slabs(first, half), from_slabs(second, half)], axis=0)
    return rows, key_row(second, rows_here)


def add_blocks(left, info, blocks, numer, denom):
    key = info[: left.shape[0], 0:1]
    scale = info[: left.shape[0], 1:2]
    right_rows = jnp.concatenate([block[0] for block in blocks], axis=0)
    right_key = jnp.concatenate([block[1] for block in blocks], axis=1)
    right_scale = jnp.concatenate([block[2] for block in blocks], axis=1)
    grams = lax.dot_general(
        left, right_rows, (((1,), (1,)), ((), ())), preferred_element_type=F32
    )
    half = jnp.tanh(grams * scale * right_scale - 1.0)
    weight = jnp.where(key == right_key, 0.5 + 0.5 * half, 0.0)
    add = jnp.dot(weight.astype(BF16), right_rows, preferred_element_type=F32)
    add_denom = jnp.sum(weight, axis=1, keepdims=True)
    if numer is None:
        return add, add_denom
    return numer + add, denom + add_denom


def left_rows(refs, rows_here):
    return jnp.concatenate([from_slabs(ref, rows_here) for ref in refs], axis=0)


def take_blocks(refs, count, rows_here):
    blocks = []
    for _ in range(count):
        rows, key = from_halves(refs.pop(0), refs.pop(0), rows_here)
        blocks.append((rows, key, to_row(scale_column(rows))))
    return blocks


def store_sides(numer, denom, outs):
    rows_here, wide = outs[0].shape
    for side, out in enumerate(outs):
        top = side * rows_here
        out[:, : wide - 128] = numer[top : top + rows_here]
        out[:, wide - 128 :] = jnp.broadcast_to(denom[top : top + rows_here], (rows_here, 128))


def start_kernel(n_blocks, own, other, *refs):
    refs = list(refs)
    rows_here = refs[-1].shape[0] // 2
    left = left_rows((own, other), rows_here)
    key = jnp.concatenate([to_column(key_row(ref, rows_here)) for ref in (own, other)], axis=0)
    scale = scale_column(left)
    info = refs.pop()
    lane = lax.broadcasted_iota(jnp.int32, info.shape, 1)
    info[...] = jnp.where(lane == 0, key, 4.0 * scale)
    first = (left[:rows_here], key_row(own, rows_here), to_row(scale[:rows_here]))
    blocks = [first] + take_blocks(refs, n_blocks, rows_here)
    store_sides(*add_blocks(left, info, blocks, None, None), refs)


def both_kernel(n_blocks, own, other, info, *refs):
    refs = list(refs)
    rows_here = refs[2 * n_blocks].shape[0]
    blocks = take_blocks(refs, n_blocks, rows_here)
    mine_in, theirs_in, mine, *theirs = refs
    wide = mine.shape[1]
    width = wide - 128
    left = left_rows((own, other), rows_here)
    numer = jnp.concatenate([ref[:, :width] for ref in (mine_in, theirs_in)], axis=0)
    denom = jnp.concatenate([ref[:, width : width + 1] for ref in (mine_in, theirs_in)], axis=0)
    numer, denom = add_blocks(left, info, blocks, numer, denom)
    store_sides(numer[:rows_here], denom[:rows_here], [mine])
    denom = denom[rows_here:]
    high = denom.astype(BF16).astype(F32)
    lane = lax.broadcasted_iota(jnp.int32, (rows_here, 128), 1)
    pair = jnp.where(lane == 0, high, denom - high).astype(BF16)
    count = rows_here // len(theirs)
    for part, out in enumerate(theirs):
        top = part * count
        out[:, :width] = numer[rows_here + top : rows_here + top + count].astype(BF16)
        out[:, width:] = pair[top : top + count]


def join_kernel(own, info, first, second, mine, *refs):
    *parts, out = refs
    rows_here, wide = out.shape
    width = wide - 128
    theirs = jnp.concatenate([ref[...] for ref in parts], axis=0)
    pair = theirs[:, width:].astype(F32)
    numer = mine[:, :width] + theirs[:, :width].astype(F32)
    denom = mine[:, width : width + 1] + (pair[:, 0:1] + pair[:, 1:2])
    blocks = take_blocks([first, second], 1, rows_here)
    left = left_rows((own,), rows_here)
    store_sides(*add_blocks(left, info, blocks, numer, denom), [out])


def last_kernel(own, info, first, second, total, out, staged, sems):
    rows_here, width = out.shape
    blocks = take_blocks([first, second], 1, rows_here)
    left = left_rows((own,), rows_here)
    numer, denom = total[:, :width], total[:, width : width + 1]
    numer, denom = add_blocks(left, info, blocks, numer, denom)
    share = 1.0 / denom
    count = rows_here // 4
    copies = []
    for part in range(4):
        rows = slice(part * count, (part + 1) * count)
        staged[rows, :] = (numer[rows] * share[rows]).astype(BF16)
        copies.append(pltpu.make_async_copy(staged.at[rows, :], out.at[rows, :], sems.at[part]))
        copies[-1].start()
    for copy in copies:
        copy.wait()


def whole_in_vmem(count):
    return [pl.BlockSpec(memory_space=pltpu.VMEM)] * count


def call(kernel, shapes, args, aliases={}):
    return pl.pallas_call(
        kernel,
        out_shape=[jax.ShapeDtypeStruct(shape, dtype) for shape, dtype in shapes],
        in_specs=whole_in_vmem(len(args)),
        out_specs=whole_in_vmem(len(shapes)),
        input_output_aliases=aliases,
        compiler_params=pltpu.CompilerParams(vmem_limit_bytes=VMEM_BYTES),
    )(*args)


def start_both(left, right, shape):
    rows_here = shape[0]
    args = list(left) + [half for block in right for half in block]
    shapes = [(shape, F32), (shape, F32), ((2 * rows_here, 128), F32)]
    return call(functools.partial(start_kernel, len(right)), shapes, args)


def add_both(left, right, before):
    args = list(left) + [half for block in right for half in block] + list(before)
    rows_here, wide = before[0].shape
    shapes = [((rows_here, wide), F32)] + [((rows_here // PARTS, wide), BF16)] * PARTS
    kernel = functools.partial(both_kernel, len(right))
    return call(kernel, shapes, args, {len(args) - 2: 0})


def finish(shape, args):
    return pl.pallas_call(
        last_kernel,
        out_shape=jax.ShapeDtypeStruct(shape, BF16),
        in_specs=whole_in_vmem(len(args)),
        out_specs=pl.BlockSpec(memory_space=pl.ANY),
        scratch_shapes=[pltpu.VMEM(shape, BF16), pltpu.SemaphoreType.DMA((4,))],
        compiler_params=pltpu.CompilerParams(vmem_limit_bytes=VMEM_BYTES),
    )(*args)


def ring(size):
    return list(range(size))[::-1]


def together(*arrays):
    return lax.optimization_barrier(arrays)


def by_block(embeddings, group_of, cluster_id):
    rows_here, width = embeddings.shape
    half = rows_here // 2
    slabs = width // 128
    n_blk = lax.axis_size("blk")
    order = ring(n_blk)
    line = (1, rows_here)

    def along(rows):
        hops = [
            (2 * order[i - 1] + core, 2 * order[i] + 1 - core)
            for i in range(n_blk)
            for core in range(2)
        ]
        return lax.ppermute(rows, ("blk", "pair"), hops)

    def across(rows):
        return lax.ppermute(rows, ("sub", "pair"), [(0, 3), (1, 2), (2, 1), (3, 0)])

    def other_core(rows):
        return lax.ppermute(rows, "pair", [(0, 1), (1, 0)])

    (first,) = call(first_pack_kernel, [((slabs * half, 128), BF16)], [embeddings])
    whole, second = call(
        pack_kernel,
        [((slabs * count + LINES, 128), BF16) for count in (rows_here, half)],
        [embeddings, group_of.reshape(line), cluster_id.reshape(line)],
    )
    along_by = [(first, second)]
    across_by = []
    for s in range(1, n_blk):
        moved = [along(piece) for piece in along_by[-1]]
        swapped = [across(piece) for piece in along_by[-1]]
        moved[0], swapped[0] = together(moved[0], swapped[0])
        if s < n_blk - 1:
            moved[1], swapped[1], _ = together(moved[1], swapped[1], moved[0])
        along_by.append(tuple(moved))
        across_by.append(tuple(swapped))
    left = (whole, other_core(whole))
    early = across_by[:-1] + along_by[1:-2]
    mine, theirs, info = start_both(left, early, (rows_here, width + 128))
    left = (*left, info)
    far_first, _, mine, theirs = together(along_by[-1][0], across_by[-1][0], mine, theirs)
    near_second, _ = together(across_by[-1][1], far_first)
    last_first, last_second = across(far_first), along(near_second)
    late = [along_by[-2], across_by[-1], along_by[-1]]
    mine, *theirs = add_both(left, late, (mine, theirs))
    back = [other_core(part) for part in theirs[:-1]]
    last_first, theirs[-1] = together(last_first, theirs[-1])
    last_second, *back = together(last_second, *back, other_core(theirs[-1]))
    (padded,) = call(pad_kernel, [(last_second.shape, BF16)], [last_first])
    last = [other_core(padded), other_core(last_second)]
    (total,) = call(
        join_kernel,
        [((rows_here, width + 128), F32)],
        [whole, info, last_first, last_second, mine, *back],
        {4: 0},
    )
    out = finish((rows_here, width), [whole, info, *last, total])
    return out


def per_device(embeddings, group_of, cluster_id):
    rows_here, width = embeddings.shape
    devices = lax.axis_size("blk") * lax.axis_size("sub") * lax.axis_size("pair")
    small = devices * rows_here * width * 2 <= GATHER_LIMIT
    fits = width % 128 == 0 and rows_here % (64 * PARTS) == 0 and rows_here <= 256
    if small and fits and lax.axis_size("sub") == 2 and lax.axis_size("pair") == 2:
        return by_block(embeddings, group_of, cluster_id)
    return by_group(embeddings, group_of, cluster_id)


def solution(mesh):
    return jax.shard_map(
        per_device,
        mesh=mesh,
        in_specs=(
            P(("island", "blk", "sub", "pair"), None),
            P(("island", "blk", "sub", "pair"), None),
            P(("island", "blk", "sub", "pair")),
        ),
        out_specs=P(("island", "blk", "sub", "pair"), None),
        check_vma=False,
    )
```

```python
import functools

import jax
import jax.numpy as jnp
from jax import lax
from jax.experimental import pallas as pl
from jax.experimental.pallas import tpu as pltpu
from jax.sharding import PartitionSpec as P

F32 = jnp.float32
BF16 = jnp.bfloat16
VMEM_BYTES = 24 * 1024 * 1024
PARTS = 3
LINES = 16
GATHER_LIMIT = 8 * 1024 * 1024


def unit_scale(rows_in):
    wide = rows_in.astype(F32)
    return lax.rsqrt(jnp.sum(wide * wide, axis=1) + 1e-06)


def tile_weights(left_rows, left_clust, left_scale, right_rows, right_clust, right_scale):
    grams = lax.dot_general(
        left_rows, right_rows, (((1,), (1,)), ((), ())), preferred_element_type=F32
    )
    cosine = grams * left_scale[:, None] * right_scale[None, :]
    same = (left_clust[:, None] == right_clust[None, :]).astype(F32)
    return jax.nn.sigmoid(8.0 * cosine - 2.0) * same


def by_group(embeddings, group_of, cluster_id):
    rows_here, width = embeddings.shape
    groups = lax.axis_size("sub") * lax.axis_size("pair")
    capacity = 2 * rows_here // groups
    slots = groups * capacity
    target = group_of[:, 0]
    onehot = (target[:, None] == jnp.arange(groups, dtype=jnp.int32)[None, :]).astype(jnp.int32)
    position = jnp.sum((jnp.cumsum(onehot, axis=0) - onehot) * onehot, axis=1)
    send_rows = jnp.zeros((groups, capacity, width), BF16).at[target, position].set(embeddings)
    send_clust = jnp.full((groups, capacity), -1, jnp.int32).at[target, position].set(cluster_id)
    recv_rows, recv_clust = (
        lax.all_to_all(send_rows, ("sub", "pair"), split_axis=0, concat_axis=0, tiled=True),
        lax.all_to_all(send_clust, ("sub", "pair"), split_axis=0, concat_axis=0, tiled=True),
    )
    own_rows = recv_rows.reshape(slots, width)
    own_clust = recv_clust.reshape(slots)
    own_scale = unit_scale(own_rows)
    piece_rows = lax.all_gather(own_rows, "blk", axis=0, tiled=True)
    piece_clust = lax.all_gather(own_clust, "blk", axis=0, tiled=True)
    weight = tile_weights(
        own_rows, own_clust, own_scale, piece_rows, piece_clust, unit_scale(piece_rows)
    )
    numer = jnp.dot(weight.astype(BF16), piece_rows, preferred_element_type=F32)
    denom = jnp.sum(weight, axis=1)
    result = (numer / denom[:, None]).astype(BF16).reshape(groups, capacity, width)
    returned = lax.all_to_all(result, ("sub", "pair"), split_axis=0, concat_axis=0, tiled=True)
    return returned[target, position]


def diagonal(size):
    shape = (size, size)
    return lax.broadcasted_iota(jnp.int32, shape, 0) == lax.broadcasted_iota(jnp.int32, shape, 1)


def to_column(row):
    size = row.shape[1]
    return jnp.sum(jnp.where(diagonal(size), row, jnp.zeros_like(row)), axis=1, keepdims=True)


def to_row(column):
    size = column.shape[0]
    return jnp.sum(jnp.where(diagonal(size), column, jnp.zeros_like(column)), axis=0, keepdims=True)


def scale_column(rows):
    wide = rows.astype(F32)
    return lax.rsqrt(jnp.sum(wide * wide, axis=1, keepdims=True) + 1e-06)


def first_pack_kernel(rows, first):
    half = rows.shape[0] // 2
    for slab in range(rows.shape[1] // 128):
        first[slab * half : (slab + 1) * half, :] = rows[:half, slab * 128 : (slab + 1) * 128]


def pack_kernel(rows, group, cluster, whole, second):
    rows_here, width = rows.shape
    slabs = width // 128
    half = rows_here // 2
    for slab in range(slabs):
        columns = rows[:, slab * 128 : (slab + 1) * 128]
        whole[slab * rows_here : (slab + 1) * rows_here, :] = columns
        second[slab * half : (slab + 1) * half, :] = columns[half:]
    line_at = lax.broadcasted_iota(jnp.int32, (LINES, 128), 0)
    named = jnp.zeros((LINES, 128), jnp.int32)
    for line in range(4):
        top = line % 2 * half
        part = (group, cluster)[line // 2][:, top : top + half]
        if half < 128:
            part = jnp.concatenate([part, jnp.zeros((1, 128 - half), jnp.int32)], axis=1)
        named = jnp.where(line_at == line, part, named)
    named = named.astype(F32).astype(BF16)
    whole[slabs * rows_here :, :] = named
    second[slabs * half :, :] = named


def pad_kernel(first, out):
    top = first.shape[0]
    out[:top, :] = first[...]
    out[top:, :] = jnp.zeros((out.shape[0] - top, 128), BF16)


def from_slabs(ref, count):
    slabs = [ref[top : top + count, :] for top in range(0, ref.shape[0] // count * count, count)]
    return jnp.concatenate(slabs, axis=1)


def key_row(ref, rows_here, line=0):
    half = rows_here // 2
    wide = ref[ref.shape[0] - LINES :, :].astype(F32)[line : line + 4, :half]
    return jnp.concatenate([wide[0:1] * 256.0 + wide[2:3], wide[1:2] * 256.0 + wide[3:4]], axis=1)


def add_names_kernel(piece, whole, out):
    top = piece.shape[0] - LINES
    out[:top, :] = piece[:top, :]
    lines = piece[top:, :].astype(F32)
    own = whole[whole.shape[0] - LINES :, :].astype(F32)
    out[top:, :] = jnp.concatenate([lines[:4], own[:4], lines[8:]], axis=0).astype(BF16)


def from_halves(first, second, rows_here):
    half = rows_here // 2
    rows = jnp.concatenate([from_slabs(first, half), from_slabs(second, half)], axis=0)
    return rows, key_row(second, rows_here)


def add_blocks(left, info, blocks, numer, denom):
    key = info[: left.shape[0], 0:1]
    scale = info[: left.shape[0], 1:2]
    right_rows = jnp.concatenate([block[0] for block in blocks], axis=0)
    right_key = jnp.concatenate([block[1] for block in blocks], axis=1)
    right_scale = jnp.concatenate([block[2] for block in blocks], axis=1)
    grams = lax.dot_general(
        left, right_rows, (((1,), (1,)), ((), ())), preferred_element_type=F32
    )
    half = jnp.tanh(grams * scale * right_scale - 1.0)
    weight = jnp.where(key == right_key, 0.5 + 0.5 * half, 0.0)
    add = jnp.dot(weight.astype(BF16), right_rows, preferred_element_type=F32)
    add_denom = jnp.sum(weight, axis=1, keepdims=True)
    if numer is None:
        return add, add_denom
    return numer + add, denom + add_denom


def left_rows(refs, rows_here):
    return jnp.concatenate([from_slabs(ref, rows_here) for ref in refs], axis=0)


def take_blocks(refs, count, rows_here):
    blocks = []
    for _ in range(count):
        rows, key = from_halves(refs.pop(0), refs.pop(0), rows_here)
        blocks.append((rows, key, to_row(scale_column(rows))))
    return blocks


def store_sides(numer, denom, outs):
    rows_here, wide = outs[0].shape
    for side, out in enumerate(outs):
        top = side * rows_here
        out[:, : wide - 128] = numer[top : top + rows_here]
        out[:, wide - 128 :] = jnp.broadcast_to(denom[top : top + rows_here], (rows_here, 128))


def start_kernel(n_blocks, own, other, crossed, *refs):
    refs = list(refs)
    rows_here = refs[-1].shape[0] // 2
    raw = crossed[...]
    crossed = (raw, key_row(refs[1], rows_here, 4), to_row(scale_column(raw)))
    left = left_rows((own, other), rows_here)
    key = jnp.concatenate([to_column(key_row(ref, rows_here)) for ref in (own, other)], axis=0)
    scale = scale_column(left)
    info = refs.pop()
    lane = lax.broadcasted_iota(jnp.int32, info.shape, 1)
    info[...] = jnp.where(lane == 0, key, 4.0 * scale)
    first = (left[:rows_here], key_row(own, rows_here), to_row(scale[:rows_here]))
    blocks = [first, crossed] + take_blocks(refs, n_blocks, rows_here)
    store_sides(*add_blocks(left, info, blocks, None, None), refs)


def both_kernel(n_blocks, own, other, info, *refs):
    refs = list(refs)
    rows_here = refs[2 * n_blocks].shape[0]
    blocks = take_blocks(refs, n_blocks, rows_here)
    mine_in, theirs_in, mine, *theirs = refs
    wide = mine.shape[1]
    width = wide - 128
    left = left_rows((own, other), rows_here)
    numer = jnp.concatenate([ref[:, :width] for ref in (mine_in, theirs_in)], axis=0)
    denom = jnp.concatenate([ref[:, width : width + 1] for ref in (mine_in, theirs_in)], axis=0)
    numer, denom = add_blocks(left, info, blocks, numer, denom)
    store_sides(numer[:rows_here], denom[:rows_here], [mine])
    denom = denom[rows_here:]
    high = denom.astype(BF16).astype(F32)
    lane = lax.broadcasted_iota(jnp.int32, (rows_here, 128), 1)
    pair = jnp.where(lane == 0, high, denom - high).astype(BF16)
    count = rows_here // len(theirs)
    for part, out in enumerate(theirs):
        top = part * count
        out[:, :width] = numer[rows_here + top : rows_here + top + count].astype(BF16)
        out[:, width:] = pair[top : top + count]


def join_kernel(own, info, first, second, mine, *refs):
    *parts, out = refs
    rows_here, wide = out.shape
    width = wide - 128
    theirs = jnp.concatenate([ref[...] for ref in parts], axis=0)
    pair = theirs[:, width:].astype(F32)
    numer = mine[:, :width] + theirs[:, :width].astype(F32)
    denom = mine[:, width : width + 1] + (pair[:, 0:1] + pair[:, 1:2])
    blocks = take_blocks([first, second], 1, rows_here)
    left = left_rows((own,), rows_here)
    store_sides(*add_blocks(left, info, blocks, numer, denom), [out])


def last_kernel(own, info, first, second, total, out, staged, sems):
    rows_here, width = out.shape
    blocks = take_blocks([first, second], 1, rows_here)
    left = left_rows((own,), rows_here)
    numer, denom = total[:, :width], total[:, width : width + 1]
    numer, denom = add_blocks(left, info, blocks, numer, denom)
    share = 1.0 / denom
    count = rows_here // 4
    copies = []
    for part in range(4):
        rows = slice(part * count, (part + 1) * count)
        staged[rows, :] = (numer[rows] * share[rows]).astype(BF16)
        copies.append(pltpu.make_async_copy(staged.at[rows, :], out.at[rows, :], sems.at[part]))
        copies[-1].start()
    for copy in copies:
        copy.wait()


def whole_in_vmem(count):
    return [pl.BlockSpec(memory_space=pltpu.VMEM)] * count


def call(kernel, shapes, args, aliases={}):
    return pl.pallas_call(
        kernel,
        out_shape=[jax.ShapeDtypeStruct(shape, dtype) for shape, dtype in shapes],
        in_specs=whole_in_vmem(len(args)),
        out_specs=whole_in_vmem(len(shapes)),
        input_output_aliases=aliases,
        compiler_params=pltpu.CompilerParams(vmem_limit_bytes=VMEM_BYTES),
    )(*args)


def start_both(left, crossed, right, shape):
    rows_here = shape[0]
    args = [*left, crossed] + [half for block in right for half in block]
    shapes = [(shape, F32), (shape, F32), ((2 * rows_here, 128), F32)]
    return call(functools.partial(start_kernel, len(right)), shapes, args)


def add_both(left, right, before):
    args = list(left) + [half for block in right for half in block] + list(before)
    rows_here, wide = before[0].shape
    shapes = [((rows_here, wide), F32)] + [((rows_here // PARTS, wide), BF16)] * PARTS
    kernel = functools.partial(both_kernel, len(right))
    return call(kernel, shapes, args, {len(args) - 2: 0})


def finish(shape, args):
    return pl.pallas_call(
        last_kernel,
        out_shape=jax.ShapeDtypeStruct(shape, BF16),
        in_specs=whole_in_vmem(len(args)),
        out_specs=pl.BlockSpec(memory_space=pl.ANY),
        scratch_shapes=[pltpu.VMEM(shape, BF16), pltpu.SemaphoreType.DMA((4,))],
        compiler_params=pltpu.CompilerParams(vmem_limit_bytes=VMEM_BYTES),
    )(*args)


def folded_ring(size):
    return list(range(0, size, 2)) + list(range(1, size, 2))[::-1]


def together(*arrays):
    return lax.optimization_barrier(arrays)


def by_block(embeddings, group_of, cluster_id):
    rows_here, width = embeddings.shape
    half = rows_here // 2
    slabs = width // 128
    n_blk = lax.axis_size("blk")
    order = folded_ring(n_blk)
    line = (1, rows_here)

    def along(rows):
        hops = [
            (2 * order[i - 1] + core, 2 * order[i] + 1 - core)
            for i in range(n_blk)
            for core in range(2)
        ]
        return lax.ppermute(rows, ("blk", "pair"), hops)

    def across(rows):
        return lax.ppermute(rows, ("sub", "pair"), [(0, 3), (1, 2), (2, 1), (3, 0)])

    def other_core(rows):
        return lax.ppermute(rows, "pair", [(0, 1), (1, 0)])

    (first,) = call(first_pack_kernel, [((slabs * half, 128), BF16)], [embeddings])
    whole, second = call(
        pack_kernel,
        [((slabs * count + LINES, 128), BF16) for count in (rows_here, half)],
        [embeddings, group_of.reshape(line), cluster_id.reshape(line)],
    )
    crossed = across(embeddings)
    moved = [along(first), along(second)]
    moved[1], crossed, _ = together(moved[1], crossed, moved[0])
    (named,) = call(add_names_kernel, [(second.shape, BF16)], [moved[1], whole])
    along_by = [(first, second), (moved[0], named)]
    across_by = [crossed]
    for s in range(2, n_blk):
        moved = [along(piece) for piece in along_by[-1]]
        swapped = [across(piece) for piece in along_by[-1]]
        moved[0], swapped[0] = together(moved[0], swapped[0])
        if s < n_blk - 1:
            moved[1], swapped[1], _ = together(moved[1], swapped[1], moved[0])
        along_by.append(tuple(moved))
        across_by.append(tuple(swapped))
    left = (whole, other_core(whole))
    early = across_by[1:-1] + along_by[1:-2]
    mine, theirs, info = start_both(left, crossed, early, (rows_here, width + 128))
    left = (*left, info)
    far_first, _, mine, theirs = together(along_by[-1][0], across_by[-1][0], mine, theirs)
    near_second, _ = together(across_by[-1][1], far_first)
    last_first, last_second = across(far_first), along(near_second)
    late = [along_by[-2], across_by[-1], along_by[-1]]
    mine, *theirs = add_both(left, late, (mine, theirs))
    back = [other_core(part) for part in theirs[:-1]]
    last_first, theirs[-1] = together(last_first, theirs[-1])
    last_second, *back = together(last_second, *back, other_core(theirs[-1]))
    (padded,) = call(pad_kernel, [(last_second.shape, BF16)], [last_first])
    last = [other_core(padded), other_core(last_second)]
    (total,) = call(
        join_kernel,
        [((rows_here, width + 128), F32)],
        [whole, info, last_first, last_second, mine, *back],
        {4: 0},
    )
    out = finish((rows_here, width), [whole, info, *last, total])
    return out


def per_device(embeddings, group_of, cluster_id):
    rows_here, width = embeddings.shape
    devices = lax.axis_size("blk") * lax.axis_size("sub") * lax.axis_size("pair")
    small = devices * rows_here * width * 2 <= GATHER_LIMIT and lax.axis_size("blk") > 3
    fits = width % 128 == 0 and rows_here % (64 * PARTS) == 0 and rows_here <= 256
    if small and fits and lax.axis_size("sub") == 2 and lax.axis_size("pair") == 2:
        return by_block(embeddings, group_of, cluster_id)
    return by_group(embeddings, group_of, cluster_id)


def solution(mesh):
    return jax.shard_map(
        per_device,
        mesh=mesh,
        in_specs=(
            P(("island", "blk", "sub", "pair"), None),
            P(("island", "blk", "sub", "pair"), None),
            P(("island", "blk", "sub", "pair")),
        ),
        out_specs=P(("island", "blk", "sub", "pair"), None),
        check_vma=False,
    )
```

```python
import functools

import jax
import jax.numpy as jnp
from jax import lax
from jax.experimental import pallas as pl
from jax.experimental.pallas import tpu as pltpu
from jax.sharding import PartitionSpec as P

F32 = jnp.float32
BF16 = jnp.bfloat16
VMEM_BYTES = 24 * 1024 * 1024
PARTS = 3
LINES = 16
GATHER_LIMIT = 8 * 1024 * 1024


def unit_scale(rows_in):
    wide = rows_in.astype(F32)
    return lax.rsqrt(jnp.sum(wide * wide, axis=1) + 1e-06)


def tile_weights(left_rows, left_clust, left_scale, right_rows, right_clust, right_scale):
    grams = lax.dot_general(
        left_rows, right_rows, (((1,), (1,)), ((), ())), preferred_element_type=F32
    )
    cosine = grams * left_scale[:, None] * right_scale[None, :]
    same = (left_clust[:, None] == right_clust[None, :]).astype(F32)
    return jax.nn.sigmoid(8.0 * cosine - 2.0) * same


def by_group(embeddings, group_of, cluster_id):
    rows_here, width = embeddings.shape
    groups = lax.axis_size("sub") * lax.axis_size("pair")
    capacity = 2 * rows_here // groups
    slots = groups * capacity
    target = group_of[:, 0]
    onehot = (target[:, None] == jnp.arange(groups, dtype=jnp.int32)[None, :]).astype(jnp.int32)
    position = jnp.sum((jnp.cumsum(onehot, axis=0) - onehot) * onehot, axis=1)
    send_rows = jnp.zeros((groups, capacity, width), BF16).at[target, position].set(embeddings)
    send_clust = jnp.full((groups, capacity), -1, jnp.int32).at[target, position].set(cluster_id)
    recv_rows, recv_clust = (
        lax.all_to_all(send_rows, ("sub", "pair"), split_axis=0, concat_axis=0, tiled=True),
        lax.all_to_all(send_clust, ("sub", "pair"), split_axis=0, concat_axis=0, tiled=True),
    )
    own_rows = recv_rows.reshape(slots, width)
    own_clust = recv_clust.reshape(slots)
    own_scale = unit_scale(own_rows)
    piece_rows = lax.all_gather(own_rows, "blk", axis=0, tiled=True)
    piece_clust = lax.all_gather(own_clust, "blk", axis=0, tiled=True)
    weight = tile_weights(
        own_rows, own_clust, own_scale, piece_rows, piece_clust, unit_scale(piece_rows)
    )
    numer = jnp.dot(weight.astype(BF16), piece_rows, preferred_element_type=F32)
    denom = jnp.sum(weight, axis=1)
    result = (numer / denom[:, None]).astype(BF16).reshape(groups, capacity, width)
    returned = lax.all_to_all(result, ("sub", "pair"), split_axis=0, concat_axis=0, tiled=True)
    return returned[target, position]


def diagonal(size):
    shape = (size, size)
    return lax.broadcasted_iota(jnp.int32, shape, 0) == lax.broadcasted_iota(jnp.int32, shape, 1)


def to_column(row):
    size = row.shape[1]
    return jnp.sum(jnp.where(diagonal(size), row, jnp.zeros_like(row)), axis=1, keepdims=True)


def to_row(column):
    size = column.shape[0]
    return jnp.sum(jnp.where(diagonal(size), column, jnp.zeros_like(column)), axis=0, keepdims=True)


def scale_column(rows):
    wide = rows.astype(F32)
    return lax.rsqrt(jnp.sum(wide * wide, axis=1, keepdims=True) + 1e-06)


def first_pack_kernel(rows, first):
    half = rows.shape[0] // 2
    for slab in range(rows.shape[1] // 128):
        first[slab * half : (slab + 1) * half, :] = rows[:half, slab * 128 : (slab + 1) * 128]


def pack_kernel(rows, group, cluster, whole, second):
    rows_here, width = rows.shape
    slabs = width // 128
    half = rows_here // 2
    for slab in range(slabs):
        columns = rows[:, slab * 128 : (slab + 1) * 128]
        whole[slab * rows_here : (slab + 1) * rows_here, :] = columns
        second[slab * half : (slab + 1) * half, :] = columns[half:]
    line_at = lax.broadcasted_iota(jnp.int32, (LINES, 128), 0)
    named = jnp.zeros((LINES, 128), jnp.int32)
    for line in range(4):
        top = line % 2 * half
        part = (group, cluster)[line // 2][:, top : top + half]
        if half < 128:
            part = jnp.concatenate([part, jnp.zeros((1, 128 - half), jnp.int32)], axis=1)
        named = jnp.where(line_at == line, part, named)
    named = named.astype(F32).astype(BF16)
    whole[slabs * rows_here :, :] = named
    second[slabs * half :, :] = named


def from_slabs(ref, count):
    slabs = [ref[top : top + count, :] for top in range(0, ref.shape[0] // count * count, count)]
    return jnp.concatenate(slabs, axis=1)


def key_rows(ref, half):
    wide = ref[ref.shape[0] - LINES :, :].astype(F32)
    return [
        wide[side : side + 1, :half] * 256.0 + wide[side + 2 : side + 3, :half]
        for side in range(2)
    ]


def key_row(ref, rows_here):
    return jnp.concatenate(key_rows(ref, rows_here // 2), axis=1)


def from_halves(first, second, rows_here):
    half = rows_here // 2
    rows = jnp.concatenate([from_slabs(first, half), from_slabs(second, half)], axis=0)
    return rows, key_row(second, rows_here)


def add_blocks(left, info, blocks, numer, denom):
    key = info[: left.shape[0], 0:1]
    scale = info[: left.shape[0], 1:2]
    right_rows = jnp.concatenate([block[0] for block in blocks], axis=0)
    right_key = jnp.concatenate([block[1] for block in blocks], axis=1)
    right_scale = jnp.concatenate([block[2] for block in blocks], axis=1)
    grams = lax.dot_general(
        left, right_rows, (((1,), (1,)), ((), ())), preferred_element_type=F32
    )
    half = jnp.tanh(grams * scale * right_scale - 1.0)
    weight = jnp.where(key == right_key, 0.5 + 0.5 * half, 0.0)
    add = jnp.dot(weight.astype(BF16), right_rows, preferred_element_type=F32)
    add_denom = jnp.sum(weight, axis=1, keepdims=True)
    if numer is None:
        return add, add_denom
    return numer + add, denom + add_denom


def left_rows(refs, rows_here):
    return jnp.concatenate([from_slabs(ref, rows_here) for ref in refs], axis=0)


def take_blocks(refs, count, rows_here):
    blocks = []
    for _ in range(count):
        rows, key = from_halves(refs.pop(0), refs.pop(0), rows_here)
        blocks.append((rows, key, to_row(scale_column(rows))))
    return blocks


def store_sides(numer, denom, outs):
    rows_here, wide = outs[0].shape
    for side, out in enumerate(outs):
        top = side * rows_here
        out[:, : wide - 128] = numer[top : top + rows_here]
        out[:, wide - 128 :] = jnp.broadcast_to(denom[top : top + rows_here], (rows_here, 128))


def store_theirs(numer, denom, outs):
    high = denom.astype(BF16).astype(F32)
    lane = lax.broadcasted_iota(jnp.int32, (denom.shape[0], 128), 1)
    pair = jnp.where(lane == 0, high, denom - high).astype(BF16)
    count, wide = outs[0].shape
    for part, out in enumerate(outs):
        rows = slice(part * count, (part + 1) * count)
        out[:, : wide - 128] = numer[rows].astype(BF16)
        out[:, wide - 128 :] = pair[rows]


def add_theirs(mine, parts):
    width = mine.shape[1] - 128
    theirs = jnp.concatenate([ref[...] for ref in parts], axis=0)
    pair = theirs[:, width:].astype(F32)
    numer = mine[:, :width] + theirs[:, :width].astype(F32)
    return numer, mine[:, width : width + 1] + (pair[:, 0:1] + pair[:, 1:2])


def back_kernel(near_first, near_second, over_first, over_second, *refs):
    refs = list(refs)
    rows_here = refs[4].shape[0]
    blocks = take_blocks(refs, 2, rows_here)
    mine, *theirs = refs
    sides = [
        from_halves(near_first, near_second, rows_here),
        from_halves(over_first, over_second, rows_here),
    ]
    left = jnp.concatenate([side[0] for side in sides], axis=0)
    key = jnp.concatenate([to_column(side[1]) for side in sides], axis=0)
    lane = lax.broadcasted_iota(jnp.int32, (2 * rows_here, 128), 1)
    info = jnp.where(lane == 0, key, 4.0 * scale_column(left))
    numer, denom = add_blocks(left, info, blocks, None, None)
    store_sides(numer[:rows_here], denom[:rows_here], [mine])
    store_theirs(numer[rows_here:], denom[rows_here:], theirs)


def back_sum_kernel(mine, *refs):
    *parts, out = refs
    rows_here = mine.shape[0]
    half = rows_here // 2
    numer, denom = add_theirs(mine, parts)
    slabs = numer.shape[1] // 128
    for slab in range(slabs):
        out[slab * rows_here : (slab + 1) * rows_here, :] = numer[
            :, slab * 128 : (slab + 1) * 128
        ].astype(BF16)
    high = denom.astype(BF16).astype(F32)
    line_at = lax.broadcasted_iota(jnp.int32, (LINES, 128), 0)
    lines = jnp.zeros((LINES, 128), F32)
    for kind, column in enumerate((high, denom - high)):
        row = to_row(column)
        for side in range(2):
            part = row[:, side * half : (side + 1) * half]
            if half < 128:
                part = jnp.concatenate([part, jnp.zeros((1, 128 - half), F32)], axis=1)
            lines = jnp.where(line_at == 2 * kind + side, part, lines)
    out[slabs * rows_here :, :] = lines.astype(BF16)


def start_kernel(n_blocks, own, other, *refs):
    refs = list(refs)
    rows_here = refs[-1].shape[0] // 2
    left = left_rows((own, other), rows_here)
    key = jnp.concatenate([to_column(key_row(ref, rows_here)) for ref in (own, other)], axis=0)
    scale = scale_column(left)
    info = refs.pop()
    lane = lax.broadcasted_iota(jnp.int32, info.shape, 1)
    info[...] = jnp.where(lane == 0, key, 4.0 * scale)
    first = (left[:rows_here], key_row(own, rows_here), to_row(scale[:rows_here]))
    blocks = [first] + take_blocks(refs, n_blocks, rows_here)
    store_sides(*add_blocks(left, info, blocks, None, None), refs)


def both_kernel(n_blocks, own, other, info, *refs):
    refs = list(refs)
    rows_here = refs[2 * n_blocks].shape[0]
    blocks = take_blocks(refs, n_blocks, rows_here)
    mine_in, theirs_in, mine, *theirs = refs
    wide = mine.shape[1]
    width = wide - 128
    left = left_rows((own, other), rows_here)
    numer = jnp.concatenate([ref[:, :width] for ref in (mine_in, theirs_in)], axis=0)
    denom = jnp.concatenate([ref[:, width : width + 1] for ref in (mine_in, theirs_in)], axis=0)
    numer, denom = add_blocks(left, info, blocks, numer, denom)
    store_sides(numer[:rows_here], denom[:rows_here], [mine])
    store_theirs(numer[rows_here:], denom[rows_here:], theirs)


def last_kernel(mine, returned, *refs):
    *parts, out, staged, sems = refs
    rows_here, width = out.shape
    half = rows_here // 2
    numer, denom = add_theirs(mine, parts)
    numer = numer + from_slabs(returned, rows_here).astype(F32)
    lines = returned[returned.shape[0] - LINES :, :].astype(F32)[:4, :half]
    total = lines[0:2] + lines[2:4]
    denom = denom + to_column(jnp.concatenate([total[0:1], total[1:2]], axis=1))
    share = 1.0 / denom
    count = rows_here // 4
    copies = []
    for part in range(4):
        rows = slice(part * count, (part + 1) * count)
        staged[rows, :] = (numer[rows] * share[rows]).astype(BF16)
        copies.append(pltpu.make_async_copy(staged.at[rows, :], out.at[rows, :], sems.at[part]))
        copies[-1].start()
    for copy in copies:
        copy.wait()


def whole_in_vmem(count):
    return [pl.BlockSpec(memory_space=pltpu.VMEM)] * count


def call(kernel, shapes, args, aliases={}):
    return pl.pallas_call(
        kernel,
        out_shape=[jax.ShapeDtypeStruct(shape, dtype) for shape, dtype in shapes],
        in_specs=whole_in_vmem(len(args)),
        out_specs=whole_in_vmem(len(shapes)),
        input_output_aliases=aliases,
        compiler_params=pltpu.CompilerParams(vmem_limit_bytes=VMEM_BYTES),
    )(*args)


def start_both(left, right, shape):
    rows_here = shape[0]
    args = list(left) + [half for block in right for half in block]
    shapes = [(shape, F32), (shape, F32), ((2 * rows_here, 128), F32)]
    return call(functools.partial(start_kernel, len(right)), shapes, args)


def add_both(left, right, before):
    args = list(left) + [half for block in right for half in block] + list(before)
    rows_here, wide = before[0].shape
    shapes = [((rows_here, wide), F32)] + [((rows_here // PARTS, wide), BF16)] * PARTS
    kernel = functools.partial(both_kernel, len(right))
    return call(kernel, shapes, args, {len(args) - 2: 0})


def finish(shape, args):
    return pl.pallas_call(
        last_kernel,
        out_shape=jax.ShapeDtypeStruct(shape, BF16),
        in_specs=whole_in_vmem(len(args)),
        out_specs=pl.BlockSpec(memory_space=pl.ANY),
        scratch_shapes=[pltpu.VMEM(shape, BF16), pltpu.SemaphoreType.DMA((4,))],
        compiler_params=pltpu.CompilerParams(vmem_limit_bytes=VMEM_BYTES),
    )(*args)


def folded_ring(size):
    return list(range(0, size, 2)) + list(range(1, size, 2))[::-1]


def together(*arrays):
    return lax.optimization_barrier(arrays)


def by_block(embeddings, group_of, cluster_id):
    rows_here, width = embeddings.shape
    half = rows_here // 2
    slabs = width // 128
    n_blk = lax.axis_size("blk")
    order = folded_ring(n_blk)
    line = (1, rows_here)

    def along(rows):
        hops = [
            (2 * order[i - 1] + core, 2 * order[i] + 1 - core)
            for i in range(n_blk)
            for core in range(2)
        ]
        return lax.ppermute(rows, ("blk", "pair"), hops)

    def back_along(rows):
        hops = [
            (2 * order[i] + core, 2 * order[i - 1] + 1 - core)
            for i in range(n_blk)
            for core in range(2)
        ]
        return lax.ppermute(rows, ("blk", "pair"), hops)

    def across(rows):
        return lax.ppermute(rows, ("sub", "pair"), [(0, 3), (1, 2), (2, 1), (3, 0)])

    def other_core(rows):
        return lax.ppermute(rows, "pair", [(0, 1), (1, 0)])

    (first,) = call(first_pack_kernel, [((slabs * half, 128), BF16)], [embeddings])
    whole, second = call(
        pack_kernel,
        [((slabs * count + LINES, 128), BF16) for count in (rows_here, half)],
        [embeddings, group_of.reshape(line), cluster_id.reshape(line)],
    )
    along_by = [(first, second)]
    across_by = []
    for s in range(1, n_blk - 1):
        moved = [along(piece) for piece in along_by[-1]]
        swapped = [across(piece) for piece in along_by[-1]]
        moved[0], swapped[0] = together(moved[0], swapped[0])
        if s != 2:
            moved[1], swapped[1], _ = together(moved[1], swapped[1], moved[0])
        else:
            moved[1], swapped[1], to_return, _ = together(
                moved[1], swapped[1], to_return, moved[0]
            )
        if s == 1:
            over = [other_core(piece) for piece in moved]
            near_sum, *over_sum = call(
                back_kernel,
                [((rows_here, width + 128), F32)]
                + [((rows_here // PARTS, width + 128), BF16)] * PARTS,
                [*moved, *over, first, second, *swapped],
            )
            (to_return,) = call(
                back_sum_kernel,
                [((slabs * rows_here + LINES, 128), BF16)],
                [near_sum, *[other_core(part) for part in over_sum]],
            )
        along_by.append(tuple(moved))
        across_by.append(tuple(swapped))
    returned = back_along(to_return)
    across_by.append(tuple(across(piece) for piece in along_by[-1]))
    left = (whole, other_core(whole))
    early = across_by[:-1] + along_by[1:-1]
    mine, theirs, info = start_both(left, early, (rows_here, width + 128))
    late = [along_by[-1], across_by[-1]]
    mine, *theirs = add_both((*left, info), late, (mine, theirs))
    out = finish(
        (rows_here, width), [mine, returned, *[other_core(part) for part in theirs]]
    )
    return out


def per_device(embeddings, group_of, cluster_id):
    rows_here, width = embeddings.shape
    devices = lax.axis_size("blk") * lax.axis_size("sub") * lax.axis_size("pair")
    small = devices * rows_here * width * 2 <= GATHER_LIMIT and lax.axis_size("blk") > 3
    fits = width % 128 == 0 and rows_here % (64 * PARTS) == 0 and rows_here <= 256
    if small and fits and lax.axis_size("sub") == 2 and lax.axis_size("pair") == 2:
        return by_block(embeddings, group_of, cluster_id)
    return by_group(embeddings, group_of, cluster_id)


def solution(mesh):
    return jax.shard_map(
        per_device,
        mesh=mesh,
        in_specs=(
            P(("island", "blk", "sub", "pair"), None),
            P(("island", "blk", "sub", "pair"), None),
            P(("island", "blk", "sub", "pair")),
        ),
        out_specs=P(("island", "blk", "sub", "pair"), None),
        check_vma=False,
    )
```

```python
import functools

import jax
import jax.numpy as jnp
from jax import lax
from jax.experimental import pallas as pl
from jax.experimental.pallas import tpu as pltpu
from jax.sharding import PartitionSpec as P

F32 = jnp.float32
BF16 = jnp.bfloat16
VMEM_BYTES = 24 * 1024 * 1024
PARTS = 3
LINES = 16
GATHER_LIMIT = 8 * 1024 * 1024


def unit_scale(rows_in):
    wide = rows_in.astype(F32)
    return lax.rsqrt(jnp.sum(wide * wide, axis=1) + 1e-06)


def tile_weights(left_rows, left_clust, left_scale, right_rows, right_clust, right_scale):
    grams = lax.dot_general(
        left_rows, right_rows, (((1,), (1,)), ((), ())), preferred_element_type=F32
    )
    cosine = grams * left_scale[:, None] * right_scale[None, :]
    same = (left_clust[:, None] == right_clust[None, :]).astype(F32)
    return jax.nn.sigmoid(8.0 * cosine - 2.0) * same


def by_group(embeddings, group_of, cluster_id):
    rows_here, width = embeddings.shape
    groups = lax.axis_size("sub") * lax.axis_size("pair")
    capacity = 2 * rows_here // groups
    slots = groups * capacity
    target = group_of[:, 0]
    onehot = (target[:, None] == jnp.arange(groups, dtype=jnp.int32)[None, :]).astype(jnp.int32)
    position = jnp.sum((jnp.cumsum(onehot, axis=0) - onehot) * onehot, axis=1)
    send_rows = jnp.zeros((groups, capacity, width), BF16).at[target, position].set(embeddings)
    send_clust = jnp.full((groups, capacity), -1, jnp.int32).at[target, position].set(cluster_id)
    recv_rows, recv_clust = (
        lax.all_to_all(send_rows, ("sub", "pair"), split_axis=0, concat_axis=0, tiled=True),
        lax.all_to_all(send_clust, ("sub", "pair"), split_axis=0, concat_axis=0, tiled=True),
    )
    own_rows = recv_rows.reshape(slots, width)
    own_clust = recv_clust.reshape(slots)
    own_scale = unit_scale(own_rows)
    piece_rows = lax.all_gather(own_rows, "blk", axis=0, tiled=True)
    piece_clust = lax.all_gather(own_clust, "blk", axis=0, tiled=True)
    weight = tile_weights(
        own_rows, own_clust, own_scale, piece_rows, piece_clust, unit_scale(piece_rows)
    )
    numer = jnp.dot(weight.astype(BF16), piece_rows, preferred_element_type=F32)
    denom = jnp.sum(weight, axis=1)
    result = (numer / denom[:, None]).astype(BF16).reshape(groups, capacity, width)
    returned = lax.all_to_all(result, ("sub", "pair"), split_axis=0, concat_axis=0, tiled=True)
    return returned[target, position]


def diagonal(size):
    shape = (size, size)
    return lax.broadcasted_iota(jnp.int32, shape, 0) == lax.broadcasted_iota(jnp.int32, shape, 1)


def to_column(row):
    size = row.shape[1]
    return jnp.sum(jnp.where(diagonal(size), row, jnp.zeros_like(row)), axis=1, keepdims=True)


def to_row(column):
    size = column.shape[0]
    return jnp.sum(jnp.where(diagonal(size), column, jnp.zeros_like(column)), axis=0, keepdims=True)


def scale_column(rows):
    wide = rows.astype(F32)
    return lax.rsqrt(jnp.sum(wide * wide, axis=1, keepdims=True) + 1e-06)


def first_pack_kernel(rows, first):
    half = rows.shape[0] // 2
    for slab in range(rows.shape[1] // 128):
        first[slab * half : (slab + 1) * half, :] = rows[:half, slab * 128 : (slab + 1) * 128]


def pack_kernel(rows, group, cluster, whole, second):
    rows_here, width = rows.shape
    slabs = width // 128
    half = rows_here // 2
    for slab in range(slabs):
        columns = rows[:, slab * 128 : (slab + 1) * 128]
        whole[slab * rows_here : (slab + 1) * rows_here, :] = columns
        second[slab * half : (slab + 1) * half, :] = columns[half:]
    line_at = lax.broadcasted_iota(jnp.int32, (LINES, 128), 0)
    named = jnp.zeros((LINES, 128), jnp.int32)
    for line in range(4):
        top = line % 2 * half
        part = (group, cluster)[line // 2][:, top : top + half]
        if half < 128:
            part = jnp.concatenate([part, jnp.zeros((1, 128 - half), jnp.int32)], axis=1)
        named = jnp.where(line_at == line, part, named)
    named = named.astype(F32).astype(BF16)
    whole[slabs * rows_here :, :] = named
    second[slabs * half :, :] = named


def from_slabs(ref, count):
    slabs = [ref[top : top + count, :] for top in range(0, ref.shape[0] // count * count, count)]
    return jnp.concatenate(slabs, axis=1)


def key_rows(ref, half):
    wide = ref[ref.shape[0] - LINES :, :].astype(F32)
    return [
        wide[side : side + 1, :half] * 256.0 + wide[side + 2 : side + 3, :half]
        for side in range(2)
    ]


def key_row(ref, rows_here):
    return jnp.concatenate(key_rows(ref, rows_here // 2), axis=1)


def from_halves(first, second, rows_here):
    half = rows_here // 2
    rows = jnp.concatenate([from_slabs(first, half), from_slabs(second, half)], axis=0)
    return rows, key_row(second, rows_here)


def add_blocks(left, info, blocks, numer, denom):
    key = info[: left.shape[0], 0:1]
    scale = info[: left.shape[0], 1:2]
    right_rows = jnp.concatenate([block[0] for block in blocks], axis=0)
    right_key = jnp.concatenate([block[1] for block in blocks], axis=1)
    right_scale = jnp.concatenate([block[2] for block in blocks], axis=1)
    grams = lax.dot_general(
        left, right_rows, (((1,), (1,)), ((), ())), preferred_element_type=F32
    )
    half = jnp.tanh(grams * scale * right_scale - 1.0)
    weight = jnp.where(key == right_key, 0.5 + 0.5 * half, 0.0)
    add = jnp.dot(weight.astype(BF16), right_rows, preferred_element_type=F32)
    add_denom = jnp.sum(weight, axis=1, keepdims=True)
    if numer is None:
        return add, add_denom
    return numer + add, denom + add_denom


def left_rows(refs, rows_here):
    return jnp.concatenate([from_slabs(ref, rows_here) for ref in refs], axis=0)


def take_blocks(refs, count, rows_here):
    blocks = []
    for _ in range(count):
        rows, key = from_halves(refs.pop(0), refs.pop(0), rows_here)
        blocks.append((rows, key, to_row(scale_column(rows))))
    return blocks


def store_sides(numer, denom, outs):
    rows_here, wide = outs[0].shape
    for side, out in enumerate(outs):
        top = side * rows_here
        out[:, : wide - 128] = numer[top : top + rows_here]
        out[:, wide - 128 :] = jnp.broadcast_to(denom[top : top + rows_here], (rows_here, 128))


def store_theirs(numer, denom, outs):
    high = denom.astype(BF16).astype(F32)
    lane = lax.broadcasted_iota(jnp.int32, (denom.shape[0], 128), 1)
    pair = jnp.where(lane == 0, high, denom - high).astype(BF16)
    count, wide = outs[0].shape
    for part, out in enumerate(outs):
        rows = slice(part * count, (part + 1) * count)
        out[:, : wide - 128] = numer[rows].astype(BF16)
        out[:, wide - 128 :] = pair[rows]


def add_theirs(mine, parts):
    width = mine.shape[1] - 128
    theirs = jnp.concatenate([ref[...] for ref in parts], axis=0)
    pair = theirs[:, width:].astype(F32)
    numer = mine[:, :width] + theirs[:, :width].astype(F32)
    return numer, mine[:, width : width + 1] + (pair[:, 0:1] + pair[:, 1:2])


def back_kernel(near_first, near_second, over_first, over_second, *refs):
    refs = list(refs)
    rows_here = refs[4].shape[0]
    blocks = take_blocks(refs, 2, rows_here)
    mine, *theirs = refs
    sides = [
        from_halves(near_first, near_second, rows_here),
        from_halves(over_first, over_second, rows_here),
    ]
    left = jnp.concatenate([side[0] for side in sides], axis=0)
    key = jnp.concatenate([to_column(side[1]) for side in sides], axis=0)
    lane = lax.broadcasted_iota(jnp.int32, (2 * rows_here, 128), 1)
    info = jnp.where(lane == 0, key, 4.0 * scale_column(left))
    numer, denom = add_blocks(left, info, blocks, None, None)
    store_sides(numer[:rows_here], denom[:rows_here], [mine])
    store_theirs(numer[rows_here:], denom[rows_here:], theirs)


def back_sum_kernel(mine, *refs):
    *parts, out = refs
    rows_here = mine.shape[0]
    half = rows_here // 2
    numer, denom = add_theirs(mine, parts)
    slabs = numer.shape[1] // 128
    for slab in range(slabs):
        out[slab * rows_here : (slab + 1) * rows_here, :] = numer[
            :, slab * 128 : (slab + 1) * 128
        ].astype(BF16)
    high = denom.astype(BF16).astype(F32)
    line_at = lax.broadcasted_iota(jnp.int32, (LINES, 128), 0)
    lines = jnp.zeros((LINES, 128), F32)
    for kind, column in enumerate((high, denom - high)):
        row = to_row(column)
        for side in range(2):
            part = row[:, side * half : (side + 1) * half]
            if half < 128:
                part = jnp.concatenate([part, jnp.zeros((1, 128 - half), F32)], axis=1)
            lines = jnp.where(line_at == 2 * kind + side, part, lines)
    out[slabs * rows_here :, :] = lines.astype(BF16)


def start_kernel(n_blocks, own, other, *refs):
    refs = list(refs)
    rows_here = refs[-1].shape[0] // 2
    left = left_rows((own, other), rows_here)
    key = jnp.concatenate([to_column(key_row(ref, rows_here)) for ref in (own, other)], axis=0)
    scale = scale_column(left)
    info = refs.pop()
    lane = lax.broadcasted_iota(jnp.int32, info.shape, 1)
    info[...] = jnp.where(lane == 0, key, 4.0 * scale)
    first = (left[:rows_here], key_row(own, rows_here), to_row(scale[:rows_here]))
    blocks = [first] + take_blocks(refs, n_blocks, rows_here)
    store_sides(*add_blocks(left, info, blocks, None, None), refs)


def both_kernel(n_blocks, own, other, info, *refs):
    refs = list(refs)
    rows_here = refs[2 * n_blocks].shape[0]
    blocks = take_blocks(refs, n_blocks, rows_here)
    mine_in, theirs_in, mine, *theirs = refs
    wide = mine.shape[1]
    width = wide - 128
    left = left_rows((own, other), rows_here)
    numer = jnp.concatenate([ref[:, :width] for ref in (mine_in, theirs_in)], axis=0)
    denom = jnp.concatenate([ref[:, width : width + 1] for ref in (mine_in, theirs_in)], axis=0)
    numer, denom = add_blocks(left, info, blocks, numer, denom)
    store_sides(numer[:rows_here], denom[:rows_here], [mine])
    store_theirs(numer[rows_here:], denom[rows_here:], theirs)


def last_kernel(mine, returned, *refs):
    *parts, out, staged, sems = refs
    rows_here, width = out.shape
    half = rows_here // 2
    numer, denom = add_theirs(mine, parts)
    numer = numer + from_slabs(returned, rows_here).astype(F32)
    lines = returned[returned.shape[0] - LINES :, :].astype(F32)[:4, :half]
    total = lines[0:2] + lines[2:4]
    denom = denom + to_column(jnp.concatenate([total[0:1], total[1:2]], axis=1))
    share = 1.0 / denom
    count = rows_here // 4
    copies = []
    for part in range(4):
        rows = slice(part * count, (part + 1) * count)
        staged[rows, :] = (numer[rows] * share[rows]).astype(BF16)
        copies.append(pltpu.make_async_copy(staged.at[rows, :], out.at[rows, :], sems.at[part]))
        copies[-1].start()
    for copy in copies:
        copy.wait()


def whole_in_vmem(count):
    return [pl.BlockSpec(memory_space=pltpu.VMEM)] * count


def call(kernel, shapes, args, aliases={}):
    return pl.pallas_call(
        kernel,
        out_shape=[jax.ShapeDtypeStruct(shape, dtype) for shape, dtype in shapes],
        in_specs=whole_in_vmem(len(args)),
        out_specs=whole_in_vmem(len(shapes)),
        input_output_aliases=aliases,
        compiler_params=pltpu.CompilerParams(vmem_limit_bytes=VMEM_BYTES),
    )(*args)


def start_both(left, right, shape):
    rows_here = shape[0]
    args = list(left) + [half for block in right for half in block]
    shapes = [(shape, F32), (shape, F32), ((2 * rows_here, 128), F32)]
    return call(functools.partial(start_kernel, len(right)), shapes, args)


def add_both(left, right, before):
    args = list(left) + [half for block in right for half in block] + list(before)
    rows_here, wide = before[0].shape
    shapes = [((rows_here, wide), F32)] + [((rows_here // PARTS, wide), BF16)] * PARTS
    kernel = functools.partial(both_kernel, len(right))
    return call(kernel, shapes, args, {len(args) - 2: 0})


def finish(shape, args):
    return pl.pallas_call(
        last_kernel,
        out_shape=jax.ShapeDtypeStruct(shape, BF16),
        in_specs=whole_in_vmem(len(args)),
        out_specs=pl.BlockSpec(memory_space=pl.ANY),
        scratch_shapes=[pltpu.VMEM(shape, BF16), pltpu.SemaphoreType.DMA((4,))],
        compiler_params=pltpu.CompilerParams(vmem_limit_bytes=VMEM_BYTES),
    )(*args)


def folded_ring(size):
    return list(range(0, size, 2)) + list(range(1, size, 2))[::-1]


def together(*arrays):
    return lax.optimization_barrier(arrays)


def by_block(embeddings, group_of, cluster_id):
    rows_here, width = embeddings.shape
    half = rows_here // 2
    slabs = width // 128
    n_blk = lax.axis_size("blk")
    order = folded_ring(n_blk)
    line = (1, rows_here)

    def along(rows):
        hops = [
            (2 * order[i - 1] + core, 2 * order[i] + 1 - core)
            for i in range(n_blk)
            for core in range(2)
        ]
        return lax.ppermute(rows, ("blk", "pair"), hops)

    def back_along(rows):
        hops = [
            (2 * order[i] + core, 2 * order[i - 1] + 1 - core)
            for i in range(n_blk)
            for core in range(2)
        ]
        return lax.ppermute(rows, ("blk", "pair"), hops)

    def across(rows):
        return lax.ppermute(rows, ("sub", "pair"), [(0, 3), (1, 2), (2, 1), (3, 0)])

    def other_core(rows):
        return lax.ppermute(rows, "pair", [(0, 1), (1, 0)])

    (first,) = call(first_pack_kernel, [((slabs * half + LINES, 128), BF16)], [embeddings])
    whole, second = call(
        pack_kernel,
        [((slabs * count + LINES, 128), BF16) for count in (rows_here, half)],
        [embeddings, group_of.reshape(line), cluster_id.reshape(line)],
    )
    along_by = [(first, second)]
    across_by = []
    for s in range(1, n_blk - 1):
        moved = [along(piece) for piece in along_by[-1]]
        swapped = [across(piece) for piece in along_by[-1]]
        moved[0], swapped[0] = together(moved[0], swapped[0])
        moved[1], swapped[1], _ = together(moved[1], swapped[1], moved[0])
        along_by.append(tuple(moved))
        across_by.append(tuple(swapped))
    near = along_by[1]
    over = [other_core(piece) for piece in near]
    over[0], _ = together(over[0], along_by[2][0])
    near_sum, *over_sum = call(
        back_kernel,
        [((rows_here, width + 128), F32)]
        + [((rows_here // PARTS, width + 128), BF16)] * PARTS,
        [*near, *over, first, second, *across_by[0]],
    )
    near_sum, _ = together(near_sum, along_by[2][1])
    (to_return,) = call(
        back_sum_kernel,
        [((slabs * rows_here + LINES, 128), BF16)],
        [near_sum, *[other_core(part) for part in over_sum]],
    )
    returned = back_along(to_return)
    first_crossed = across(along_by[-1][0])
    last_half, first_crossed = together(along_by[-1][1], first_crossed)
    across_by.append((first_crossed, across(last_half)))
    left = (whole, other_core(whole))
    early = across_by[:-1] + along_by[1:-1]
    mine, theirs, info = start_both(left, early, (rows_here, width + 128))
    late = [along_by[-1], across_by[-1]]
    mine, *theirs = add_both((*left, info), late, (mine, theirs))
    out = finish(
        (rows_here, width), [mine, returned, *[other_core(part) for part in theirs]]
    )
    return out


def per_device(embeddings, group_of, cluster_id):
    rows_here, width = embeddings.shape
    devices = lax.axis_size("blk") * lax.axis_size("sub") * lax.axis_size("pair")
    small = devices * rows_here * width * 2 <= GATHER_LIMIT and lax.axis_size("blk") > 3
    fits = width % 128 == 0 and rows_here % (64 * PARTS) == 0 and rows_here <= 256
    if small and fits and lax.axis_size("sub") == 2 and lax.axis_size("pair") == 2:
        return by_block(embeddings, group_of, cluster_id)
    return by_group(embeddings, group_of, cluster_id)


def solution(mesh):
    return jax.shard_map(
        per_device,
        mesh=mesh,
        in_specs=(
            P(("island", "blk", "sub", "pair"), None),
            P(("island", "blk", "sub", "pair"), None),
            P(("island", "blk", "sub", "pair")),
        ),
        out_specs=P(("island", "blk", "sub", "pair"), None),
        check_vma=False,
    )
```

```python
import functools

import jax
import jax.numpy as jnp
from jax import lax
from jax.experimental import pallas as pl
from jax.experimental.pallas import tpu as pltpu
from jax.sharding import PartitionSpec as P

F32 = jnp.float32
BF16 = jnp.bfloat16
VMEM_BYTES = 24 * 1024 * 1024
PARTS = 3
LINES = 16
GATHER_LIMIT = 8 * 1024 * 1024


def unit_scale(rows_in):
    wide = rows_in.astype(F32)
    return lax.rsqrt(jnp.sum(wide * wide, axis=1) + 1e-06)


def tile_weights(left_rows, left_clust, left_scale, right_rows, right_clust, right_scale):
    grams = lax.dot_general(
        left_rows, right_rows, (((1,), (1,)), ((), ())), preferred_element_type=F32
    )
    cosine = grams * left_scale[:, None] * right_scale[None, :]
    same = (left_clust[:, None] == right_clust[None, :]).astype(F32)
    return jax.nn.sigmoid(8.0 * cosine - 2.0) * same


def by_group(embeddings, group_of, cluster_id):
    rows_here, width = embeddings.shape
    groups = lax.axis_size("sub") * lax.axis_size("pair")
    capacity = 2 * rows_here // groups
    slots = groups * capacity
    target = group_of[:, 0]
    onehot = (target[:, None] == jnp.arange(groups, dtype=jnp.int32)[None, :]).astype(jnp.int32)
    position = jnp.sum((jnp.cumsum(onehot, axis=0) - onehot) * onehot, axis=1)
    send_rows = jnp.zeros((groups, capacity, width), BF16).at[target, position].set(embeddings)
    send_clust = jnp.full((groups, capacity), -1, jnp.int32).at[target, position].set(cluster_id)
    recv_rows, recv_clust = (
        lax.all_to_all(send_rows, ("sub", "pair"), split_axis=0, concat_axis=0, tiled=True),
        lax.all_to_all(send_clust, ("sub", "pair"), split_axis=0, concat_axis=0, tiled=True),
    )
    own_rows = recv_rows.reshape(slots, width)
    own_clust = recv_clust.reshape(slots)
    own_scale = unit_scale(own_rows)
    piece_rows = lax.all_gather(own_rows, "blk", axis=0, tiled=True)
    piece_clust = lax.all_gather(own_clust, "blk", axis=0, tiled=True)
    weight = tile_weights(
        own_rows, own_clust, own_scale, piece_rows, piece_clust, unit_scale(piece_rows)
    )
    numer = jnp.dot(weight.astype(BF16), piece_rows, preferred_element_type=F32)
    denom = jnp.sum(weight, axis=1)
    result = (numer / denom[:, None]).astype(BF16).reshape(groups, capacity, width)
    returned = lax.all_to_all(result, ("sub", "pair"), split_axis=0, concat_axis=0, tiled=True)
    return returned[target, position]


def diagonal(size):
    shape = (size, size)
    return lax.broadcasted_iota(jnp.int32, shape, 0) == lax.broadcasted_iota(jnp.int32, shape, 1)


def to_column(row):
    size = row.shape[1]
    return jnp.sum(jnp.where(diagonal(size), row, jnp.zeros_like(row)), axis=1, keepdims=True)


def to_row(column):
    size = column.shape[0]
    return jnp.sum(jnp.where(diagonal(size), column, jnp.zeros_like(column)), axis=0, keepdims=True)


def scale_column(rows):
    wide = rows.astype(F32)
    return lax.rsqrt(jnp.sum(wide * wide, axis=1, keepdims=True) + 1e-06)


def first_pack_kernel(rows, first):
    half = rows.shape[0] // 2
    for slab in range(rows.shape[1] // 128):
        first[slab * half : (slab + 1) * half, :] = rows[:half, slab * 128 : (slab + 1) * 128]


def pack_kernel(rows, group, cluster, whole, second):
    rows_here, width = rows.shape
    slabs = width // 128
    half = rows_here // 2
    for slab in range(slabs):
        columns = rows[:, slab * 128 : (slab + 1) * 128]
        whole[slab * rows_here : (slab + 1) * rows_here, :] = columns
        second[slab * half : (slab + 1) * half, :] = columns[half:]
    line_at = lax.broadcasted_iota(jnp.int32, (LINES, 128), 0)
    named = jnp.zeros((LINES, 128), jnp.int32)
    for line in range(4):
        top = line % 2 * half
        part = (group, cluster)[line // 2][:, top : top + half]
        if half < 128:
            part = jnp.concatenate([part, jnp.zeros((1, 128 - half), jnp.int32)], axis=1)
        named = jnp.where(line_at == line, part, named)
    named = named.astype(F32).astype(BF16)
    whole[slabs * rows_here :, :] = named
    second[slabs * half :, :] = named


def from_slabs(ref, count):
    slabs = [ref[top : top + count, :] for top in range(0, ref.shape[0] // count * count, count)]
    return jnp.concatenate(slabs, axis=1)


def key_rows(ref, half):
    wide = ref[ref.shape[0] - LINES :, :].astype(F32)
    return [
        wide[side : side + 1, :half] * 256.0 + wide[side + 2 : side + 3, :half]
        for side in range(2)
    ]


def key_row(ref, rows_here):
    return jnp.concatenate(key_rows(ref, rows_here // 2), axis=1)


def from_halves(first, second, rows_here):
    half = rows_here // 2
    rows = jnp.concatenate([from_slabs(first, half), from_slabs(second, half)], axis=0)
    return rows, key_row(second, rows_here)


def add_blocks(left, info, blocks, numer, denom):
    key = info[: left.shape[0], 0:1]
    scale = info[: left.shape[0], 1:2]
    right_rows = jnp.concatenate([block[0] for block in blocks], axis=0)
    right_key = jnp.concatenate([block[1] for block in blocks], axis=1)
    right_scale = jnp.concatenate([block[2] for block in blocks], axis=1)
    grams = lax.dot_general(
        left, right_rows, (((1,), (1,)), ((), ())), preferred_element_type=F32
    )
    half = jnp.tanh(grams * scale * right_scale - 1.0)
    weight = jnp.where(key == right_key, 0.5 + 0.5 * half, 0.0)
    add = jnp.dot(weight.astype(BF16), right_rows, preferred_element_type=F32)
    add_denom = jnp.sum(weight, axis=1, keepdims=True)
    if numer is None:
        return add, add_denom
    return numer + add, denom + add_denom


def left_rows(refs, rows_here):
    return jnp.concatenate([from_slabs(ref, rows_here) for ref in refs], axis=0)


def take_blocks(refs, count, rows_here):
    blocks = []
    for _ in range(count):
        rows, key = from_halves(refs.pop(0), refs.pop(0), rows_here)
        blocks.append((rows, key, to_row(scale_column(rows))))
    return blocks


def store_sides(numer, denom, outs):
    rows_here, wide = outs[0].shape
    for side, out in enumerate(outs):
        top = side * rows_here
        out[:, : wide - 128] = numer[top : top + rows_here]
        out[:, wide - 128 :] = jnp.broadcast_to(denom[top : top + rows_here], (rows_here, 128))


def store_theirs(numer, denom, outs):
    high = denom.astype(BF16).astype(F32)
    lane = lax.broadcasted_iota(jnp.int32, (denom.shape[0], 128), 1)
    pair = jnp.where(lane == 0, high, denom - high).astype(BF16)
    count, wide = outs[0].shape
    for part, out in enumerate(outs):
        rows = slice(part * count, (part + 1) * count)
        out[:, : wide - 128] = numer[rows].astype(BF16)
        out[:, wide - 128 :] = pair[rows]


def add_theirs(mine, parts):
    width = mine.shape[1] - 128
    theirs = jnp.concatenate([ref[...] for ref in parts], axis=0)
    pair = theirs[:, width:].astype(F32)
    numer = mine[:, :width] + theirs[:, :width].astype(F32)
    return numer, mine[:, width : width + 1] + (pair[:, 0:1] + pair[:, 1:2])


def back_kernel(near_first, near_second, over_first, over_second, *refs):
    refs = list(refs)
    rows_here = refs[4].shape[0]
    blocks = take_blocks(refs, 2, rows_here)
    mine, *theirs = refs
    sides = [
        from_halves(near_first, near_second, rows_here),
        from_halves(over_first, over_second, rows_here),
    ]
    left = jnp.concatenate([side[0] for side in sides], axis=0)
    key = jnp.concatenate([to_column(side[1]) for side in sides], axis=0)
    lane = lax.broadcasted_iota(jnp.int32, (2 * rows_here, 128), 1)
    info = jnp.where(lane == 0, key, 4.0 * scale_column(left))
    numer, denom = add_blocks(left, info, blocks, None, None)
    store_sides(numer[:rows_here], denom[:rows_here], [mine])
    store_theirs(numer[rows_here:], denom[rows_here:], theirs)


def back_sum_kernel(mine, *refs):
    *parts, out = refs
    rows_here = mine.shape[0]
    half = rows_here // 2
    numer, denom = add_theirs(mine, parts)
    slabs = numer.shape[1] // 128
    for slab in range(slabs):
        out[slab * rows_here : (slab + 1) * rows_here, :] = numer[
            :, slab * 128 : (slab + 1) * 128
        ].astype(BF16)
    high = denom.astype(BF16).astype(F32)
    line_at = lax.broadcasted_iota(jnp.int32, (LINES, 128), 0)
    lines = jnp.zeros((LINES, 128), F32)
    for kind, column in enumerate((high, denom - high)):
        row = to_row(column)
        for side in range(2):
            part = row[:, side * half : (side + 1) * half]
            if half < 128:
                part = jnp.concatenate([part, jnp.zeros((1, 128 - half), F32)], axis=1)
            lines = jnp.where(line_at == 2 * kind + side, part, lines)
    out[slabs * rows_here :, :] = lines.astype(BF16)


def start_kernel(n_blocks, own, other, *refs):
    refs = list(refs)
    rows_here = refs[-1].shape[0] // 2
    left = left_rows((own, other), rows_here)
    key = jnp.concatenate([to_column(key_row(ref, rows_here)) for ref in (own, other)], axis=0)
    scale = scale_column(left)
    info = refs.pop()
    lane = lax.broadcasted_iota(jnp.int32, info.shape, 1)
    info[...] = jnp.where(lane == 0, key, 4.0 * scale)
    first = (left[:rows_here], key_row(own, rows_here), to_row(scale[:rows_here]))
    blocks = [first] + take_blocks(refs, n_blocks, rows_here)
    store_sides(*add_blocks(left, info, blocks, None, None), refs)


def both_kernel(n_blocks, own, other, info, *refs):
    refs = list(refs)
    rows_here = refs[2 * n_blocks].shape[0]
    blocks = take_blocks(refs, n_blocks, rows_here)
    mine_in, theirs_in, mine, *theirs = refs
    wide = mine.shape[1]
    width = wide - 128
    left = left_rows((own, other), rows_here)
    numer = jnp.concatenate([ref[:, :width] for ref in (mine_in, theirs_in)], axis=0)
    denom = jnp.concatenate([ref[:, width : width + 1] for ref in (mine_in, theirs_in)], axis=0)
    numer, denom = add_blocks(left, info, blocks, numer, denom)
    store_sides(numer[:rows_here], denom[:rows_here], [mine])
    store_theirs(numer[rows_here:], denom[rows_here:], theirs)


def last_kernel(mine, returned, *refs):
    *parts, out, staged, sems = refs
    rows_here, width = out.shape
    half = rows_here // 2
    numer, denom = add_theirs(mine, parts)
    numer = numer + from_slabs(returned, rows_here).astype(F32)
    lines = returned[returned.shape[0] - LINES :, :].astype(F32)[:4, :half]
    total = lines[0:2] + lines[2:4]
    denom = denom + to_column(jnp.concatenate([total[0:1], total[1:2]], axis=1))
    share = 1.0 / denom
    count = rows_here // 4
    copies = []
    for part in range(4):
        rows = slice(part * count, (part + 1) * count)
        staged[rows, :] = (numer[rows] * share[rows]).astype(BF16)
        copies.append(pltpu.make_async_copy(staged.at[rows, :], out.at[rows, :], sems.at[part]))
        copies[-1].start()
    for copy in copies:
        copy.wait()


def whole_in_vmem(count):
    return [pl.BlockSpec(memory_space=pltpu.VMEM)] * count


def call(kernel, shapes, args, aliases={}):
    return pl.pallas_call(
        kernel,
        out_shape=[jax.ShapeDtypeStruct(shape, dtype) for shape, dtype in shapes],
        in_specs=whole_in_vmem(len(args)),
        out_specs=whole_in_vmem(len(shapes)),
        input_output_aliases=aliases,
        compiler_params=pltpu.CompilerParams(vmem_limit_bytes=VMEM_BYTES),
    )(*args)


def start_both(left, right, shape):
    rows_here = shape[0]
    args = list(left) + [half for block in right for half in block]
    shapes = [(shape, F32), (shape, F32), ((2 * rows_here, 128), F32)]
    return call(functools.partial(start_kernel, len(right)), shapes, args)


def add_both(left, right, before):
    args = list(left) + [half for block in right for half in block] + list(before)
    rows_here, wide = before[0].shape
    shapes = [((rows_here, wide), F32)] + [((rows_here // PARTS, wide), BF16)] * PARTS
    kernel = functools.partial(both_kernel, len(right))
    return call(kernel, shapes, args, {len(args) - 2: 0})


def finish(shape, args):
    return pl.pallas_call(
        last_kernel,
        out_shape=jax.ShapeDtypeStruct(shape, BF16),
        in_specs=whole_in_vmem(len(args)),
        out_specs=pl.BlockSpec(memory_space=pl.ANY),
        scratch_shapes=[pltpu.VMEM(shape, BF16), pltpu.SemaphoreType.DMA((4,))],
        compiler_params=pltpu.CompilerParams(vmem_limit_bytes=VMEM_BYTES),
    )(*args)


def folded_ring(size):
    return list(range(0, size, 2)) + list(range(1, size, 2))[::-1]


def together(*arrays):
    return lax.optimization_barrier(arrays)


def by_block(embeddings, group_of, cluster_id):
    rows_here, width = embeddings.shape
    half = rows_here // 2
    slabs = width // 128
    n_blk = lax.axis_size("blk")
    order = folded_ring(n_blk)
    line = (1, rows_here)

    def along(rows):
        hops = [
            (2 * order[i - 1] + core, 2 * order[i] + 1 - core)
            for i in range(n_blk)
            for core in range(2)
        ]
        return lax.ppermute(rows, ("blk", "pair"), hops)

    def back_along(rows):
        hops = [
            (2 * order[i] + core, 2 * order[i - 1] + 1 - core)
            for i in range(n_blk)
            for core in range(2)
        ]
        return lax.ppermute(rows, ("blk", "pair"), hops)

    def across(rows):
        return lax.ppermute(rows, ("sub", "pair"), [(0, 3), (1, 2), (2, 1), (3, 0)])

    def other_core(rows):
        return lax.ppermute(rows, "pair", [(0, 1), (1, 0)])

    (first,) = call(first_pack_kernel, [((slabs * half + LINES, 128), BF16)], [embeddings])
    whole, second = call(
        pack_kernel,
        [((slabs * count + LINES, 128), BF16) for count in (rows_here, half)],
        [embeddings, group_of.reshape(line), cluster_id.reshape(line)],
    )
    along_by = [(first, second)]
    across_by = []
    for s in range(1, n_blk - 1):
        moved = [along(piece) for piece in along_by[-1]]
        swapped = [across(piece) for piece in along_by[-1]]
        moved[0], swapped[0] = together(moved[0], swapped[0])
        moved[1], swapped[1], _ = together(moved[1], swapped[1], moved[0])
        along_by.append(tuple(moved))
        across_by.append(tuple(swapped))
    near = along_by[1]
    over = [other_core(piece) for piece in near]
    over[0], _ = together(over[0], along_by[2][0])
    near_sum, *over_sum = call(
        back_kernel,
        [((rows_here, width + 128), F32)]
        + [((rows_here // PARTS, width + 128), BF16)] * PARTS,
        [*near, *over, first, second, *across_by[0]],
    )
    over_sum[-1], _ = together(over_sum[-1], along_by[2][1])
    (to_return,) = call(
        back_sum_kernel,
        [((slabs * rows_here + LINES, 128), BF16)],
        [near_sum, *[other_core(part) for part in over_sum]],
    )
    returned = back_along(to_return)
    first_crossed = across(along_by[-1][0])
    last_half, first_crossed = together(along_by[-1][1], first_crossed)
    across_by.append((first_crossed, across(last_half)))
    left = (whole, other_core(whole))
    early = across_by[:-1] + along_by[1:-1]
    mine, theirs, info = start_both(left, early, (rows_here, width + 128))
    late = [along_by[-1], across_by[-1]]
    mine, *theirs = add_both((*left, info), late, (mine, theirs))
    out = finish(
        (rows_here, width), [mine, returned, *[other_core(part) for part in theirs]]
    )
    return out


def per_device(embeddings, group_of, cluster_id):
    rows_here, width = embeddings.shape
    devices = lax.axis_size("blk") * lax.axis_size("sub") * lax.axis_size("pair")
    small = devices * rows_here * width * 2 <= GATHER_LIMIT and lax.axis_size("blk") > 3
    fits = width % 128 == 0 and rows_here % (64 * PARTS) == 0 and rows_here <= 256
    if small and fits and lax.axis_size("sub") == 2 and lax.axis_size("pair") == 2:
        return by_block(embeddings, group_of, cluster_id)
    return by_group(embeddings, group_of, cluster_id)


def solution(mesh):
    return jax.shard_map(
        per_device,
        mesh=mesh,
        in_specs=(
            P(("island", "blk", "sub", "pair"), None),
            P(("island", "blk", "sub", "pair"), None),
            P(("island", "blk", "sub", "pair")),
        ),
        out_specs=P(("island", "blk", "sub", "pair"), None),
        check_vma=False,
    )
```

```python
import functools

import jax
import jax.numpy as jnp
from jax import lax
from jax.experimental import pallas as pl
from jax.experimental.pallas import tpu as pltpu
from jax.sharding import PartitionSpec as P

F32 = jnp.float32
BF16 = jnp.bfloat16
VMEM_BYTES = 24 * 1024 * 1024
PARTS = 3
LINES = 16
GATHER_LIMIT = 8 * 1024 * 1024


def unit_scale(rows_in):
    wide = rows_in.astype(F32)
    return lax.rsqrt(jnp.sum(wide * wide, axis=1) + 1e-06)


def tile_weights(left_rows, left_clust, left_scale, right_rows, right_clust, right_scale):
    grams = lax.dot_general(
        left_rows, right_rows, (((1,), (1,)), ((), ())), preferred_element_type=F32
    )
    cosine = grams * left_scale[:, None] * right_scale[None, :]
    same = (left_clust[:, None] == right_clust[None, :]).astype(F32)
    return jax.nn.sigmoid(8.0 * cosine - 2.0) * same


def by_group(embeddings, group_of, cluster_id):
    rows_here, width = embeddings.shape
    groups = lax.axis_size("sub") * lax.axis_size("pair")
    capacity = 2 * rows_here // groups
    slots = groups * capacity
    target = group_of[:, 0]
    onehot = (target[:, None] == jnp.arange(groups, dtype=jnp.int32)[None, :]).astype(jnp.int32)
    position = jnp.sum((jnp.cumsum(onehot, axis=0) - onehot) * onehot, axis=1)
    send_rows = jnp.zeros((groups, capacity, width), BF16).at[target, position].set(embeddings)
    send_clust = jnp.full((groups, capacity), -1, jnp.int32).at[target, position].set(cluster_id)
    recv_rows, recv_clust = (
        lax.all_to_all(send_rows, ("sub", "pair"), split_axis=0, concat_axis=0, tiled=True),
        lax.all_to_all(send_clust, ("sub", "pair"), split_axis=0, concat_axis=0, tiled=True),
    )
    own_rows = recv_rows.reshape(slots, width)
    own_clust = recv_clust.reshape(slots)
    own_scale = unit_scale(own_rows)
    piece_rows = lax.all_gather(own_rows, "blk", axis=0, tiled=True)
    piece_clust = lax.all_gather(own_clust, "blk", axis=0, tiled=True)
    weight = tile_weights(
        own_rows, own_clust, own_scale, piece_rows, piece_clust, unit_scale(piece_rows)
    )
    numer = jnp.dot(weight.astype(BF16), piece_rows, preferred_element_type=F32)
    denom = jnp.sum(weight, axis=1)
    result = (numer / denom[:, None]).astype(BF16).reshape(groups, capacity, width)
    returned = lax.all_to_all(result, ("sub", "pair"), split_axis=0, concat_axis=0, tiled=True)
    return returned[target, position]


def diagonal(size):
    shape = (size, size)
    return lax.broadcasted_iota(jnp.int32, shape, 0) == lax.broadcasted_iota(jnp.int32, shape, 1)


def to_column(row):
    size = row.shape[1]
    return jnp.sum(jnp.where(diagonal(size), row, jnp.zeros_like(row)), axis=1, keepdims=True)


def to_row(column):
    size = column.shape[0]
    return jnp.sum(jnp.where(diagonal(size), column, jnp.zeros_like(column)), axis=0, keepdims=True)


def scale_column(rows):
    wide = rows.astype(F32)
    return lax.rsqrt(jnp.sum(wide * wide, axis=1, keepdims=True) + 1e-06)


def first_pack_kernel(rows, first):
    half = rows.shape[0] // 2
    for slab in range(rows.shape[1] // 128):
        first[slab * half : (slab + 1) * half, :] = rows[:half, slab * 128 : (slab + 1) * 128]


def pack_kernel(rows, group, cluster, whole, second):
    rows_here, width = rows.shape
    slabs = width // 128
    half = rows_here // 2
    for slab in range(slabs):
        columns = rows[:, slab * 128 : (slab + 1) * 128]
        whole[slab * rows_here : (slab + 1) * rows_here, :] = columns
        second[slab * half : (slab + 1) * half, :] = columns[half:]
    line_at = lax.broadcasted_iota(jnp.int32, (LINES, 128), 0)
    named = jnp.zeros((LINES, 128), jnp.int32)
    for line in range(4):
        top = line % 2 * half
        part = (group, cluster)[line // 2][:, top : top + half]
        if half < 128:
            part = jnp.concatenate([part, jnp.zeros((1, 128 - half), jnp.int32)], axis=1)
        named = jnp.where(line_at == line, part, named)
    named = named.astype(F32).astype(BF16)
    whole[slabs * rows_here :, :] = named
    second[slabs * half :, :] = named


def from_slabs(ref, count):
    slabs = [ref[top : top + count, :] for top in range(0, ref.shape[0] // count * count, count)]
    return jnp.concatenate(slabs, axis=1)


def key_rows(ref, half):
    wide = ref[ref.shape[0] - LINES :, :].astype(F32)
    return [
        wide[side : side + 1, :half] * 256.0 + wide[side + 2 : side + 3, :half]
        for side in range(2)
    ]


def key_row(ref, rows_here):
    return jnp.concatenate(key_rows(ref, rows_here // 2), axis=1)


def from_halves(first, second, rows_here):
    half = rows_here // 2
    rows = jnp.concatenate([from_slabs(first, half), from_slabs(second, half)], axis=0)
    return rows, key_row(second, rows_here)


def add_blocks(left, info, blocks, numer, denom):
    key = info[: left.shape[0], 0:1]
    scale = info[: left.shape[0], 1:2]
    right_rows = jnp.concatenate([block[0] for block in blocks], axis=0)
    right_key = jnp.concatenate([block[1] for block in blocks], axis=1)
    right_scale = jnp.concatenate([block[2] for block in blocks], axis=1)
    grams = lax.dot_general(
        left, right_rows, (((1,), (1,)), ((), ())), preferred_element_type=F32
    )
    half = jnp.tanh(grams * scale * right_scale - 1.0)
    weight = jnp.where(key == right_key, 0.5 + 0.5 * half, 0.0)
    add = jnp.dot(weight.astype(BF16), right_rows, preferred_element_type=F32)
    add_denom = jnp.sum(weight, axis=1, keepdims=True)
    if numer is None:
        return add, add_denom
    return numer + add, denom + add_denom


def left_rows(refs, rows_here):
    return jnp.concatenate([from_slabs(ref, rows_here) for ref in refs], axis=0)


def take_blocks(refs, count, rows_here):
    blocks = []
    for _ in range(count):
        rows, key = from_halves(refs.pop(0), refs.pop(0), rows_here)
        blocks.append((rows, key, to_row(scale_column(rows))))
    return blocks


def store_sides(numer, denom, outs):
    rows_here, wide = outs[0].shape
    for side, out in enumerate(outs):
        top = side * rows_here
        out[:, : wide - 128] = numer[top : top + rows_here]
        out[:, wide - 128 :] = jnp.broadcast_to(denom[top : top + rows_here], (rows_here, 128))


def store_theirs(numer, denom, outs):
    high = denom.astype(BF16).astype(F32)
    lane = lax.broadcasted_iota(jnp.int32, (denom.shape[0], 128), 1)
    pair = jnp.where(lane == 0, high, denom - high).astype(BF16)
    count, wide = outs[0].shape
    for part, out in enumerate(outs):
        rows = slice(part * count, (part + 1) * count)
        out[:, : wide - 128] = numer[rows].astype(BF16)
        out[:, wide - 128 :] = pair[rows]


def add_theirs(mine, parts):
    width = mine.shape[1] - 128
    theirs = jnp.concatenate([ref[...] for ref in parts], axis=0)
    pair = theirs[:, width:].astype(F32)
    numer = mine[:, :width] + theirs[:, :width].astype(F32)
    return numer, mine[:, width : width + 1] + (pair[:, 0:1] + pair[:, 1:2])


def back_kernel(near_first, near_second, over_first, over_second, *refs):
    refs = list(refs)
    rows_here = refs[4].shape[0]
    blocks = take_blocks(refs, 2, rows_here)
    mine, *theirs = refs
    sides = [
        from_halves(near_first, near_second, rows_here),
        from_halves(over_first, over_second, rows_here),
    ]
    left = jnp.concatenate([side[0] for side in sides], axis=0)
    key = jnp.concatenate([to_column(side[1]) for side in sides], axis=0)
    lane = lax.broadcasted_iota(jnp.int32, (2 * rows_here, 128), 1)
    info = jnp.where(lane == 0, key, 4.0 * scale_column(left))
    numer, denom = add_blocks(left, info, blocks, None, None)
    store_sides(numer[:rows_here], denom[:rows_here], [mine])
    store_theirs(numer[rows_here:], denom[rows_here:], theirs)


def back_sum_kernel(mine, *refs):
    *parts, out = refs
    rows_here = mine.shape[0]
    half = rows_here // 2
    numer, denom = add_theirs(mine, parts)
    slabs = numer.shape[1] // 128
    for slab in range(slabs):
        out[slab * rows_here : (slab + 1) * rows_here, :] = numer[
            :, slab * 128 : (slab + 1) * 128
        ].astype(BF16)
    high = denom.astype(BF16).astype(F32)
    line_at = lax.broadcasted_iota(jnp.int32, (LINES, 128), 0)
    lines = jnp.zeros((LINES, 128), F32)
    for kind, column in enumerate((high, denom - high)):
        row = to_row(column)
        for side in range(2):
            part = row[:, side * half : (side + 1) * half]
            if half < 128:
                part = jnp.concatenate([part, jnp.zeros((1, 128 - half), F32)], axis=1)
            lines = jnp.where(line_at == 2 * kind + side, part, lines)
    out[slabs * rows_here :, :] = lines.astype(BF16)


def start_kernel(n_blocks, own, other, *refs):
    refs = list(refs)
    rows_here = refs[-1].shape[0] // 2
    left = left_rows((own, other), rows_here)
    key = jnp.concatenate([to_column(key_row(ref, rows_here)) for ref in (own, other)], axis=0)
    scale = scale_column(left)
    info = refs.pop()
    lane = lax.broadcasted_iota(jnp.int32, info.shape, 1)
    info[...] = jnp.where(lane == 0, key, 4.0 * scale)
    first = (left[:rows_here], key_row(own, rows_here), to_row(scale[:rows_here]))
    blocks = [first] + take_blocks(refs, n_blocks, rows_here)
    store_sides(*add_blocks(left, info, blocks, None, None), refs)


def both_kernel(n_blocks, own, other, info, *refs):
    refs = list(refs)
    rows_here = refs[2 * n_blocks].shape[0]
    blocks = take_blocks(refs, n_blocks, rows_here)
    mine_in, theirs_in, mine, *theirs = refs
    wide = mine.shape[1]
    width = wide - 128
    left = left_rows((own, other), rows_here)
    numer = jnp.concatenate([ref[:, :width] for ref in (mine_in, theirs_in)], axis=0)
    denom = jnp.concatenate([ref[:, width : width + 1] for ref in (mine_in, theirs_in)], axis=0)
    numer, denom = add_blocks(left, info, blocks, numer, denom)
    store_sides(numer[:rows_here], denom[:rows_here], [mine])
    store_theirs(numer[rows_here:], denom[rows_here:], theirs)


def join_kernel(own, info, first, second, mine, *refs):
    *parts, out = refs
    rows_here = out.shape[0]
    numer, denom = add_theirs(mine, parts)
    blocks = take_blocks([first, second], 1, rows_here)
    left = left_rows((own,), rows_here)
    store_sides(*add_blocks(left, info, blocks, numer, denom), [out])


def last_kernel(own, info, first, second, total, returned, out, staged, sems):
    rows_here, width = out.shape
    half = rows_here // 2
    blocks = take_blocks([first, second], 1, rows_here)
    left = left_rows((own,), rows_here)
    numer = total[:, :width] + from_slabs(returned, rows_here).astype(F32)
    lines = returned[returned.shape[0] - LINES :, :].astype(F32)[:4, :half]
    added = lines[0:2] + lines[2:4]
    added = to_column(jnp.concatenate([added[0:1], added[1:2]], axis=1))
    numer, denom = add_blocks(left, info, blocks, numer, total[:, width : width + 1] + added)
    share = 1.0 / denom
    count = rows_here // 4
    copies = []
    for part in range(4):
        rows = slice(part * count, (part + 1) * count)
        staged[rows, :] = (numer[rows] * share[rows]).astype(BF16)
        copies.append(pltpu.make_async_copy(staged.at[rows, :], out.at[rows, :], sems.at[part]))
        copies[-1].start()
    for copy in copies:
        copy.wait()


def whole_in_vmem(count):
    return [pl.BlockSpec(memory_space=pltpu.VMEM)] * count


def call(kernel, shapes, args, aliases={}):
    return pl.pallas_call(
        kernel,
        out_shape=[jax.ShapeDtypeStruct(shape, dtype) for shape, dtype in shapes],
        in_specs=whole_in_vmem(len(args)),
        out_specs=whole_in_vmem(len(shapes)),
        input_output_aliases=aliases,
        compiler_params=pltpu.CompilerParams(vmem_limit_bytes=VMEM_BYTES),
    )(*args)


def start_both(left, right, shape):
    rows_here = shape[0]
    args = list(left) + [half for block in right for half in block]
    shapes = [(shape, F32), (shape, F32), ((2 * rows_here, 128), F32)]
    return call(functools.partial(start_kernel, len(right)), shapes, args)


def add_both(left, right, before):
    args = list(left) + [half for block in right for half in block] + list(before)
    rows_here, wide = before[0].shape
    shapes = [((rows_here, wide), F32)] + [((rows_here // PARTS, wide), BF16)] * PARTS
    kernel = functools.partial(both_kernel, len(right))
    return call(kernel, shapes, args, {len(args) - 2: 0})


def finish(shape, args):
    return pl.pallas_call(
        last_kernel,
        out_shape=jax.ShapeDtypeStruct(shape, BF16),
        in_specs=whole_in_vmem(len(args)),
        out_specs=pl.BlockSpec(memory_space=pl.ANY),
        scratch_shapes=[pltpu.VMEM(shape, BF16), pltpu.SemaphoreType.DMA((4,))],
        compiler_params=pltpu.CompilerParams(vmem_limit_bytes=VMEM_BYTES),
    )(*args)


def folded_ring(size):
    return list(range(0, size, 2)) + list(range(1, size, 2))[::-1]


def together(*arrays):
    return lax.optimization_barrier(arrays)


def by_block(embeddings, group_of, cluster_id):
    rows_here, width = embeddings.shape
    half = rows_here // 2
    slabs = width // 128
    n_blk = lax.axis_size("blk")
    order = folded_ring(n_blk)
    line = (1, rows_here)

    def along(rows):
        hops = [
            (2 * order[i - 1] + core, 2 * order[i] + 1 - core)
            for i in range(n_blk)
            for core in range(2)
        ]
        return lax.ppermute(rows, ("blk", "pair"), hops)

    def back_along(rows):
        hops = [
            (2 * order[i] + core, 2 * order[i - 1] + 1 - core)
            for i in range(n_blk)
            for core in range(2)
        ]
        return lax.ppermute(rows, ("blk", "pair"), hops)

    def across(rows):
        return lax.ppermute(rows, ("sub", "pair"), [(0, 3), (1, 2), (2, 1), (3, 0)])

    def other_core(rows):
        return lax.ppermute(rows, "pair", [(0, 1), (1, 0)])

    (first,) = call(first_pack_kernel, [((slabs * half + LINES, 128), BF16)], [embeddings])
    whole, second = call(
        pack_kernel,
        [((slabs * count + LINES, 128), BF16) for count in (rows_here, half)],
        [embeddings, group_of.reshape(line), cluster_id.reshape(line)],
    )
    along_by = [(first, second)]
    across_by = []
    for s in range(1, n_blk - 1):
        moved = [along(piece) for piece in along_by[-1]]
        swapped = [across(piece) for piece in along_by[-1]]
        moved[0], swapped[0] = together(moved[0], swapped[0])
        moved[1], swapped[1], _ = together(moved[1], swapped[1], moved[0])
        along_by.append(tuple(moved))
        across_by.append(tuple(swapped))
    near = along_by[1]
    over = [other_core(piece) for piece in near]
    over[0], _ = together(over[0], along_by[2][0])
    near_sum, *over_sum = call(
        back_kernel,
        [((rows_here, width + 128), F32)]
        + [((rows_here // PARTS, width + 128), BF16)] * PARTS,
        [*near, *over, first, second, *across_by[0]],
    )
    near_sum, _ = together(near_sum, along_by[2][1])
    (to_return,) = call(
        back_sum_kernel,
        [((slabs * rows_here + LINES, 128), BF16)],
        [near_sum, *[other_core(part) for part in over_sum]],
    )
    returned = back_along(to_return)
    first_crossed = across(along_by[-1][0])
    last_half, first_crossed = together(along_by[-1][1], first_crossed)
    across_by.append((first_crossed, across(last_half)))
    left = (whole, other_core(whole))
    early = across_by[:-1] + along_by[1:-1]
    mine, theirs, info = start_both(left, early, (rows_here, width + 128))
    mine, *theirs = add_both((*left, info), [along_by[-1]], (mine, theirs))
    last_first, last_second = across_by[-1]
    back = [other_core(part) for part in theirs[:-1]]
    last_first, theirs[-1] = together(last_first, theirs[-1])
    last_second, *back = together(last_second, *back, other_core(theirs[-1]))
    last = [other_core(last_first), other_core(last_second)]
    (total,) = call(
        join_kernel,
        [((rows_here, width + 128), F32)],
        [whole, info, last_first, last_second, mine, *back],
        {4: 0},
    )
    out = finish((rows_here, width), [whole, info, *last, total, returned])
    return out


def per_device(embeddings, group_of, cluster_id):
    rows_here, width = embeddings.shape
    devices = lax.axis_size("blk") * lax.axis_size("sub") * lax.axis_size("pair")
    small = devices * rows_here * width * 2 <= GATHER_LIMIT and lax.axis_size("blk") > 3
    fits = width % 128 == 0 and rows_here % (64 * PARTS) == 0 and rows_here <= 256
    if small and fits and lax.axis_size("sub") == 2 and lax.axis_size("pair") == 2:
        return by_block(embeddings, group_of, cluster_id)
    return by_group(embeddings, group_of, cluster_id)


def solution(mesh):
    return jax.shard_map(
        per_device,
        mesh=mesh,
        in_specs=(
            P(("island", "blk", "sub", "pair"), None),
            P(("island", "blk", "sub", "pair"), None),
            P(("island", "blk", "sub", "pair")),
        ),
        out_specs=P(("island", "blk", "sub", "pair"), None),
        check_vma=False,
    )
```

```python
import functools

import jax
import jax.numpy as jnp
from jax import lax
from jax.experimental import pallas as pl
from jax.experimental.pallas import tpu as pltpu
from jax.sharding import PartitionSpec as P

F32 = jnp.float32
BF16 = jnp.bfloat16
VMEM_BYTES = 24 * 1024 * 1024
PARTS = 3
LINES = 16
GATHER_LIMIT = 8 * 1024 * 1024


def unit_scale(rows_in):
    wide = rows_in.astype(F32)
    return lax.rsqrt(jnp.sum(wide * wide, axis=1) + 1e-06)


def tile_weights(left_rows, left_clust, left_scale, right_rows, right_clust, right_scale):
    grams = lax.dot_general(
        left_rows, right_rows, (((1,), (1,)), ((), ())), preferred_element_type=F32
    )
    cosine = grams * left_scale[:, None] * right_scale[None, :]
    same = (left_clust[:, None] == right_clust[None, :]).astype(F32)
    return jax.nn.sigmoid(8.0 * cosine - 2.0) * same


def by_group(embeddings, group_of, cluster_id):
    rows_here, width = embeddings.shape
    groups = lax.axis_size("sub") * lax.axis_size("pair")
    capacity = 2 * rows_here // groups
    slots = groups * capacity
    target = group_of[:, 0]
    onehot = (target[:, None] == jnp.arange(groups, dtype=jnp.int32)[None, :]).astype(jnp.int32)
    position = jnp.sum((jnp.cumsum(onehot, axis=0) - onehot) * onehot, axis=1)
    send_rows = jnp.zeros((groups, capacity, width), BF16).at[target, position].set(embeddings)
    send_clust = jnp.full((groups, capacity), -1, jnp.int32).at[target, position].set(cluster_id)
    recv_rows, recv_clust = (
        lax.all_to_all(send_rows, ("sub", "pair"), split_axis=0, concat_axis=0, tiled=True),
        lax.all_to_all(send_clust, ("sub", "pair"), split_axis=0, concat_axis=0, tiled=True),
    )
    own_rows = recv_rows.reshape(slots, width)
    own_clust = recv_clust.reshape(slots)
    own_scale = unit_scale(own_rows)
    piece_rows = lax.all_gather(own_rows, "blk", axis=0, tiled=True)
    piece_clust = lax.all_gather(own_clust, "blk", axis=0, tiled=True)
    weight = tile_weights(
        own_rows, own_clust, own_scale, piece_rows, piece_clust, unit_scale(piece_rows)
    )
    numer = jnp.dot(weight.astype(BF16), piece_rows, preferred_element_type=F32)
    denom = jnp.sum(weight, axis=1)
    result = (numer / denom[:, None]).astype(BF16).reshape(groups, capacity, width)
    returned = lax.all_to_all(result, ("sub", "pair"), split_axis=0, concat_axis=0, tiled=True)
    return returned[target, position]


def diagonal(size):
    shape = (size, size)
    return lax.broadcasted_iota(jnp.int32, shape, 0) == lax.broadcasted_iota(jnp.int32, shape, 1)


def to_column(row):
    size = row.shape[1]
    return jnp.sum(jnp.where(diagonal(size), row, jnp.zeros_like(row)), axis=1, keepdims=True)


def to_row(column):
    size = column.shape[0]
    return jnp.sum(jnp.where(diagonal(size), column, jnp.zeros_like(column)), axis=0, keepdims=True)


def scale_column(rows):
    wide = rows.astype(F32)
    return lax.rsqrt(jnp.sum(wide * wide, axis=1, keepdims=True) + 1e-06)


def first_pack_kernel(rows, first):
    half = rows.shape[0] // 2
    for slab in range(rows.shape[1] // 128):
        first[slab * half : (slab + 1) * half, :] = rows[:half, slab * 128 : (slab + 1) * 128]


def pack_kernel(rows, group, cluster, whole, second):
    rows_here, width = rows.shape
    slabs = width // 128
    half = rows_here // 2
    for slab in range(slabs):
        columns = rows[:, slab * 128 : (slab + 1) * 128]
        whole[slab * rows_here : (slab + 1) * rows_here, :] = columns
        second[slab * half : (slab + 1) * half, :] = columns[half:]
    line_at = lax.broadcasted_iota(jnp.int32, (LINES, 128), 0)
    named = jnp.zeros((LINES, 128), jnp.int32)
    for line in range(4):
        top = line % 2 * half
        part = (group, cluster)[line // 2][:, top : top + half]
        if half < 128:
            part = jnp.concatenate([part, jnp.zeros((1, 128 - half), jnp.int32)], axis=1)
        named = jnp.where(line_at == line, part, named)
    named = named.astype(F32).astype(BF16)
    whole[slabs * rows_here :, :] = named
    second[slabs * half :, :] = named


def from_slabs(ref, count):
    slabs = [ref[top : top + count, :] for top in range(0, ref.shape[0] // count * count, count)]
    return jnp.concatenate(slabs, axis=1)


def key_rows(ref, half):
    wide = ref[ref.shape[0] - LINES :, :].astype(F32)
    return [
        wide[side : side + 1, :half] * 256.0 + wide[side + 2 : side + 3, :half]
        for side in range(2)
    ]


def key_row(ref, rows_here):
    return jnp.concatenate(key_rows(ref, rows_here // 2), axis=1)


def from_halves(first, second, rows_here):
    half = rows_here // 2
    rows = jnp.concatenate([from_slabs(first, half), from_slabs(second, half)], axis=0)
    return rows, key_row(second, rows_here)


def add_blocks(left, info, blocks, numer, denom):
    key = info[: left.shape[0], 0:1]
    scale = info[: left.shape[0], 1:2]
    right_rows = jnp.concatenate([block[0] for block in blocks], axis=0)
    right_key = jnp.concatenate([block[1] for block in blocks], axis=1)
    right_scale = jnp.concatenate([block[2] for block in blocks], axis=1)
    grams = lax.dot_general(
        left, right_rows, (((1,), (1,)), ((), ())), preferred_element_type=F32
    )
    half = jnp.tanh(grams * scale * right_scale - 1.0)
    weight = jnp.where(key == right_key, 0.5 + 0.5 * half, 0.0)
    add = jnp.dot(weight.astype(BF16), right_rows, preferred_element_type=F32)
    add_denom = jnp.sum(weight, axis=1, keepdims=True)
    if numer is None:
        return add, add_denom
    return numer + add, denom + add_denom


def left_rows(refs, rows_here):
    return jnp.concatenate([from_slabs(ref, rows_here) for ref in refs], axis=0)


def take_blocks(refs, count, rows_here):
    blocks = []
    for _ in range(count):
        rows, key = from_halves(refs.pop(0), refs.pop(0), rows_here)
        blocks.append((rows, key, to_row(scale_column(rows))))
    return blocks


def store_sides(numer, denom, outs):
    rows_here, wide = outs[0].shape
    for side, out in enumerate(outs):
        top = side * rows_here
        out[:, : wide - 128] = numer[top : top + rows_here]
        out[:, wide - 128 :] = jnp.broadcast_to(denom[top : top + rows_here], (rows_here, 128))


def store_theirs(numer, denom, outs):
    high = denom.astype(BF16).astype(F32)
    lane = lax.broadcasted_iota(jnp.int32, (denom.shape[0], 128), 1)
    pair = jnp.where(lane == 0, high, denom - high).astype(BF16)
    count = outs[0].shape[0]
    width = numer.shape[1]
    for part, out in enumerate(outs):
        rows = slice(part * count, (part + 1) * count)
        out[:, :width] = numer[rows].astype(BF16)
        out[:, width : width + 128] = pair[rows]


def add_theirs(mine, parts):
    width = mine.shape[1] - 128
    theirs = jnp.concatenate([ref[...] for ref in parts], axis=0)
    pair = theirs[:, width:].astype(F32)
    numer = mine[:, :width] + theirs[:, :width].astype(F32)
    return numer, mine[:, width : width + 1] + (pair[:, 0:1] + pair[:, 1:2])


def back_kernel(near_first, near_second, over_first, over_second, *refs):
    refs = list(refs)
    rows_here = refs[4].shape[0]
    blocks = take_blocks(refs, 2, rows_here)
    mine, *theirs = refs
    sides = [
        from_halves(near_first, near_second, rows_here),
        from_halves(over_first, over_second, rows_here),
    ]
    left = jnp.concatenate([side[0] for side in sides], axis=0)
    key = jnp.concatenate([to_column(side[1]) for side in sides], axis=0)
    lane = lax.broadcasted_iota(jnp.int32, (2 * rows_here, 128), 1)
    info = jnp.where(lane == 0, key, 4.0 * scale_column(left))
    numer, denom = add_blocks(left, info, blocks, None, None)
    store_sides(numer[:rows_here], denom[:rows_here], [mine])
    store_theirs(numer[rows_here:], denom[rows_here:], theirs)


def back_sum_kernel(mine, *refs):
    *parts, out = refs
    rows_here = mine.shape[0]
    half = rows_here // 2
    numer, denom = add_theirs(mine, parts)
    slabs = numer.shape[1] // 128
    for slab in range(slabs):
        out[slab * rows_here : (slab + 1) * rows_here, :] = numer[
            :, slab * 128 : (slab + 1) * 128
        ].astype(BF16)
    high = denom.astype(BF16).astype(F32)
    line_at = lax.broadcasted_iota(jnp.int32, (LINES, 128), 0)
    lines = jnp.zeros((LINES, 128), F32)
    for kind, column in enumerate((high, denom - high)):
        row = to_row(column)
        for side in range(2):
            part = row[:, side * half : (side + 1) * half]
            if half < 128:
                part = jnp.concatenate([part, jnp.zeros((1, 128 - half), F32)], axis=1)
            lines = jnp.where(line_at == 2 * kind + side, part, lines)
    out[slabs * rows_here :, :] = lines.astype(BF16)


def start_kernel(n_blocks, own, other, *refs):
    refs = list(refs)
    rows_here = refs[-1].shape[0] // 2
    left = left_rows((own, other), rows_here)
    key = jnp.concatenate([to_column(key_row(ref, rows_here)) for ref in (own, other)], axis=0)
    scale = scale_column(left)
    info = refs.pop()
    lane = lax.broadcasted_iota(jnp.int32, info.shape, 1)
    info[...] = jnp.where(lane == 0, key, 4.0 * scale)
    first = (left[:rows_here], key_row(own, rows_here), to_row(scale[:rows_here]))
    blocks = [first] + take_blocks(refs, n_blocks, rows_here)
    store_sides(*add_blocks(left, info, blocks, None, None), refs)


def both_kernel(n_blocks, own, other, info, *refs):
    refs = list(refs)
    rows_here = refs[2 * n_blocks].shape[0]
    blocks = take_blocks(refs, n_blocks, rows_here)
    mine_in, theirs_in, mine, *theirs = refs
    wide = mine.shape[1]
    width = wide - 128
    left = left_rows((own, other), rows_here)
    numer = jnp.concatenate([ref[:, :width] for ref in (mine_in, theirs_in)], axis=0)
    denom = jnp.concatenate([ref[:, width : width + 1] for ref in (mine_in, theirs_in)], axis=0)
    numer, denom = add_blocks(left, info, blocks, numer, denom)
    store_sides(numer[:rows_here], denom[:rows_here], [mine])
    store_theirs(numer[rows_here:], denom[rows_here:], theirs)


def last_kernel(mine, returned, *refs):
    *parts, out, staged, sems = refs
    rows_here, width = out.shape
    half = rows_here // 2
    numer, denom = add_theirs(mine, parts)
    numer = numer + from_slabs(returned, rows_here).astype(F32)
    lines = returned[returned.shape[0] - LINES :, :].astype(F32)[:4, :half]
    total = lines[0:2] + lines[2:4]
    denom = denom + to_column(jnp.concatenate([total[0:1], total[1:2]], axis=1))
    share = 1.0 / denom
    count = rows_here // 4
    copies = []
    for part in range(4):
        rows = slice(part * count, (part + 1) * count)
        staged[rows, :] = (numer[rows] * share[rows]).astype(BF16)
        copies.append(pltpu.make_async_copy(staged.at[rows, :], out.at[rows, :], sems.at[part]))
        copies[-1].start()
    for copy in copies:
        copy.wait()


def whole_in_vmem(count):
    return [pl.BlockSpec(memory_space=pltpu.VMEM)] * count


def call(kernel, shapes, args, aliases={}):
    return pl.pallas_call(
        kernel,
        out_shape=[jax.ShapeDtypeStruct(shape, dtype) for shape, dtype in shapes],
        in_specs=whole_in_vmem(len(args)),
        out_specs=whole_in_vmem(len(shapes)),
        input_output_aliases=aliases,
        compiler_params=pltpu.CompilerParams(vmem_limit_bytes=VMEM_BYTES),
    )(*args)


def start_both(left, right, shape):
    rows_here = shape[0]
    args = list(left) + [half for block in right for half in block]
    shapes = [(shape, F32), (shape, F32), ((2 * rows_here, 128), F32)]
    return call(functools.partial(start_kernel, len(right)), shapes, args)


def add_both(left, right, before):
    args = list(left) + [half for block in right for half in block] + list(before)
    rows_here, wide = before[0].shape
    shapes = [((rows_here, wide), F32)] + [((rows_here // PARTS, wide), BF16)] * PARTS
    kernel = functools.partial(both_kernel, len(right))
    return call(kernel, shapes, args, {len(args) - 2: 0})


def finish(shape, args):
    return pl.pallas_call(
        last_kernel,
        out_shape=jax.ShapeDtypeStruct(shape, BF16),
        in_specs=whole_in_vmem(len(args)),
        out_specs=pl.BlockSpec(memory_space=pl.ANY),
        scratch_shapes=[pltpu.VMEM(shape, BF16), pltpu.SemaphoreType.DMA((4,))],
        compiler_params=pltpu.CompilerParams(vmem_limit_bytes=VMEM_BYTES),
    )(*args)


def folded_ring(size):
    return list(range(0, size, 2)) + list(range(1, size, 2))[::-1]


def together(*arrays):
    return lax.optimization_barrier(arrays)


def by_block(embeddings, group_of, cluster_id):
    rows_here, width = embeddings.shape
    half = rows_here // 2
    slabs = width // 128
    n_blk = lax.axis_size("blk")
    order = folded_ring(n_blk)
    line = (1, rows_here)

    def along(rows):
        hops = [
            (2 * order[i - 1] + core, 2 * order[i] + 1 - core)
            for i in range(n_blk)
            for core in range(2)
        ]
        return lax.ppermute(rows, ("blk", "pair"), hops)

    def back_along(rows):
        hops = [
            (2 * order[i] + core, 2 * order[i - 1] + 1 - core)
            for i in range(n_blk)
            for core in range(2)
        ]
        return lax.ppermute(rows, ("blk", "pair"), hops)

    def across(rows):
        return lax.ppermute(rows, ("sub", "pair"), [(0, 3), (1, 2), (2, 1), (3, 0)])

    def other_core(rows):
        return lax.ppermute(rows, "pair", [(0, 1), (1, 0)])

    (first,) = call(first_pack_kernel, [((slabs * half + LINES, 128), BF16)], [embeddings])
    whole, second = call(
        pack_kernel,
        [((slabs * count + LINES, 128), BF16) for count in (rows_here, half)],
        [embeddings, group_of.reshape(line), cluster_id.reshape(line)],
    )
    along_by = [(first, second)]
    across_by = []
    for s in range(1, n_blk - 1):
        moved = [along(piece) for piece in along_by[-1]]
        swapped = [across(piece) for piece in along_by[-1]]
        moved[0], swapped[0] = together(moved[0], swapped[0])
        moved[1], swapped[1], _ = together(moved[1], swapped[1], moved[0])
        along_by.append(tuple(moved))
        across_by.append(tuple(swapped))
    near = along_by[1]
    over = [other_core(piece) for piece in near]
    over[0], _ = together(over[0], along_by[2][0])
    near_sum, *over_sum = call(
        back_kernel,
        [((rows_here, width + 128), F32)]
        + [((rows_here // PARTS, width + 256), BF16)] * PARTS,
        [*near, *over, first, second, *across_by[0]],
    )
    near_sum, _ = together(near_sum, along_by[2][1])
    (to_return,) = call(
        back_sum_kernel,
        [((slabs * rows_here + LINES, 128), BF16)],
        [near_sum, *[other_core(part) for part in over_sum]],
    )
    returned = back_along(to_return)
    first_crossed = across(along_by[-1][0])
    last_half, first_crossed = together(along_by[-1][1], first_crossed)
    across_by.append((first_crossed, across(last_half)))
    left = (whole, other_core(whole))
    early = across_by[:-1] + along_by[1:]
    mine, theirs, info = start_both(left, early, (rows_here, width + 128))
    late = [across_by[-1]]
    mine, *theirs = add_both((*left, info), late, (mine, theirs))
    out = finish(
        (rows_here, width), [mine, returned, *[other_core(part) for part in theirs]]
    )
    return out


def per_device(embeddings, group_of, cluster_id):
    rows_here, width = embeddings.shape
    devices = lax.axis_size("blk") * lax.axis_size("sub") * lax.axis_size("pair")
    small = devices * rows_here * width * 2 <= GATHER_LIMIT and lax.axis_size("blk") > 3
    fits = width % 128 == 0 and rows_here % (64 * PARTS) == 0 and rows_here <= 256
    if small and fits and lax.axis_size("sub") == 2 and lax.axis_size("pair") == 2:
        return by_block(embeddings, group_of, cluster_id)
    return by_group(embeddings, group_of, cluster_id)


def solution(mesh):
    return jax.shard_map(
        per_device,
        mesh=mesh,
        in_specs=(
            P(("island", "blk", "sub", "pair"), None),
            P(("island", "blk", "sub", "pair"), None),
            P(("island", "blk", "sub", "pair")),
        ),
        out_specs=P(("island", "blk", "sub", "pair"), None),
        check_vma=False,
    )
```

```python
import functools

import jax
import jax.numpy as jnp
from jax import lax
from jax.experimental import pallas as pl
from jax.experimental.pallas import tpu as pltpu
from jax.sharding import PartitionSpec as P

F32 = jnp.float32
BF16 = jnp.bfloat16
VMEM_BYTES = 24 * 1024 * 1024
PARTS = 3
LINES = 16
GATHER_LIMIT = 8 * 1024 * 1024


def unit_scale(rows_in):
    wide = rows_in.astype(F32)
    return lax.rsqrt(jnp.sum(wide * wide, axis=1) + 1e-06)


def tile_weights(left_rows, left_clust, left_scale, right_rows, right_clust, right_scale):
    grams = lax.dot_general(
        left_rows, right_rows, (((1,), (1,)), ((), ())), preferred_element_type=F32
    )
    cosine = grams * left_scale[:, None] * right_scale[None, :]
    same = (left_clust[:, None] == right_clust[None, :]).astype(F32)
    return jax.nn.sigmoid(8.0 * cosine - 2.0) * same


def by_group(embeddings, group_of, cluster_id):
    rows_here, width = embeddings.shape
    groups = lax.axis_size("sub") * lax.axis_size("pair")
    capacity = 2 * rows_here // groups
    slots = groups * capacity
    target = group_of[:, 0]
    onehot = (target[:, None] == jnp.arange(groups, dtype=jnp.int32)[None, :]).astype(jnp.int32)
    position = jnp.sum((jnp.cumsum(onehot, axis=0) - onehot) * onehot, axis=1)
    send_rows = jnp.zeros((groups, capacity, width), BF16).at[target, position].set(embeddings)
    send_clust = jnp.full((groups, capacity), -1, jnp.int32).at[target, position].set(cluster_id)
    recv_rows, recv_clust = (
        lax.all_to_all(send_rows, ("sub", "pair"), split_axis=0, concat_axis=0, tiled=True),
        lax.all_to_all(send_clust, ("sub", "pair"), split_axis=0, concat_axis=0, tiled=True),
    )
    own_rows = recv_rows.reshape(slots, width)
    own_clust = recv_clust.reshape(slots)
    own_scale = unit_scale(own_rows)
    piece_rows = lax.all_gather(own_rows, "blk", axis=0, tiled=True)
    piece_clust = lax.all_gather(own_clust, "blk", axis=0, tiled=True)
    weight = tile_weights(
        own_rows, own_clust, own_scale, piece_rows, piece_clust, unit_scale(piece_rows)
    )
    numer = jnp.dot(weight.astype(BF16), piece_rows, preferred_element_type=F32)
    denom = jnp.sum(weight, axis=1)
    result = (numer / denom[:, None]).astype(BF16).reshape(groups, capacity, width)
    returned = lax.all_to_all(result, ("sub", "pair"), split_axis=0, concat_axis=0, tiled=True)
    return returned[target, position]


def diagonal(size):
    shape = (size, size)
    return lax.broadcasted_iota(jnp.int32, shape, 0) == lax.broadcasted_iota(jnp.int32, shape, 1)


def to_column(row):
    size = row.shape[1]
    return jnp.sum(jnp.where(diagonal(size), row, jnp.zeros_like(row)), axis=1, keepdims=True)


def to_row(column):
    size = column.shape[0]
    return jnp.sum(jnp.where(diagonal(size), column, jnp.zeros_like(column)), axis=0, keepdims=True)


def scale_column(rows):
    wide = rows.astype(F32)
    return lax.rsqrt(jnp.sum(wide * wide, axis=1, keepdims=True) + 1e-06)


def first_pack_kernel(rows, first):
    half = rows.shape[0] // 2
    for slab in range(rows.shape[1] // 128):
        first[slab * half : (slab + 1) * half, :] = rows[:half, slab * 128 : (slab + 1) * 128]


def pack_kernel(rows, group, cluster, whole, second):
    rows_here, width = rows.shape
    slabs = width // 128
    half = rows_here // 2
    for slab in range(slabs):
        columns = rows[:, slab * 128 : (slab + 1) * 128]
        whole[slab * rows_here : (slab + 1) * rows_here, :] = columns
        second[slab * half : (slab + 1) * half, :] = columns[half:]
    line_at = lax.broadcasted_iota(jnp.int32, (LINES, 128), 0)
    named = jnp.zeros((LINES, 128), jnp.int32)
    for line in range(4):
        top = line % 2 * half
        part = (group, cluster)[line // 2][:, top : top + half]
        if half < 128:
            part = jnp.concatenate([part, jnp.zeros((1, 128 - half), jnp.int32)], axis=1)
        named = jnp.where(line_at == line, part, named)
    named = named.astype(F32).astype(BF16)
    whole[slabs * rows_here :, :] = named
    second[slabs * half :, :] = named


def from_slabs(ref, count):
    slabs = [ref[top : top + count, :] for top in range(0, ref.shape[0] // count * count, count)]
    return jnp.concatenate(slabs, axis=1)


def key_rows(ref, half):
    wide = ref[ref.shape[0] - LINES :, :].astype(F32)
    return [
        wide[side : side + 1, :half] * 256.0 + wide[side + 2 : side + 3, :half]
        for side in range(2)
    ]


def key_row(ref, rows_here):
    return jnp.concatenate(key_rows(ref, rows_here // 2), axis=1)


def from_halves(first, second, rows_here):
    half = rows_here // 2
    rows = jnp.concatenate([from_slabs(first, half), from_slabs(second, half)], axis=0)
    return rows, key_row(second, rows_here)


def add_blocks(left, info, blocks, numer, denom):
    key = info[: left.shape[0], 0:1]
    scale = info[: left.shape[0], 1:2]
    right_rows = jnp.concatenate([block[0] for block in blocks], axis=0)
    right_key = jnp.concatenate([block[1] for block in blocks], axis=1)
    right_scale = jnp.concatenate([block[2] for block in blocks], axis=1)
    grams = lax.dot_general(
        left, right_rows, (((1,), (1,)), ((), ())), preferred_element_type=F32
    )
    half = jnp.tanh(grams * scale * right_scale - 1.0)
    weight = jnp.where(key == right_key, 0.5 + 0.5 * half, 0.0)
    add = jnp.dot(weight.astype(BF16), right_rows, preferred_element_type=F32)
    add_denom = jnp.sum(weight, axis=1, keepdims=True)
    if numer is None:
        return add, add_denom
    return numer + add, denom + add_denom


def left_rows(refs, rows_here):
    return jnp.concatenate([from_slabs(ref, rows_here) for ref in refs], axis=0)


def take_blocks(refs, count, rows_here):
    blocks = []
    for _ in range(count):
        rows, key = from_halves(refs.pop(0), refs.pop(0), rows_here)
        blocks.append((rows, key, to_row(scale_column(rows))))
    return blocks


def store_sides(numer, denom, outs):
    rows_here, wide = outs[0].shape
    for side, out in enumerate(outs):
        top = side * rows_here
        out[:, : wide - 128] = numer[top : top + rows_here]
        out[:, wide - 128 :] = jnp.broadcast_to(denom[top : top + rows_here], (rows_here, 128))


def store_theirs(numer, denom, outs):
    high = denom.astype(BF16).astype(F32)
    lane = lax.broadcasted_iota(jnp.int32, (denom.shape[0], 128), 1)
    pair = jnp.where(lane == 0, high, denom - high).astype(BF16)
    count, wide = outs[0].shape
    for part, out in enumerate(outs):
        rows = slice(part * count, (part + 1) * count)
        out[:, : wide - 128] = numer[rows].astype(BF16)
        out[:, wide - 128 :] = pair[rows]


def add_theirs(mine, parts):
    width = mine.shape[1] - 128
    theirs = jnp.concatenate([ref[...] for ref in parts], axis=0)
    pair = theirs[:, width:].astype(F32)
    numer = mine[:, :width] + theirs[:, :width].astype(F32)
    return numer, mine[:, width : width + 1] + (pair[:, 0:1] + pair[:, 1:2])


def back_kernel(near_first, near_second, over_first, over_second, *refs):
    refs = list(refs)
    rows_here = refs[4].shape[0]
    blocks = take_blocks(refs, 2, rows_here)
    mine, *theirs = refs
    sides = [
        from_halves(near_first, near_second, rows_here),
        from_halves(over_first, over_second, rows_here),
    ]
    left = jnp.concatenate([side[0] for side in sides], axis=0)
    key = jnp.concatenate([to_column(side[1]) for side in sides], axis=0)
    lane = lax.broadcasted_iota(jnp.int32, (2 * rows_here, 128), 1)
    info = jnp.where(lane == 0, key, 4.0 * scale_column(left))
    numer, denom = add_blocks(left, info, blocks, None, None)
    store_sides(numer[:rows_here], denom[:rows_here], [mine])
    store_theirs(numer[rows_here:], denom[rows_here:], theirs)


def back_sum_kernel(mine, *refs):
    *parts, out = refs
    rows_here = mine.shape[0]
    half = rows_here // 2
    numer, denom = add_theirs(mine, parts)
    slabs = numer.shape[1] // 128
    for slab in range(slabs):
        out[slab * rows_here : (slab + 1) * rows_here, :] = numer[
            :, slab * 128 : (slab + 1) * 128
        ].astype(BF16)
    high = denom.astype(BF16).astype(F32)
    line_at = lax.broadcasted_iota(jnp.int32, (LINES, 128), 0)
    lines = jnp.zeros((LINES, 128), F32)
    for kind, column in enumerate((high, denom - high)):
        row = to_row(column)
        for side in range(2):
            part = row[:, side * half : (side + 1) * half]
            if half < 128:
                part = jnp.concatenate([part, jnp.zeros((1, 128 - half), F32)], axis=1)
            lines = jnp.where(line_at == 2 * kind + side, part, lines)
    out[slabs * rows_here :, :] = lines.astype(BF16)


def start_kernel(n_blocks, own, other, *refs):
    refs = list(refs)
    rows_here = refs[-1].shape[0] // 2
    left = left_rows((own, other), rows_here)
    key = jnp.concatenate([to_column(key_row(ref, rows_here)) for ref in (own, other)], axis=0)
    scale = scale_column(left)
    info = refs.pop()
    lane = lax.broadcasted_iota(jnp.int32, info.shape, 1)
    info[...] = jnp.where(lane == 0, key, 4.0 * scale)
    first = (left[:rows_here], key_row(own, rows_here), to_row(scale[:rows_here]))
    blocks = [first] + take_blocks(refs, n_blocks, rows_here)
    store_sides(*add_blocks(left, info, blocks, None, None), refs)


def both_kernel(n_blocks, own, other, info, *refs):
    refs = list(refs)
    rows_here = refs[2 * n_blocks].shape[0]
    blocks = take_blocks(refs, n_blocks, rows_here)
    mine_in, theirs_in, mine, *theirs = refs
    wide = mine.shape[1]
    width = wide - 128
    left = left_rows((own, other), rows_here)
    numer = jnp.concatenate([ref[:, :width] for ref in (mine_in, theirs_in)], axis=0)
    denom = jnp.concatenate([ref[:, width : width + 1] for ref in (mine_in, theirs_in)], axis=0)
    numer, denom = add_blocks(left, info, blocks, numer, denom)
    store_sides(numer[:rows_here], denom[:rows_here], [mine])
    store_theirs(numer[rows_here:], denom[rows_here:], theirs)


def last_kernel(mine, returned, *refs):
    *parts, out, staged, sems = refs
    rows_here, width = out.shape
    half = rows_here // 2
    numer, denom = add_theirs(mine, parts)
    numer = numer + from_slabs(returned, rows_here).astype(F32)
    lines = returned[returned.shape[0] - LINES :, :].astype(F32)[:4, :half]
    total = lines[0:2] + lines[2:4]
    denom = denom + to_column(jnp.concatenate([total[0:1], total[1:2]], axis=1))
    share = 1.0 / denom
    count = rows_here // 4
    copies = []
    for part in range(4):
        rows = slice(part * count, (part + 1) * count)
        staged[rows, :] = (numer[rows] * share[rows]).astype(BF16)
        copies.append(pltpu.make_async_copy(staged.at[rows, :], out.at[rows, :], sems.at[part]))
        copies[-1].start()
    for copy in copies:
        copy.wait()


def whole_in_vmem(count):
    return [pl.BlockSpec(memory_space=pltpu.VMEM)] * count


def call(kernel, shapes, args, aliases={}):
    return pl.pallas_call(
        kernel,
        out_shape=[jax.ShapeDtypeStruct(shape, dtype) for shape, dtype in shapes],
        in_specs=whole_in_vmem(len(args)),
        out_specs=whole_in_vmem(len(shapes)),
        input_output_aliases=aliases,
        compiler_params=pltpu.CompilerParams(vmem_limit_bytes=VMEM_BYTES),
    )(*args)


def start_both(left, right, shape):
    rows_here = shape[0]
    args = list(left) + [half for block in right for half in block]
    shapes = [(shape, F32), (shape, F32), ((2 * rows_here, 128), F32)]
    return call(functools.partial(start_kernel, len(right)), shapes, args)


def add_both(left, right, before):
    args = list(left) + [half for block in right for half in block] + list(before)
    rows_here, wide = before[0].shape
    shapes = [((rows_here, wide), F32)] + [((rows_here // PARTS, wide), BF16)] * PARTS
    kernel = functools.partial(both_kernel, len(right))
    return call(kernel, shapes, args, {len(args) - 2: 0})


def finish(shape, args):
    return pl.pallas_call(
        last_kernel,
        out_shape=jax.ShapeDtypeStruct(shape, BF16),
        in_specs=whole_in_vmem(len(args)),
        out_specs=pl.BlockSpec(memory_space=pl.ANY),
        scratch_shapes=[pltpu.VMEM(shape, BF16), pltpu.SemaphoreType.DMA((4,))],
        compiler_params=pltpu.CompilerParams(vmem_limit_bytes=VMEM_BYTES),
    )(*args)


def folded_ring(size):
    return list(range(0, size, 2)) + list(range(1, size, 2))[::-1]


def together(*arrays):
    return lax.optimization_barrier(arrays)


def by_block(embeddings, group_of, cluster_id):
    rows_here, width = embeddings.shape
    half = rows_here // 2
    slabs = width // 128
    n_blk = lax.axis_size("blk")
    order = folded_ring(n_blk)
    line = (1, rows_here)

    def along(rows):
        hops = [
            (2 * order[i - 1] + core, 2 * order[i] + 1 - core)
            for i in range(n_blk)
            for core in range(2)
        ]
        return lax.ppermute(rows, ("blk", "pair"), hops)

    def back_along(rows):
        hops = [
            (2 * order[i] + core, 2 * order[i - 1] + 1 - core)
            for i in range(n_blk)
            for core in range(2)
        ]
        return lax.ppermute(rows, ("blk", "pair"), hops)

    def across(rows):
        return lax.ppermute(rows, ("sub", "pair"), [(0, 3), (1, 2), (2, 1), (3, 0)])

    def other_core(rows):
        return lax.ppermute(rows, "pair", [(0, 1), (1, 0)])

    (first,) = call(first_pack_kernel, [((slabs * half + LINES, 128), BF16)], [embeddings])
    whole, second = call(
        pack_kernel,
        [((slabs * count + LINES, 128), BF16) for count in (rows_here, half)],
        [embeddings, group_of.reshape(line), cluster_id.reshape(line)],
    )
    along_by = [(first, second)]
    across_by = []
    for s in range(1, n_blk - 1):
        moved = [along(piece) for piece in along_by[-1]]
        swapped = [across(piece) for piece in along_by[-1]]
        moved[0], swapped[0] = together(moved[0], swapped[0])
        moved[1], swapped[1], _ = together(moved[1], swapped[1], moved[0])
        along_by.append(tuple(moved))
        across_by.append(tuple(swapped))
    near = along_by[1]
    over = [other_core(piece) for piece in near]
    over[0], _ = together(over[0], along_by[2][0])
    near_sum, *over_sum = call(
        back_kernel,
        [((rows_here, width + 128), F32)]
        + [((rows_here // PARTS, width + 128), BF16)] * PARTS,
        [*near, *over, first, second, *across_by[0]],
    )
    near_sum, _ = together(near_sum, along_by[2][1])
    (to_return,) = call(
        back_sum_kernel,
        [((slabs * rows_here + LINES, 128), BF16)],
        [near_sum, *[other_core(part) for part in over_sum]],
    )
    returned = back_along(to_return)
    first_crossed = across(along_by[-1][0])
    last_half, first_crossed = together(along_by[-1][1], first_crossed)
    across_by.append((first_crossed, across(last_half)))
    left = (whole, other_core(whole))
    early = across_by[:-1] + along_by[1:]
    mine, theirs, info = start_both(left, early, (rows_here, width + 128))
    late = [across_by[-1]]
    mine, *theirs = add_both((*left, info), late, (mine, theirs))
    out = finish(
        (rows_here, width), [mine, returned, *[other_core(part) for part in theirs]]
    )
    return out


def per_device(embeddings, group_of, cluster_id):
    rows_here, width = embeddings.shape
    devices = lax.axis_size("blk") * lax.axis_size("sub") * lax.axis_size("pair")
    small = devices * rows_here * width * 2 <= GATHER_LIMIT and lax.axis_size("blk") > 3
    fits = width % 128 == 0 and rows_here % (64 * PARTS) == 0 and rows_here <= 256
    if small and fits and lax.axis_size("sub") == 2 and lax.axis_size("pair") == 2:
        return by_block(embeddings, group_of, cluster_id)
    return by_group(embeddings, group_of, cluster_id)


def solution(mesh):
    return jax.shard_map(
        per_device,
        mesh=mesh,
        in_specs=(
            P(("island", "blk", "sub", "pair"), None),
            P(("island", "blk", "sub", "pair"), None),
            P(("island", "blk", "sub", "pair")),
        ),
        out_specs=P(("island", "blk", "sub", "pair"), None),
        check_vma=False,
    )
```

```python
import functools

import jax
import jax.numpy as jnp
from jax import lax
from jax.experimental import pallas as pl
from jax.experimental.pallas import tpu as pltpu
from jax.sharding import PartitionSpec as P

F32 = jnp.float32
BF16 = jnp.bfloat16
VMEM_BYTES = 24 * 1024 * 1024
PARTS = 3
LINES = 16
GATHER_LIMIT = 8 * 1024 * 1024


def unit_scale(rows_in):
    wide = rows_in.astype(F32)
    return lax.rsqrt(jnp.sum(wide * wide, axis=1) + 1e-06)


def tile_weights(left_rows, left_clust, left_scale, right_rows, right_clust, right_scale):
    grams = lax.dot_general(
        left_rows, right_rows, (((1,), (1,)), ((), ())), preferred_element_type=F32
    )
    cosine = grams * left_scale[:, None] * right_scale[None, :]
    same = (left_clust[:, None] == right_clust[None, :]).astype(F32)
    return jax.nn.sigmoid(8.0 * cosine - 2.0) * same


def by_group(embeddings, group_of, cluster_id):
    rows_here, width = embeddings.shape
    groups = lax.axis_size("sub") * lax.axis_size("pair")
    capacity = 2 * rows_here // groups
    slots = groups * capacity
    target = group_of[:, 0]
    onehot = (target[:, None] == jnp.arange(groups, dtype=jnp.int32)[None, :]).astype(jnp.int32)
    position = jnp.sum((jnp.cumsum(onehot, axis=0) - onehot) * onehot, axis=1)
    send_rows = jnp.zeros((groups, capacity, width), BF16).at[target, position].set(embeddings)
    send_clust = jnp.full((groups, capacity), -1, jnp.int32).at[target, position].set(cluster_id)
    recv_rows, recv_clust = (
        lax.all_to_all(send_rows, ("sub", "pair"), split_axis=0, concat_axis=0, tiled=True),
        lax.all_to_all(send_clust, ("sub", "pair"), split_axis=0, concat_axis=0, tiled=True),
    )
    own_rows = recv_rows.reshape(slots, width)
    own_clust = recv_clust.reshape(slots)
    own_scale = unit_scale(own_rows)
    piece_rows = lax.all_gather(own_rows, "blk", axis=0, tiled=True)
    piece_clust = lax.all_gather(own_clust, "blk", axis=0, tiled=True)
    weight = tile_weights(
        own_rows, own_clust, own_scale, piece_rows, piece_clust, unit_scale(piece_rows)
    )
    numer = jnp.dot(weight.astype(BF16), piece_rows, preferred_element_type=F32)
    denom = jnp.sum(weight, axis=1)
    result = (numer / denom[:, None]).astype(BF16).reshape(groups, capacity, width)
    returned = lax.all_to_all(result, ("sub", "pair"), split_axis=0, concat_axis=0, tiled=True)
    return returned[target, position]


def diagonal(size):
    shape = (size, size)
    return lax.broadcasted_iota(jnp.int32, shape, 0) == lax.broadcasted_iota(jnp.int32, shape, 1)


def to_column(row):
    size = row.shape[1]
    return jnp.sum(jnp.where(diagonal(size), row, jnp.zeros_like(row)), axis=1, keepdims=True)


def to_row(column):
    size = column.shape[0]
    return jnp.sum(jnp.where(diagonal(size), column, jnp.zeros_like(column)), axis=0, keepdims=True)


def scale_column(rows):
    wide = rows.astype(F32)
    return lax.rsqrt(jnp.sum(wide * wide, axis=1, keepdims=True) + 1e-06)


def first_pack_kernel(rows, first):
    half = rows.shape[0] // 2
    for slab in range(rows.shape[1] // 128):
        first[slab * half : (slab + 1) * half, :] = rows[:half, slab * 128 : (slab + 1) * 128]


def pack_kernel(rows, group, cluster, whole, second):
    rows_here, width = rows.shape
    slabs = width // 128
    half = rows_here // 2
    for slab in range(slabs):
        columns = rows[:, slab * 128 : (slab + 1) * 128]
        whole[slab * rows_here : (slab + 1) * rows_here, :] = columns
        second[slab * half : (slab + 1) * half, :] = columns[half:]
    line_at = lax.broadcasted_iota(jnp.int32, (LINES, 128), 0)
    named = jnp.zeros((LINES, 128), jnp.int32)
    for line in range(4):
        top = line % 2 * half
        part = (group, cluster)[line // 2][:, top : top + half]
        if half < 128:
            part = jnp.concatenate([part, jnp.zeros((1, 128 - half), jnp.int32)], axis=1)
        named = jnp.where(line_at == line, part, named)
    named = named.astype(F32).astype(BF16)
    whole[slabs * rows_here :, :] = named
    second[slabs * half :, :] = named


def from_slabs(ref, count):
    slabs = [ref[top : top + count, :] for top in range(0, ref.shape[0] // count * count, count)]
    return jnp.concatenate(slabs, axis=1)


def key_rows(ref, half):
    wide = ref[ref.shape[0] - LINES :, :].astype(F32)
    return [
        wide[side : side + 1, :half] * 256.0 + wide[side + 2 : side + 3, :half]
        for side in range(2)
    ]


def key_row(ref, rows_here):
    return jnp.concatenate(key_rows(ref, rows_here // 2), axis=1)


def from_halves(first, second, rows_here):
    half = rows_here // 2
    rows = jnp.concatenate([from_slabs(first, half), from_slabs(second, half)], axis=0)
    return rows, key_row(second, rows_here)


def add_blocks(left, info, blocks, numer, denom):
    key = info[: left.shape[0], 0:1]
    scale = info[: left.shape[0], 1:2]
    right_rows = jnp.concatenate([block[0] for block in blocks], axis=0)
    right_key = jnp.concatenate([block[1] for block in blocks], axis=1)
    right_scale = jnp.concatenate([block[2] for block in blocks], axis=1)
    grams = lax.dot_general(
        left, right_rows, (((1,), (1,)), ((), ())), preferred_element_type=F32
    )
    half = jnp.tanh(grams * scale * right_scale - 1.0)
    weight = jnp.where(key == right_key, 0.5 + 0.5 * half, 0.0)
    add = jnp.dot(weight.astype(BF16), right_rows, preferred_element_type=F32)
    add_denom = jnp.sum(weight, axis=1, keepdims=True)
    if numer is None:
        return add, add_denom
    return numer + add, denom + add_denom


def left_rows(refs, rows_here):
    return jnp.concatenate([from_slabs(ref, rows_here) for ref in refs], axis=0)


def take_blocks(refs, count, rows_here):
    blocks = []
    for _ in range(count):
        rows, key = from_halves(refs.pop(0), refs.pop(0), rows_here)
        blocks.append((rows, key, to_row(scale_column(rows))))
    return blocks


def store_sides(numer, denom, outs):
    rows_here, wide = outs[0].shape
    for side, out in enumerate(outs):
        top = side * rows_here
        out[:, : wide - 128] = numer[top : top + rows_here]
        out[:, wide - 128 :] = jnp.broadcast_to(denom[top : top + rows_here], (rows_here, 128))


def store_theirs(numer, denom, outs):
    high = denom.astype(BF16).astype(F32)
    lane = lax.broadcasted_iota(jnp.int32, (denom.shape[0], 128), 1)
    pair = jnp.where(lane == 0, high, denom - high).astype(BF16)
    count, wide = outs[0].shape
    for part, out in enumerate(outs):
        rows = slice(part * count, (part + 1) * count)
        out[:, : wide - 128] = numer[rows].astype(BF16)
        out[:, wide - 128 :] = pair[rows]


def add_theirs(mine, parts):
    width = mine.shape[1] - 128
    theirs = jnp.concatenate([ref[...] for ref in parts], axis=0)
    pair = theirs[:, width:].astype(F32)
    numer = mine[:, :width] + theirs[:, :width].astype(F32)
    return numer, mine[:, width : width + 1] + (pair[:, 0:1] + pair[:, 1:2])


def back_kernel(near_first, near_second, over_first, over_second, *refs):
    refs = list(refs)
    rows_here = refs[4].shape[0]
    blocks = take_blocks(refs, 2, rows_here)
    mine, *theirs = refs
    sides = [
        from_halves(near_first, near_second, rows_here),
        from_halves(over_first, over_second, rows_here),
    ]
    left = jnp.concatenate([side[0] for side in sides], axis=0)
    key = jnp.concatenate([to_column(side[1]) for side in sides], axis=0)
    lane = lax.broadcasted_iota(jnp.int32, (2 * rows_here, 128), 1)
    info = jnp.where(lane == 0, key, 4.0 * scale_column(left))
    numer, denom = add_blocks(left, info, blocks, None, None)
    store_sides(numer[:rows_here], denom[:rows_here], [mine])
    store_theirs(numer[rows_here:], denom[rows_here:], theirs)


def back_sum_kernel(mine, *refs):
    *parts, out = refs
    rows_here = mine.shape[0]
    half = rows_here // 2
    numer, denom = add_theirs(mine, parts)
    slabs = numer.shape[1] // 128
    for slab in range(slabs):
        out[slab * rows_here : (slab + 1) * rows_here, :] = numer[
            :, slab * 128 : (slab + 1) * 128
        ].astype(BF16)
    high = denom.astype(BF16).astype(F32)
    line_at = lax.broadcasted_iota(jnp.int32, (LINES, 128), 0)
    lines = jnp.zeros((LINES, 128), F32)
    for kind, column in enumerate((high, denom - high)):
        row = to_row(column)
        for side in range(2):
            part = row[:, side * half : (side + 1) * half]
            if half < 128:
                part = jnp.concatenate([part, jnp.zeros((1, 128 - half), F32)], axis=1)
            lines = jnp.where(line_at == 2 * kind + side, part, lines)
    out[slabs * rows_here :, :] = lines.astype(BF16)


def start_kernel(n_blocks, own, other, *refs):
    refs = list(refs)
    rows_here = refs[-1].shape[0] // 2
    left = left_rows((own, other), rows_here)
    key = jnp.concatenate([to_column(key_row(ref, rows_here)) for ref in (own, other)], axis=0)
    scale = scale_column(left)
    info = refs.pop()
    lane = lax.broadcasted_iota(jnp.int32, info.shape, 1)
    info[...] = jnp.where(lane == 0, key, 4.0 * scale)
    first = (left[:rows_here], key_row(own, rows_here), to_row(scale[:rows_here]))
    blocks = [first] + take_blocks(refs, n_blocks, rows_here)
    store_sides(*add_blocks(left, info, blocks, None, None), refs)


def both_kernel(n_blocks, own, other, info, *refs):
    refs = list(refs)
    rows_here = refs[2 * n_blocks].shape[0]
    blocks = take_blocks(refs, n_blocks, rows_here)
    mine_in, theirs_in, mine, *theirs = refs
    wide = mine.shape[1]
    width = wide - 128
    left = left_rows((own, other), rows_here)
    numer = jnp.concatenate([ref[:, :width] for ref in (mine_in, theirs_in)], axis=0)
    denom = jnp.concatenate([ref[:, width : width + 1] for ref in (mine_in, theirs_in)], axis=0)
    numer, denom = add_blocks(left, info, blocks, numer, denom)
    store_sides(numer[:rows_here], denom[:rows_here], [mine])
    store_theirs(numer[rows_here:], denom[rows_here:], theirs)


def last_kernel(mine, returned, *refs):
    *parts, out, staged, sems = refs
    rows_here, width = out.shape
    half = rows_here // 2
    numer, denom = add_theirs(mine, parts)
    numer = numer + from_slabs(returned, rows_here).astype(F32)
    lines = returned[returned.shape[0] - LINES :, :].astype(F32)[:4, :half]
    total = lines[0:2] + lines[2:4]
    denom = denom + to_column(jnp.concatenate([total[0:1], total[1:2]], axis=1))
    share = 1.0 / denom
    count = rows_here // 4
    copies = []
    for part in range(4):
        rows = slice(part * count, (part + 1) * count)
        staged[rows, :] = (numer[rows] * share[rows]).astype(BF16)
        copies.append(pltpu.make_async_copy(staged.at[rows, :], out.at[rows, :], sems.at[part]))
        copies[-1].start()
    for copy in copies:
        copy.wait()


def whole_in_vmem(count):
    return [pl.BlockSpec(memory_space=pltpu.VMEM)] * count


def call(kernel, shapes, args, aliases={}):
    return pl.pallas_call(
        kernel,
        out_shape=[jax.ShapeDtypeStruct(shape, dtype) for shape, dtype in shapes],
        in_specs=whole_in_vmem(len(args)),
        out_specs=whole_in_vmem(len(shapes)),
        input_output_aliases=aliases,
        compiler_params=pltpu.CompilerParams(vmem_limit_bytes=VMEM_BYTES),
    )(*args)


def start_both(left, right, shape):
    rows_here = shape[0]
    args = list(left) + [half for block in right for half in block]
    shapes = [(shape, F32), (shape, F32), ((2 * rows_here, 128), F32)]
    return call(functools.partial(start_kernel, len(right)), shapes, args)


def add_both(left, right, before):
    args = list(left) + [half for block in right for half in block] + list(before)
    rows_here, wide = before[0].shape
    shapes = [((rows_here, wide), F32)] + [((rows_here // PARTS, wide), BF16)] * PARTS
    kernel = functools.partial(both_kernel, len(right))
    return call(kernel, shapes, args, {len(args) - 2: 0})


def finish(shape, args):
    return pl.pallas_call(
        last_kernel,
        out_shape=jax.ShapeDtypeStruct(shape, BF16),
        in_specs=whole_in_vmem(len(args)),
        out_specs=pl.BlockSpec(memory_space=pl.ANY),
        scratch_shapes=[pltpu.VMEM(shape, BF16), pltpu.SemaphoreType.DMA((4,))],
        compiler_params=pltpu.CompilerParams(vmem_limit_bytes=VMEM_BYTES),
    )(*args)


def folded_ring(size):
    return list(range(0, size, 2)) + list(range(1, size, 2))[::-1]


def together(*arrays):
    return lax.optimization_barrier(arrays)


def by_block(embeddings, group_of, cluster_id):
    rows_here, width = embeddings.shape
    half = rows_here // 2
    slabs = width // 128
    n_blk = lax.axis_size("blk")
    order = folded_ring(n_blk)
    line = (1, rows_here)

    def along(rows):
        hops = [
            (2 * order[i - 1] + core, 2 * order[i] + 1 - core)
            for i in range(n_blk)
            for core in range(2)
        ]
        return lax.ppermute(rows, ("blk", "pair"), hops)

    def back_along(rows):
        hops = [
            (2 * order[i] + core, 2 * order[i - 1] + 1 - core)
            for i in range(n_blk)
            for core in range(2)
        ]
        return lax.ppermute(rows, ("blk", "pair"), hops)

    def across(rows):
        return lax.ppermute(rows, ("sub", "pair"), [(0, 3), (1, 2), (2, 1), (3, 0)])

    def other_core(rows):
        return lax.ppermute(rows, "pair", [(0, 1), (1, 0)])

    (first,) = call(first_pack_kernel, [((slabs * half + LINES // 2, 128), BF16)], [embeddings])
    whole, second = call(
        pack_kernel,
        [((slabs * count + LINES, 128), BF16) for count in (rows_here, half)],
        [embeddings, group_of.reshape(line), cluster_id.reshape(line)],
    )
    along_by = [(first, second)]
    across_by = []
    for s in range(1, n_blk - 1):
        moved = [along(piece) for piece in along_by[-1]]
        swapped = [across(piece) for piece in along_by[-1]]
        moved[0], swapped[0] = together(moved[0], swapped[0])
        moved[1], swapped[1], _ = together(moved[1], swapped[1], moved[0])
        along_by.append(tuple(moved))
        across_by.append(tuple(swapped))
    near = along_by[1]
    over = [other_core(piece) for piece in near]
    over[0], _ = together(over[0], along_by[2][0])
    near_sum, *over_sum = call(
        back_kernel,
        [((rows_here, width + 128), F32)]
        + [((rows_here // PARTS, width + 128), BF16)] * PARTS,
        [*near, *over, first, second, *across_by[0]],
    )
    near_sum, _ = together(near_sum, along_by[2][1])
    (to_return,) = call(
        back_sum_kernel,
        [((slabs * rows_here + LINES, 128), BF16)],
        [near_sum, *[other_core(part) for part in over_sum]],
    )
    returned = back_along(to_return)
    first_crossed = across(along_by[-1][0])
    last_half, first_crossed = together(along_by[-1][1], first_crossed)
    across_by.append((first_crossed, across(last_half)))
    left = (whole, other_core(whole))
    early = across_by[:-1] + along_by[1:]
    mine, theirs, info = start_both(left, early, (rows_here, width + 128))
    late = [across_by[-1]]
    mine, *theirs = add_both((*left, info), late, (mine, theirs))
    out = finish(
        (rows_here, width), [mine, returned, *[other_core(part) for part in theirs]]
    )
    return out


def per_device(embeddings, group_of, cluster_id):
    rows_here, width = embeddings.shape
    devices = lax.axis_size("blk") * lax.axis_size("sub") * lax.axis_size("pair")
    small = devices * rows_here * width * 2 <= GATHER_LIMIT and lax.axis_size("blk") > 3
    fits = width % 128 == 0 and rows_here % (64 * PARTS) == 0 and rows_here <= 256
    if small and fits and lax.axis_size("sub") == 2 and lax.axis_size("pair") == 2:
        return by_block(embeddings, group_of, cluster_id)
    return by_group(embeddings, group_of, cluster_id)


def solution(mesh):
    return jax.shard_map(
        per_device,
        mesh=mesh,
        in_specs=(
            P(("island", "blk", "sub", "pair"), None),
            P(("island", "blk", "sub", "pair"), None),
            P(("island", "blk", "sub", "pair")),
        ),
        out_specs=P(("island", "blk", "sub", "pair"), None),
        check_vma=False,
    )
```

```python
import functools

import jax
import jax.numpy as jnp
from jax import lax
from jax.experimental import pallas as pl
from jax.experimental.pallas import tpu as pltpu
from jax.sharding import PartitionSpec as P

F32 = jnp.float32
BF16 = jnp.bfloat16
VMEM_BYTES = 24 * 1024 * 1024
PARTS = 3
LINES = 16
GATHER_LIMIT = 8 * 1024 * 1024


def unit_scale(rows_in):
    wide = rows_in.astype(F32)
    return lax.rsqrt(jnp.sum(wide * wide, axis=1) + 1e-06)


def tile_weights(left_rows, left_clust, left_scale, right_rows, right_clust, right_scale):
    grams = lax.dot_general(
        left_rows, right_rows, (((1,), (1,)), ((), ())), preferred_element_type=F32
    )
    cosine = grams * left_scale[:, None] * right_scale[None, :]
    same = (left_clust[:, None] == right_clust[None, :]).astype(F32)
    return jax.nn.sigmoid(8.0 * cosine - 2.0) * same


def by_group(embeddings, group_of, cluster_id):
    rows_here, width = embeddings.shape
    groups = lax.axis_size("sub") * lax.axis_size("pair")
    capacity = 2 * rows_here // groups
    slots = groups * capacity
    target = group_of[:, 0]
    onehot = (target[:, None] == jnp.arange(groups, dtype=jnp.int32)[None, :]).astype(jnp.int32)
    position = jnp.sum((jnp.cumsum(onehot, axis=0) - onehot) * onehot, axis=1)
    send_rows = jnp.zeros((groups, capacity, width), BF16).at[target, position].set(embeddings)
    send_clust = jnp.full((groups, capacity), -1, jnp.int32).at[target, position].set(cluster_id)
    recv_rows, recv_clust = (
        lax.all_to_all(send_rows, ("sub", "pair"), split_axis=0, concat_axis=0, tiled=True),
        lax.all_to_all(send_clust, ("sub", "pair"), split_axis=0, concat_axis=0, tiled=True),
    )
    own_rows = recv_rows.reshape(slots, width)
    own_clust = recv_clust.reshape(slots)
    own_scale = unit_scale(own_rows)
    piece_rows = lax.all_gather(own_rows, "blk", axis=0, tiled=True)
    piece_clust = lax.all_gather(own_clust, "blk", axis=0, tiled=True)
    weight = tile_weights(
        own_rows, own_clust, own_scale, piece_rows, piece_clust, unit_scale(piece_rows)
    )
    numer = jnp.dot(weight.astype(BF16), piece_rows, preferred_element_type=F32)
    denom = jnp.sum(weight, axis=1)
    result = (numer / denom[:, None]).astype(BF16).reshape(groups, capacity, width)
    returned = lax.all_to_all(result, ("sub", "pair"), split_axis=0, concat_axis=0, tiled=True)
    return returned[target, position]


def diagonal(size):
    shape = (size, size)
    return lax.broadcasted_iota(jnp.int32, shape, 0) == lax.broadcasted_iota(jnp.int32, shape, 1)


def to_column(row):
    size = row.shape[1]
    return jnp.sum(jnp.where(diagonal(size), row, jnp.zeros_like(row)), axis=1, keepdims=True)


def to_row(column):
    size = column.shape[0]
    return jnp.sum(jnp.where(diagonal(size), column, jnp.zeros_like(column)), axis=0, keepdims=True)


def scale_column(rows):
    wide = rows.astype(F32)
    return lax.rsqrt(jnp.sum(wide * wide, axis=1, keepdims=True) + 1e-06)


def first_pack_kernel(rows, first):
    half = rows.shape[0] // 2
    for slab in range(rows.shape[1] // 128):
        first[slab * half : (slab + 1) * half, :] = rows[:half, slab * 128 : (slab + 1) * 128]


def pack_kernel(rows, group, cluster, whole, second):
    rows_here, width = rows.shape
    slabs = width // 128
    half = rows_here // 2
    for slab in range(slabs):
        columns = rows[:, slab * 128 : (slab + 1) * 128]
        whole[slab * rows_here : (slab + 1) * rows_here, :] = columns
        second[slab * half : (slab + 1) * half, :] = columns[half:]
    line_at = lax.broadcasted_iota(jnp.int32, (LINES, 128), 0)
    named = jnp.zeros((LINES, 128), jnp.int32)
    for line in range(4):
        top = line % 2 * half
        part = (group, cluster)[line // 2][:, top : top + half]
        if half < 128:
            part = jnp.concatenate([part, jnp.zeros((1, 128 - half), jnp.int32)], axis=1)
        named = jnp.where(line_at == line, part, named)
    named = named.astype(F32).astype(BF16)
    whole[slabs * rows_here :, :] = named
    second[slabs * half :, :] = named


def from_slabs(ref, count):
    slabs = [ref[top : top + count, :] for top in range(0, ref.shape[0] // count * count, count)]
    return jnp.concatenate(slabs, axis=1)


def key_rows(ref, half):
    wide = ref[ref.shape[0] - LINES :, :].astype(F32)
    return [
        wide[side : side + 1, :half] * 256.0 + wide[side + 2 : side + 3, :half]
        for side in range(2)
    ]


def key_row(ref, rows_here):
    return jnp.concatenate(key_rows(ref, rows_here // 2), axis=1)


def from_halves(first, second, rows_here):
    half = rows_here // 2
    rows = jnp.concatenate([from_slabs(first, half), from_slabs(second, half)], axis=0)
    return rows, key_row(second, rows_here)


def add_blocks(left, info, blocks, numer, denom):
    key = info[: left.shape[0], 0:1]
    scale = info[: left.shape[0], 1:2]
    right_rows = jnp.concatenate([block[0] for block in blocks], axis=0)
    right_key = jnp.concatenate([block[1] for block in blocks], axis=1)
    right_scale = jnp.concatenate([block[2] for block in blocks], axis=1)
    grams = lax.dot_general(
        left, right_rows, (((1,), (1,)), ((), ())), preferred_element_type=F32
    )
    half = jnp.tanh(grams * scale * right_scale - 1.0)
    weight = jnp.where(key == right_key, 0.5 + 0.5 * half, 0.0)
    add = jnp.dot(weight.astype(BF16), right_rows, preferred_element_type=F32)
    add_denom = jnp.sum(weight, axis=1, keepdims=True)
    if numer is None:
        return add, add_denom
    return numer + add, denom + add_denom


def left_rows(refs, rows_here):
    return jnp.concatenate([from_slabs(ref, rows_here) for ref in refs], axis=0)


def take_blocks(refs, count, rows_here):
    blocks = []
    for _ in range(count):
        rows, key = from_halves(refs.pop(0), refs.pop(0), rows_here)
        blocks.append((rows, key, to_row(scale_column(rows))))
    return blocks


def store_sides(numer, denom, outs):
    rows_here, wide = outs[0].shape
    for side, out in enumerate(outs):
        top = side * rows_here
        out[:, : wide - 128] = numer[top : top + rows_here]
        out[:, wide - 128 :] = jnp.broadcast_to(denom[top : top + rows_here], (rows_here, 128))


def store_theirs(numer, denom, outs):
    high = denom.astype(BF16).astype(F32)
    lane = lax.broadcasted_iota(jnp.int32, (denom.shape[0], 128), 1)
    pair = jnp.where(lane == 0, high, denom - high).astype(BF16)
    count, wide = outs[0].shape
    for part, out in enumerate(outs):
        rows = slice(part * count, (part + 1) * count)
        out[:, : wide - 128] = numer[rows].astype(BF16)
        out[:, wide - 128 :] = pair[rows]


def add_theirs(mine, parts):
    width = mine.shape[1] - 128
    theirs = jnp.concatenate([ref[...] for ref in parts], axis=0)
    pair = theirs[:, width:].astype(F32)
    numer = mine[:, :width] + theirs[:, :width].astype(F32)
    return numer, mine[:, width : width + 1] + (pair[:, 0:1] + pair[:, 1:2])


def back_kernel(near_first, near_second, over_first, over_second, *refs):
    refs = list(refs)
    rows_here = refs[4].shape[0]
    blocks = take_blocks(refs, 2, rows_here)
    mine, *theirs = refs
    sides = [
        from_halves(near_first, near_second, rows_here),
        from_halves(over_first, over_second, rows_here),
    ]
    left = jnp.concatenate([side[0] for side in sides], axis=0)
    key = jnp.concatenate([to_column(side[1]) for side in sides], axis=0)
    lane = lax.broadcasted_iota(jnp.int32, (2 * rows_here, 128), 1)
    info = jnp.where(lane == 0, key, 4.0 * scale_column(left))
    numer, denom = add_blocks(left, info, blocks, None, None)
    store_sides(numer[:rows_here], denom[:rows_here], [mine])
    store_theirs(numer[rows_here:], denom[rows_here:], theirs)


def back_sum_kernel(mine, *refs):
    *parts, out = refs
    rows_here = mine.shape[0]
    half = rows_here // 2
    numer, denom = add_theirs(mine, parts)
    slabs = numer.shape[1] // 128
    for slab in range(slabs):
        out[slab * rows_here : (slab + 1) * rows_here, :] = numer[
            :, slab * 128 : (slab + 1) * 128
        ].astype(BF16)
    high = denom.astype(BF16).astype(F32)
    line_at = lax.broadcasted_iota(jnp.int32, (LINES, 128), 0)
    lines = jnp.zeros((LINES, 128), F32)
    for kind, column in enumerate((high, denom - high)):
        row = to_row(column)
        for side in range(2):
            part = row[:, side * half : (side + 1) * half]
            if half < 128:
                part = jnp.concatenate([part, jnp.zeros((1, 128 - half), F32)], axis=1)
            lines = jnp.where(line_at == 2 * kind + side, part, lines)
    out[slabs * rows_here :, :] = lines.astype(BF16)


def start_kernel(n_blocks, own, other, *refs):
    refs = list(refs)
    rows_here = refs[-1].shape[0] // 2
    left = left_rows((own, other), rows_here)
    key = jnp.concatenate([to_column(key_row(ref, rows_here)) for ref in (own, other)], axis=0)
    scale = scale_column(left)
    info = refs.pop()
    lane = lax.broadcasted_iota(jnp.int32, info.shape, 1)
    info[...] = jnp.where(lane == 0, key, 4.0 * scale)
    first = (left[:rows_here], key_row(own, rows_here), to_row(scale[:rows_here]))
    blocks = [first] + take_blocks(refs, n_blocks, rows_here)
    store_sides(*add_blocks(left, info, blocks, None, None), refs)


def both_kernel(n_blocks, own, other, info, *refs):
    refs = list(refs)
    rows_here = refs[2 * n_blocks].shape[0]
    blocks = take_blocks(refs, n_blocks, rows_here)
    mine_in, theirs_in, mine, *theirs = refs
    wide = mine.shape[1]
    width = wide - 128
    left = left_rows((own, other), rows_here)
    numer = jnp.concatenate([ref[:, :width] for ref in (mine_in, theirs_in)], axis=0)
    denom = jnp.concatenate([ref[:, width : width + 1] for ref in (mine_in, theirs_in)], axis=0)
    numer, denom = add_blocks(left, info, blocks, numer, denom)
    store_sides(numer[:rows_here], denom[:rows_here], [mine])
    store_theirs(numer[rows_here:], denom[rows_here:], theirs)


def last_kernel(mine, returned, *refs):
    *parts, out, staged, sems = refs
    rows_here, width = out.shape
    half = rows_here // 2
    numer, denom = add_theirs(mine, parts)
    numer = numer + from_slabs(returned, rows_here).astype(F32)
    lines = returned[returned.shape[0] - LINES :, :].astype(F32)[:4, :half]
    total = lines[0:2] + lines[2:4]
    denom = denom + to_column(jnp.concatenate([total[0:1], total[1:2]], axis=1))
    share = 1.0 / denom
    count = rows_here // 4
    copies = []
    for part in range(4):
        rows = slice(part * count, (part + 1) * count)
        staged[rows, :] = (numer[rows] * share[rows]).astype(BF16)
        copies.append(pltpu.make_async_copy(staged.at[rows, :], out.at[rows, :], sems.at[part]))
        copies[-1].start()
    for copy in copies:
        copy.wait()


def whole_in_vmem(count):
    return [pl.BlockSpec(memory_space=pltpu.VMEM)] * count


def call(kernel, shapes, args, aliases={}):
    return pl.pallas_call(
        kernel,
        out_shape=[jax.ShapeDtypeStruct(shape, dtype) for shape, dtype in shapes],
        in_specs=whole_in_vmem(len(args)),
        out_specs=whole_in_vmem(len(shapes)),
        input_output_aliases=aliases,
        compiler_params=pltpu.CompilerParams(vmem_limit_bytes=VMEM_BYTES),
    )(*args)


def start_both(left, right, shape):
    rows_here = shape[0]
    args = list(left) + [half for block in right for half in block]
    shapes = [(shape, F32), (shape, F32), ((2 * rows_here, 128), F32)]
    return call(functools.partial(start_kernel, len(right)), shapes, args)


def add_both(left, right, before):
    args = list(left) + [half for block in right for half in block] + list(before)
    rows_here, wide = before[0].shape
    shapes = [((rows_here, wide), F32)] + [((rows_here // 2, wide), BF16)] * 2
    kernel = functools.partial(both_kernel, len(right))
    return call(kernel, shapes, args, {len(args) - 2: 0})


def finish(shape, args):
    return pl.pallas_call(
        last_kernel,
        out_shape=jax.ShapeDtypeStruct(shape, BF16),
        in_specs=whole_in_vmem(len(args)),
        out_specs=pl.BlockSpec(memory_space=pl.ANY),
        scratch_shapes=[pltpu.VMEM(shape, BF16), pltpu.SemaphoreType.DMA((4,))],
        compiler_params=pltpu.CompilerParams(vmem_limit_bytes=VMEM_BYTES),
    )(*args)


def folded_ring(size):
    return list(range(0, size, 2)) + list(range(1, size, 2))[::-1]


def together(*arrays):
    return lax.optimization_barrier(arrays)


def by_block(embeddings, group_of, cluster_id):
    rows_here, width = embeddings.shape
    half = rows_here // 2
    slabs = width // 128
    n_blk = lax.axis_size("blk")
    order = folded_ring(n_blk)
    line = (1, rows_here)

    def along(rows):
        hops = [
            (2 * order[i - 1] + core, 2 * order[i] + 1 - core)
            for i in range(n_blk)
            for core in range(2)
        ]
        return lax.ppermute(rows, ("blk", "pair"), hops)

    def back_along(rows):
        hops = [
            (2 * order[i] + core, 2 * order[i - 1] + 1 - core)
            for i in range(n_blk)
            for core in range(2)
        ]
        return lax.ppermute(rows, ("blk", "pair"), hops)

    def across(rows):
        return lax.ppermute(rows, ("sub", "pair"), [(0, 3), (1, 2), (2, 1), (3, 0)])

    def other_core(rows):
        return lax.ppermute(rows, "pair", [(0, 1), (1, 0)])

    (first,) = call(first_pack_kernel, [((slabs * half + LINES // 2, 128), BF16)], [embeddings])
    whole, second = call(
        pack_kernel,
        [((slabs * count + LINES, 128), BF16) for count in (rows_here, half)],
        [embeddings, group_of.reshape(line), cluster_id.reshape(line)],
    )
    along_by = [(first, second)]
    across_by = []
    for s in range(1, n_blk - 1):
        moved = [along(piece) for piece in along_by[-1]]
        swapped = [across(piece) for piece in along_by[-1]]
        moved[0], swapped[0] = together(moved[0], swapped[0])
        moved[1], swapped[1], _ = together(moved[1], swapped[1], moved[0])
        along_by.append(tuple(moved))
        across_by.append(tuple(swapped))
    near = along_by[1]
    over = [other_core(piece) for piece in near]
    over[0], _ = together(over[0], along_by[2][0])
    near_sum, *over_sum = call(
        back_kernel,
        [((rows_here, width + 128), F32)]
        + [((rows_here // PARTS, width + 128), BF16)] * PARTS,
        [*near, *over, first, second, *across_by[0]],
    )
    near_sum, _ = together(near_sum, along_by[2][1])
    (to_return,) = call(
        back_sum_kernel,
        [((slabs * rows_here + LINES, 128), BF16)],
        [near_sum, *[other_core(part) for part in over_sum]],
    )
    returned = back_along(to_return)
    first_crossed = across(along_by[-1][0])
    last_half, first_crossed = together(along_by[-1][1], first_crossed)
    across_by.append((first_crossed, across(last_half)))
    left = (whole, other_core(whole))
    early = across_by[:-1] + along_by[1:]
    mine, theirs, info = start_both(left, early, (rows_here, width + 128))
    late = [across_by[-1]]
    mine, *theirs = add_both((*left, info), late, (mine, theirs))
    out = finish(
        (rows_here, width), [mine, returned, *[other_core(part) for part in theirs]]
    )
    return out


def per_device(embeddings, group_of, cluster_id):
    rows_here, width = embeddings.shape
    devices = lax.axis_size("blk") * lax.axis_size("sub") * lax.axis_size("pair")
    small = devices * rows_here * width * 2 <= GATHER_LIMIT and lax.axis_size("blk") > 3
    fits = width % 128 == 0 and rows_here % (64 * PARTS) == 0 and rows_here <= 256
    if small and fits and lax.axis_size("sub") == 2 and lax.axis_size("pair") == 2:
        return by_block(embeddings, group_of, cluster_id)
    return by_group(embeddings, group_of, cluster_id)


def solution(mesh):
    return jax.shard_map(
        per_device,
        mesh=mesh,
        in_specs=(
            P(("island", "blk", "sub", "pair"), None),
            P(("island", "blk", "sub", "pair"), None),
            P(("island", "blk", "sub", "pair")),
        ),
        out_specs=P(("island", "blk", "sub", "pair"), None),
        check_vma=False,
    )
```
